32 devices in a mesh: groups: 2 (over x), dom: 16 (over z, y, core).
Axes of the slice: x: 2, y: 2, z: 4, core: 2. Of those that a mesh axis runs over, the one named last changes fastest.
Arguments:
- particle_fourier: float32 [3072, 1024], P(('groups', 'dom')), parts along dimension 0, may hold values from -90 to 90, as said below
- defocus: float32 [3072], P(('groups', 'dom')), parts along dimension 0, may hold values from 20 to 80
- particle_offset: int32 [3072, 2], P(('groups', 'dom')), parts along dimension 0, may hold values from -4 to 4
- prior_rotation: int32 [3072], P(('groups', 'dom')), parts along dimension 0, may hold values from 0 to 15
- group_id: int32 [3072], P(('groups', 'dom')), parts along dimension 0, may hold values from 0 to 127, never falling along the last dimension, each value on 1 to 24 neighbouring positions
- live_count: int32 [32], P(('groups', 'dom')), parts along dimension 0, may hold values from 24 to 96, as said below
- noise_power: float32 [256, 512], P('groups'), parts along dimension 0, may hold values from 0.5 to 2
- signal_power: float32 [1024], P('groups'), parts along dimension 0, may hold values from 0.5 to 4
- class_refs: float32 [64, 16, 1024], P(('groups', 'dom')), parts along dimension 0, may hold values from -0.5 to 0.5
Outputs:
- expected_shift: float32 [3072, 2], P(('groups', 'dom')), parts along dimension 0
- new_refs: float32 [64, 16, 1024], P(('groups', 'dom')), parts along dimension 0
The draws below stay inside these ranges and needn't reach their ends.
There are 2 independent parts, one for each index of `groups`. The reference program is written for one: setup_inputs(seed, part) draws one part's arguments, and reference() takes and returns one part's arrays. A program takes and returns all parts, laid end to end along the dimension named above; each array names one. Nothing has to cross between parts.
Inputs may be any that keep to these rules, and one draw needn't show every extreme that they name: `particle_fourier`: drawn alike for all particles. `live_count`: devices of even index along dom hold at most 96 live slots, and one of them exactly 96; devices of odd index at most 48, and one of them exactly that many. Live slots come first on each device.
All inputs are finite; a program needn't handle non-finite values.
Results may differ from the reference program's by a relative error of at most 0.0003.
Values sent between devices are 32-bit elements; how exact they have to be, the bound alone decides.
No kernel may reach another device: no remote copies, remote signals or barrier semaphores. Data moves between devices by JAX's collectives and lax.ppermute only.
A program may use at most 128 MiB of HBM per device.

```python
import math
import jax
import jax.numpy as jnp
import numpy as np
from jax import lax

SLOTS = 96
ROT = 16
SIDE = 3
BOX = 128
FY = 32
SHIFTS = 9
FREQ = 512
CLASSES = 32
PARTICLES = 1536
GROUPS = 128


def shared_draw(key):
    key_refs, key_focus, key_offsets = jax.random.split(key, 3)
    references = 0.125 * jax.random.truncated_normal(key_refs, -4.0, 4.0, (CLASSES, ROT, 2 * FREQ), jnp.float32)
    focus = jnp.exp(jax.random.uniform(key_focus, (PARTICLES,), jnp.float32, math.log(20.0), math.log(80.0)))
    offsets = jax.random.randint(key_offsets, (PARTICLES, 2), -4, 5, dtype=jnp.int32)
    return (references, focus, offsets)


def draw_class_refs(key, part):
    references, focus, offsets = shared_draw(key)
    return references


def draw_defocus(key, part):
    references, focus, offsets = shared_draw(key)
    return focus


def draw_particle_offset(key, part):
    references, focus, offsets = shared_draw(key)
    return offsets


def draw_particle_fourier(key, part):
    key = jax.random.fold_in(key, 7)
    subkeys = jax.random.split(key, 1)
    return jax.random.normal(subkeys[0], (PARTICLES, 2 * FREQ), jnp.float32)


def draw_live_count(key, part):
    key = jax.random.fold_in(key, 11)
    subkeys = jax.random.split(key, 4)
    devices = PARTICLES // SLOTS
    position = jnp.arange(devices, dtype=jnp.int32)
    heavy = jax.random.randint(subkeys[0], (devices,), SLOTS // 2, SLOTS + 1, dtype=jnp.int32)
    light = jax.random.randint(subkeys[1], (devices,), SLOTS // 4, SLOTS // 2 + 1, dtype=jnp.int32)
    full_even = 2 * jax.random.randint(subkeys[2], (), 0, devices // 2, dtype=jnp.int32)
    full_odd = 2 * jax.random.randint(subkeys[3], (), 0, devices // 2, dtype=jnp.int32) + 1
    counts = jnp.where(position % 2 == 0, heavy, light)
    counts = jnp.where(position == full_even, SLOTS, counts)
    counts = jnp.where(position == full_odd, SLOTS // 2, counts)
    return counts.astype(jnp.int32)


def set_ends(drawn, key, smallest, top_value):
    spot = [jax.random.randint(jax.random.fold_in(key, axis), (), 0, length) for axis, length in enumerate(drawn.shape)]
    widest = drawn.shape.index(max(drawn.shape))
    neighbour = spot[:widest] + [(spot[widest] + 1) % drawn.shape[widest]] + spot[widest + 1:]
    return drawn.at[tuple(spot)].set(smallest).at[tuple(neighbour)].set(top_value)


def length_profile(amount, total, most, slope):
    portions = [(1 << 20) // math.isqrt(standing ** slope) + 1 for standing in range(2, amount + 1)]
    surplus, given = total - most - (amount - 1), [1] * (amount - 1)
    while surplus > 0:
        free = [i for i in range(amount - 1) if given[i] < most]
        whole, budget = sum([portions[i] for i in free]), surplus
        for i in free:
            more = min(most - given[i], max(1, budget * portions[i] // whole), surplus)
            given[i] = given[i] + more
            surplus = surplus - more
    return np.array([most] + given)


def uneven_parts(key, number_of, total, bound, skew):
    if number_of == 2:
        one = jax.random.randint(key, (), max(1, total - bound), min(bound, total - 1) + 1)
        return jnp.stack([one, total - one])
    lengths = jnp.asarray(length_profile(number_of, total, bound, skew), jnp.int32)
    couples = (number_of - 1) // 2
    donor, taker = lengths[1:1 + 2 * couples:2], lengths[2:2 + 2 * couples:2]
    slack = jnp.minimum(donor - 1, bound - taker)
    passed = jax.random.randint(jax.random.fold_in(key, 1), (couples,), 0, 1 << 20) % (slack + 1)
    lengths = lengths.at[1:1 + 2 * couples:2].set(donor - passed).at[2:2 + 2 * couples:2].set(taker + passed)
    return lengths[jax.random.permutation(jax.random.fold_in(key, 2), number_of)]


def setup_inputs(seed: int = 0, part: int = 0) -> dict:
    key_list = jax.random.split(jax.random.key(seed), 10)
    part_splits = jax.random.split(jax.random.fold_in(key_list[9], part), 10)
    particle_fourier = draw_particle_fourier(jax.random.fold_in(jax.random.fold_in(key_list[9], part), 71), part)
    defocus = draw_defocus(jax.random.fold_in(jax.random.fold_in(key_list[9], part), 71), part)
    particle_offset = draw_particle_offset(jax.random.fold_in(jax.random.fold_in(key_list[9], part), 71), part)
    prior_rotation = set_ends(jax.random.randint(part_splits[3], (PARTICLES,), 0, ROT), jax.random.fold_in(part_splits[3], 1), 0, ROT - 1).astype(jnp.int32)
    group_id = jnp.searchsorted(jnp.cumsum(uneven_parts(part_splits[4], GROUPS, PARTICLES, 24, 2)), jnp.arange(PARTICLES), side="right").astype(jnp.int32)
    live_count = draw_live_count(jax.random.fold_in(jax.random.fold_in(key_list[9], part), 71), part)
    noise_power = jnp.clip(jnp.exp(jax.random.uniform(part_splits[6], (GROUPS, FREQ), jnp.float32, math.log(0.5), math.log(2.0))), 0.5, 2.0)
    signal_power = jnp.clip(jnp.exp(jax.random.uniform(part_splits[7], (FREQ,), jnp.float32, math.log(0.5), math.log(4.0))), 0.5, 4.0)
    class_refs = draw_class_refs(jax.random.fold_in(jax.random.fold_in(key_list[9], part), 71), part)
    return {"particle_fourier": particle_fourier, "defocus": defocus, "particle_offset": particle_offset, "prior_rotation": prior_rotation, "group_id": group_id, "live_count": live_count, "noise_power": noise_power, "signal_power": signal_power, "class_refs": class_refs}


prior_strength = 2.0


def freq_index():
    coeff = jnp.arange(FREQ, dtype=jnp.int32)
    freq_x = (coeff // FY).astype(jnp.float32)
    freq_y = (coeff % FY - FY // 2).astype(jnp.float32)
    return freq_x, freq_y


def shift_grid():
    shift_id = jnp.arange(SIDE * SIDE, dtype=jnp.int32)
    grid_x = (shift_id // SIDE - SIDE // 2).astype(jnp.float32)
    grid_y = (shift_id % SIDE - SIDE // 2).astype(jnp.float32)
    return grid_x, grid_y


def spectra(fourier, focus, offsets, noise_rows):
    freq_x, freq_y = freq_index()
    phase_chi = focus[:, None] * ((freq_x * freq_x + freq_y * freq_y) / 1024.0)[None, :]
    ctf = -(0.995 * jnp.sin(phase_chi) + 0.1 * jnp.cos(phase_chi))
    scaled = ctf / noise_rows
    ctf_power = ctf * scaled
    half_width = fourier.shape[1] // 2
    real_part = fourier[:, :half_width]
    imag_part = fourier[:, half_width:]
    grid_x, grid_y = shift_grid()
    total_x = offsets[:, 0].astype(jnp.float32)[:, None] + grid_x[None, :]
    total_y = offsets[:, 1].astype(jnp.float32)[:, None] + grid_y[None, :]
    angles = (2.0 * math.pi / BOX) * (freq_x[None, None, :] * total_x[:, :, None] + freq_y[None, None, :] * total_y[:, :, None])
    cosine = jnp.cos(angles)
    sine = jnp.sin(angles)
    shifted_real = scaled[:, None, :] * (real_part[:, None, :] * cosine - imag_part[:, None, :] * sine)
    shifted_imag = scaled[:, None, :] * (real_part[:, None, :] * sine + imag_part[:, None, :] * cosine)
    return jnp.concatenate([shifted_real, shifted_imag], axis=2), ctf_power


def block_scores(shifted_rows, ctf_power, prior_rows, ref_rows, first_col):
    particles_here = ctf_power.shape[0]
    half_width = ctf_power.shape[1]
    hypotheses = ref_rows.shape[0]
    cross = jnp.einsum("rf,kf->rk", shifted_rows, ref_rows, precision=lax.Precision.HIGHEST)
    power = ref_rows[:, :half_width] * ref_rows[:, :half_width] + ref_rows[:, half_width:] * ref_rows[:, half_width:]
    quadratic = jnp.einsum("pf,kf->pk", ctf_power, power, precision=lax.Precision.HIGHEST)
    rotation = (first_col + jnp.arange(hypotheses, dtype=jnp.int32)) % ROT
    distance = (rotation[None, :] - prior_rows[:, None]).astype(jnp.float32)
    prior_term = prior_strength * jnp.cos((2.0 * math.pi / ROT) * distance)
    return cross.reshape(particles_here, SHIFTS, hypotheses) - 0.5 * quadratic[:, None, :] + prior_term[:, None, :]


def posterior(scores):
    highest = jnp.max(scores, axis=(1, 2), keepdims=True)
    normaliser = jnp.sum(jnp.exp(scores - highest), axis=(1, 2), keepdims=True)
    weights = jnp.exp(scores - highest - jnp.log(normaliser))
    over_shifts = jnp.sum(weights, axis=2)
    grid_x, grid_y = shift_grid()
    shift_mean = jnp.stack([jnp.sum(over_shifts * grid_x[None, :], axis=1), jnp.sum(over_shifts * grid_y[None, :], axis=1)], axis=-1)
    return weights, shift_mean


def reference(particle_fourier, defocus, particle_offset, prior_rotation, group_id, live_count, noise_power, signal_power, class_refs):
    blocks = PARTICLES // SLOTS
    ref_rows = class_refs.reshape(CLASSES * ROT, 2 * FREQ)
    noise_rows = noise_power[group_id]
    positions = jnp.arange(PARTICLES, dtype=jnp.int32)
    live = ((positions % SLOTS) < live_count[positions // SLOTS]).astype(jnp.float32)

    def one_block(carry, inputs):
        fourier, focus, offsets, prior_rows, noise_block, live_rows = inputs
        shifted, ctf_power = spectra(fourier, focus, offsets, noise_block)
        shifted_rows = shifted.reshape(SLOTS * SHIFTS, 2 * FREQ)
        scores = block_scores(shifted_rows, ctf_power, prior_rows, ref_rows, jnp.int32(0))
        weights, shift_mean = posterior(scores)
        masked = weights * live_rows[:, None, None]
        data_part = jnp.einsum("rk,rf->kf", masked.reshape(SLOTS * SHIFTS, CLASSES * ROT), shifted_rows, precision=lax.Precision.HIGHEST)
        weight_part = jnp.einsum("pk,pf->kf", jnp.sum(masked, axis=1), ctf_power, precision=lax.Precision.HIGHEST)
        return (carry[0] + data_part, carry[1] + weight_part), shift_mean * live_rows[:, None]

    inputs = (particle_fourier.reshape(blocks, SLOTS, 2 * FREQ), defocus.reshape(blocks, SLOTS),
              particle_offset.reshape(blocks, SLOTS, 2), prior_rotation.reshape(blocks, SLOTS),
              noise_rows.reshape(blocks, SLOTS, FREQ), live.reshape(blocks, SLOTS))
    start = (jnp.zeros((CLASSES * ROT, 2 * FREQ), jnp.float32), jnp.zeros((CLASSES * ROT, FREQ), jnp.float32))
    (data_sum, weight_sum), shifts = lax.scan(one_block, start, inputs)
    inverse = 1.0 / signal_power
    denominator = weight_sum + inverse[None, :]
    updated = data_sum / jnp.concatenate([denominator, denominator], axis=1)
    return shifts.reshape(PARTICLES, 2), updated.reshape(CLASSES, ROT, 2 * FREQ)
```

```python
import math

import jax
import jax.numpy as jnp
from jax import lax
from jax.experimental import pallas as pl
from jax.experimental.pallas import tpu as pltpu
from jax.sharding import PartitionSpec as P

ROT = 16
SIDE = 3
BOX = 128
FY = 32
SHIFTS = 9
TEAM = 4
PRIOR = 2.0
CTF_SIZE = math.hypot(0.995, 0.1)
CTF_TURN = math.atan2(0.1, 0.995)
SINE = (
    9.99999976e-01,
    -1.66666476e-01,
    8.33289854e-03,
    -1.98008185e-04,
    2.59032780e-06,
)
TWO_PI = 2.0 * math.pi
PI_A = 3.140625
PI_B = 0.0009670257568359375
PI_C = math.pi - PI_A - PI_B
HIGHEST = lax.Precision.HIGHEST
GRID = tuple((t // SIDE - SIDE // 2, t % SIDE - SIDE // 2) for t in range(SHIFTS))
LIMIT = 56 * 1024 * 1024


def half_turn_sine(x):
    s = x * x
    p = SINE[4]
    for c in SINE[3::-1]:
        p = p * s + c
    return x * p


def turn_cos(turns):
    t = jnp.abs(turns - jnp.round(turns))
    return half_turn_sine(TWO_PI * (0.25 - t))


def turn_sin(turns):
    return turn_cos(turns - 0.25)


def freq_rows(width, rows):
    f = lax.broadcasted_iota(jnp.int32, (rows, width), 1)
    kx = (f // FY).astype(jnp.float32)
    ky = (f % FY - FY // 2).astype(jnp.float32)
    return kx, ky


def dot_nt(a, b):
    return lax.dot_general(
        a, b, (((1,), (1,)), ((), ())), precision=HIGHEST, preferred_element_type=jnp.float32
    )


def dot_nn(a, b):
    return lax.dot_general(
        a, b, (((1,), (0,)), ((), ())), precision=HIGHEST, preferred_element_type=jnp.float32
    )


def grid_phases(width):
    kx, ky = freq_rows(width, 1)
    out = []
    for t, (gx, gy) in enumerate(GRID):
        if t < SHIFTS // 2:
            m = (kx * gx + ky * gy) * (1.0 / BOX)
            out.append((turn_cos(m), turn_sin(m)))
    return out


def phase_of(phases, t):
    mid = SHIFTS // 2
    if t < mid:
        return phases[t]
    c, s = phases[SHIFTS - 1 - t]
    return c, -s


def score_kernel(blocks, slots, own, cnb, ynb, cynb, *rest):
    refs = rest[:blocks]
    noise, e_out, y_out, power_out, stats_out, raw, scal, sems = rest[blocks:]
    half = slots // 2
    group = slots + half
    live_rows = 2 * group
    width = own.shape[1]
    freq = width // 2
    me = lax.axis_index("dom")
    core = me % 2
    yy = (me // 2) % 2

    sources = ((own, 0, 0), (cnb, 0, 1), (ynb, 1, 0), (cynb, 1, 1))
    copies = []
    for n, (src, dy, dc) in enumerate(sources):
        y_s = (yy + dy) % 2
        c_s = (core + dc) % 2
        at = pl.multiple_of(y_s * group + c_s * slots, 8)
        low = pltpu.make_async_copy(
            src.at[pl.ds(0, half)], raw.at[pl.ds(at, half)], sems.at[n]
        )
        high = pltpu.make_async_copy(
            src.at[pl.ds(half, half)], raw.at[pl.ds(at + half, half)], sems.at[4 + n]
        )
        facts = pltpu.make_async_copy(
            src.at[pl.ds(slots, 8), pl.ds(0, 128)], scal.at[2 * y_s + c_s], sems.at[8 + n]
        )
        facts.start()
        low.start()

        @pl.when(c_s == 0)
        def _(high=high):
            high.start()

        copies.append((low, high, facts, c_s))

    inverse = 1.0 / noise[...]
    for low, high, facts, c_s in copies:
        facts.wait()

    lane = lax.broadcasted_iota(jnp.int32, (8, 128), 1)
    a, b, c, d = scal[0], scal[1], scal[2], scal[3]
    b96 = pltpu.roll(b, 96, 1)
    d112 = pltpu.roll(d, 112, 1)
    tiles = (
        jnp.where(lane < 96, a, b96),
        jnp.where(lane < 16, b96, jnp.where(lane < 112, pltpu.roll(c, 16, 1), d112)),
        jnp.where(lane < 32, d112, 0.0),
    )
    row_facts = jnp.concatenate(tiles, axis=1)[:, :live_rows]
    col_facts = jnp.concatenate(
        [jnp.concatenate([t, jnp.zeros((120, 128), jnp.float32)], axis=0).T for t in tiles], axis=0
    )[:live_rows]
    focus = col_facts[:, 0:1]
    off_x = col_facts[:, 1:2]
    off_y = col_facts[:, 2:3]
    group_col = col_facts[:, 4:5]

    total = noise.shape[0]
    onehot = (
        group_col == lax.broadcasted_iota(jnp.int32, (live_rows, total), 1).astype(jnp.float32)
    ).astype(jnp.float32)
    noise_rows = dot_nn(onehot, inverse)

    kx, ky = freq_rows(freq, 1)
    chi = focus * ((kx * kx + ky * ky) * (1.0 / 1024.0))
    k = jnp.round(chi * (1.0 / math.pi))
    rest_angle = ((chi - k * PI_A) - k * PI_B) - k * PI_C
    shifted_angle = rest_angle + CTF_TURN
    over = shifted_angle > (0.5 * math.pi)
    folded = jnp.where(over, math.pi - shifted_angle, shifted_angle)
    parity = 0.5 * k
    sign = (parity - jnp.floor(parity)) * (4.0 * CTF_SIZE) - CTF_SIZE
    ctf = half_turn_sine(folded) * sign
    scaled = ctf * noise_rows
    power = ctf * scaled
    power_out[...] = power

    kx0, ky0 = freq_rows(128, 1)
    m = (kx0 * off_x + ky0 * off_y) * (1.0 / BOX)
    pc, ps = turn_cos(m), turn_sin(m)
    step = off_x * ((128 // FY) / BOX) + jnp.zeros((live_rows, 128), jnp.float32)
    sc, ss = turn_cos(step), turn_sin(step)
    cos_parts, sin_parts = [], []
    for _ in range(freq // 128):
        cos_parts.append(pc)
        sin_parts.append(ps)
        pc, ps = pc * sc - ps * ss, ps * sc + pc * ss
    cosine = jnp.concatenate(cos_parts, axis=1) * scaled
    sine = jnp.concatenate(sin_parts, axis=1) * scaled

    for low, high, facts, c_s in copies:
        low.wait()

        @pl.when(c_s == 0)
        def _(high=high):
            high.wait()

    xr = raw[:, :freq]
    xi = raw[:, freq:]
    y_out[:, :freq] = xr * cosine - xi * sine
    y_out[:, freq:] = xr * sine + xi * cosine

    per = refs[0].shape[0]
    r = (lax.broadcasted_iota(jnp.int32, (per, live_rows), 0) % ROT).astype(jnp.float32)
    prior = PRIOR * turn_cos((r - row_facts[3:4, :]) * (1.0 / ROT))
    phases = grid_phases(freq)
    y = y_out[...]
    high = None
    for n in range(blocks):
        rr = refs[n][:, :freq]
        ri = refs[n][:, freq:]
        quad = dot_nt(rr * rr + ri * ri, power)
        base = prior - 0.5 * quad
        rows = []
        for t in range(SHIFTS):
            if t == SHIFTS // 2:
                rows.append(refs[n][...])
            else:
                cg, sg = phase_of(phases, t)
                rows.append(jnp.concatenate([rr * cg + ri * sg, ri * cg - rr * sg], axis=1))
        score = dot_nt(jnp.concatenate(rows, axis=0), y)
        score = score.reshape(SHIFTS, per, live_rows) + base[None]
        e_out[n] = score
        top = jnp.max(score, axis=0)
        high = top if high is None else jnp.maximum(high, top)
    high = jnp.max(high, axis=0, keepdims=True)
    sums = [jnp.zeros((per, live_rows), jnp.float32) for _ in range(SHIFTS)]
    for n in range(blocks):
        for t in range(SHIFTS):
            e = jnp.exp(e_out[n, t] - high)
            e_out[n, t] = e
            sums[t] = sums[t] + e
    sums = [jnp.sum(s, axis=0, keepdims=True) for s in sums]
    mass = sum(sums)
    mean_x = sum(s * float(gx) for s, (gx, gy) in zip(sums, GRID) if gx)
    mean_y = sum(s * float(gy) for s, (gx, gy) in zip(sums, GRID) if gy)
    stats_out[...] = jnp.zeros_like(stats_out)
    stats_out[0:1, :live_rows] = high
    stats_out[1:2, :live_rows] = mass
    stats_out[2:3, :live_rows] = mean_x
    stats_out[3:4, :live_rows] = mean_y
    stats_out[4:5, :live_rows] = row_facts[5:6, :]


def sum_kernel(stats_own, stats_all, e_ref, y_ref, power_ref, part_out, shift_out):
    live_rows, width = y_ref.shape
    freq = width // 2
    mine = stats_own[:, :live_rows]
    team = [stats_all[n][:, :live_rows] for n in range(TEAM)]
    top = team[0][0:1]
    for s in team[1:]:
        top = jnp.maximum(top, s[0:1])
    gains = [jnp.exp(s[0:1] - top) for s in team]
    mass = sum(g * s[1:2] for g, s in zip(gains, team))
    live = mine[4:5] / mass
    own_gain = jnp.exp(mine[0:1] - top) * live
    shift_out[...] = jnp.zeros_like(shift_out)
    shift_out[0:1, :live_rows] = sum(g * s[2:3] for g, s in zip(gains, team)) * live
    shift_out[1:2, :live_rows] = sum(g * s[3:4] for g, s in zip(gains, team)) * live
    per = e_ref.shape[1]
    w = e_ref[...] * own_gain[None]
    flat = dot_nn(w.reshape(SHIFTS * per, live_rows), y_ref[...])
    phases = grid_phases(freq)
    mid = SHIFTS // 2
    re = flat[mid * per : (mid + 1) * per, :freq]
    im = flat[mid * per : (mid + 1) * per, freq:]
    for t in range(SHIFTS):
        if t == mid:
            continue
        cg, sg = phase_of(phases, t)
        ar = flat[t * per : (t + 1) * per, :freq]
        ai = flat[t * per : (t + 1) * per, freq:]
        re = re + (ar * cg - ai * sg)
        im = im + (ar * sg + ai * cg)
    part_out[:, :freq] = re
    part_out[:, freq:width] = im
    part_out[:, width:] = dot_nn(jnp.sum(w, axis=0), power_ref[...])


def final_kernel(own, others, signal, out):
    width = out.shape[1]
    freq = width // 2
    total = own[...]
    for n in range(others.shape[0]):
        total = total + others[n]
    denominator = total[:, width:] + 1.0 / signal[...]
    out[:, :freq] = total[:, :freq] / denominator
    out[:, freq:] = total[:, freq:width] / denominator


def params():
    return pltpu.CompilerParams(vmem_limit_bytes=LIMIT)


def crossed(block, mask):
    size = lax.axis_size("dom")
    return lax.ppermute(block, "dom", [(i, i ^ mask) for i in range(size)])


def on_device(
    particle_fourier,
    defocus,
    particle_offset,
    prior_rotation,
    group_id,
    live_count,
    noise_power,
    signal_power,
    class_refs,
):
    slots, width = particle_fourier.shape
    freq = width // 2
    live_rows = 3 * slots
    size = lax.axis_size("dom")
    blocks = size // TEAM
    refs_own = class_refs.reshape(-1, width)
    per = refs_own.shape[0]

    live = (jnp.arange(slots, dtype=jnp.int32) < live_count[0]).astype(jnp.float32)
    facts = jnp.stack(
        [
            defocus,
            particle_offset[:, 0].astype(jnp.float32),
            particle_offset[:, 1].astype(jnp.float32),
            prior_rotation.astype(jnp.float32),
            group_id.astype(jnp.float32),
            live,
        ]
    )
    facts = jnp.pad(facts, ((0, 2), (0, width - slots)))
    packed = jnp.concatenate([particle_fourier, facts], axis=0)
    ynb = crossed(packed, 2)
    cnb = crossed(packed, 1)
    refs = [refs_own] + [crossed(refs_own, TEAM * n) for n in range(1, blocks)]
    cynb = crossed(ynb, 1)

    anywhere = pl.BlockSpec(memory_space=pl.ANY)
    vmem = pl.BlockSpec(memory_space=pltpu.VMEM)
    f32 = jnp.float32
    e_all, y, power, stats = pl.pallas_call(
        lambda *a: score_kernel(blocks, slots, *a),
        out_shape=(
            jax.ShapeDtypeStruct((blocks, SHIFTS, per, live_rows), f32),
            jax.ShapeDtypeStruct((live_rows, width), f32),
            jax.ShapeDtypeStruct((live_rows, freq), f32),
            jax.ShapeDtypeStruct((8, 384), f32),
        ),
        in_specs=[anywhere] * 4 + [vmem] * (blocks + 1),
        out_specs=(vmem,) * 4,
        scratch_shapes=[
            pltpu.VMEM((live_rows, width), f32),
            pltpu.VMEM((4, 8, 128), f32),
            pltpu.SemaphoreType.DMA((12,)),
        ],
        compiler_params=params(),
        name="scores",
    )(packed, cnb, ynb, cynb, *refs, noise_power)

    teams = [[TEAM * n + j for j in range(TEAM)] for n in range(blocks)]
    stats_all = lax.all_to_all(
        jnp.broadcast_to(stats[None], (TEAM, 8, 384)),
        "dom",
        0,
        0,
        axis_index_groups=teams,
        tiled=True,
    )

    def sums(n):
        return pl.pallas_call(
            sum_kernel,
            grid=(1,),
            out_shape=(
                jax.ShapeDtypeStruct((per, width + freq), f32),
                jax.ShapeDtypeStruct((8, 384), f32),
            ),
            in_specs=[
                pl.BlockSpec((8, 384), lambda i: (0, 0)),
                pl.BlockSpec((TEAM, 8, 384), lambda i: (0, 0, 0)),
                pl.BlockSpec((None, SHIFTS, per, live_rows), lambda i: (n, 0, 0, 0)),
                pl.BlockSpec((live_rows, width), lambda i: (0, 0)),
                pl.BlockSpec((live_rows, freq), lambda i: (0, 0)),
            ],
            out_specs=(
                pl.BlockSpec((per, width + freq), lambda i: (0, 0)),
                pl.BlockSpec((8, 384), lambda i: (0, 0)),
            ),
            compiler_params=params(),
            name="sums",
        )(stats, stats_all, e_all, y, power)

    arrived = []
    for n in sorted(range(1, blocks), key=lambda n: -n):
        part, _ = sums(n)
        arrived.append(crossed(part, TEAM * n))
    own_part, shift_rows = sums(0)

    refs_new = pl.pallas_call(
        final_kernel,
        out_shape=jax.ShapeDtypeStruct((per, width), f32),
        in_specs=[vmem] * 3,
        out_specs=vmem,
        compiler_params=params(),
        name="update",
    )(own_part, jnp.stack(arrived), signal_power.reshape(1, freq))

    me = lax.axis_index("dom")
    half = slots // 2
    at = (me // 2) % 2 * (slots + half) + me % 2 * slots
    at = jnp.minimum(at, live_rows - half)
    low = lax.dynamic_slice(shift_rows, (0, at), (2, half))
    high = lax.dynamic_slice(shift_rows, (0, at + half), (2, half))
    high = jnp.where(me % 2 == 0, high, 0.0)
    expected = jnp.concatenate([low, high], axis=1).T
    return (expected, refs_new.reshape(class_refs.shape))


def solution(mesh):
    in_specs = (
        P(("groups", "dom"), None),
        P(("groups", "dom")),
        P(("groups", "dom"), None),
        P(("groups", "dom")),
        P(("groups", "dom")),
        P(("groups", "dom")),
        P("groups", None),
        P("groups"),
        P(("groups", "dom"), None, None),
    )
    out_specs = (P(("groups", "dom"), None), P(("groups", "dom"), None, None))
    return jax.shard_map(
        on_device, mesh=mesh, in_specs=in_specs, out_specs=out_specs, check_vma=False
    )
```

```python
import math

import jax
import jax.numpy as jnp
from jax import lax
from jax.experimental import pallas as pl
from jax.experimental.pallas import tpu as pltpu
from jax.sharding import PartitionSpec as P

ROT = 16
SIDE = 3
BOX = 128
FY = 32
SHIFTS = 9
TEAM = 4
PRIOR = 2.0
CTF_SIZE = math.hypot(0.995, 0.1)
CTF_TURN = math.atan2(0.1, 0.995)
SINE = (
    9.99999976e-01,
    -1.66666476e-01,
    8.33289854e-03,
    -1.98008185e-04,
    2.59032780e-06,
)
TWO_PI = 2.0 * math.pi
PI_A = 3.140625
PI_B = 0.0009670257568359375
PI_C = math.pi - PI_A - PI_B
HIGHEST = lax.Precision.HIGHEST
GRID = tuple((t // SIDE - SIDE // 2, t % SIDE - SIDE // 2) for t in range(SHIFTS))


def half_turn_sine(x):
    s = x * x
    p = SINE[4]
    for c in SINE[3::-1]:
        p = p * s + c
    return x * p


def turn_cos(turns):
    t = jnp.abs(turns - jnp.round(turns))
    return half_turn_sine(TWO_PI * (0.25 - t))


def turn_sin(turns):
    return turn_cos(turns - 0.25)


def freq_rows(width, rows):
    f = lax.broadcasted_iota(jnp.int32, (rows, width), 1)
    kx = (f // FY).astype(jnp.float32)
    ky = (f % FY - FY // 2).astype(jnp.float32)
    return kx, ky


def dot_nt(a, b):
    return lax.dot_general(
        a, b, (((1,), (1,)), ((), ())), preferred_element_type=jnp.float32
    )


def dot_nn(a, b):
    return lax.dot_general(
        a, b, (((1,), (0,)), ((), ())), preferred_element_type=jnp.float32
    )


def exact_dot_nn(a, b):
    return lax.dot_general(
        a, b, (((1,), (0,)), ((), ())), precision=HIGHEST, preferred_element_type=jnp.float32
    )


def halves(x):
    high = x.astype(jnp.bfloat16)
    return high, (x - high.astype(jnp.float32)).astype(jnp.bfloat16)


def deep_rows(high, low):
    rows = high.shape[0]
    main = rows // 256 * 256
    left = rows - main
    parts = [high[:main], low[:main], high[:main], high[main:], low[main:], high[main:]]
    parts.append(jnp.zeros((128 - 3 * left, high.shape[1]), high.dtype))
    return jnp.concatenate(parts, axis=0)


def deep_lanes(x):
    rows, lanes = x.shape
    main = lanes // 256 * 256
    left = lanes - main
    high, low = halves(x[:, :main])
    tail = jnp.concatenate(
        [x[:, main:], jnp.zeros((rows, 128 - left), jnp.float32)], axis=1
    )
    tail_high = tail.astype(jnp.bfloat16).astype(jnp.float32)
    tail_low = tail - tail_high
    mixed = tail_high + pltpu.roll(tail_high, left, 1) + pltpu.roll(tail_low, 2 * left, 1)
    return jnp.concatenate([high, high, low, mixed.astype(jnp.bfloat16)], axis=1)


def grid_phases(width):
    kx, ky = freq_rows(width, 1)
    out = []
    for t, (gx, gy) in enumerate(GRID):
        if t < SHIFTS // 2:
            m = (kx * gx + ky * gy) * (1.0 / BOX)
            out.append((turn_cos(m), turn_sin(m)))
    return out


def phase_of(phases, t):
    mid = SHIFTS // 2
    if t < mid:
        return phases[t]
    c, s = phases[SHIFTS - 1 - t]
    return c, -s


def facts_kernel(own_facts, ynb_facts, noise, out, rows_out):
    both, freq = out.shape[0], out.shape[1] // 3
    slots = both // 2
    first = (lax.axis_index("dom") // 2) % 2 == 0
    rows_own, rows_ynb = own_facts[...], ynb_facts[...]
    col_facts = jnp.concatenate(
        [
            jnp.concatenate([t, jnp.zeros((120, 128), jnp.float32)], axis=0).T[:slots]
            for t in (rows_own, rows_ynb)
        ],
        axis=0,
    )
    focus = col_facts[:, 0:1]
    off_x = col_facts[:, 1:2]
    off_y = col_facts[:, 2:3]
    group_col = col_facts[:, 4:5]

    total = noise.shape[0]
    onehot = (
        group_col == lax.broadcasted_iota(jnp.int32, (both, total), 1).astype(jnp.float32)
    ).astype(jnp.float32)
    noise_rows = exact_dot_nn(onehot, 1.0 / noise[...])

    kx, ky = freq_rows(freq, 1)
    chi = focus * ((kx * kx + ky * ky) * (1.0 / 1024.0))
    k = jnp.round(chi * (1.0 / math.pi))
    rest_angle = ((chi - k * PI_A) - k * PI_B) - k * PI_C
    shifted_angle = rest_angle + CTF_TURN
    over = shifted_angle > (0.5 * math.pi)
    folded = jnp.where(over, math.pi - shifted_angle, shifted_angle)
    parity = 0.5 * k
    sign = (parity - jnp.floor(parity)) * (4.0 * CTF_SIZE) - CTF_SIZE
    ctf = half_turn_sine(folded) * sign
    scaled = ctf * noise_rows
    power = ctf * scaled

    kx0, ky0 = freq_rows(128, 1)
    m = (kx0 * off_x + ky0 * off_y) * (1.0 / BOX)
    pc, ps = turn_cos(m), turn_sin(m)
    step = off_x * ((128 // FY) / BOX) + jnp.zeros((both, 128), jnp.float32)
    sc, ss = turn_cos(step), turn_sin(step)
    for n in range(freq // 128):
        part = slice(128 * n, 128 * (n + 1))
        twin = slice(freq + 128 * n, freq + 128 * (n + 1))
        out[:, part] = pc * scaled[:, part]
        out[:, twin] = ps * scaled[:, part]
        pc, ps = pc * sc - ps * ss, ps * sc + pc * ss
    out[:, 2 * freq :] = power

    lane = lax.broadcasted_iota(jnp.int32, (8, 128), 1)
    a = jnp.where(first, rows_own, rows_ynb)
    b = pltpu.roll(jnp.where(first, rows_ynb, rows_own), slots, 1)
    rows_out[:, :128] = jnp.where(lane < slots, a, b)
    rows_out[:, 128:] = b


def prepare_kernel(own, ynb, spectrum, rows, *rest):
    out = rest[-1]
    slots, width = own.shape
    freq = width // 2
    both = 2 * slots
    first = (lax.axis_index("dom") // 2) % 2 == 0
    at_own = pl.multiple_of(jnp.where(first, 0, slots), 8)
    at_ynb = pl.multiple_of(jnp.where(first, slots, 0), 8)
    for src, rows_of, at in ((own, slice(0, slots), at_own), (ynb, slice(slots, both), at_ynb)):
        to = pl.ds(at, slots)
        xr, xi = src[:, :freq], src[:, freq:]
        co, si = spectrum[rows_of, :freq], spectrum[rows_of, freq:width]
        out[to, :freq] = xr * co - xi * si
        out[to, freq:width] = xr * si + xi * co
        out[to, width:] = spectrum[rows_of, width:]
    out[both:, :256] = rows[...]
    out[both:, 256:] = jnp.zeros((8, width + freq - 256), jnp.float32)


def score_kernel(blocks, mine, other, *rest):
    refs = rest[:blocks]
    e_out, y_out, power_out, stats_out, y_high, y_low, p_high, p_low = rest[blocks:]
    width = y_high.shape[1]
    freq = width // 2
    both = mine.shape[0] - 8
    slots = both // 2
    half = slots // 2
    live_rows = both + slots
    even = lax.axis_index("dom") % 2 == 0

    def place(src, at, to, size):
        rows = slice(at, at + size)
        dest = slice(to, to + size)
        high, low = halves(src[rows, :width])
        y_high[dest] = high
        y_low[dest] = low
        high, low = halves(src[rows, width:])
        p_high[dest] = high
        p_low[dest] = low

    def place_all(heavy, light):
        place(heavy, 0, 0, both)
        place(light, 0, both, half)
        place(light, slots, both + half, half)

    @pl.when(even)
    def _():
        place_all(mine, other)

    @pl.when(jnp.logical_not(even))
    def _():
        place_all(other, mine)

    lane = lax.broadcasted_iota(jnp.int32, (8, 128), 1)
    mine0, mine1 = mine[both:, :128], mine[both:, 128:256]
    other0, other1 = other[both:, :128], other[both:, 128:256]
    a0, a1 = jnp.where(even, mine0, other0), jnp.where(even, mine1, other1)
    b0, b1 = jnp.where(even, other0, mine0), jnp.where(even, other1, mine1)
    b0_16 = pltpu.roll(b0, 16, 1)
    row_facts = jnp.concatenate(
        [
            a0,
            jnp.where(lane < 64, a1, jnp.where(lane < 112, pltpu.roll(b0, 64, 1), b0_16)),
            jnp.where(lane < 16, b0_16, pltpu.roll(b1, 16, 1)),
        ],
        axis=1,
    )[:, :live_rows]

    yh, yl = y_high[...], y_low[...]
    y_out[...] = deep_rows(yh, yl)
    ph, plow = p_high[...], p_low[...]
    power_out[...] = deep_rows(ph, plow)

    per = refs[0].shape[0]
    r = (lax.broadcasted_iota(jnp.int32, (per, live_rows), 0) % ROT).astype(jnp.float32)
    prior = PRIOR * turn_cos((r - row_facts[3:4, :]) * (1.0 / ROT))
    phases = grid_phases(freq)
    high = None
    for n in range(blocks):
        rr = refs[n][:, :freq]
        ri = refs[n][:, freq:]
        qh, ql = halves(rr * rr + ri * ri)
        quad = dot_nt(qh, ph) + dot_nt(ql, ph) + dot_nt(qh, plow)
        base = prior - 0.5 * quad
        rows = []
        for t in range(SHIFTS):
            if t == SHIFTS // 2:
                rows.append(refs[n][...])
            else:
                cg, sg = phase_of(phases, t)
                rows.append(jnp.concatenate([rr * cg + ri * sg, ri * cg - rr * sg], axis=1))
        rh, rl = halves(jnp.concatenate(rows, axis=0))
        score = dot_nt(rh, yh) + dot_nt(rl, yh) + dot_nt(rh, yl)
        score = score.reshape(SHIFTS, per, live_rows) + base[None]
        e_out[n] = score
        top = jnp.max(score, axis=0)
        high = top if high is None else jnp.maximum(high, top)
    high = jnp.max(high, axis=0, keepdims=True)
    sums = [jnp.zeros((per, live_rows), jnp.float32) for _ in range(SHIFTS)]
    for n in range(blocks):
        for t in range(SHIFTS):
            e = jnp.exp(e_out[n, t] - high)
            e_out[n, t] = e
            sums[t] = sums[t] + e
    sums = [jnp.sum(s, axis=0, keepdims=True) for s in sums]
    mass = sum(sums)
    mean_x = sum(s * float(gx) for s, (gx, gy) in zip(sums, GRID) if gx)
    mean_y = sum(s * float(gy) for s, (gx, gy) in zip(sums, GRID) if gy)
    stats_out[...] = jnp.zeros_like(stats_out)
    stats_out[0:1, :live_rows] = high
    stats_out[1:2, :live_rows] = mass
    stats_out[2:3, :live_rows] = mean_x
    stats_out[3:4, :live_rows] = mean_y
    stats_out[4:5, :live_rows] = row_facts[5:6, :]


def sum_kernel(n, own, s1, s2, s3, e_ref, y_ref, power_ref, part_out, shift_out):
    live_rows = e_ref.shape[3]
    width = y_ref.shape[1]
    freq = width // 2
    team = [s[:, :live_rows] for s in (own, s1, s2, s3)]
    top = team[0][0:1]
    for s in team[1:]:
        top = jnp.maximum(top, s[0:1])
    gains = [jnp.exp(s[0:1] - top) for s in team]
    mass = sum(g * s[1:2] for g, s in zip(gains, team))
    live = team[0][4:5] / mass
    own_gain = gains[0] * live
    shift_out[...] = jnp.zeros_like(shift_out)
    shift_out[0:1, :live_rows] = sum(g * s[2:3] for g, s in zip(gains, team)) * live
    shift_out[1:2, :live_rows] = sum(g * s[3:4] for g, s in zip(gains, team)) * live
    per = e_ref.shape[2]
    w = e_ref[n] * own_gain[None]
    flat = dot_nn(deep_lanes(w.reshape(SHIFTS * per, live_rows)), y_ref[...])
    phases = grid_phases(freq)
    mid = SHIFTS // 2
    re = flat[mid * per : (mid + 1) * per, :freq]
    im = flat[mid * per : (mid + 1) * per, freq:]
    for t in range(SHIFTS):
        if t == mid:
            continue
        cg, sg = phase_of(phases, t)
        ar = flat[t * per : (t + 1) * per, :freq]
        ai = flat[t * per : (t + 1) * per, freq:]
        re = re + (ar * cg - ai * sg)
        im = im + (ar * sg + ai * cg)
    part_out[:, :freq] = re
    part_out[:, freq:width] = im
    part_out[:, width:] = dot_nn(deep_lanes(jnp.sum(w, axis=0)), power_ref[...])


def final_kernel(*refs):
    own, *others, signal, out = refs
    width = out.shape[1]
    freq = width // 2
    total = own[...]
    for other in others:
        total = total + other[...]
    denominator = total[:, width:] + 1.0 / signal[...]
    out[:, :freq] = total[:, :freq] / denominator
    out[:, freq:] = total[:, freq:width] / denominator


def params(blocks):
    return pltpu.CompilerParams(vmem_limit_bytes=(12 + 2 * blocks) * 1024 * 1024)


def crossed(block, mask):
    size = lax.axis_size("dom")
    return lax.ppermute(block, "dom", [(i, i ^ mask) for i in range(size)])


def on_device(
    particle_fourier,
    defocus,
    particle_offset,
    prior_rotation,
    group_id,
    live_count,
    noise_power,
    signal_power,
    class_refs,
):
    slots, width = particle_fourier.shape
    freq = width // 2
    live_rows = 3 * slots
    size = lax.axis_size("dom")
    blocks = size // TEAM
    refs_own = class_refs.reshape(-1, width)
    per = refs_own.shape[0]
    f32 = jnp.float32
    vmem = pl.BlockSpec(memory_space=pltpu.VMEM)
    no_cost = pl.CostEstimate(flops=0, bytes_accessed=0, transcendentals=0)

    ynb = crossed(particle_fourier, 2)
    refs = [refs_own] + [crossed(refs_own, TEAM * n) for n in range(1, blocks)]
    live = (jnp.arange(slots, dtype=jnp.int32) < live_count[0]).astype(f32)
    facts = jnp.stack(
        [
            defocus,
            particle_offset[:, 0].astype(f32),
            particle_offset[:, 1].astype(f32),
            prior_rotation.astype(f32),
            group_id.astype(f32),
            live,
        ]
    )
    facts = jnp.pad(facts, ((0, 2), (0, 128 - slots)))
    spectrum, rows = pl.pallas_call(
        facts_kernel,
        out_shape=(
            jax.ShapeDtypeStruct((2 * slots, width + freq), f32),
            jax.ShapeDtypeStruct((8, 256), f32),
        ),
        in_specs=[vmem] * 3,
        out_specs=(vmem,) * 2,
        compiler_params=params(blocks),
        cost_estimate=no_cost,
        name="facts",
    )(facts, crossed(facts, 2), noise_power)
    anywhere = pl.BlockSpec(memory_space=pl.ANY)
    prepared = pl.pallas_call(
        prepare_kernel,
        out_shape=jax.ShapeDtypeStruct((2 * slots + 8, width + freq), f32),
        in_specs=[vmem] * 4 + [anywhere] * (blocks - 1),
        out_specs=vmem,
        compiler_params=params(blocks),
        cost_estimate=no_cost,
        name="prepare",
    )(particle_fourier, ynb, spectrum, rows, *refs[1:])
    partner = crossed(prepared, 1)

    deep = 3 * (live_rows // 256 * 256) + 128
    bf16 = jnp.bfloat16
    e_all, y, power, stats = pl.pallas_call(
        lambda *a: score_kernel(blocks, *a),
        out_shape=(
            jax.ShapeDtypeStruct((blocks, SHIFTS, per, live_rows), f32),
            jax.ShapeDtypeStruct((deep, width), bf16),
            jax.ShapeDtypeStruct((deep, freq), bf16),
            jax.ShapeDtypeStruct((8, 384), f32),
        ),
        in_specs=[vmem] * (blocks + 2),
        out_specs=(vmem,) * 4,
        scratch_shapes=[
            pltpu.VMEM((live_rows, width), bf16),
            pltpu.VMEM((live_rows, width), bf16),
            pltpu.VMEM((live_rows, freq), bf16),
            pltpu.VMEM((live_rows, freq), bf16),
        ],
        compiler_params=params(blocks),
        name="scores",
    )(prepared, partner, *refs)

    team = [stats] + [crossed(stats, n) for n in range(1, TEAM)]

    def sums(n):
        return pl.pallas_call(
            lambda *a: sum_kernel(n, *a),
            out_shape=(
                jax.ShapeDtypeStruct((per, width + freq), f32),
                jax.ShapeDtypeStruct((8, 384), f32),
            ),
            in_specs=[vmem] * (TEAM + 3),
            out_specs=(vmem,) * 2,
            compiler_params=params(blocks),
            name="sums",
        )(*team, e_all, y, power)

    arrived = []
    for n in range(blocks - 1, 0, -1):
        part, _ = sums(n)
        arrived.append(crossed(part, TEAM * n))
    own_part, shift_rows = sums(0)

    refs_new = pl.pallas_call(
        final_kernel,
        out_shape=jax.ShapeDtypeStruct((per, width), f32),
        in_specs=[vmem] * (blocks + 1),
        out_specs=vmem,
        compiler_params=params(blocks),
        name="update",
    )(own_part, *arrived[::-1], signal_power.reshape(1, freq))

    me = lax.axis_index("dom")
    half = slots // 2
    odd = me % 2
    at = (me // 2) % 2 * jnp.where(odd == 0, slots, half) + odd * (2 * slots)
    low = lax.dynamic_slice(shift_rows, (0, at), (2, half))
    high = lax.dynamic_slice(shift_rows, (0, at + half), (2, half))
    high = jnp.where(odd == 0, high, 0.0)
    expected = jnp.concatenate([low, high], axis=1).T
    return (expected, refs_new.reshape(class_refs.shape))


def solution(mesh):
    in_specs = (
        P(("groups", "dom"), None),
        P(("groups", "dom")),
        P(("groups", "dom"), None),
        P(("groups", "dom")),
        P(("groups", "dom")),
        P(("groups", "dom")),
        P("groups", None),
        P("groups"),
        P(("groups", "dom"), None, None),
    )
    out_specs = (P(("groups", "dom"), None), P(("groups", "dom"), None, None))
    return jax.shard_map(
        on_device, mesh=mesh, in_specs=in_specs, out_specs=out_specs, check_vma=False
    )
```

```python
import math

import jax
import jax.numpy as jnp
from jax import lax
from jax.experimental import pallas as pl
from jax.experimental.pallas import tpu as pltpu
from jax.sharding import PartitionSpec as P

ROT = 16
SIDE = 3
BOX = 128
FY = 32
SHIFTS = 9
TEAM = 4
PRIOR = 2.0
CTF_SIZE = math.hypot(0.995, 0.1)
CTF_TURN = math.atan2(0.1, 0.995)
SINE = (
    9.99999976e-01,
    -1.66666476e-01,
    8.33289854e-03,
    -1.98008185e-04,
    2.59032780e-06,
)
TWO_PI = 2.0 * math.pi
PI_A = 3.140625
PI_B = 0.0009670257568359375
PI_C = math.pi - PI_A - PI_B
HIGHEST = lax.Precision.HIGHEST
GRID = tuple((t // SIDE - SIDE // 2, t % SIDE - SIDE // 2) for t in range(SHIFTS))


def half_turn_sine(x):
    s = x * x
    p = SINE[4]
    for c in SINE[3::-1]:
        p = p * s + c
    return x * p


def turn_cos(turns):
    t = jnp.abs(turns - jnp.round(turns))
    return half_turn_sine(TWO_PI * (0.25 - t))


def turn_sin(turns):
    return turn_cos(turns - 0.25)


def freq_rows(width, rows):
    f = lax.broadcasted_iota(jnp.int32, (rows, width), 1)
    kx = (f // FY).astype(jnp.float32)
    ky = (f % FY - FY // 2).astype(jnp.float32)
    return kx, ky


def dot_nt(a, b):
    return lax.dot_general(
        a, b, (((1,), (1,)), ((), ())), preferred_element_type=jnp.float32
    )


def dot_nn(a, b):
    return lax.dot_general(
        a, b, (((1,), (0,)), ((), ())), preferred_element_type=jnp.float32
    )


def exact_dot_nn(a, b):
    return lax.dot_general(
        a, b, (((1,), (0,)), ((), ())), precision=HIGHEST, preferred_element_type=jnp.float32
    )


def halves(x):
    high = x.astype(jnp.bfloat16)
    return high, (x - high.astype(jnp.float32)).astype(jnp.bfloat16)


def deep_rows(high, low):
    rows = high.shape[0]
    main = rows // 256 * 256
    left = rows - main
    parts = [high[:main], low[:main], high[:main], high[main:], low[main:], high[main:]]
    parts.append(jnp.zeros((128 - 3 * left, high.shape[1]), high.dtype))
    return jnp.concatenate(parts, axis=0)


def deep_lanes(x):
    rows, lanes = x.shape
    main = lanes // 256 * 256
    left = lanes - main
    high, low = halves(x[:, :main])
    tail = jnp.concatenate(
        [x[:, main:], jnp.zeros((rows, 128 - left), jnp.float32)], axis=1
    )
    tail_high = tail.astype(jnp.bfloat16).astype(jnp.float32)
    tail_low = tail - tail_high
    mixed = tail_high + pltpu.roll(tail_high, left, 1) + pltpu.roll(tail_low, 2 * left, 1)
    return jnp.concatenate([high, high, low, mixed.astype(jnp.bfloat16)], axis=1)


def grid_phases(width):
    kx, ky = freq_rows(width, 1)
    out = []
    for t, (gx, gy) in enumerate(GRID):
        if t < SHIFTS // 2:
            m = (kx * gx + ky * gy) * (1.0 / BOX)
            out.append((turn_cos(m), turn_sin(m)))
    return out


def phase_of(phases, t):
    mid = SHIFTS // 2
    if t < mid:
        return phases[t]
    c, s = phases[SHIFTS - 1 - t]
    return c, -s


def prepared_rows(src, facts, inverse_noise, out):
    slots, width = src.shape
    freq = width // 2
    columns = jnp.concatenate([facts, jnp.zeros((120, 128), jnp.float32)], axis=0).T[:slots]
    focus = columns[:, 0:1]
    off_x = columns[:, 1:2]
    off_y = columns[:, 2:3]
    group_col = columns[:, 4:5]

    kx, ky = freq_rows(freq, 1)
    chi = focus * ((kx * kx + ky * ky) * (1.0 / 1024.0))
    k = jnp.round(chi * (1.0 / math.pi))
    rest_angle = ((chi - k * PI_A) - k * PI_B) - k * PI_C
    shifted_angle = rest_angle + CTF_TURN
    over = shifted_angle > (0.5 * math.pi)
    folded = jnp.where(over, math.pi - shifted_angle, shifted_angle)
    parity = 0.5 * k
    sign = (parity - jnp.floor(parity)) * (4.0 * CTF_SIZE) - CTF_SIZE
    ctf = half_turn_sine(folded) * sign
    kx0, ky0 = freq_rows(128, 1)
    m = (kx0 * off_x + ky0 * off_y) * (1.0 / BOX)
    pc, ps = turn_cos(m), turn_sin(m)
    step = off_x * ((128 // FY) / BOX) + jnp.zeros((slots, 128), jnp.float32)
    sc, ss = turn_cos(step), turn_sin(step)

    total = inverse_noise.shape[0]
    onehot = (
        group_col == lax.broadcasted_iota(jnp.int32, (slots, total), 1).astype(jnp.float32)
    ).astype(jnp.float32)
    noise_rows = exact_dot_nn(onehot, inverse_noise)
    scaled = ctf * noise_rows
    out[:slots, width:] = ctf * scaled
    for n in range(freq // 128):
        part = slice(128 * n, 128 * (n + 1))
        twin = slice(freq + 128 * n, freq + 128 * (n + 1))
        co = pc * scaled[:, part]
        si = ps * scaled[:, part]
        pc, ps = pc * sc - ps * ss, ps * sc + pc * ss
        xr, xi = src[:, part], src[:, twin]
        out[:slots, part] = xr * co - xi * si
        out[:slots, twin] = xr * si + xi * co
    out[slots:, :128] = facts
    out[slots:, 128:] = jnp.zeros((8, width + freq - 128), jnp.float32)


def own_kernel(
    src_at, focus_at, offsets_at, prior_at, group_at, noise_at, live_count, out, facts_out,
    inverse_out, src, focus, offsets, prior, group, noise, sems
):
    moves = (
        (focus_at, focus), (offsets_at, offsets), (prior_at, prior), (group_at, group),
        (noise_at, noise), (src_at, src),
    )
    copies = [pltpu.make_async_copy(x, y, sems.at[n]) for n, (x, y) in enumerate(moves)]
    for copy in copies:
        copy.start()
    slots = src.shape[0]
    facts_out[...] = jnp.zeros_like(facts_out)
    slot = lax.broadcasted_iota(jnp.int32, (1, slots), 1)
    facts_out[5:6, :slots] = (slot < live_count[0]).astype(jnp.float32)
    for copy in copies:
        copy.wait()
    facts_out[0:1, :slots] = focus[...]
    facts_out[1:3, :slots] = offsets[...].astype(jnp.float32)
    facts_out[3:4, :slots] = prior[...].astype(jnp.float32)
    facts_out[4:5, :slots] = group[...].astype(jnp.float32)
    inverse = 1.0 / noise[...]
    inverse_out[...] = inverse
    prepared_rows(src, facts_out[...], inverse, out)


def neighbour_kernel(src, facts, inverse_noise, out):
    prepared_rows(src, facts[...], inverse_noise[...], out)


def score_kernel(blocks, own, cnb, ynb, cynb, *rest):
    refs = rest[:blocks]
    e_outs = rest[blocks : 2 * blocks]
    y_out, power_out, stats_out, y_high, y_low, p_high, p_low = rest[2 * blocks :]
    width = y_high.shape[1]
    freq = width // 2
    slots = own.shape[0] - 8
    half = slots // 2
    live_rows = 3 * slots
    me = lax.axis_index("dom")
    even = me % 2 == 0
    first = (me // 2) % 2 == 0

    def place(src, to, size):
        dest = pl.ds(pl.multiple_of(to, 16), size)
        high, low = halves(src[:size, :width])
        y_high[dest] = high
        y_low[dest] = low
        high, low = halves(src[:size, width:])
        p_high[dest] = high
        p_low[dest] = low

    def place_all(heavy, light):
        place(heavy[0], jnp.where(first, 0, slots), slots)
        place(heavy[1], jnp.where(first, slots, 0), slots)
        place(light[0], 2 * slots + jnp.where(first, 0, half), half)
        place(light[1], 2 * slots + jnp.where(first, half, 0), half)

    @pl.when(even)
    def _():
        place_all((own, ynb), (cnb, cynb))

    @pl.when(jnp.logical_not(even))
    def _():
        place_all((cnb, cynb), (own, ynb))

    lane = lax.broadcasted_iota(jnp.int32, (8, 128), 1)
    fo, fc, fy, fcy = (f[slots:, :128] for f in (own, cnb, ynb, cynb))
    heavy = (jnp.where(even, fo, fc), jnp.where(even, fy, fcy))
    light = (jnp.where(even, fc, fo), jnp.where(even, fcy, fy))
    a0, b0 = (jnp.where(first, f[0], f[1]) for f in (heavy, light))
    a1, b1 = (jnp.where(first, f[1], f[0]) for f in (heavy, light))
    a1 = pltpu.roll(a1, 96, 1)
    b1 = pltpu.roll(b1, 112, 1)
    row_facts = jnp.concatenate(
        [
            jnp.where(lane < 96, a0, a1),
            jnp.where(lane < 64, a1, jnp.where(lane < 112, pltpu.roll(b0, 64, 1), b1)),
            b1,
        ],
        axis=1,
    )[:, :live_rows]

    yh, yl = y_high[...], y_low[...]
    y_out[...] = deep_rows(yh, yl)
    ph, plow = p_high[...], p_low[...]
    power_out[...] = deep_rows(ph, plow)

    per = refs[0].shape[0]
    r = (lax.broadcasted_iota(jnp.int32, (per, live_rows), 0) % ROT).astype(jnp.float32)
    prior = PRIOR * turn_cos((r - row_facts[3:4, :]) * (1.0 / ROT))
    phases = grid_phases(freq)
    high = None
    for n in range(blocks):
        rr = refs[n][:, :freq]
        ri = refs[n][:, freq:]
        qh, ql = halves(rr * rr + ri * ri)
        quad = dot_nt(qh, ph) + dot_nt(ql, ph) + dot_nt(qh, plow)
        base = prior - 0.5 * quad
        rows = []
        for t in range(SHIFTS):
            if t == SHIFTS // 2:
                rows.append(refs[n][...])
            else:
                cg, sg = phase_of(phases, t)
                rows.append(jnp.concatenate([rr * cg + ri * sg, ri * cg - rr * sg], axis=1))
        rh, rl = halves(jnp.concatenate(rows, axis=0))
        score = dot_nt(rh, yh) + dot_nt(rl, yh) + dot_nt(rh, yl)
        score = score.reshape(SHIFTS, per, live_rows) + base[None]
        e_outs[n][...] = score
        top = jnp.max(score, axis=0)
        high = top if high is None else jnp.maximum(high, top)
    high = jnp.max(high, axis=0, keepdims=True)
    sums = [jnp.zeros((per, live_rows), jnp.float32) for _ in range(SHIFTS)]
    for n in range(blocks):
        for t in range(SHIFTS):
            e = jnp.exp(e_outs[n][t] - high)
            e_outs[n][t] = e
            sums[t] = sums[t] + e
    sums = [jnp.sum(s, axis=0, keepdims=True) for s in sums]
    mass = sum(sums)
    mean_x = sum(s * float(gx) for s, (gx, gy) in zip(sums, GRID) if gx)
    mean_y = sum(s * float(gy) for s, (gx, gy) in zip(sums, GRID) if gy)
    stats_out[...] = jnp.zeros_like(stats_out)
    stats_out[0:1, :live_rows] = high
    stats_out[1:2, :live_rows] = mass
    stats_out[2:3, :live_rows] = mean_x
    stats_out[3:4, :live_rows] = mean_y
    stats_out[4:5, :live_rows] = row_facts[5:6, :]


def sum_kernel(own, s1, s2, s3, e_ref, y_ref, power_ref, part_out, shift_out):
    live_rows = e_ref.shape[2]
    width = y_ref.shape[1]
    freq = width // 2
    team = [s[:, :live_rows] for s in (own, s1, s2, s3)]
    top = team[0][0:1]
    for s in team[1:]:
        top = jnp.maximum(top, s[0:1])
    gains = [jnp.exp(s[0:1] - top) for s in team]
    mass = sum(g * s[1:2] for g, s in zip(gains, team))
    live = team[0][4:5] / mass
    own_gain = gains[0] * live
    shift_out[...] = jnp.zeros_like(shift_out)
    shift_out[0:1, :live_rows] = sum(g * s[2:3] for g, s in zip(gains, team)) * live
    shift_out[1:2, :live_rows] = sum(g * s[3:4] for g, s in zip(gains, team)) * live
    per = e_ref.shape[1]
    w = e_ref[...] * own_gain[None]
    flat = dot_nn(deep_lanes(w.reshape(SHIFTS * per, live_rows)), y_ref[...])
    phases = grid_phases(freq)
    mid = SHIFTS // 2
    re = flat[mid * per : (mid + 1) * per, :freq]
    im = flat[mid * per : (mid + 1) * per, freq:]
    for t in range(SHIFTS):
        if t == mid:
            continue
        cg, sg = phase_of(phases, t)
        ar = flat[t * per : (t + 1) * per, :freq]
        ai = flat[t * per : (t + 1) * per, freq:]
        re = re + (ar * cg - ai * sg)
        im = im + (ar * sg + ai * cg)
    part_out[:, :freq] = re
    part_out[:, freq:width] = im
    part_out[:, width:] = dot_nn(deep_lanes(jnp.sum(w, axis=0)), power_ref[...])


def final_kernel(*refs):
    own, *others, signal, out = refs
    width = out.shape[1]
    freq = width // 2
    total = own[...]
    for other in others:
        total = total + other[...]
    denominator = total[:, width:] + 1.0 / signal[...]
    out[:, :freq] = total[:, :freq] / denominator
    out[:, freq:] = total[:, freq:width] / denominator


def params(blocks):
    return pltpu.CompilerParams(vmem_limit_bytes=(12 + 2 * blocks) * 1024 * 1024)


def crossed(block, mask):
    size = lax.axis_size("dom")
    return lax.ppermute(block, "dom", [(i, i ^ mask) for i in range(size)])


def on_device(
    particle_fourier,
    defocus,
    particle_offset,
    prior_rotation,
    group_id,
    live_count,
    noise_power,
    signal_power,
    class_refs,
):
    slots, width = particle_fourier.shape
    freq = width // 2
    live_rows = 3 * slots
    size = lax.axis_size("dom")
    blocks = size // TEAM
    refs_own = class_refs.reshape(-1, width)
    per = refs_own.shape[0]
    f32 = jnp.float32
    vmem = pl.BlockSpec(memory_space=pltpu.VMEM)
    no_cost = pl.CostEstimate(flops=0, bytes_accessed=0, transcendentals=0)

    ynb = crossed(particle_fourier, 2)
    refs = [refs_own] + [crossed(refs_own, TEAM * n) for n in range(1, blocks) if n != 2]
    refs.insert(2, crossed(refs[2], TEAM))
    anywhere = pl.BlockSpec(memory_space=pl.ANY)
    own_facts = (
        particle_fourier,
        defocus.reshape(1, slots),
        particle_offset.T,
        prior_rotation.reshape(1, slots),
        group_id.reshape(1, slots),
        noise_power,
    )
    own, facts, inverse_noise = pl.pallas_call(
        own_kernel,
        out_shape=(
            jax.ShapeDtypeStruct((slots + 8, width + freq), f32),
            jax.ShapeDtypeStruct((8, 128), f32),
            jax.ShapeDtypeStruct(noise_power.shape, f32),
        ),
        in_specs=[anywhere] * 6 + [pl.BlockSpec(memory_space=pltpu.SMEM)],
        out_specs=(vmem,) * 3,
        scratch_shapes=[pltpu.VMEM(x.shape, x.dtype) for x in own_facts]
        + [pltpu.SemaphoreType.DMA((6,))],
        compiler_params=params(blocks),
        cost_estimate=no_cost,
        name="own",
    )(*(pltpu.with_memory_space_constraint(x, pltpu.HBM) for x in own_facts), live_count)
    cnb = crossed(own, 1)
    ynb = pl.pallas_call(
        neighbour_kernel,
        out_shape=jax.ShapeDtypeStruct((slots + 8, width + freq), f32),
        in_specs=[vmem] * 3,
        out_specs=vmem,
        compiler_params=params(blocks),
        cost_estimate=no_cost,
        name="neighbour",
    )(ynb, crossed(facts, 2), inverse_noise)
    ynb = pl.pallas_call(
        lambda *a: None,
        out_shape=jax.ShapeDtypeStruct(ynb.shape, f32),
        in_specs=[anywhere] * blocks,
        out_specs=anywhere,
        input_output_aliases={0: 0},
        compiler_params=params(blocks),
        cost_estimate=no_cost,
        name="gate",
    )(ynb, *refs[1:])
    cynb = crossed(ynb, 1)

    deep = 3 * (live_rows // 256 * 256) + 128
    bf16 = jnp.bfloat16
    *e_all, y, power, stats = pl.pallas_call(
        lambda *a: score_kernel(blocks, *a),
        out_shape=(
            *[jax.ShapeDtypeStruct((SHIFTS, per, live_rows), f32)] * blocks,
            jax.ShapeDtypeStruct((deep, width), bf16),
            jax.ShapeDtypeStruct((deep, freq), bf16),
            jax.ShapeDtypeStruct((8, 384), f32),
        ),
        in_specs=[vmem] * (blocks + 4),
        out_specs=(vmem,) * (blocks + 3),
        scratch_shapes=[
            pltpu.VMEM((live_rows, width), bf16),
            pltpu.VMEM((live_rows, width), bf16),
            pltpu.VMEM((live_rows, freq), bf16),
            pltpu.VMEM((live_rows, freq), bf16),
        ],
        compiler_params=params(blocks),
        name="scores",
    )(own, cnb, ynb, cynb, *refs)

    team = [stats] + [crossed(stats, n) for n in range(1, TEAM)]

    def sums(n):
        return pl.pallas_call(
            sum_kernel,
            out_shape=(
                jax.ShapeDtypeStruct((per, width + freq), f32),
                jax.ShapeDtypeStruct((8, 384), f32),
            ),
            in_specs=[vmem] * (TEAM + 3),
            out_specs=(vmem,) * 2,
            compiler_params=params(blocks),
            name="sums",
        )(*team, e_all[n], y, power)

    arrived = []
    for n in range(blocks - 1, 0, -1):
        part, _ = sums(n)
        arrived.append(crossed(part, TEAM * n))
    own_part, shift_rows = sums(0)

    refs_new = pl.pallas_call(
        final_kernel,
        out_shape=jax.ShapeDtypeStruct((per, width), f32),
        in_specs=[vmem] * (blocks + 1),
        out_specs=vmem,
        compiler_params=params(blocks),
        name="update",
    )(own_part, *arrived[::-1], signal_power.reshape(1, freq))

    me = lax.axis_index("dom")
    half = slots // 2
    odd = me % 2
    at = (me // 2) % 2 * jnp.where(odd == 0, slots, half) + odd * (2 * slots)
    low = lax.dynamic_slice(shift_rows, (0, at), (2, half))
    high = lax.dynamic_slice(shift_rows, (0, at + half), (2, half))
    high = jnp.where(odd == 0, high, 0.0)
    expected = jnp.concatenate([low, high], axis=1).T
    return (expected, refs_new.reshape(class_refs.shape))


def solution(mesh):
    in_specs = (
        P(("groups", "dom"), None),
        P(("groups", "dom")),
        P(("groups", "dom"), None),
        P(("groups", "dom")),
        P(("groups", "dom")),
        P(("groups", "dom")),
        P("groups", None),
        P("groups"),
        P(("groups", "dom"), None, None),
    )
    out_specs = (P(("groups", "dom"), None), P(("groups", "dom"), None, None))
    return jax.shard_map(
        on_device, mesh=mesh, in_specs=in_specs, out_specs=out_specs, check_vma=False
    )
```

```python
import math

import jax
import jax.numpy as jnp
from jax import lax
from jax.experimental import pallas as pl
from jax.experimental.pallas import tpu as pltpu
from jax.sharding import PartitionSpec as P

ROT = 16
SIDE = 3
BOX = 128
FY = 32
SHIFTS = 9
TEAM = 4
PRIOR = 2.0
CTF_SIZE = math.hypot(0.995, 0.1)
CTF_TURN = math.atan2(0.1, 0.995)
SINE = (
    9.99999976e-01,
    -1.66666476e-01,
    8.33289854e-03,
    -1.98008185e-04,
    2.59032780e-06,
)
TWO_PI = 2.0 * math.pi
PI_A = 3.140625
PI_B = 0.0009670257568359375
PI_C = math.pi - PI_A - PI_B
HIGHEST = lax.Precision.HIGHEST
GRID = tuple((t // SIDE - SIDE // 2, t % SIDE - SIDE // 2) for t in range(SHIFTS))


def half_turn_sine(x):
    s = x * x
    p = SINE[4]
    for c in SINE[3::-1]:
        p = p * s + c
    return x * p


def turn_cos(turns):
    t = jnp.abs(turns - jnp.round(turns))
    return half_turn_sine(TWO_PI * (0.25 - t))


def turn_sin(turns):
    return turn_cos(turns - 0.25)


def freq_rows(width, rows):
    f = lax.broadcasted_iota(jnp.int32, (rows, width), 1)
    kx = (f // FY).astype(jnp.float32)
    ky = (f % FY - FY // 2).astype(jnp.float32)
    return kx, ky


def dot_nt(a, b):
    return lax.dot_general(
        a, b, (((1,), (1,)), ((), ())), preferred_element_type=jnp.float32
    )


def dot_nn(a, b):
    return lax.dot_general(
        a, b, (((1,), (0,)), ((), ())), preferred_element_type=jnp.float32
    )


def exact_dot_nn(a, b):
    return lax.dot_general(
        a, b, (((1,), (0,)), ((), ())), precision=HIGHEST, preferred_element_type=jnp.float32
    )


def halves(x):
    high = x.astype(jnp.bfloat16)
    return high, (x - high.astype(jnp.float32)).astype(jnp.bfloat16)


def deep_rows(high, low):
    rows = high.shape[0]
    main = rows // 256 * 256
    left = rows - main
    parts = [high[:main], low[:main], high[:main], high[main:], low[main:], high[main:]]
    parts.append(jnp.zeros((128 - 3 * left, high.shape[1]), high.dtype))
    return jnp.concatenate(parts, axis=0)


def deep_lanes(x):
    rows, lanes = x.shape
    main = lanes // 256 * 256
    left = lanes - main
    high, low = halves(x[:, :main])
    tail = jnp.concatenate(
        [x[:, main:], jnp.zeros((rows, 128 - left), jnp.float32)], axis=1
    )
    tail_high = tail.astype(jnp.bfloat16).astype(jnp.float32)
    tail_low = tail - tail_high
    mixed = tail_high + pltpu.roll(tail_high, left, 1) + pltpu.roll(tail_low, 2 * left, 1)
    return jnp.concatenate([high, high, low, mixed.astype(jnp.bfloat16)], axis=1)


def grid_phases(width):
    kx, ky = freq_rows(width, 1)
    out = []
    for t, (gx, gy) in enumerate(GRID):
        if t < SHIFTS // 2:
            m = (kx * gx + ky * gy) * (1.0 / BOX)
            out.append((turn_cos(m), turn_sin(m)))
    return out


def phase_of(phases, t):
    mid = SHIFTS // 2
    if t < mid:
        return phases[t]
    c, s = phases[SHIFTS - 1 - t]
    return c, -s


def prepared_rows(src, facts, inverse_noise, out):
    slots, width = src.shape
    freq = width // 2
    columns = jnp.concatenate([facts, jnp.zeros((120, 128), jnp.float32)], axis=0).T[:slots]
    focus = columns[:, 0:1]
    off_x = columns[:, 1:2]
    off_y = columns[:, 2:3]
    group_col = columns[:, 4:5]

    kx, ky = freq_rows(freq, 1)
    chi = focus * ((kx * kx + ky * ky) * (1.0 / 1024.0))
    k = jnp.round(chi * (1.0 / math.pi))
    rest_angle = ((chi - k * PI_A) - k * PI_B) - k * PI_C
    shifted_angle = rest_angle + CTF_TURN
    over = shifted_angle > (0.5 * math.pi)
    folded = jnp.where(over, math.pi - shifted_angle, shifted_angle)
    parity = 0.5 * k
    sign = (parity - jnp.floor(parity)) * (4.0 * CTF_SIZE) - CTF_SIZE
    ctf = half_turn_sine(folded) * sign
    kx0, ky0 = freq_rows(128, 1)
    m = (kx0 * off_x + ky0 * off_y) * (1.0 / BOX)
    pc, ps = turn_cos(m), turn_sin(m)
    step = off_x * ((128 // FY) / BOX) + jnp.zeros((slots, 128), jnp.float32)
    sc, ss = turn_cos(step), turn_sin(step)

    total = inverse_noise.shape[0]
    onehot = (
        group_col == lax.broadcasted_iota(jnp.int32, (slots, total), 1).astype(jnp.float32)
    ).astype(jnp.float32)
    noise_rows = exact_dot_nn(onehot, inverse_noise)
    scaled = ctf * noise_rows
    out[:slots, width:] = ctf * scaled
    for n in range(freq // 128):
        part = slice(128 * n, 128 * (n + 1))
        twin = slice(freq + 128 * n, freq + 128 * (n + 1))
        co = pc * scaled[:, part]
        si = ps * scaled[:, part]
        pc, ps = pc * sc - ps * ss, ps * sc + pc * ss
        xr, xi = src[:, part], src[:, twin]
        out[:slots, part] = xr * co - xi * si
        out[:slots, twin] = xr * si + xi * co
    out[slots:, :128] = facts
    out[slots:, 128:] = jnp.zeros((8, width + freq - 128), jnp.float32)


def own_kernel(
    src_at, focus_at, offsets_at, prior_at, group_at, noise_at, live_count, out, facts_out,
    inverse_out, src, focus, offsets, prior, group, noise, sems
):
    moves = (
        (focus_at, focus), (offsets_at, offsets), (prior_at, prior), (group_at, group),
        (noise_at, noise), (src_at, src),
    )
    copies = [pltpu.make_async_copy(x, y, sems.at[n]) for n, (x, y) in enumerate(moves)]
    for copy in copies:
        copy.start()
    slots = src.shape[0]
    facts_out[...] = jnp.zeros_like(facts_out)
    slot = lax.broadcasted_iota(jnp.int32, (1, slots), 1)
    facts_out[5:6, :slots] = (slot < live_count[0]).astype(jnp.float32)
    for copy in copies:
        copy.wait()
    facts_out[0:1, :slots] = focus[...]
    facts_out[1:3, :slots] = offsets[...].astype(jnp.float32)
    facts_out[3:4, :slots] = prior[...].astype(jnp.float32)
    facts_out[4:5, :slots] = group[...].astype(jnp.float32)
    inverse = 1.0 / noise[...]
    inverse_out[...] = inverse
    prepared_rows(src, facts_out[...], inverse, out)


def neighbour_kernel(src, facts, inverse_noise, out):
    prepared_rows(src, facts[...], inverse_noise[...], out)


def score_kernel(blocks, own, cnb, ynb, cynb, *rest):
    refs = rest[:blocks]
    e_outs = rest[blocks : 2 * blocks]
    y_out, power_out, stats_out, y_high, y_low, p_high, p_low = rest[2 * blocks :]
    width = y_high.shape[1]
    freq = width // 2
    slots = own.shape[0] - 8
    half = slots // 2
    live_rows = 3 * slots
    me = lax.axis_index("dom")
    even = me % 2 == 0
    first = (me // 2) % 2 == 0

    def place(src, to, size):
        dest = pl.ds(pl.multiple_of(to, 16), size)
        high, low = halves(src[:size, :width])
        y_high[dest] = high
        y_low[dest] = low
        high, low = halves(src[:size, width:])
        p_high[dest] = high
        p_low[dest] = low

    def place_all(heavy, light):
        place(heavy[0], jnp.where(first, 0, slots), slots)
        place(heavy[1], jnp.where(first, slots, 0), slots)
        place(light[0], 2 * slots + jnp.where(first, 0, half), half)
        place(light[1], 2 * slots + jnp.where(first, half, 0), half)

    @pl.when(even)
    def _():
        place_all((own, ynb), (cnb, cynb))

    @pl.when(jnp.logical_not(even))
    def _():
        place_all((cnb, cynb), (own, ynb))

    lane = lax.broadcasted_iota(jnp.int32, (8, 128), 1)
    fo, fc, fy, fcy = (f[slots:, :128] for f in (own, cnb, ynb, cynb))
    heavy = (jnp.where(even, fo, fc), jnp.where(even, fy, fcy))
    light = (jnp.where(even, fc, fo), jnp.where(even, fcy, fy))
    a0, b0 = (jnp.where(first, f[0], f[1]) for f in (heavy, light))
    a1, b1 = (jnp.where(first, f[1], f[0]) for f in (heavy, light))
    a1 = pltpu.roll(a1, 96, 1)
    b1 = pltpu.roll(b1, 112, 1)
    row_facts = jnp.concatenate(
        [
            jnp.where(lane < 96, a0, a1),
            jnp.where(lane < 64, a1, jnp.where(lane < 112, pltpu.roll(b0, 64, 1), b1)),
            b1,
        ],
        axis=1,
    )[:, :live_rows]

    yh, yl = y_high[...], y_low[...]
    y_out[...] = deep_rows(yh, yl)
    ph, plow = p_high[...], p_low[...]
    power_out[...] = deep_rows(ph, plow)

    per = refs[0].shape[0]
    r = (lax.broadcasted_iota(jnp.int32, (per, live_rows), 0) % ROT).astype(jnp.float32)
    prior = PRIOR * turn_cos((r - row_facts[3:4, :]) * (1.0 / ROT))
    phases = grid_phases(freq)
    high = None
    for n in range(blocks):
        rr = refs[n][:, :freq]
        ri = refs[n][:, freq:]
        qh, ql = halves(rr * rr + ri * ri)
        quad = dot_nt(qh, ph) + dot_nt(ql, ph) + dot_nt(qh, plow)
        base = prior - 0.5 * quad
        rows = []
        for t in range(SHIFTS):
            if t == SHIFTS // 2:
                rows.append(refs[n][...])
            else:
                cg, sg = phase_of(phases, t)
                rows.append(jnp.concatenate([rr * cg + ri * sg, ri * cg - rr * sg], axis=1))
        rh, rl = halves(jnp.concatenate(rows, axis=0))
        score = dot_nt(rh, yh) + dot_nt(rl, yh) + dot_nt(rh, yl)
        score = score.reshape(SHIFTS, per, live_rows) + base[None]
        e_outs[n][...] = score
        top = jnp.max(score, axis=0)
        high = top if high is None else jnp.maximum(high, top)
    high = jnp.max(high, axis=0, keepdims=True)
    sums = [jnp.zeros((per, live_rows), jnp.float32) for _ in range(SHIFTS)]
    for n in range(blocks):
        for t in range(SHIFTS):
            e = jnp.exp(e_outs[n][t] - high)
            e_outs[n][t] = e
            sums[t] = sums[t] + e
    sums = [jnp.sum(s, axis=0, keepdims=True) for s in sums]
    mass = sum(sums)
    mean_x = sum(s * float(gx) for s, (gx, gy) in zip(sums, GRID) if gx)
    mean_y = sum(s * float(gy) for s, (gx, gy) in zip(sums, GRID) if gy)
    stats_out[...] = jnp.zeros_like(stats_out)
    stats_out[0:1, :live_rows] = high
    stats_out[1:2, :live_rows] = mass
    stats_out[2:3, :live_rows] = mean_x
    stats_out[3:4, :live_rows] = mean_y
    stats_out[4:5, :live_rows] = row_facts[5:6, :]


def sum_kernel(own, s1, s2, s3, e_ref, y_ref, power_ref, part_out, shift_out):
    live_rows = e_ref.shape[2]
    width = y_ref.shape[1]
    freq = width // 2
    team = [s[:, :live_rows] for s in (own, s1, s2, s3)]
    top = team[0][0:1]
    for s in team[1:]:
        top = jnp.maximum(top, s[0:1])
    gains = [jnp.exp(s[0:1] - top) for s in team]
    mass = sum(g * s[1:2] for g, s in zip(gains, team))
    live = team[0][4:5] / mass
    own_gain = gains[0] * live
    shift_out[...] = jnp.zeros_like(shift_out)
    shift_out[0:1, :live_rows] = sum(g * s[2:3] for g, s in zip(gains, team)) * live
    shift_out[1:2, :live_rows] = sum(g * s[3:4] for g, s in zip(gains, team)) * live
    per = e_ref.shape[1]
    w = e_ref[...] * own_gain[None]
    flat = dot_nn(deep_lanes(w.reshape(SHIFTS * per, live_rows)), y_ref[...])
    phases = grid_phases(freq)
    mid = SHIFTS // 2
    re = flat[mid * per : (mid + 1) * per, :freq]
    im = flat[mid * per : (mid + 1) * per, freq:]
    for t in range(SHIFTS):
        if t == mid:
            continue
        cg, sg = phase_of(phases, t)
        ar = flat[t * per : (t + 1) * per, :freq]
        ai = flat[t * per : (t + 1) * per, freq:]
        re = re + (ar * cg - ai * sg)
        im = im + (ar * sg + ai * cg)
    part_out[:, :freq] = re
    part_out[:, freq:width] = im
    part_out[:, width:] = dot_nn(deep_lanes(jnp.sum(w, axis=0)), power_ref[...])


def add_kernel(a, b, out):
    out[...] = a[...] + b[...]


def final_kernel(*refs):
    own, *others, signal, out = refs
    width = out.shape[1]
    freq = width // 2
    total = own[...]
    for other in others:
        total = total + other[...]
    denominator = total[:, width:] + 1.0 / signal[...]
    out[:, :freq] = total[:, :freq] / denominator
    out[:, freq:] = total[:, freq:width] / denominator


def params(mib):
    return pltpu.CompilerParams(vmem_limit_bytes=mib * 1024 * 1024)


def crossed(block, mask):
    size = lax.axis_size("dom")
    return lax.ppermute(block, "dom", [(i, i ^ mask) for i in range(size)])


def on_device(
    particle_fourier,
    defocus,
    particle_offset,
    prior_rotation,
    group_id,
    live_count,
    noise_power,
    signal_power,
    class_refs,
):
    slots, width = particle_fourier.shape
    freq = width // 2
    live_rows = 3 * slots
    size = lax.axis_size("dom")
    blocks = size // TEAM
    refs_own = class_refs.reshape(-1, width)
    per = refs_own.shape[0]
    f32 = jnp.float32
    vmem = pl.BlockSpec(memory_space=pltpu.VMEM)
    no_cost = pl.CostEstimate(flops=0, bytes_accessed=0, transcendentals=0)

    ynb = crossed(particle_fourier, 2)
    refs = [refs_own] + [crossed(refs_own, TEAM * n) for n in range(1, blocks)]
    anywhere = pl.BlockSpec(memory_space=pl.ANY)
    own_facts = (
        particle_fourier,
        defocus.reshape(1, slots),
        particle_offset.T,
        prior_rotation.reshape(1, slots),
        group_id.reshape(1, slots),
        noise_power,
    )
    own, facts, inverse_noise = pl.pallas_call(
        own_kernel,
        out_shape=(
            jax.ShapeDtypeStruct((slots + 8, width + freq), f32),
            jax.ShapeDtypeStruct((8, 128), f32),
            jax.ShapeDtypeStruct(noise_power.shape, f32),
        ),
        in_specs=[anywhere] * 6 + [pl.BlockSpec(memory_space=pltpu.SMEM)],
        out_specs=(vmem,) * 3,
        scratch_shapes=[pltpu.VMEM(x.shape, x.dtype) for x in own_facts]
        + [pltpu.SemaphoreType.DMA((6,))],
        compiler_params=params(6),
        cost_estimate=no_cost,
        name="own",
    )(*(pltpu.with_memory_space_constraint(x, pltpu.HBM) for x in own_facts), live_count)
    cnb = crossed(own, 1)
    ynb = pl.pallas_call(
        neighbour_kernel,
        out_shape=jax.ShapeDtypeStruct((slots + 8, width + freq), f32),
        in_specs=[vmem] * 3,
        out_specs=vmem,
        compiler_params=params(6),
        cost_estimate=no_cost,
        name="neighbour",
    )(ynb, crossed(facts, 2), inverse_noise)
    ynb = pl.pallas_call(
        lambda *a: None,
        out_shape=jax.ShapeDtypeStruct(ynb.shape, f32),
        in_specs=[anywhere] * blocks,
        out_specs=anywhere,
        input_output_aliases={0: 0},
        compiler_params=params(1),
        cost_estimate=no_cost,
        name="gate",
    )(ynb, *refs[1:])
    cynb = crossed(ynb, 1)

    deep = 3 * (live_rows // 256 * 256) + 128
    bf16 = jnp.bfloat16
    *e_all, y, power, stats = pl.pallas_call(
        lambda *a: score_kernel(blocks, *a),
        out_shape=(
            *[jax.ShapeDtypeStruct((SHIFTS, per, live_rows), f32)] * blocks,
            jax.ShapeDtypeStruct((deep, width), bf16),
            jax.ShapeDtypeStruct((deep, freq), bf16),
            jax.ShapeDtypeStruct((8, 384), f32),
        ),
        in_specs=[vmem] * (blocks + 4),
        out_specs=(vmem,) * (blocks + 3),
        scratch_shapes=[
            pltpu.VMEM((live_rows, width), bf16),
            pltpu.VMEM((live_rows, width), bf16),
            pltpu.VMEM((live_rows, freq), bf16),
            pltpu.VMEM((live_rows, freq), bf16),
        ],
        compiler_params=params(8 + 2 * blocks),
        name="scores",
    )(own, cnb, ynb, cynb, *refs)

    team = [stats] + [crossed(stats, n) for n in range(1, TEAM)]

    def sums(n):
        return pl.pallas_call(
            sum_kernel,
            out_shape=(
                jax.ShapeDtypeStruct((per, width + freq), f32),
                jax.ShapeDtypeStruct((8, 384), f32),
            ),
            in_specs=[vmem] * (TEAM + 3),
            out_specs=(vmem,) * 2,
            compiler_params=params(8),
            name="sums",
        )(*team, e_all[n], y, power)

    def combined(n, other):
        return pl.pallas_call(
            add_kernel,
            out_shape=jax.ShapeDtypeStruct((per, width + freq), f32),
            in_specs=[vmem] * 2,
            out_specs=vmem,
            compiler_params=params(4),
            name="combined",
        )(sums(n)[0], other)

    arrived = [crossed(sums(1)[0], TEAM)]
    for n in range(2, blocks, 2):
        handed = crossed(sums(n)[0], TEAM)
        arrived.append(crossed(combined(n + 1, handed), TEAM * (n + 1)))
    own_part, shift_rows = sums(0)

    refs_new = pl.pallas_call(
        final_kernel,
        out_shape=jax.ShapeDtypeStruct((per, width), f32),
        in_specs=[vmem] * (len(arrived) + 2),
        out_specs=vmem,
        compiler_params=params(2 + blocks),
        name="update",
    )(own_part, *arrived[::-1], signal_power.reshape(1, freq))

    me = lax.axis_index("dom")
    half = slots // 2
    odd = me % 2
    at = (me // 2) % 2 * jnp.where(odd == 0, slots, half) + odd * (2 * slots)
    low = lax.dynamic_slice(shift_rows, (0, at), (2, half))
    high = lax.dynamic_slice(shift_rows, (0, at + half), (2, half))
    high = jnp.where(odd == 0, high, 0.0)
    expected = jnp.concatenate([low, high], axis=1).T
    return (expected, refs_new.reshape(class_refs.shape))


def solution(mesh):
    in_specs = (
        P(("groups", "dom"), None),
        P(("groups", "dom")),
        P(("groups", "dom"), None),
        P(("groups", "dom")),
        P(("groups", "dom")),
        P(("groups", "dom")),
        P("groups", None),
        P("groups"),
        P(("groups", "dom"), None, None),
    )
    out_specs = (P(("groups", "dom"), None), P(("groups", "dom"), None, None))
    return jax.shard_map(
        on_device, mesh=mesh, in_specs=in_specs, out_specs=out_specs, check_vma=False
    )
```

```python
import math

import jax
import jax.numpy as jnp
from jax import lax
from jax.experimental import pallas as pl
from jax.experimental.pallas import tpu as pltpu
from jax.sharding import PartitionSpec as P

ROT = 16
SIDE = 3
BOX = 128
FY = 32
SHIFTS = 9
TEAM = 4
PRIOR = 2.0
CTF_SIZE = math.hypot(0.995, 0.1)
CTF_TURN = math.atan2(0.1, 0.995)
SINE = (
    9.99999976e-01,
    -1.66666476e-01,
    8.33289854e-03,
    -1.98008185e-04,
    2.59032780e-06,
)
TWO_PI = 2.0 * math.pi
PI_A = 3.140625
PI_B = 0.0009670257568359375
PI_C = math.pi - PI_A - PI_B
HIGHEST = lax.Precision.HIGHEST
GRID = tuple((t // SIDE - SIDE // 2, t % SIDE - SIDE // 2) for t in range(SHIFTS))


def half_turn_sine(x):
    s = x * x
    p = SINE[4]
    for c in SINE[3::-1]:
        p = p * s + c
    return x * p


def turn_cos(turns):
    t = jnp.abs(turns - jnp.round(turns))
    return half_turn_sine(TWO_PI * (0.25 - t))


def turn_sin(turns):
    return turn_cos(turns - 0.25)


def freq_rows(width, rows):
    f = lax.broadcasted_iota(jnp.int32, (rows, width), 1)
    kx = (f // FY).astype(jnp.float32)
    ky = (f % FY - FY // 2).astype(jnp.float32)
    return kx, ky


def dot_nt(a, b):
    return lax.dot_general(
        a, b, (((1,), (1,)), ((), ())), preferred_element_type=jnp.float32
    )


def dot_nn(a, b):
    return lax.dot_general(
        a, b, (((1,), (0,)), ((), ())), preferred_element_type=jnp.float32
    )


def exact_dot_nn(a, b):
    return lax.dot_general(
        a, b, (((1,), (0,)), ((), ())), precision=HIGHEST, preferred_element_type=jnp.float32
    )


def halves(x):
    high = x.astype(jnp.bfloat16)
    return high, (x - high.astype(jnp.float32)).astype(jnp.bfloat16)


def deep_rows(a_high, a_low, b_high, b_low):
    rows = a_high.shape[0]
    main, left = slice(0, 128), slice(128, rows)
    order = ((a_high, b_high), (a_low, b_low), (a_high, b_high))
    parts = [x[main] for pair in order for x in pair]
    parts += [x[left] for pair in order for x in pair]
    parts.append(jnp.zeros((128 - 6 * (rows - 128), a_high.shape[1]), a_high.dtype))
    return jnp.concatenate(parts, axis=0)


def deep_lanes(a, b):
    rows, lanes = a.shape
    left = lanes - 128
    high, low = halves(jnp.concatenate([a[:, :128], b[:, :128]], axis=1))
    empty = jnp.zeros((rows, 128 - left), jnp.float32)
    tail = jnp.concatenate([a[:, 128:], empty], axis=1) + pltpu.roll(
        jnp.concatenate([b[:, 128:], empty], axis=1), left, 1
    )
    tail_high = tail.astype(jnp.bfloat16).astype(jnp.float32)
    tail_low = tail - tail_high
    mixed = (
        tail_high + pltpu.roll(tail_high, 2 * left, 1) + pltpu.roll(tail_low, 4 * left, 1)
    )
    return jnp.concatenate([high, high, low, mixed.astype(jnp.bfloat16)], axis=1)


def grid_phases(width):
    kx, ky = freq_rows(width, 1)
    out = []
    for t, (gx, gy) in enumerate(GRID):
        if t < SHIFTS // 2:
            m = (kx * gx + ky * gy) * (1.0 / BOX)
            out.append((turn_cos(m), turn_sin(m)))
    return out


def phase_of(phases, t):
    mid = SHIFTS // 2
    if t < mid:
        return phases[t]
    c, s = phases[SHIFTS - 1 - t]
    return c, -s


def prepared_rows(src, facts, inverse_noise, out):
    slots, width = src.shape
    freq = width // 2
    columns = jnp.concatenate([facts, jnp.zeros((120, 128), jnp.float32)], axis=0).T[:slots]
    focus = columns[:, 0:1]
    off_x = columns[:, 1:2]
    off_y = columns[:, 2:3]
    group_col = columns[:, 4:5]

    kx, ky = freq_rows(freq, 1)
    chi = focus * ((kx * kx + ky * ky) * (1.0 / 1024.0))
    k = jnp.round(chi * (1.0 / math.pi))
    rest_angle = ((chi - k * PI_A) - k * PI_B) - k * PI_C
    shifted_angle = rest_angle + CTF_TURN
    over = shifted_angle > (0.5 * math.pi)
    folded = jnp.where(over, math.pi - shifted_angle, shifted_angle)
    parity = 0.5 * k
    sign = (parity - jnp.floor(parity)) * (4.0 * CTF_SIZE) - CTF_SIZE
    ctf = half_turn_sine(folded) * sign
    kx0, ky0 = freq_rows(128, 1)
    m = (kx0 * off_x + ky0 * off_y) * (1.0 / BOX)
    pc, ps = turn_cos(m), turn_sin(m)
    step = off_x * ((128 // FY) / BOX) + jnp.zeros((slots, 128), jnp.float32)
    sc, ss = turn_cos(step), turn_sin(step)

    total = inverse_noise.shape[0]
    onehot = (
        group_col == lax.broadcasted_iota(jnp.int32, (slots, total), 1).astype(jnp.float32)
    ).astype(jnp.float32)
    noise_rows = exact_dot_nn(onehot, inverse_noise)
    scaled = ctf * noise_rows
    out[:slots, width:] = ctf * scaled
    for n in range(freq // 128):
        part = slice(128 * n, 128 * (n + 1))
        twin = slice(freq + 128 * n, freq + 128 * (n + 1))
        co = pc * scaled[:, part]
        si = ps * scaled[:, part]
        pc, ps = pc * sc - ps * ss, ps * sc + pc * ss
        xr, xi = src[:, part], src[:, twin]
        out[:slots, part] = xr * co - xi * si
        out[:slots, twin] = xr * si + xi * co
    out[slots:, :128] = facts
    out[slots:, 128:] = jnp.zeros((8, width + freq - 128), jnp.float32)


def own_kernel(
    src_at, focus_at, offsets_at, prior_at, group_at, noise_at, live_count, out, facts_out,
    inverse_out, src, focus, offsets, prior, group, noise, sems
):
    moves = (
        (focus_at, focus), (offsets_at, offsets), (prior_at, prior), (group_at, group),
        (noise_at, noise), (src_at, src),
    )
    copies = [pltpu.make_async_copy(x, y, sems.at[n]) for n, (x, y) in enumerate(moves)]
    for copy in copies:
        copy.start()
    slots = src.shape[0]
    facts_out[...] = jnp.zeros_like(facts_out)
    slot = lax.broadcasted_iota(jnp.int32, (1, slots), 1)
    facts_out[5:6, :slots] = (slot < live_count[0]).astype(jnp.float32)
    for copy in copies:
        copy.wait()
    facts_out[0:1, :slots] = focus[...]
    facts_out[1:3, :slots] = offsets[...].astype(jnp.float32)
    facts_out[3:4, :slots] = prior[...].astype(jnp.float32)
    facts_out[4:5, :slots] = group[...].astype(jnp.float32)
    inverse = 1.0 / noise[...]
    inverse_out[...] = inverse
    prepared_rows(src, facts_out[...], inverse, out)


def neighbour_kernel(src, facts, inverse_noise, wait, out):
    prepared_rows(src, facts[...], inverse_noise[...], out)


def even_core():
    return lax.axis_index("dom") % 2 == 0


def place_half(mine, other, y_high, y_low, p_high, p_low):
    width = y_high.shape[1]
    slots = mine.shape[0] - 8

    def place(src, to, size):
        dest = slice(to, to + size)
        high, low = halves(src[:size, :width])
        y_high[dest] = high
        y_low[dest] = low
        high, low = halves(src[:size, width:])
        p_high[dest] = high
        p_low[dest] = low

    even = even_core()

    @pl.when(even)
    def _():
        place(mine, 0, slots)
        place(other, slots, slots // 2)

    @pl.when(jnp.logical_not(even))
    def _():
        place(other, 0, slots)
        place(mine, slots, slots // 2)


def half_facts(mine, other):
    slots = mine.shape[0] - 8
    even = even_core()
    x, y = mine[slots:, :128], other[slots:, :128]
    heavy = jnp.where(even, x, y)
    light = pltpu.roll(jnp.where(even, y, x), 96, 1)
    lane = lax.broadcasted_iota(jnp.int32, (8, 128), 1)
    return jnp.concatenate([jnp.where(lane < 96, heavy, light), light], axis=1)


def prior_rows(facts, per, lanes):
    r = (lax.broadcasted_iota(jnp.int32, (per, lanes), 0) % ROT).astype(jnp.float32)
    return PRIOR * turn_cos((r - facts[3:4, :lanes]) * (1.0 / ROT))


def prepare_refs(ref, phases, r_high, r_low, q_high, q_low):
    per, width = ref.shape
    freq = width // 2
    rr, ri = ref[:, :freq], ref[:, freq:]
    mid = SHIFTS // 2

    def store(t, re, im):
        rows = slice(t * per, (t + 1) * per)
        r_high[rows, :freq], r_low[rows, :freq] = halves(re)
        r_high[rows, freq:], r_low[rows, freq:] = halves(im)

    store(mid, rr, ri)
    for t in range(mid):
        c, s = phases[t]
        a, b, d, e = rr * c, ri * s, ri * c, rr * s
        store(t, a + b, d - e)
        store(SHIFTS - 1 - t, a - b, d + e)
    q_high[...], q_low[...] = halves(rr * rr + ri * ri)


def block_scores(prepared, particles, prior):
    r_high, r_low, q_high, q_low = (x[...] for x in prepared)
    y_high, y_low, p_high, p_low = particles
    quad = dot_nt(q_high, p_high) + dot_nt(q_low, p_high) + dot_nt(q_high, p_low)
    score = dot_nt(r_high, y_high) + dot_nt(r_low, y_high) + dot_nt(r_high, y_low)
    per, lanes = prior.shape
    return score.reshape(SHIFTS, per, lanes) + (prior - 0.5 * quad)[None]


def weigh(scores, facts, e_outs, stats_out):
    per, lanes = scores[0].shape[1:]
    top = None
    for score in scores:
        top_here = jnp.max(score[...], axis=0)
        top = top_here if top is None else jnp.maximum(top, top_here)
    top = jnp.max(top, axis=0, keepdims=True)
    sums = [jnp.zeros((per, lanes), jnp.float32) for _ in range(SHIFTS)]
    for score, e_out in zip(scores, e_outs):
        for t in range(SHIFTS):
            e = jnp.exp(score[t] - top)
            e_out[t] = e
            sums[t] = sums[t] + e
    sums = [jnp.sum(s, axis=0, keepdims=True) for s in sums]
    stats_out[...] = jnp.zeros_like(stats_out)
    stats_out[0:1, :lanes] = top
    stats_out[1:2, :lanes] = sum(sums)
    stats_out[2:3, :lanes] = sum(s * float(gx) for s, (gx, gy) in zip(sums, GRID) if gx)
    stats_out[3:4, :lanes] = sum(s * float(gy) for s, (gx, gy) in zip(sums, GRID) if gy)
    stats_out[4:5, :lanes] = facts[5:6, :lanes]


def early_kernel(count, *rest):
    refs, prepared = rest[:count], rest[count:]
    phases = grid_phases(refs[0].shape[1] // 2)
    for n in range(count):
        prepare_refs(refs[n], phases, *prepared[4 * n : 4 * n + 4])


def middle_kernel(count, early, own, cnb, *rest):
    refs, rest = rest[:count], rest[count:]
    ready, rest = rest[: 4 * early], rest[4 * early :]
    particles, rest = rest[:4], rest[4:]
    prepared, rest = rest[: 4 * count], rest[4 * count :]
    e_outs, stats_out = rest[:-1], rest[-1]
    place_half(own, cnb, *particles)
    particles = [x[...] for x in particles]
    facts = half_facts(own, cnb)
    prior = prior_rows(facts, refs[0].shape[0], particles[0].shape[0])
    phases = grid_phases(refs[0].shape[1] // 2)
    for n in range(early):
        e_outs[n][...] = block_scores(ready[4 * n : 4 * n + 4], particles, prior)
    for n in range(count):
        block = prepared[4 * n : 4 * n + 4]
        prepare_refs(refs[n], phases, *block)
        e_outs[early + n][...] = block_scores(block, particles, prior)
    weigh(e_outs, facts, e_outs, stats_out)


def late_kernel(blocks, ynb, cynb, early_stats, *rest):
    prepared, rest = rest[: 4 * blocks], rest[4 * blocks :]
    first_half, rest = rest[:4], rest[4:]
    e_outs, rest = rest[:blocks], rest[blocks:]
    y_out, power_out, stats_out, late_stats, *particles = rest
    place_half(ynb, cynb, *particles)
    half = [x[...] for x in particles]
    early = [x[...] for x in first_half]
    y_out[...] = deep_rows(early[0], early[1], half[0], half[1])
    power_out[...] = deep_rows(early[2], early[3], half[2], half[3])
    per = e_outs[0].shape[1]
    facts = half_facts(ynb, cynb)
    prior = prior_rows(facts, per, half[0].shape[0])
    for n in range(blocks):
        e_outs[n][...] = block_scores(prepared[4 * n : 4 * n + 4], half, prior)
    weigh(e_outs, facts, e_outs, late_stats)
    first = (lax.axis_index("dom") // 2) % 2 == 0
    mine, others = early_stats[...], late_stats[...]
    stats_out[:, :256] = jnp.where(first, mine, others)
    stats_out[:, 256:] = jnp.where(first, others, mine)


def sum_kernel(cuts, shifts, waits, *rest):
    team, rest = rest[:TEAM], rest[TEAM + waits :]
    ea_ref, eb_ref, y_ref, power_ref, *outs = rest
    per, lanes = ea_ref.shape[1:]
    width = y_ref.shape[1]
    freq = width // 2
    first = (lax.axis_index("dom") // 2) % 2 == 0
    team = [s[...] for s in team]
    top = team[0][0:1]
    for s in team[1:]:
        top = jnp.maximum(top, s[0:1])
    gains = [jnp.exp(s[0:1] - top) for s in team]
    mass = sum(g * s[1:2] for g, s in zip(gains, team))
    live = team[0][4:5] / mass
    own_gain = gains[0] * live
    gain_a = jnp.where(first, own_gain[:, :256], own_gain[:, 256:])[:, :lanes]
    gain_b = jnp.where(first, own_gain[:, 256:], own_gain[:, :256])[:, :lanes]
    if shifts:
        move = jnp.concatenate(
            [sum(g * s[k : k + 1] for g, s in zip(gains, team)) * live for k in (2, 3)], axis=0
        )
        move = jnp.concatenate([move, jnp.zeros((6, 512), jnp.float32)], axis=0)
        move = jnp.where(first, move[:, :256], move[:, 256:])
        lane = lax.broadcasted_iota(jnp.int32, (8, 128), 1)
        light = jnp.where(
            lane < 32, pltpu.roll(move[:, :128], 32, 1), pltpu.roll(move[:, 128:], 32, 1)
        )
        light = jnp.where(lane < 48, light, 0.0)
        shift_out = outs.pop()
        slots = shift_out.shape[1]
        shift_out[...] = jnp.where(even_core(), move[:, :128], light)[:2, :slots]
    wa = ea_ref[...] * gain_a[None]
    wb = eb_ref[...] * gain_b[None]
    rows = SHIFTS * per
    flat = dot_nn(deep_lanes(wa.reshape(rows, lanes), wb.reshape(rows, lanes)), y_ref[...])
    phases = grid_phases(freq)
    mid = SHIFTS // 2

    def block(t):
        return flat[t * per : (t + 1) * per, :freq], flat[t * per : (t + 1) * per, freq:]

    re, im = block(mid)
    for t in range(mid):
        c, s = phases[t]
        ar, ai = block(t)
        br, bi = block(SHIFTS - 1 - t)
        re = re + (ar + br) * c - (ai - bi) * s
        im = im + (ar - br) * s + (ai + bi) * c
    weight = dot_nn(deep_lanes(jnp.sum(wa, axis=0), jnp.sum(wb, axis=0)), power_ref[...])
    for start, stop, out in zip(cuts, cuts[1:], outs):
        part = slice(start, stop)
        out[:, :freq] = re[part]
        out[:, freq:width] = im[part]
        out[:, width:] = weight[part]


def add_kernel(a, b, out):
    out[...] = a[...] + b[...]


def final_kernel(row_cuts, *refs):
    own, *parts, signal, out = refs
    rows, width = out.shape
    freq = width // 2
    inverse = 1.0 / signal[...]
    every = sorted({cut for cuts in row_cuts for cut in cuts})
    for start, stop in zip(every, every[1:]):
        total = own[start:stop]
        at = 0
        for cuts in row_cuts:
            for low, high in zip(cuts, cuts[1:]):
                if low <= start and stop <= high:
                    total = total + parts[at][start - low : stop - low]
                at += 1
        denominator = total[:, width:] + inverse
        out[start:stop, :freq] = total[:, :freq] / denominator
        out[start:stop, freq:] = total[:, freq:width] / denominator


def params(mib):
    return pltpu.CompilerParams(vmem_limit_bytes=mib * 1024 * 1024)


def crossed(block, mask):
    size = lax.axis_size("dom")
    return lax.ppermute(block, "dom", [(i, i ^ mask) for i in range(size)])


def on_device(
    particle_fourier,
    defocus,
    particle_offset,
    prior_rotation,
    group_id,
    live_count,
    noise_power,
    signal_power,
    class_refs,
):
    slots, width = particle_fourier.shape
    freq = width // 2
    size = lax.axis_size("dom")
    blocks = size // TEAM
    refs_own = class_refs.reshape(-1, width)
    per = refs_own.shape[0]
    f32 = jnp.float32
    vmem = pl.BlockSpec(memory_space=pltpu.VMEM)
    no_cost = pl.CostEstimate(flops=0, bytes_accessed=0, transcendentals=0)

    ynb = crossed(particle_fourier, 2)
    anywhere = pl.BlockSpec(memory_space=pl.ANY)
    def gated(x, *waits):
        return pl.pallas_call(
            lambda *a: None,
            out_shape=jax.ShapeDtypeStruct(x.shape, x.dtype),
            in_specs=[anywhere] * (1 + len(waits)),
            out_specs=anywhere,
            input_output_aliases={0: 0},
            compiler_params=params(1),
            cost_estimate=no_cost,
            name="gate",
        )(x, *waits)

    ynb = crossed(particle_fourier, 2)
    refs = {0: refs_own}
    for n in (n for n in range(1, blocks) if n % 2):
        refs[n] = crossed(refs_own, TEAM * n)
    own_facts = (
        particle_fourier,
        defocus.reshape(1, slots),
        particle_offset.T,
        prior_rotation.reshape(1, slots),
        group_id.reshape(1, slots),
        noise_power,
    )
    own, facts, inverse_noise = pl.pallas_call(
        own_kernel,
        out_shape=(
            jax.ShapeDtypeStruct((slots + 8, width + freq), f32),
            jax.ShapeDtypeStruct((8, 128), f32),
            jax.ShapeDtypeStruct(noise_power.shape, f32),
        ),
        in_specs=[anywhere] * 6 + [pl.BlockSpec(memory_space=pltpu.SMEM)],
        out_specs=(vmem,) * 3,
        scratch_shapes=[pltpu.VMEM(x.shape, x.dtype) for x in own_facts]
        + [pltpu.SemaphoreType.DMA((6,))],
        compiler_params=params(6),
        cost_estimate=no_cost,
        name="own",
    )(*(pltpu.with_memory_space_constraint(x, pltpu.HBM) for x in own_facts), live_count)
    cnb = crossed(own, 1)
    for n in range(2, blocks, 2):
        refs[n + 1] = gated(refs[n + 1], facts)
        refs[n] = crossed(refs[n + 1], TEAM)
    refs = [refs[n] for n in range(blocks)]
    half = slots + slots // 2
    bf16 = jnp.bfloat16
    early = 2

    def shaped(rows, cols, dtype=f32):
        return jax.ShapeDtypeStruct((rows, cols), dtype)

    half_shapes = [shaped(half, width, bf16)] * 2 + [shaped(half, freq, bf16)] * 2
    block_shapes = [shaped(SHIFTS * per, width, bf16)] * 2 + [shaped(per, freq, bf16)] * 2
    score_shape = jax.ShapeDtypeStruct((SHIFTS, per, half), f32)

    def call(kernel, operands, out_shape, name, mib, waits=(), scratch=()):
        return pl.pallas_call(
            kernel,
            out_shape=tuple(out_shape),
            in_specs=[vmem] * len(operands),
            out_specs=(vmem,) * len(out_shape),
            scratch_shapes=list(scratch),
            compiler_params=params(mib),
            name=name,
        )(*operands)

    prepared = call(
        lambda *a: early_kernel(early, *a), refs[:early], block_shapes * early, "early", 8
    )
    ynb_prepared = pl.pallas_call(
        neighbour_kernel,
        out_shape=jax.ShapeDtypeStruct((slots + 8, width + freq), f32),
        in_specs=[vmem] * 3 + [anywhere],
        out_specs=vmem,
        compiler_params=params(6),
        cost_estimate=no_cost,
        name="neighbour",
    )(ynb, crossed(facts, 2), inverse_noise, prepared[2])
    ynb_prepared = gated(ynb_prepared, *refs[early:])
    cynb = crossed(ynb_prepared, 1)

    late = blocks - early
    outs = call(
        lambda *a: middle_kernel(late, early, *a),
        (own, cnb, *refs[early:], *prepared),
        half_shapes + block_shapes * late + [score_shape] * blocks + [shaped(8, 256)],
        "middle",
        8 + 2 * blocks,
    )
    particles, outs = outs[:4], outs[4:]
    prepared = (*prepared, *outs[: 4 * late])
    e_own, early_stats = outs[4 * late : -1], outs[-1]

    deep = 3 * 256 + 128
    outs = call(
        lambda *a: late_kernel(blocks, *a),
        (ynb_prepared, cynb, early_stats, *prepared, *particles),
        [score_shape] * blocks + [shaped(deep, width, bf16), shaped(deep, freq, bf16), shaped(8, 512)],
        "late",
        8 + 2 * blocks,
        scratch=[pltpu.VMEM((8, 256), f32)] + [pltpu.VMEM(x.shape, x.dtype) for x in half_shapes],
    )
    e_other, (y, power, stats) = outs[:blocks], outs[blocks:]

    team = [stats] + [crossed(stats, n) for n in range(1, TEAM)]

    def sums(n, cuts, shifts=False, waits=()):
        out_shape = [shaped(b - a, width + freq) for a, b in zip(cuts, cuts[1:])]
        if shifts:
            out_shape.append(shaped(2, slots))
        return pl.pallas_call(
            lambda *a: sum_kernel(cuts, shifts, len(waits), *a),
            out_shape=tuple(out_shape),
            in_specs=[vmem] * TEAM + [anywhere] * len(waits) + [vmem] * 4,
            out_specs=(vmem,) * len(out_shape),
            compiler_params=params(8),
            name="sums",
        )(*team, *waits, e_own[n], e_other[n], y, power)

    def combined(mine, other):
        return pl.pallas_call(
            add_kernel,
            out_shape=jax.ShapeDtypeStruct(mine.shape, f32),
            in_specs=[vmem] * 2,
            out_specs=vmem,
            compiler_params=params(4),
            name="combined",
        )(mine, other)

    uneven = (0, per // 2, per)
    even = (0, per // 2, per)
    row_cuts = []
    parts = []
    waits = []
    for n in range(2, blocks, 2):
        handed = [crossed(x, TEAM) for x in sums(n, uneven)]
        joined = [combined(x, y) for x, y in zip(sums(n + 1, uneven), handed)]
        parts.extend(crossed(x, TEAM * (n + 1)) for x in joined)
        row_cuts.append(uneven)
        waits.extend(joined)
    own_part, shift = sums(0, (0, per), shifts=True, waits=waits)
    parts += [crossed(x, TEAM) for x in sums(1, even, waits=waits)]
    row_cuts.append(even)

    refs_new = pl.pallas_call(
        lambda *a: final_kernel(row_cuts, *a),
        out_shape=jax.ShapeDtypeStruct((per, width), f32),
        in_specs=[vmem] * (len(parts) + 2),
        out_specs=vmem,
        compiler_params=params(2 + blocks),
        name="update",
    )(own_part, *parts, signal_power.reshape(1, freq))

    return (shift.T, refs_new.reshape(class_refs.shape))


def solution(mesh):
    in_specs = (
        P(("groups", "dom"), None),
        P(("groups", "dom")),
        P(("groups", "dom"), None),
        P(("groups", "dom")),
        P(("groups", "dom")),
        P(("groups", "dom")),
        P("groups", None),
        P("groups"),
        P(("groups", "dom"), None, None),
    )
    out_specs = (P(("groups", "dom"), None), P(("groups", "dom"), None, None))
    return jax.shard_map(
        on_device, mesh=mesh, in_specs=in_specs, out_specs=out_specs, check_vma=False
    )
```

```python
import math

import jax
import jax.numpy as jnp
from jax import lax
from jax.experimental import pallas as pl
from jax.experimental.pallas import tpu as pltpu
from jax.sharding import PartitionSpec as P

ROT = 16
SIDE = 3
BOX = 128
FY = 32
SHIFTS = 9
TEAM = 4
PRIOR = 2.0
CTF_SIZE = math.hypot(0.995, 0.1)
CTF_TURN = math.atan2(0.1, 0.995)
SINE = (
    9.99999976e-01,
    -1.66666476e-01,
    8.33289854e-03,
    -1.98008185e-04,
    2.59032780e-06,
)
TWO_PI = 2.0 * math.pi
PI_A = 3.140625
PI_B = 0.0009670257568359375
PI_C = math.pi - PI_A - PI_B
HIGHEST = lax.Precision.HIGHEST
GRID = tuple((t // SIDE - SIDE // 2, t % SIDE - SIDE // 2) for t in range(SHIFTS))


def half_turn_sine(x):
    s = x * x
    p = SINE[4]
    for c in SINE[3::-1]:
        p = p * s + c
    return x * p


def turn_cos(turns):
    t = jnp.abs(turns - jnp.round(turns))
    return half_turn_sine(TWO_PI * (0.25 - t))


def turn_sin(turns):
    return turn_cos(turns - 0.25)


def freq_rows(width, rows):
    f = lax.broadcasted_iota(jnp.int32, (rows, width), 1)
    kx = (f // FY).astype(jnp.float32)
    ky = (f % FY - FY // 2).astype(jnp.float32)
    return kx, ky


def dot_nt(a, b):
    return lax.dot_general(
        a, b, (((1,), (1,)), ((), ())), preferred_element_type=jnp.float32
    )


def dot_nn(a, b):
    return lax.dot_general(
        a, b, (((1,), (0,)), ((), ())), preferred_element_type=jnp.float32
    )


def exact_dot_nn(a, b):
    return lax.dot_general(
        a, b, (((1,), (0,)), ((), ())), precision=HIGHEST, preferred_element_type=jnp.float32
    )


def halves(x):
    high = x.astype(jnp.bfloat16)
    return high, (x - high.astype(jnp.float32)).astype(jnp.bfloat16)


def deep_rows(a_high, a_low, b_high, b_low):
    rows = a_high.shape[0]
    main, left = slice(0, 128), slice(128, rows)
    order = ((a_high, b_high), (a_low, b_low), (a_high, b_high))
    parts = [x[main] for pair in order for x in pair]
    parts += [x[left] for pair in order for x in pair]
    parts.append(jnp.zeros((128 - 6 * (rows - 128), a_high.shape[1]), a_high.dtype))
    return jnp.concatenate(parts, axis=0)


def deep_lanes(a, b):
    rows, lanes = a.shape
    left = lanes - 128
    high, low = halves(jnp.concatenate([a[:, :128], b[:, :128]], axis=1))
    empty = jnp.zeros((rows, 128 - left), jnp.float32)
    tail = jnp.concatenate([a[:, 128:], empty], axis=1) + pltpu.roll(
        jnp.concatenate([b[:, 128:], empty], axis=1), left, 1
    )
    tail_high = tail.astype(jnp.bfloat16).astype(jnp.float32)
    tail_low = tail - tail_high
    mixed = (
        tail_high + pltpu.roll(tail_high, 2 * left, 1) + pltpu.roll(tail_low, 4 * left, 1)
    )
    return jnp.concatenate([high, high, low, mixed.astype(jnp.bfloat16)], axis=1)


def grid_phases(width):
    kx, ky = freq_rows(width, 1)
    out = []
    for t, (gx, gy) in enumerate(GRID):
        if t < SHIFTS // 2:
            m = (kx * gx + ky * gy) * (1.0 / BOX)
            out.append((turn_cos(m), turn_sin(m)))
    return out


def phase_of(phases, t):
    mid = SHIFTS // 2
    if t < mid:
        return phases[t]
    c, s = phases[SHIFTS - 1 - t]
    return c, -s


def prepared_rows(src, facts, inverse_noise, out):
    slots, width = src.shape
    freq = width // 2
    columns = jnp.concatenate([facts, jnp.zeros((120, 128), jnp.float32)], axis=0).T[:slots]
    focus = columns[:, 0:1]
    off_x = columns[:, 1:2]
    off_y = columns[:, 2:3]
    group_col = columns[:, 4:5]

    kx, ky = freq_rows(freq, 1)
    chi = focus * ((kx * kx + ky * ky) * (1.0 / 1024.0))
    k = jnp.round(chi * (1.0 / math.pi))
    rest_angle = ((chi - k * PI_A) - k * PI_B) - k * PI_C
    shifted_angle = rest_angle + CTF_TURN
    over = shifted_angle > (0.5 * math.pi)
    folded = jnp.where(over, math.pi - shifted_angle, shifted_angle)
    parity = 0.5 * k
    sign = (parity - jnp.floor(parity)) * (4.0 * CTF_SIZE) - CTF_SIZE
    ctf = half_turn_sine(folded) * sign
    kx0, ky0 = freq_rows(128, 1)
    m = (kx0 * off_x + ky0 * off_y) * (1.0 / BOX)
    pc, ps = turn_cos(m), turn_sin(m)
    step = off_x * ((128 // FY) / BOX) + jnp.zeros((slots, 128), jnp.float32)
    sc, ss = turn_cos(step), turn_sin(step)

    total = inverse_noise.shape[0]
    onehot = (
        group_col == lax.broadcasted_iota(jnp.int32, (slots, total), 1).astype(jnp.float32)
    ).astype(jnp.float32)
    noise_rows = exact_dot_nn(onehot, inverse_noise)
    scaled = ctf * noise_rows
    out[:slots, width:] = ctf * scaled
    for n in range(freq // 128):
        part = slice(128 * n, 128 * (n + 1))
        twin = slice(freq + 128 * n, freq + 128 * (n + 1))
        co = pc * scaled[:, part]
        si = ps * scaled[:, part]
        pc, ps = pc * sc - ps * ss, ps * sc + pc * ss
        xr, xi = src[:, part], src[:, twin]
        out[:slots, part] = xr * co - xi * si
        out[:slots, twin] = xr * si + xi * co
    out[slots:, :128] = facts
    out[slots:, 128:] = jnp.zeros((8, width + freq - 128), jnp.float32)


def own_kernel(
    src_at, focus_at, offsets_at, prior_at, group_at, noise_at, live_count, out, facts_out,
    inverse_out, src, focus, offsets, prior, group, noise, sems
):
    moves = (
        (focus_at, focus), (offsets_at, offsets), (prior_at, prior), (group_at, group),
        (noise_at, noise), (src_at, src),
    )
    copies = [pltpu.make_async_copy(x, y, sems.at[n]) for n, (x, y) in enumerate(moves)]
    for copy in copies:
        copy.start()
    slots = src.shape[0]
    facts_out[...] = jnp.zeros_like(facts_out)
    slot = lax.broadcasted_iota(jnp.int32, (1, slots), 1)
    for copy in copies:
        copy.wait()
    facts_out[5:6, :slots] = (slot < live_count[0]).astype(jnp.float32)
    facts_out[0:1, :slots] = focus[...]
    facts_out[1:3, :slots] = offsets[...].astype(jnp.float32)
    facts_out[3:4, :slots] = prior[...].astype(jnp.float32)
    facts_out[4:5, :slots] = group[...].astype(jnp.float32)
    inverse = 1.0 / noise[...]
    inverse_out[...] = inverse
    prepared_rows(src, facts_out[...], inverse, out)


def neighbour_kernel(src_even, src_odd, facts, inverse_noise, wait, out, src):
    half = src_odd.shape[0]
    even = even_core()

    @pl.when(even)
    def _():
        src[...] = src_even[...]

    @pl.when(jnp.logical_not(even))
    def _():
        src[:half] = src_odd[...]
        src[half:] = jnp.zeros_like(src[half:])

    prepared_rows(src, facts[...], inverse_noise[...], out)


def even_core():
    return lax.axis_index("dom") % 2 == 0


def place_half(mine, other, y_high, y_low, p_high, p_low):
    width = y_high.shape[1]
    slots = mine.shape[0] - 8

    def place(src, to, size):
        dest = slice(to, to + size)
        high, low = halves(src[:size, :width])
        y_high[dest] = high
        y_low[dest] = low
        high, low = halves(src[:size, width:])
        p_high[dest] = high
        p_low[dest] = low

    even = even_core()

    @pl.when(even)
    def _():
        place(mine, 0, slots)
        place(other, slots, slots // 2)

    @pl.when(jnp.logical_not(even))
    def _():
        place(other, 0, slots)
        place(mine, slots, slots // 2)


def half_facts(mine, other):
    slots = mine.shape[0] - 8
    even = even_core()
    x, y = mine[slots:, :128], other[slots:, :128]
    heavy = jnp.where(even, x, y)
    light = pltpu.roll(jnp.where(even, y, x), 96, 1)
    lane = lax.broadcasted_iota(jnp.int32, (8, 128), 1)
    return jnp.concatenate([jnp.where(lane < 96, heavy, light), light], axis=1)


def prior_rows(facts, per, lanes):
    r = (lax.broadcasted_iota(jnp.int32, (per, lanes), 0) % ROT).astype(jnp.float32)
    return PRIOR * turn_cos((r - facts[3:4, :lanes]) * (1.0 / ROT))


def prepare_refs(ref, phases, r_high, r_low, q_high, q_low):
    per, width = ref.shape
    freq = width // 2
    rr, ri = ref[:, :freq], ref[:, freq:]
    mid = SHIFTS // 2

    def store(t, re, im):
        rows = slice(t * per, (t + 1) * per)
        r_high[rows, :freq], r_low[rows, :freq] = halves(re)
        r_high[rows, freq:], r_low[rows, freq:] = halves(im)

    store(mid, rr, ri)
    for t in range(mid):
        c, s = phases[t]
        a, b, d, e = rr * c, ri * s, ri * c, rr * s
        store(t, a + b, d - e)
        store(SHIFTS - 1 - t, a - b, d + e)
    q_high[...], q_low[...] = halves(rr * rr + ri * ri)


def block_scores(prepared, particles, prior):
    r_high, r_low, q_high, q_low = (x[...] for x in prepared)
    y_high, y_low, p_high, p_low = particles
    quad = dot_nt(q_high, p_high) + dot_nt(q_low, p_high) + dot_nt(q_high, p_low)
    score = dot_nt(r_high, y_high) + dot_nt(r_low, y_high) + dot_nt(r_high, y_low)
    per, lanes = prior.shape
    return score.reshape(SHIFTS, per, lanes) + (prior - 0.5 * quad)[None]


def weigh(scores, facts, e_outs, stats_out):
    per, lanes = scores[0].shape[1:]
    top = None
    for score in scores:
        top_here = jnp.max(score[...], axis=0)
        top = top_here if top is None else jnp.maximum(top, top_here)
    top = jnp.max(top, axis=0, keepdims=True)
    sums = [jnp.zeros((per, lanes), jnp.float32) for _ in range(SHIFTS)]
    for score, e_out in zip(scores, e_outs):
        for t in range(SHIFTS):
            e = jnp.exp(score[t] - top)
            e_out[t] = e
            sums[t] = sums[t] + e
    sums = [jnp.sum(s, axis=0, keepdims=True) for s in sums]
    stats_out[...] = jnp.zeros_like(stats_out)
    stats_out[0:1, :lanes] = top
    stats_out[1:2, :lanes] = sum(sums)
    stats_out[2:3, :lanes] = sum(s * float(gx) for s, (gx, gy) in zip(sums, GRID) if gx)
    stats_out[3:4, :lanes] = sum(s * float(gy) for s, (gx, gy) in zip(sums, GRID) if gy)
    stats_out[4:5, :lanes] = facts[5:6, :lanes]


def early_kernel(own_at, near, *rest):
    *prepared, own, sem = rest
    copy = pltpu.make_async_copy(own_at, own, sem)
    copy.start()
    phases = grid_phases(own.shape[1] // 2)
    prepare_refs(near, phases, *prepared[4:])
    copy.wait()
    prepare_refs(own, phases, *prepared[:4])


def middle_kernel(count, early, own, cnb, *rest):
    refs, rest = rest[:count], rest[count:]
    ready, rest = rest[: 4 * early], rest[4 * early :]
    particles, rest = rest[:4], rest[4:]
    prepared, rest = rest[: 4 * count], rest[4 * count :]
    e_outs, stats_out = rest[:-1], rest[-1]
    place_half(own, cnb, *particles)
    particles = [x[...] for x in particles]
    facts = half_facts(own, cnb)
    prior = prior_rows(facts, refs[0].shape[0], particles[0].shape[0])
    phases = grid_phases(refs[0].shape[1] // 2)
    for n in range(early):
        e_outs[n][...] = block_scores(ready[4 * n : 4 * n + 4], particles, prior)
    for n in range(count):
        block = prepared[4 * n : 4 * n + 4]
        prepare_refs(refs[n], phases, *block)
        e_outs[early + n][...] = block_scores(block, particles, prior)
    weigh(e_outs, facts, e_outs, stats_out)


def late_kernel(blocks, ynb, cynb, early_stats, *rest):
    prepared, rest = rest[: 4 * blocks], rest[4 * blocks :]
    first_half, rest = rest[:4], rest[4:]
    e_outs, rest = rest[:blocks], rest[blocks:]
    y_out, power_out, stats_out, late_stats, *particles = rest
    place_half(ynb, cynb, *particles)
    half = [x[...] for x in particles]
    early = [x[...] for x in first_half]
    y_out[...] = deep_rows(early[0], early[1], half[0], half[1])
    power_out[...] = deep_rows(early[2], early[3], half[2], half[3])
    per = e_outs[0].shape[1]
    facts = half_facts(ynb, cynb)
    prior = prior_rows(facts, per, half[0].shape[0])
    for n in range(blocks):
        e_outs[n][...] = block_scores(prepared[4 * n : 4 * n + 4], half, prior)
    weigh(e_outs, facts, e_outs, late_stats)
    first = (lax.axis_index("dom") // 2) % 2 == 0
    mine, others = early_stats[...], late_stats[...]
    stats_out[:, :256] = jnp.where(first, mine, others)
    stats_out[:, 256:] = jnp.where(first, others, mine)


def sum_kernel(cuts, shifts, waits, *rest):
    team, rest = rest[:TEAM], rest[TEAM + waits :]
    ea_ref, eb_ref, y_ref, power_ref, *outs = rest
    per, lanes = ea_ref.shape[1:]
    width = y_ref.shape[1]
    freq = width // 2
    first = (lax.axis_index("dom") // 2) % 2 == 0
    team = [s[...] for s in team]
    top = team[0][0:1]
    for s in team[1:]:
        top = jnp.maximum(top, s[0:1])
    gains = [jnp.exp(s[0:1] - top) for s in team]
    mass = sum(g * s[1:2] for g, s in zip(gains, team))
    live = team[0][4:5] / mass
    own_gain = gains[0] * live
    gain_a = jnp.where(first, own_gain[:, :256], own_gain[:, 256:])[:, :lanes]
    gain_b = jnp.where(first, own_gain[:, 256:], own_gain[:, :256])[:, :lanes]
    if shifts:
        move = jnp.concatenate(
            [sum(g * s[k : k + 1] for g, s in zip(gains, team)) * live for k in (2, 3)], axis=0
        )
        move = jnp.concatenate([move, jnp.zeros((6, 512), jnp.float32)], axis=0)
        move = jnp.where(first, move[:, :256], move[:, 256:])
        lane = lax.broadcasted_iota(jnp.int32, (8, 128), 1)
        light = jnp.where(
            lane < 32, pltpu.roll(move[:, :128], 32, 1), pltpu.roll(move[:, 128:], 32, 1)
        )
        light = jnp.where(lane < 48, light, 0.0)
        shift_out = outs.pop()
        slots = shift_out.shape[1]
        shift_out[...] = jnp.where(even_core(), move[:, :128], light)[:2, :slots]
    wa = ea_ref[...] * gain_a[None]
    wb = eb_ref[...] * gain_b[None]
    rows = SHIFTS * per
    flat = dot_nn(deep_lanes(wa.reshape(rows, lanes), wb.reshape(rows, lanes)), y_ref[...])
    phases = grid_phases(freq)
    mid = SHIFTS // 2

    def block(t):
        return flat[t * per : (t + 1) * per, :freq], flat[t * per : (t + 1) * per, freq:]

    re, im = block(mid)
    for t in range(mid):
        c, s = phases[t]
        ar, ai = block(t)
        br, bi = block(SHIFTS - 1 - t)
        re = re + (ar + br) * c - (ai - bi) * s
        im = im + (ar - br) * s + (ai + bi) * c
    weight = dot_nn(deep_lanes(jnp.sum(wa, axis=0), jnp.sum(wb, axis=0)), power_ref[...])
    for start, stop, out in zip(cuts, cuts[1:], outs):
        part = slice(start, stop)
        out[:, :freq] = re[part]
        out[:, freq:width] = im[part]
        out[:, width:] = weight[part]


def add_kernel(a, b, out):
    out[...] = a[...] + b[...]


def final_kernel(row_cuts, *refs):
    own, *parts, signal, out = refs
    rows, width = out.shape
    freq = width // 2
    inverse = 1.0 / signal[...]
    every = sorted({cut for cuts in row_cuts for cut in cuts})
    for start, stop in zip(every, every[1:]):
        total = own[start:stop]
        at = 0
        for cuts in row_cuts:
            for low, high in zip(cuts, cuts[1:]):
                if low <= start and stop <= high:
                    total = total + parts[at][start - low : stop - low]
                at += 1
        denominator = total[:, width:] + inverse
        out[start:stop, :freq] = total[:, :freq] / denominator
        out[start:stop, freq:] = total[:, freq:width] / denominator


def params(mib):
    return pltpu.CompilerParams(vmem_limit_bytes=mib * 1024 * 1024)


def crossed(block, mask, core=None):
    devices = [i for i in range(lax.axis_size("dom")) if core is None or i % 2 == core]
    return lax.ppermute(block, "dom", [(i, i ^ mask) for i in devices])


def on_device(
    particle_fourier,
    defocus,
    particle_offset,
    prior_rotation,
    group_id,
    live_count,
    noise_power,
    signal_power,
    class_refs,
):
    slots, width = particle_fourier.shape
    freq = width // 2
    size = lax.axis_size("dom")
    blocks = size // TEAM
    refs_own = class_refs.reshape(-1, width)
    per = refs_own.shape[0]
    f32 = jnp.float32
    vmem = pl.BlockSpec(memory_space=pltpu.VMEM)
    no_cost = pl.CostEstimate(flops=0, bytes_accessed=0, transcendentals=0)

    ynb = crossed(particle_fourier, 2)
    anywhere = pl.BlockSpec(memory_space=pl.ANY)
    def gated(arrays, waits, cost):
        return pl.pallas_call(
            lambda *a: None,
            out_shape=tuple(jax.ShapeDtypeStruct(x.shape, x.dtype) for x in arrays),
            in_specs=[anywhere] * (len(arrays) + len(waits)),
            out_specs=(anywhere,) * len(arrays),
            input_output_aliases={n: n for n in range(len(arrays))},
            compiler_params=params(1),
            cost_estimate=cost,
            name="gate",
        )(*arrays, *waits)

    ynb = crossed(particle_fourier, 2)
    anywhere = pl.BlockSpec(memory_space=pl.ANY)
    ynb_even = crossed(particle_fourier, 2, 0)
    ynb_odd = crossed(particle_fourier[: slots // 2], 2, 1)
    refs = {0: refs_own, 1: crossed(refs_own, TEAM)}
    for n in range(2, blocks, 2):
        refs[n] = crossed(refs_own, TEAM * n)
    own_facts = (
        particle_fourier,
        defocus.reshape(1, slots),
        particle_offset.T,
        prior_rotation.reshape(1, slots),
        group_id.reshape(1, slots),
        noise_power,
    )
    own, facts, inverse_noise = pl.pallas_call(
        own_kernel,
        out_shape=(
            jax.ShapeDtypeStruct((slots + 8, width + freq), f32),
            jax.ShapeDtypeStruct((8, 128), f32),
            jax.ShapeDtypeStruct(noise_power.shape, f32),
        ),
        in_specs=[anywhere] * 6 + [pl.BlockSpec(memory_space=pltpu.SMEM)],
        out_specs=(vmem,) * 3,
        scratch_shapes=[pltpu.VMEM(x.shape, x.dtype) for x in own_facts]
        + [pltpu.SemaphoreType.DMA((6,))],
        compiler_params=params(6),
        cost_estimate=no_cost,
        name="own",
    )(*(pltpu.with_memory_space_constraint(x, pltpu.HBM) for x in own_facts), live_count)
    cnb = crossed(own, 1)
    for n in range(2, blocks, 2):
        (refs[n],) = gated([refs[n]], [facts], no_cost)
        refs[n + 1] = crossed(refs[n], TEAM)
    refs = [refs[n] for n in range(blocks)]
    half = slots + slots // 2
    bf16 = jnp.bfloat16
    early = 2

    def shaped(rows, cols, dtype=f32):
        return jax.ShapeDtypeStruct((rows, cols), dtype)

    half_shapes = [shaped(half, width, bf16)] * 2 + [shaped(half, freq, bf16)] * 2
    block_shapes = [shaped(SHIFTS * per, width, bf16)] * 2 + [shaped(per, freq, bf16)] * 2
    score_shape = jax.ShapeDtypeStruct((SHIFTS, per, half), f32)

    def call(kernel, operands, out_shape, name, mib, cost=None, scratch=()):
        return pl.pallas_call(
            kernel,
            cost_estimate=cost,
            out_shape=tuple(out_shape),
            in_specs=[vmem] * len(operands),
            out_specs=(vmem,) * len(out_shape),
            scratch_shapes=list(scratch),
            compiler_params=params(mib),
            name=name,
        )(*operands)

    prepared = pl.pallas_call(
        early_kernel,
        out_shape=tuple(block_shapes * early),
        in_specs=[anywhere, vmem],
        out_specs=(vmem,) * (4 * early),
        scratch_shapes=[pltpu.VMEM(refs_own.shape, f32), pltpu.SemaphoreType.DMA],
        compiler_params=params(8),
        name="early",
    )(pltpu.with_memory_space_constraint(refs_own, pltpu.HBM), refs[1])
    ynb_prepared = pl.pallas_call(
        neighbour_kernel,
        out_shape=jax.ShapeDtypeStruct((slots + 8, width + freq), f32),
        in_specs=[vmem] * 4 + [anywhere],
        out_specs=vmem,
        compiler_params=params(6),
        scratch_shapes=[pltpu.VMEM((slots, width), f32)],
        cost_estimate=no_cost,
        name="neighbour",
    )(ynb_even, ynb_odd, crossed(facts, 2), inverse_noise, prepared[2])
    (ynb_prepared,) = gated([ynb_prepared], refs[early:], no_cost)
    cynb = crossed(ynb_prepared, 1)

    late = blocks - early
    outs = call(
        lambda *a: middle_kernel(late, early, *a),
        (own, cnb, *refs[early:], *prepared),
        half_shapes + block_shapes * late + [score_shape] * blocks + [shaped(8, 256)],
        "middle",
        8 + 2 * blocks,
    )
    particles, outs = outs[:4], outs[4:]
    prepared = (*prepared, *outs[: 4 * late])
    e_own, early_stats = outs[4 * late : -1], outs[-1]

    deep = 3 * 256 + 128
    outs = call(
        lambda *a: late_kernel(blocks, *a),
        (ynb_prepared, cynb, early_stats, *prepared, *particles),
        [score_shape] * blocks + [shaped(deep, width, bf16), shaped(deep, freq, bf16), shaped(8, 512)],
        "late",
        8 + 2 * blocks,
        scratch=[pltpu.VMEM((8, 256), f32)] + [pltpu.VMEM(x.shape, x.dtype) for x in half_shapes],
    )
    e_other, (y, power, stats) = outs[:blocks], outs[blocks:]

    team = [stats] + [crossed(stats, n) for n in range(1, TEAM)]

    def sums(n, cuts, shifts=False, waits=()):
        out_shape = [shaped(b - a, width + freq) for a, b in zip(cuts, cuts[1:])]
        if shifts:
            out_shape.append(shaped(2, slots))
        return pl.pallas_call(
            lambda *a: sum_kernel(cuts, shifts, len(waits), *a),
            out_shape=tuple(out_shape),
            in_specs=[vmem] * TEAM + [anywhere] * len(waits) + [vmem] * 4,
            out_specs=(vmem,) * len(out_shape),
            compiler_params=params(8),
            name="sums",
        )(*team, *waits, e_own[n], e_other[n], y, power)

    def combined(mine, other):
        return pl.pallas_call(
            add_kernel,
            out_shape=jax.ShapeDtypeStruct(mine.shape, f32),
            in_specs=[vmem] * 2,
            out_specs=vmem,
            compiler_params=params(4),
            name="combined",
        )(mine, other)

    cut = (0, per // 2, per)
    far = []
    waits = []
    for n in range(2, blocks, 2):
        handed = [crossed(x, TEAM) for x in sums(n + 1, cut)]
        joined = [combined(x, y) for x, y in zip(sums(n, cut), handed)]
        far.extend(crossed(x, TEAM * n) for x in joined)
        waits.extend(joined)
    own_part, shift = sums(0, (0, per), shifts=True, waits=waits)
    near = crossed(sums(1, (0, per), waits=waits)[0], TEAM)
    far = gated(far, [], pl.CostEstimate(flops=16 * 10**9, bytes_accessed=0, transcendentals=0))
    parts = [near, *far]
    row_cuts = [(0, per)] + [cut] * (len(far) // 2)

    refs_new = pl.pallas_call(
        lambda *a: final_kernel(row_cuts, *a),
        out_shape=jax.ShapeDtypeStruct((per, width), f32),
        in_specs=[vmem] * (len(parts) + 2),
        out_specs=vmem,
        compiler_params=params(2 + blocks),
        name="update",
    )(own_part, *parts, signal_power.reshape(1, freq))

    return (shift.T, refs_new.reshape(class_refs.shape))


def solution(mesh):
    in_specs = (
        P(("groups", "dom"), None),
        P(("groups", "dom")),
        P(("groups", "dom"), None),
        P(("groups", "dom")),
        P(("groups", "dom")),
        P(("groups", "dom")),
        P("groups", None),
        P("groups"),
        P(("groups", "dom"), None, None),
    )
    out_specs = (P(("groups", "dom"), None), P(("groups", "dom"), None, None))
    return jax.shard_map(
        on_device, mesh=mesh, in_specs=in_specs, out_specs=out_specs, check_vma=False
    )
```

```python
import math

import jax
import jax.numpy as jnp
from jax import lax
from jax.experimental import pallas as pl
from jax.experimental.pallas import tpu as pltpu
from jax.sharding import PartitionSpec as P

ROT = 16
SIDE = 3
BOX = 128
FY = 32
SHIFTS = 9
TEAM = 4
PRIOR = 2.0
CTF_SIZE = math.hypot(0.995, 0.1)
CTF_TURN = math.atan2(0.1, 0.995)
SINE = (
    9.99999976e-01,
    -1.66666476e-01,
    8.33289854e-03,
    -1.98008185e-04,
    2.59032780e-06,
)
TWO_PI = 2.0 * math.pi
PI_A = 3.140625
PI_B = 0.0009670257568359375
PI_C = math.pi - PI_A - PI_B
HIGHEST = lax.Precision.HIGHEST
GRID = tuple((t // SIDE - SIDE // 2, t % SIDE - SIDE // 2) for t in range(SHIFTS))


def half_turn_sine(x):
    s = x * x
    p = SINE[4]
    for c in SINE[3::-1]:
        p = p * s + c
    return x * p


def turn_cos(turns):
    t = jnp.abs(turns - jnp.round(turns))
    return half_turn_sine(TWO_PI * (0.25 - t))


def turn_sin(turns):
    return turn_cos(turns - 0.25)


def freq_rows(width, rows):
    f = lax.broadcasted_iota(jnp.int32, (rows, width), 1)
    kx = (f // FY).astype(jnp.float32)
    ky = (f % FY - FY // 2).astype(jnp.float32)
    return kx, ky


def dot_nt(a, b):
    return lax.dot_general(
        a, b, (((1,), (1,)), ((), ())), preferred_element_type=jnp.float32
    )


def dot_nn(a, b):
    return lax.dot_general(
        a, b, (((1,), (0,)), ((), ())), preferred_element_type=jnp.float32
    )


def exact_dot_nn(a, b):
    return lax.dot_general(
        a, b, (((1,), (0,)), ((), ())), precision=HIGHEST, preferred_element_type=jnp.float32
    )


def halves(x):
    high = x.astype(jnp.bfloat16)
    return high, (x - high.astype(jnp.float32)).astype(jnp.bfloat16)


def main_rows(half, part):
    return 256 * part + 128 * half


def left_rows(half, part, left):
    return 768 + 2 * left * part + left * half


def deep_lanes(a, b):
    rows, lanes = a.shape
    left = lanes - 128
    high, low = halves(jnp.concatenate([a[:, :128], b[:, :128]], axis=1))
    empty = jnp.zeros((rows, 128 - left), jnp.float32)
    tail = jnp.concatenate([a[:, 128:], empty], axis=1) + pltpu.roll(
        jnp.concatenate([b[:, 128:], empty], axis=1), left, 1
    )
    tail_high = tail.astype(jnp.bfloat16).astype(jnp.float32)
    tail_low = tail - tail_high
    mixed = (
        tail_high + pltpu.roll(tail_high, 2 * left, 1) + pltpu.roll(tail_low, 4 * left, 1)
    )
    return jnp.concatenate([high, high, low, mixed.astype(jnp.bfloat16)], axis=1)


def grid_phases(width):
    kx, ky = freq_rows(width, 1)
    out = []
    for t, (gx, gy) in enumerate(GRID):
        if t < SHIFTS // 2:
            m = (kx * gx + ky * gy) * (1.0 / BOX)
            out.append((turn_cos(m), turn_sin(m)))
    return out


def phase_of(phases, t):
    mid = SHIFTS // 2
    if t < mid:
        return phases[t]
    c, s = phases[SHIFTS - 1 - t]
    return c, -s


def prepared_rows(src, facts, inverse_noise, out):
    slots, width = src.shape
    freq = width // 2
    columns = jnp.concatenate([facts, jnp.zeros((120, 128), jnp.float32)], axis=0).T[:slots]
    focus = columns[:, 0:1]
    off_x = columns[:, 1:2]
    off_y = columns[:, 2:3]
    group_col = columns[:, 4:5]

    kx, ky = freq_rows(freq, 1)
    chi = focus * ((kx * kx + ky * ky) * (1.0 / 1024.0))
    k = jnp.round(chi * (1.0 / math.pi))
    rest_angle = ((chi - k * PI_A) - k * PI_B) - k * PI_C
    shifted_angle = rest_angle + CTF_TURN
    over = shifted_angle > (0.5 * math.pi)
    folded = jnp.where(over, math.pi - shifted_angle, shifted_angle)
    parity = 0.5 * k
    sign = (parity - jnp.floor(parity)) * (4.0 * CTF_SIZE) - CTF_SIZE
    ctf = half_turn_sine(folded) * sign
    kx0, ky0 = freq_rows(128, 1)
    m = (kx0 * off_x + ky0 * off_y) * (1.0 / BOX)
    pc, ps = turn_cos(m), turn_sin(m)
    step = off_x * ((128 // FY) / BOX) + jnp.zeros((slots, 128), jnp.float32)
    sc, ss = turn_cos(step), turn_sin(step)

    total = inverse_noise.shape[0]
    onehot = (
        group_col == lax.broadcasted_iota(jnp.int32, (slots, total), 1).astype(jnp.float32)
    ).astype(jnp.float32)
    noise_rows = exact_dot_nn(onehot, inverse_noise)
    scaled = ctf * noise_rows
    out[:slots, width:] = ctf * scaled
    for n in range(freq // 128):
        part = slice(128 * n, 128 * (n + 1))
        twin = slice(freq + 128 * n, freq + 128 * (n + 1))
        co = pc * scaled[:, part]
        si = ps * scaled[:, part]
        pc, ps = pc * sc - ps * ss, ps * sc + pc * ss
        xr, xi = src[:, part], src[:, twin]
        out[:slots, part] = xr * co - xi * si
        out[:slots, twin] = xr * si + xi * co
    out[slots:, :128] = facts
    out[slots:, 128:] = jnp.zeros((8, width + freq - 128), jnp.float32)


def own_kernel(
    src_at, focus_at, offsets_at, prior_at, group_at, noise_at, live_count, out, facts_out,
    inverse_out, src, focus, offsets, prior, group, noise, sems
):
    moves = (
        (focus_at, focus), (offsets_at, offsets), (prior_at, prior), (group_at, group),
        (noise_at, noise), (src_at, src),
    )
    copies = [pltpu.make_async_copy(x, y, sems.at[n]) for n, (x, y) in enumerate(moves)]
    for copy in copies:
        copy.start()
    slots = src.shape[0]
    facts_out[...] = jnp.zeros_like(facts_out)
    slot = lax.broadcasted_iota(jnp.int32, (1, slots), 1)
    for copy in copies:
        copy.wait()
    facts_out[5:6, :slots] = (slot < live_count[0]).astype(jnp.float32)
    facts_out[0:1, :slots] = focus[...]
    facts_out[1:3, :slots] = offsets[...].astype(jnp.float32)
    facts_out[3:4, :slots] = prior[...].astype(jnp.float32)
    facts_out[4:5, :slots] = group[...].astype(jnp.float32)
    inverse = 1.0 / noise[...]
    inverse_out[...] = inverse
    prepared_rows(src, facts_out[...], inverse, out)


def neighbour_kernel(src, facts, inverse_noise, wait, out):
    prepared_rows(src, facts[...], inverse_noise[...], out)


def even_core():
    return lax.axis_index("dom") % 2 == 0


def place_half(half, mine, other, y_out, power_out):
    width = y_out.shape[1]
    slots = mine.shape[0] - 8
    left = slots + slots // 2 - 128

    def place(src, rows, to):
        for cols, out in ((slice(0, width), y_out), (slice(width, None), power_out)):
            high, low = halves(src[rows, cols])
            for part, value in enumerate((high, low, high)):
                if to < 128:
                    at = main_rows(half, part) + to
                else:
                    at = left_rows(half, part, left) + to - 128
                out[at : at + value.shape[0]] = value

    def place_both(heavy, light):
        place(heavy, slice(0, slots), 0)
        place(light, slice(0, 128 - slots), slots)
        place(light, slice(128 - slots, slots // 2), 128)

    even = even_core()

    @pl.when(even)
    def _():
        place_both(mine, other)

    @pl.when(jnp.logical_not(even))
    def _():
        place_both(other, mine)


def placed(half, part, left, out):
    main, tail = main_rows(half, part), left_rows(half, part, left)
    return jnp.concatenate([out[main : main + 128], out[tail : tail + left]], axis=0)


def half_facts(mine, other):
    slots = mine.shape[0] - 8
    even = even_core()
    x, y = mine[slots:, :128], other[slots:, :128]
    heavy = jnp.where(even, x, y)
    light = pltpu.roll(jnp.where(even, y, x), 96, 1)
    lane = lax.broadcasted_iota(jnp.int32, (8, 128), 1)
    return jnp.concatenate([jnp.where(lane < 96, heavy, light), light], axis=1)


def prior_rows(facts, per, lanes):
    r = (lax.broadcasted_iota(jnp.int32, (per, lanes), 0) % ROT).astype(jnp.float32)
    return PRIOR * turn_cos((r - facts[3:4, :lanes]) * (1.0 / ROT))


def prepare_refs(ref, phases, r_high, r_low, q_high, q_low):
    per, width = ref.shape
    freq = width // 2
    rr, ri = ref[:, :freq], ref[:, freq:]
    mid = SHIFTS // 2

    def store(t, re, im):
        rows = slice(t * per, (t + 1) * per)
        r_high[rows, :freq], r_low[rows, :freq] = halves(re)
        r_high[rows, freq:], r_low[rows, freq:] = halves(im)

    store(mid, rr, ri)
    for t in range(mid):
        c, s = phases[t]
        a, b, d, e = rr * c, ri * s, ri * c, rr * s
        store(t, a + b, d - e)
        store(SHIFTS - 1 - t, a - b, d + e)
    q_high[...], q_low[...] = halves(rr * rr + ri * ri)


def block_scores(prepared, particles, prior):
    r_high, r_low, q_high, q_low = (x[...] for x in prepared)
    y_high, y_low, p_high, p_low = particles
    quad = dot_nt(q_high, p_high) + dot_nt(q_low, p_high) + dot_nt(q_high, p_low)
    score = dot_nt(r_high, y_high) + dot_nt(r_low, y_high) + dot_nt(r_high, y_low)
    per, lanes = prior.shape
    return score.reshape(SHIFTS, per, lanes) + (prior - 0.5 * quad)[None]


def weigh(scores, facts, e_outs, stats_out):
    per, lanes = scores[0].shape[1:]
    top = None
    for score in scores:
        top_here = jnp.max(score[...], axis=0)
        top = top_here if top is None else jnp.maximum(top, top_here)
    top = jnp.max(top, axis=0, keepdims=True)
    sums = [jnp.zeros((per, lanes), jnp.float32) for _ in range(SHIFTS)]
    for score, e_out in zip(scores, e_outs):
        for t in range(SHIFTS):
            e = jnp.exp(score[t] - top)
            e_out[t] = e
            sums[t] = sums[t] + e
    sums = [jnp.sum(s, axis=0, keepdims=True) for s in sums]
    stats_out[...] = jnp.zeros_like(stats_out)
    stats_out[0:1, :lanes] = top
    stats_out[1:2, :lanes] = sum(sums)
    stats_out[2:3, :lanes] = sum(s * float(gx) for s, (gx, gy) in zip(sums, GRID) if gx)
    stats_out[3:4, :lanes] = sum(s * float(gy) for s, (gx, gy) in zip(sums, GRID) if gy)
    stats_out[4:5, :lanes] = facts[5:6, :lanes]


def early_kernel(own_at, near, *rest):
    *prepared, own, sem = rest
    copy = pltpu.make_async_copy(own_at, own, sem)
    copy.start()
    phases = grid_phases(own.shape[1] // 2)
    prepare_refs(near, phases, *prepared[4:])
    copy.wait()
    prepare_refs(own, phases, *prepared[:4])


def middle_kernel(*rest):
    count = len(rest) // 5
    refs, prepared = rest[:count], rest[count:]
    phases = grid_phases(refs[0].shape[1] // 2)
    for n in range(count):
        prepare_refs(refs[n], phases, *prepared[4 * n : 4 * n + 4])


def late_kernel(blocks, own, cnb, ynb, cynb, *rest):
    prepared, rest = rest[: 4 * blocks], rest[4 * blocks :]
    e_outs, rest = (rest[:blocks], rest[blocks : 2 * blocks]), rest[2 * blocks :]
    y_out, power_out, stats_out, *half_stats = rest
    per, lanes = e_outs[0][0].shape[1:]
    left = lanes - 128
    pairs = ((own, cnb), (ynb, cynb))
    facts = [half_facts(*pair) for pair in pairs]
    for half, pair in enumerate(pairs):
        place_half(half, *pair, y_out, power_out)
        empty = 768 + 6 * left
    for out in (y_out, power_out):
        out[empty:] = jnp.zeros_like(out[empty:])
    for half in range(2):
        particles = [placed(half, part, left, out) for out in (y_out, power_out) for part in (0, 1)]
        prior = prior_rows(facts[half], per, lanes)
        for n in range(blocks):
            e_outs[half][n][...] = block_scores(prepared[4 * n : 4 * n + 4], particles, prior)
        weigh(e_outs[half], facts[half], e_outs[half], half_stats[half])
    first = (lax.axis_index("dom") // 2) % 2 == 0
    mine, others = half_stats[0][...], half_stats[1][...]
    stats_out[:, :256] = jnp.where(first, mine, others)
    stats_out[:, 256:] = jnp.where(first, others, mine)


def sum_kernel(cuts, last, waits, *rest):
    team, rest = rest[:TEAM], rest[TEAM + waits :]
    if last:
        *near, ea_ref, eb_ref, y_ref, power_ref, part_out, shift_out = rest
        near = jnp.concatenate([x[...] for x in near], axis=0)
        rest = ea_ref, eb_ref, y_ref, power_ref, part_out, shift_out
    ea_ref, eb_ref, y_ref, power_ref, *outs = rest
    per, lanes = ea_ref.shape[1:]
    width = y_ref.shape[1]
    freq = width // 2
    first = (lax.axis_index("dom") // 2) % 2 == 0
    team = [s[...] for s in team]
    top = team[0][0:1]
    for s in team[1:]:
        top = jnp.maximum(top, s[0:1])
    gains = [jnp.exp(s[0:1] - top) for s in team]
    mass = sum(g * s[1:2] for g, s in zip(gains, team))
    live = team[0][4:5] / mass
    own_gain = gains[0] * live
    gain_a = jnp.where(first, own_gain[:, :256], own_gain[:, 256:])[:, :lanes]
    gain_b = jnp.where(first, own_gain[:, 256:], own_gain[:, :256])[:, :lanes]
    if last:
        move = jnp.concatenate(
            [sum(g * s[k : k + 1] for g, s in zip(gains, team)) * live for k in (2, 3)], axis=0
        )
        move = jnp.concatenate([move, jnp.zeros((6, 512), jnp.float32)], axis=0)
        move = jnp.where(first, move[:, :256], move[:, 256:])
        lane = lax.broadcasted_iota(jnp.int32, (8, 128), 1)
        light = jnp.where(
            lane < 32, pltpu.roll(move[:, :128], 32, 1), pltpu.roll(move[:, 128:], 32, 1)
        )
        light = jnp.where(lane < 48, light, 0.0)
        shift_out = outs.pop()
        slots = shift_out.shape[1]
        shift_out[...] = jnp.where(even_core(), move[:, :128], light)[:2, :slots]
    wa = ea_ref[...] * gain_a[None]
    wb = eb_ref[...] * gain_b[None]
    rows = SHIFTS * per
    flat = dot_nn(deep_lanes(wa.reshape(rows, lanes), wb.reshape(rows, lanes)), y_ref[...])
    phases = grid_phases(freq)
    mid = SHIFTS // 2

    def block(t):
        return flat[t * per : (t + 1) * per, :freq], flat[t * per : (t + 1) * per, freq:]

    re, im = block(mid)
    for t in range(mid):
        c, s = phases[t]
        ar, ai = block(t)
        br, bi = block(SHIFTS - 1 - t)
        re = re + (ar + br) * c - (ai - bi) * s
        im = im + (ar - br) * s + (ai + bi) * c
    weight = dot_nn(deep_lanes(jnp.sum(wa, axis=0), jnp.sum(wb, axis=0)), power_ref[...])
    if last:
        re = re + near[:, :freq]
        im = im + near[:, freq:width]
        weight = weight + near[:, width:]
    for start, stop, out in zip(cuts, cuts[1:], outs):
        part = slice(start, stop)
        out[:, :freq] = re[part]
        out[:, freq:width] = im[part]
        out[:, width:] = weight[part]


def add_kernel(a, b, out):
    out[...] = a[...] + b[...]


def final_kernel(row_cuts, *refs):
    own, *parts, signal, out = refs
    rows, width = out.shape
    freq = width // 2
    inverse = 1.0 / signal[...]
    every = sorted({cut for cuts in row_cuts for cut in cuts})
    for start, stop in zip(every, every[1:]):
        total = own[start:stop]
        at = 0
        for cuts in row_cuts:
            for low, high in zip(cuts, cuts[1:]):
                if low <= start and stop <= high:
                    total = total + parts[at][start - low : stop - low]
                at += 1
        denominator = total[:, width:] + inverse
        out[start:stop, :freq] = total[:, :freq] / denominator
        out[start:stop, freq:] = total[:, freq:width] / denominator


def params(mib):
    return pltpu.CompilerParams(vmem_limit_bytes=mib * 1024 * 1024)


def crossed(block, mask):
    size = lax.axis_size("dom")
    return lax.ppermute(block, "dom", [(i, i ^ mask) for i in range(size)])


def on_device(
    particle_fourier,
    defocus,
    particle_offset,
    prior_rotation,
    group_id,
    live_count,
    noise_power,
    signal_power,
    class_refs,
):
    slots, width = particle_fourier.shape
    freq = width // 2
    size = lax.axis_size("dom")
    blocks = size // TEAM
    refs_own = class_refs.reshape(-1, width)
    per = refs_own.shape[0]
    f32 = jnp.float32
    vmem = pl.BlockSpec(memory_space=pltpu.VMEM)
    no_cost = pl.CostEstimate(flops=0, bytes_accessed=0, transcendentals=0)

    ynb = crossed(particle_fourier, 2)
    anywhere = pl.BlockSpec(memory_space=pl.ANY)
    ynb = crossed(particle_fourier, 2)
    anywhere = pl.BlockSpec(memory_space=pl.ANY)
    def gated(arrays, waits, cost):
        return pl.pallas_call(
            lambda *a: None,
            out_shape=tuple(jax.ShapeDtypeStruct(x.shape, x.dtype) for x in arrays),
            in_specs=[anywhere] * (len(arrays) + len(waits)),
            out_specs=(anywhere,) * len(arrays),
            input_output_aliases={n: n for n in range(len(arrays))},
            compiler_params=params(1),
            cost_estimate=cost,
            name="gate",
        )(*arrays, *waits)

    ynb = crossed(particle_fourier, 2)
    anywhere = pl.BlockSpec(memory_space=pl.ANY)
    ynb = crossed(particle_fourier, 2)
    refs = [refs_own] + [crossed(refs_own, TEAM * n) for n in range(1, blocks)]
    own_facts = (
        particle_fourier,
        defocus.reshape(1, slots),
        particle_offset.T,
        prior_rotation.reshape(1, slots),
        group_id.reshape(1, slots),
        noise_power,
    )
    own, facts, inverse_noise = pl.pallas_call(
        own_kernel,
        out_shape=(
            jax.ShapeDtypeStruct((slots + 8, width + freq), f32),
            jax.ShapeDtypeStruct((8, 128), f32),
            jax.ShapeDtypeStruct(noise_power.shape, f32),
        ),
        in_specs=[anywhere] * 6 + [pl.BlockSpec(memory_space=pltpu.SMEM)],
        out_specs=(vmem,) * 3,
        scratch_shapes=[pltpu.VMEM(x.shape, x.dtype) for x in own_facts]
        + [pltpu.SemaphoreType.DMA((6,))],
        compiler_params=params(6),
        cost_estimate=no_cost,
        name="own",
    )(*(pltpu.with_memory_space_constraint(x, pltpu.HBM) for x in own_facts), live_count)
    cnb = crossed(own, 1)
    half = slots + slots // 2
    bf16 = jnp.bfloat16
    early = 2

    def shaped(rows, cols, dtype=f32):
        return jax.ShapeDtypeStruct((rows, cols), dtype)

    block_shapes = [shaped(SHIFTS * per, width, bf16)] * 2 + [shaped(per, freq, bf16)] * 2
    score_shape = jax.ShapeDtypeStruct((SHIFTS, per, half), f32)

    def call(kernel, operands, out_shape, name, mib, cost=None, scratch=()):
        return pl.pallas_call(
            kernel,
            cost_estimate=cost,
            out_shape=tuple(out_shape),
            in_specs=[vmem] * len(operands),
            out_specs=(vmem,) * len(out_shape),
            scratch_shapes=list(scratch),
            compiler_params=params(mib),
            name=name,
        )(*operands)

    prepared = pl.pallas_call(
        early_kernel,
        out_shape=tuple(block_shapes * early),
        in_specs=[anywhere, vmem],
        out_specs=(vmem,) * (4 * early),
        scratch_shapes=[pltpu.VMEM(refs_own.shape, f32), pltpu.SemaphoreType.DMA],
        compiler_params=params(8),
        name="early",
    )(pltpu.with_memory_space_constraint(refs_own, pltpu.HBM), refs[1])
    ynb_prepared = pl.pallas_call(
        neighbour_kernel,
        out_shape=jax.ShapeDtypeStruct((slots + 8, width + freq), f32),
        in_specs=[vmem] * 3 + [anywhere],
        out_specs=vmem,
        compiler_params=params(6),
        cost_estimate=no_cost,
        name="neighbour",
    )(ynb, crossed(facts, 2), inverse_noise, prepared[2])
    cynb = crossed(ynb_prepared, 1)

    late = blocks - early
    outs = call(
        middle_kernel,
        refs[early:],
        block_shapes * late,
        "middle",
        4 + 2 * blocks,
        pl.CostEstimate(flops=16 * 10**9, bytes_accessed=0, transcendentals=0),
    )
    prepared = (*prepared, *outs)
    deep = 3 * 256 + 128
    outs = call(
        lambda *a: late_kernel(blocks, *a),
        (own, cnb, ynb_prepared, cynb, *prepared),
        [score_shape] * (2 * blocks)
        + [shaped(deep, width, bf16), shaped(deep, freq, bf16), shaped(8, 512)],
        "late",
        8 + 2 * blocks,
        scratch=[pltpu.VMEM((8, 256), f32)] * 2,
    )
    e_own, e_other, (y, power, stats) = outs[:blocks], outs[blocks : 2 * blocks], outs[2 * blocks :]

    team = [stats] + [crossed(stats, n) for n in range(1, TEAM)]

    def sums(n, cuts, near=(), waits=()):
        out_shape = [shaped(b - a, width + freq) for a, b in zip(cuts, cuts[1:])]
        if near:
            out_shape.append(shaped(2, slots))
        return pl.pallas_call(
            lambda *a: sum_kernel(cuts, bool(near), len(waits), *a),
            out_shape=tuple(out_shape),
            in_specs=[vmem] * TEAM + [anywhere] * len(waits) + [vmem] * (4 + len(near)),
            out_specs=(vmem,) * len(out_shape),
            compiler_params=params(8),
            name="sums",
        )(*team, *waits, *near, e_own[n], e_other[n], y, power)

    def combined(mine, other):
        return pl.pallas_call(
            add_kernel,
            out_shape=jax.ShapeDtypeStruct(mine.shape, f32),
            in_specs=[vmem] * 2,
            out_specs=vmem,
            compiler_params=params(4),
            name="combined",
        )(mine, other)

    whole, cut = (0, per), (0, per // 2, per)
    far = []
    waits = []
    for n in range(2, blocks, 2):
        handed = [crossed(x, TEAM) for x in sums(n + 1, cut)]
        if n == 2:
            near = sums(1, cut)
        joined = [combined(x, y) for x, y in zip(sums(n, cut, waits=near[:1]), handed)]
        far.extend(crossed(x, TEAM * n) for x in joined)
        waits.extend(joined)
    own_part, shift = sums(0, whole, near=[crossed(x, TEAM) for x in near], waits=waits)
    row_cuts = [cut] * (len(far) // 2)

    refs_new = pl.pallas_call(
        lambda *a: final_kernel(row_cuts, *a),
        out_shape=jax.ShapeDtypeStruct((per, width), f32),
        in_specs=[vmem] * (len(far) + 2),
        out_specs=vmem,
        compiler_params=params(2 + blocks),
        name="update",
    )(own_part, *far, signal_power.reshape(1, freq))

    return (shift.T, refs_new.reshape(class_refs.shape))


def solution(mesh):
    in_specs = (
        P(("groups", "dom"), None),
        P(("groups", "dom")),
        P(("groups", "dom"), None),
        P(("groups", "dom")),
        P(("groups", "dom")),
        P(("groups", "dom")),
        P("groups", None),
        P("groups"),
        P(("groups", "dom"), None, None),
    )
    out_specs = (P(("groups", "dom"), None), P(("groups", "dom"), None, None))
    return jax.shard_map(
        on_device, mesh=mesh, in_specs=in_specs, out_specs=out_specs, check_vma=False
    )
```

```python
import math

import jax
import jax.numpy as jnp
from jax import lax
from jax.experimental import pallas as pl
from jax.experimental.pallas import tpu as pltpu
from jax.sharding import PartitionSpec as P

ROT = 16
SIDE = 3
BOX = 128
FY = 32
SHIFTS = 9
TEAM = 4
PRIOR = 2.0
CTF_SIZE = math.hypot(0.995, 0.1)
CTF_TURN = math.atan2(0.1, 0.995)
SINE = (
    9.99999976e-01,
    -1.66666476e-01,
    8.33289854e-03,
    -1.98008185e-04,
    2.59032780e-06,
)
TWO_PI = 2.0 * math.pi
PI_A = 3.140625
PI_B = 0.0009670257568359375
PI_C = math.pi - PI_A - PI_B
HIGHEST = lax.Precision.HIGHEST
GRID = tuple((t // SIDE - SIDE // 2, t % SIDE - SIDE // 2) for t in range(SHIFTS))


def half_turn_sine(x):
    s = x * x
    p = SINE[4]
    for c in SINE[3::-1]:
        p = p * s + c
    return x * p


def turn_cos(turns):
    t = jnp.abs(turns - jnp.round(turns))
    return half_turn_sine(TWO_PI * (0.25 - t))


def turn_sin(turns):
    return turn_cos(turns - 0.25)


def freq_rows(width, rows):
    f = lax.broadcasted_iota(jnp.int32, (rows, width), 1)
    kx = (f // FY).astype(jnp.float32)
    ky = (f % FY - FY // 2).astype(jnp.float32)
    return kx, ky


def dot_nt(a, b):
    return lax.dot_general(
        a, b, (((1,), (1,)), ((), ())), preferred_element_type=jnp.float32
    )


def dot_nn(a, b):
    return lax.dot_general(
        a, b, (((1,), (0,)), ((), ())), preferred_element_type=jnp.float32
    )


def exact_dot_nn(a, b):
    return lax.dot_general(
        a, b, (((1,), (0,)), ((), ())), precision=HIGHEST, preferred_element_type=jnp.float32
    )


def halves(x):
    high = x.astype(jnp.bfloat16)
    return high, (x - high.astype(jnp.float32)).astype(jnp.bfloat16)


def main_rows(half, part):
    return 256 * part + 128 * half


def left_rows(half, part, left):
    return 768 + 2 * left * part + left * half


def deep_lanes(a, b):
    rows, lanes = a.shape
    left = lanes - 128
    high, low = halves(jnp.concatenate([a[:, :128], b[:, :128]], axis=1))
    empty = jnp.zeros((rows, 128 - left), jnp.float32)
    tail = jnp.concatenate([a[:, 128:], empty], axis=1) + pltpu.roll(
        jnp.concatenate([b[:, 128:], empty], axis=1), left, 1
    )
    tail_high = tail.astype(jnp.bfloat16).astype(jnp.float32)
    tail_low = tail - tail_high
    mixed = (
        tail_high + pltpu.roll(tail_high, 2 * left, 1) + pltpu.roll(tail_low, 4 * left, 1)
    )
    return jnp.concatenate([high, high, low, mixed.astype(jnp.bfloat16)], axis=1)


def grid_phases(width):
    kx, ky = freq_rows(width, 1)
    out = []
    for t, (gx, gy) in enumerate(GRID):
        if t < SHIFTS // 2:
            m = (kx * gx + ky * gy) * (1.0 / BOX)
            out.append((turn_cos(m), turn_sin(m)))
    return out


def phase_of(phases, t):
    mid = SHIFTS // 2
    if t < mid:
        return phases[t]
    c, s = phases[SHIFTS - 1 - t]
    return c, -s


def prepared_rows(src, facts, inverse_noise, out):
    slots, width = src.shape
    freq = width // 2
    columns = jnp.concatenate([facts, jnp.zeros((120, 128), jnp.float32)], axis=0).T[:slots]
    focus = columns[:, 0:1]
    off_x = columns[:, 1:2]
    off_y = columns[:, 2:3]
    group_col = columns[:, 4:5]

    kx, ky = freq_rows(freq, 1)
    chi = focus * ((kx * kx + ky * ky) * (1.0 / 1024.0))
    k = jnp.round(chi * (1.0 / math.pi))
    rest_angle = ((chi - k * PI_A) - k * PI_B) - k * PI_C
    shifted_angle = rest_angle + CTF_TURN
    over = shifted_angle > (0.5 * math.pi)
    folded = jnp.where(over, math.pi - shifted_angle, shifted_angle)
    parity = 0.5 * k
    sign = (parity - jnp.floor(parity)) * (4.0 * CTF_SIZE) - CTF_SIZE
    ctf = half_turn_sine(folded) * sign
    kx0, ky0 = freq_rows(128, 1)
    m = (kx0 * off_x + ky0 * off_y) * (1.0 / BOX)
    pc, ps = turn_cos(m), turn_sin(m)
    step = off_x * ((128 // FY) / BOX) + jnp.zeros((slots, 128), jnp.float32)
    sc, ss = turn_cos(step), turn_sin(step)

    total = inverse_noise.shape[0]
    onehot = (
        group_col == lax.broadcasted_iota(jnp.int32, (slots, total), 1).astype(jnp.float32)
    ).astype(jnp.float32)
    noise_rows = exact_dot_nn(onehot, inverse_noise)
    scaled = ctf * noise_rows
    out[:slots, width:] = ctf * scaled
    for n in range(freq // 128):
        part = slice(128 * n, 128 * (n + 1))
        twin = slice(freq + 128 * n, freq + 128 * (n + 1))
        co = pc * scaled[:, part]
        si = ps * scaled[:, part]
        pc, ps = pc * sc - ps * ss, ps * sc + pc * ss
        xr, xi = src[:, part], src[:, twin]
        out[:slots, part] = xr * co - xi * si
        out[:slots, twin] = xr * si + xi * co
    out[slots:, :128] = facts
    out[slots:, 128:] = jnp.zeros((8, width + freq - 128), jnp.float32)


def own_kernel(
    src_at, focus_at, offsets_at, prior_at, group_at, noise_at, live_count, out, facts_out,
    inverse_out, src, focus, offsets, prior, group, noise, sems
):
    moves = (
        (focus_at, focus), (offsets_at, offsets), (prior_at, prior), (group_at, group),
        (noise_at, noise), (src_at, src),
    )
    copies = [pltpu.make_async_copy(x, y, sems.at[n]) for n, (x, y) in enumerate(moves)]
    for copy in copies:
        copy.start()
    slots = src.shape[0]
    facts_out[...] = jnp.zeros_like(facts_out)
    slot = lax.broadcasted_iota(jnp.int32, (1, slots), 1)
    for copy in copies:
        copy.wait()
    facts_out[5:6, :slots] = (slot < live_count[0]).astype(jnp.float32)
    facts_out[0:1, :slots] = focus[...]
    facts_out[1:3, :slots] = offsets[...].astype(jnp.float32)
    facts_out[3:4, :slots] = prior[...].astype(jnp.float32)
    facts_out[4:5, :slots] = group[...].astype(jnp.float32)
    inverse = 1.0 / noise[...]
    inverse_out[...] = inverse
    prepared_rows(src, facts_out[...], inverse, out)


def neighbour_kernel(src, facts, inverse_noise, wait, out):
    prepared_rows(src, facts[...], inverse_noise[...], out)


def even_core():
    return lax.axis_index("dom") % 2 == 0


def place_half(half, mine, other, y_out, power_out):
    width = y_out.shape[1]
    slots = mine.shape[0] - 8
    left = slots + slots // 2 - 128

    def place(src, rows, to):
        for cols, out in ((slice(0, width), y_out), (slice(width, None), power_out)):
            high, low = halves(src[rows, cols])
            for part, value in enumerate((high, low, high)):
                if to < 128:
                    at = main_rows(half, part) + to
                else:
                    at = left_rows(half, part, left) + to - 128
                out[at : at + value.shape[0]] = value

    def place_both(heavy, light):
        place(heavy, slice(0, slots), 0)
        place(light, slice(0, 128 - slots), slots)
        place(light, slice(128 - slots, slots // 2), 128)

    even = even_core()

    @pl.when(even)
    def _():
        place_both(mine, other)

    @pl.when(jnp.logical_not(even))
    def _():
        place_both(other, mine)


def placed(half, part, left, out):
    main, tail = main_rows(half, part), left_rows(half, part, left)
    return jnp.concatenate([out[main : main + 128], out[tail : tail + left]], axis=0)


def half_facts(mine, other):
    slots = mine.shape[0] - 8
    even = even_core()
    x, y = mine[slots:, :128], other[slots:, :128]
    heavy = jnp.where(even, x, y)
    light = pltpu.roll(jnp.where(even, y, x), 96, 1)
    lane = lax.broadcasted_iota(jnp.int32, (8, 128), 1)
    return jnp.concatenate([jnp.where(lane < 96, heavy, light), light], axis=1)


def prior_rows(facts, per, lanes):
    r = (lax.broadcasted_iota(jnp.int32, (per, lanes), 0) % ROT).astype(jnp.float32)
    return PRIOR * turn_cos((r - facts[3:4, :lanes]) * (1.0 / ROT))


def prepare_refs(ref, phases, r_high, r_low, q_high, q_low):
    per, width = ref.shape
    freq = width // 2
    rr, ri = ref[:, :freq], ref[:, freq:]
    mid = SHIFTS // 2

    def store(t, re, im):
        rows = slice(t * per, (t + 1) * per)
        r_high[rows, :freq], r_low[rows, :freq] = halves(re)
        r_high[rows, freq:], r_low[rows, freq:] = halves(im)

    store(mid, rr, ri)
    for t in range(mid):
        c, s = phases[t]
        a, b, d, e = rr * c, ri * s, ri * c, rr * s
        store(t, a + b, d - e)
        store(SHIFTS - 1 - t, a - b, d + e)
    q_high[...], q_low[...] = halves(rr * rr + ri * ri)


def block_scores(prepared, particles, prior):
    r_high, r_low, q_high, q_low = (x[...] for x in prepared)
    y_high, y_low, p_high, p_low = particles
    quad = dot_nt(q_high, p_high) + dot_nt(q_low, p_high) + dot_nt(q_high, p_low)
    score = dot_nt(r_high, y_high) + dot_nt(r_low, y_high) + dot_nt(r_high, y_low)
    per, lanes = prior.shape
    return score.reshape(SHIFTS, per, lanes) + (prior - 0.5 * quad)[None]


def weigh(score, e_out):
    top = jnp.max(jnp.max(score, axis=0), axis=0, keepdims=True)
    e = jnp.exp(score - top[None])
    e_out[...] = e
    side = SIDE // 2
    by_x = [sum(e[SIDE * x + y] for y in range(SIDE)) for x in range(SIDE)]
    by_y = [sum(e[SIDE * x + y] for x in range(SIDE)) for y in range(SIDE)]
    sums = [sum(by_x)]
    for by in (by_x, by_y):
        sums.append(sum(by[k] * float(k - side) for k in range(SIDE) if k != side))
    return top, [jnp.sum(x, axis=0, keepdims=True) for x in sums]


def joined_sums(tops, sums):
    top = tops[0]
    for other in tops[1:]:
        top = jnp.maximum(top, other)
    factors = [jnp.exp(other - top) for other in tops]
    return top, [sum(f * x for f, x in zip(factors, column)) for column in zip(*sums)]


def early_kernel(own_at, near, *rest):
    *prepared, own, sem = rest
    copy = pltpu.make_async_copy(own_at, own, sem)
    copy.start()
    phases = grid_phases(own.shape[1] // 2)
    prepare_refs(near, phases, *prepared[4:])
    copy.wait()
    prepare_refs(own, phases, *prepared[:4])


def middle_kernel(*rest):
    count = len(rest) // 5
    refs, prepared = rest[:count], rest[count:]
    phases = grid_phases(refs[0].shape[1] // 2)
    for n in range(count):
        prepare_refs(refs[n], phases, *prepared[4 * n : 4 * n + 4])


def late_kernel(blocks, own, cnb, ynb, cynb, *rest):
    prepared, rest = rest[: 4 * blocks], rest[4 * blocks :]
    e_outs, rest = (rest[:blocks], rest[blocks : 2 * blocks]), rest[2 * blocks :]
    y_out, power_out, stats_out, tops_out, *half_out = rest
    half_stats, half_tops = half_out[:2], half_out[2:]
    per, lanes = e_outs[0][0].shape[1:]
    left = lanes - 128
    pairs = ((own, cnb), (ynb, cynb))
    facts = [half_facts(*pair) for pair in pairs]
    for half, pair in enumerate(pairs):
        place_half(half, *pair, y_out, power_out)
    for out in (y_out, power_out):
        empty = 768 + 6 * left
        out[empty:] = jnp.zeros_like(out[empty:])
    for out in half_out:
        out[...] = jnp.zeros_like(out)
    for half in range(2):
        particles = [placed(half, part, left, out) for out in (y_out, power_out) for part in (0, 1)]
        prior = prior_rows(facts[half], per, lanes)
        tops, sums = [], []
        for n in range(blocks):
            score = block_scores(prepared[4 * n : 4 * n + 4], particles, prior)
            top, sums_here = weigh(score, e_outs[half][n])
            half_tops[half][n : n + 1, :lanes] = top
            tops.append(top)
            sums.append(sums_here)
        top, sums = joined_sums(tops, sums)
        for k, row in enumerate((top, *sums, facts[half][5:6, :lanes])):
            half_stats[half][k : k + 1, :lanes] = row
    first = (lax.axis_index("dom") // 2) % 2 == 0
    for out, (mine, others) in ((stats_out, half_stats), (tops_out, half_tops)):
        mine, others = mine[...], others[...]
        out[:, :256] = jnp.where(first, mine, others)
        out[:, 256:] = jnp.where(first, others, mine)


def chip_kernel(mine, other, out):
    pair = (mine[...], other[...])
    top, sums = joined_sums([x[0:1] for x in pair], [[x[k : k + 1] for k in (1, 2, 3)] for x in pair])
    out[...] = pair[0]
    for k, row in enumerate((top, *sums)):
        out[k : k + 1] = row


def sum_kernel(n, cuts, last, waits, here, there, tops, *rest):
    ea_ref, eb_ref, y_ref, power_ref, *outs = rest[waits:]
    per, lanes = ea_ref.shape[1:]
    width = y_ref.shape[1]
    freq = width // 2
    first = (lax.axis_index("dom") // 2) % 2 == 0
    pair = (here[...], there[...])
    top, (mass, *move) = joined_sums(
        [x[0:1] for x in pair], [[x[k : k + 1] for k in (1, 2, 3)] for x in pair]
    )
    live = pair[0][4:5] / mass
    gain = jnp.exp(tops[n : n + 1] - top) * live
    gain_a = jnp.where(first, gain[:, :256], gain[:, 256:])[:, :lanes]
    gain_b = jnp.where(first, gain[:, 256:], gain[:, :256])[:, :lanes]
    if last:
        move = jnp.concatenate([x * live for x in move], axis=0)
        move = jnp.concatenate([move, jnp.zeros((6, 512), jnp.float32)], axis=0)
        move = jnp.where(first, move[:, :256], move[:, 256:])
        lane = lax.broadcasted_iota(jnp.int32, (8, 128), 1)
        light = jnp.where(
            lane < 32, pltpu.roll(move[:, :128], 32, 1), pltpu.roll(move[:, 128:], 32, 1)
        )
        light = jnp.where(lane < 48, light, 0.0)
        shift_out = outs.pop()
        slots = shift_out.shape[1]
        shift_out[...] = jnp.where(even_core(), move[:, :128], light)[:2, :slots]
    wa = ea_ref[...] * gain_a[None]
    wb = eb_ref[...] * gain_b[None]
    rows = SHIFTS * per
    flat = dot_nn(deep_lanes(wa.reshape(rows, lanes), wb.reshape(rows, lanes)), y_ref[...])
    phases = grid_phases(freq)
    mid = SHIFTS // 2

    def block(t):
        return flat[t * per : (t + 1) * per, :freq], flat[t * per : (t + 1) * per, freq:]

    re, im = block(mid)
    for t in range(mid):
        c, s = phases[t]
        ar, ai = block(t)
        br, bi = block(SHIFTS - 1 - t)
        re = re + (ar + br) * c - (ai - bi) * s
        im = im + (ar - br) * s + (ai + bi) * c
    weight = dot_nn(deep_lanes(jnp.sum(wa, axis=0), jnp.sum(wb, axis=0)), power_ref[...])
    for start, stop, out in zip(cuts, cuts[1:], outs):
        part = slice(start, stop)
        out[:, :freq] = re[part]
        out[:, freq:width] = im[part]
        out[:, width:] = weight[part]


def add_kernel(a, *rest):
    *parts, out = rest
    at = 0
    for part in parts:
        rows = slice(at, at + part.shape[0])
        out[rows] = a[rows] + part[...]
        at += part.shape[0]


def final_kernel(row_cuts, *refs):
    own, *parts, signal, out = refs
    rows, width = out.shape
    freq = width // 2
    inverse = 1.0 / signal[...]
    every = sorted({cut for cuts in row_cuts for cut in cuts})
    for start, stop in zip(every, every[1:]):
        total = own[start:stop]
        at = 0
        for cuts in row_cuts:
            for low, high in zip(cuts, cuts[1:]):
                if low <= start and stop <= high:
                    total = total + parts[at][start - low : stop - low]
                at += 1
        denominator = total[:, width:] + inverse
        out[start:stop, :freq] = total[:, :freq] / denominator
        out[start:stop, freq:] = total[:, freq:width] / denominator


def params(mib):
    return pltpu.CompilerParams(vmem_limit_bytes=mib * 1024 * 1024)


def crossed(block, mask):
    size = lax.axis_size("dom")
    return lax.ppermute(block, "dom", [(i, i ^ mask) for i in range(size)])


def on_device(
    particle_fourier,
    defocus,
    particle_offset,
    prior_rotation,
    group_id,
    live_count,
    noise_power,
    signal_power,
    class_refs,
):
    slots, width = particle_fourier.shape
    freq = width // 2
    size = lax.axis_size("dom")
    blocks = size // TEAM
    refs_own = class_refs.reshape(-1, width)
    per = refs_own.shape[0]
    f32 = jnp.float32
    vmem = pl.BlockSpec(memory_space=pltpu.VMEM)
    no_cost = pl.CostEstimate(flops=0, bytes_accessed=0, transcendentals=0)
    much = pl.CostEstimate(flops=16 * 10**9, bytes_accessed=0, transcendentals=0)

    ynb = crossed(particle_fourier, 2)
    anywhere = pl.BlockSpec(memory_space=pl.ANY)
    ynb = crossed(particle_fourier, 2)
    anywhere = pl.BlockSpec(memory_space=pl.ANY)
    def gated(arrays, waits, cost):
        return pl.pallas_call(
            lambda *a: None,
            out_shape=tuple(jax.ShapeDtypeStruct(x.shape, x.dtype) for x in arrays),
            in_specs=[anywhere] * (len(arrays) + len(waits)),
            out_specs=(anywhere,) * len(arrays),
            input_output_aliases={n: n for n in range(len(arrays))},
            compiler_params=params(1),
            cost_estimate=cost,
            name="gate",
        )(*arrays, *waits)

    ynb = crossed(particle_fourier, 2)
    anywhere = pl.BlockSpec(memory_space=pl.ANY)
    ynb = crossed(particle_fourier, 2)
    refs = [refs_own] + [crossed(refs_own, TEAM * n) for n in range(1, blocks)]
    own_facts = (
        particle_fourier,
        defocus.reshape(1, slots),
        particle_offset.T,
        prior_rotation.reshape(1, slots),
        group_id.reshape(1, slots),
        noise_power,
    )
    own, facts, inverse_noise = pl.pallas_call(
        own_kernel,
        out_shape=(
            jax.ShapeDtypeStruct((slots + 8, width + freq), f32),
            jax.ShapeDtypeStruct((8, 128), f32),
            jax.ShapeDtypeStruct(noise_power.shape, f32),
        ),
        in_specs=[anywhere] * 6 + [pl.BlockSpec(memory_space=pltpu.SMEM)],
        out_specs=(vmem,) * 3,
        scratch_shapes=[pltpu.VMEM(x.shape, x.dtype) for x in own_facts]
        + [pltpu.SemaphoreType.DMA((6,))],
        compiler_params=params(6),
        cost_estimate=no_cost,
        name="own",
    )(*(pltpu.with_memory_space_constraint(x, pltpu.HBM) for x in own_facts), live_count)
    cnb = crossed(own, 1)
    half = slots + slots // 2
    bf16 = jnp.bfloat16
    early = 2

    def shaped(rows, cols, dtype=f32):
        return jax.ShapeDtypeStruct((rows, cols), dtype)

    block_shapes = [shaped(SHIFTS * per, width, bf16)] * 2 + [shaped(per, freq, bf16)] * 2
    score_shape = jax.ShapeDtypeStruct((SHIFTS, per, half), f32)

    def call(kernel, operands, out_shape, name, mib, cost=None, scratch=()):
        return pl.pallas_call(
            kernel,
            cost_estimate=cost,
            out_shape=tuple(out_shape),
            in_specs=[vmem] * len(operands),
            out_specs=(vmem,) * len(out_shape),
            scratch_shapes=list(scratch),
            compiler_params=params(mib),
            name=name,
        )(*operands)

    prepared = pl.pallas_call(
        early_kernel,
        out_shape=tuple(block_shapes * early),
        in_specs=[anywhere, vmem],
        out_specs=(vmem,) * (4 * early),
        scratch_shapes=[pltpu.VMEM(refs_own.shape, f32), pltpu.SemaphoreType.DMA],
        compiler_params=params(8),
        name="early",
    )(pltpu.with_memory_space_constraint(refs_own, pltpu.HBM), refs[1])
    ynb_prepared = pl.pallas_call(
        neighbour_kernel,
        out_shape=jax.ShapeDtypeStruct((slots + 8, width + freq), f32),
        in_specs=[vmem] * 3 + [anywhere],
        out_specs=vmem,
        compiler_params=params(6),
        cost_estimate=no_cost,
        name="neighbour",
    )(ynb, crossed(facts, 2), inverse_noise, prepared[2])
    cynb = crossed(ynb_prepared, 1)

    late = blocks - early
    outs = call(
        middle_kernel,
        refs[early:],
        block_shapes * late,
        "middle",
        4 + 2 * blocks,
        much,
    )
    prepared = (*prepared, *outs)
    deep = 3 * 256 + 128
    top_rows = -(-blocks // 8) * 8
    outs = call(
        lambda *a: late_kernel(blocks, *a),
        (own, cnb, ynb_prepared, cynb, *prepared),
        [score_shape] * (2 * blocks)
        + [shaped(deep, width, bf16), shaped(deep, freq, bf16), shaped(8, 512)]
        + [shaped(top_rows, 512)],
        "late",
        8 + 2 * blocks,
        scratch=[pltpu.VMEM((8, 256), f32)] * 2 + [pltpu.VMEM((top_rows, 256), f32)] * 2,
    )
    e_own, e_other = outs[:blocks], outs[blocks : 2 * blocks]
    y, power, stats, tops = outs[2 * blocks :]

    (here,) = call(chip_kernel, (stats, crossed(stats, 1)), [shaped(8, 512)], "chip", 1)
    there = crossed(here, 2)

    def sums(n, cuts, last=False, waits=()):
        out_shape = [shaped(b - a, width + freq) for a, b in zip(cuts, cuts[1:])]
        if last:
            out_shape.append(shaped(2, slots))
        return pl.pallas_call(
            lambda *a: sum_kernel(n, cuts, last, len(waits), *a),
            out_shape=tuple(out_shape),
            in_specs=[vmem] * 3 + [anywhere] * len(waits) + [vmem] * 4,
            out_specs=(vmem,) * len(out_shape),
            compiler_params=params(8),
            name="sums",
        )(here, there, tops, *waits, e_own[n], e_other[n], y, power)

    def combined(mine, others, cost=None):
        return pl.pallas_call(
            add_kernel,
            out_shape=jax.ShapeDtypeStruct(mine.shape, f32),
            in_specs=[vmem] * (1 + len(others)),
            out_specs=vmem,
            compiler_params=params(4),
            cost_estimate=cost,
            name="combined",
        )(mine, *others)

    whole, cut = (0, per), (0, per // 2, per)
    far = []
    waits = []
    for n in range(2, blocks, 2):
        handed = [crossed(x, TEAM) for x in sums(n + 1, cut)]
        if n == 2:
            near = sums(1, cut)
        joined = [combined(x, [y]) for x, y in zip(sums(n, cut, waits=near[:1]), handed)]
        far.extend(crossed(x, TEAM * n) for x in joined)
        waits.extend(joined)
    own_part, shift = sums(0, whole, last=True, waits=waits)
    own_part = combined(own_part, [crossed(x, TEAM) for x in near], much)
    row_cuts = [cut] * (len(far) // 2)

    refs_new = pl.pallas_call(
        lambda *a: final_kernel(row_cuts, *a),
        out_shape=jax.ShapeDtypeStruct((per, width), f32),
        in_specs=[vmem] * (len(far) + 2),
        out_specs=vmem,
        compiler_params=params(2 + blocks),
        name="update",
    )(own_part, *far, signal_power.reshape(1, freq))

    return (shift.T, refs_new.reshape(class_refs.shape))


def solution(mesh):
    in_specs = (
        P(("groups", "dom"), None),
        P(("groups", "dom")),
        P(("groups", "dom"), None),
        P(("groups", "dom")),
        P(("groups", "dom")),
        P(("groups", "dom")),
        P("groups", None),
        P("groups"),
        P(("groups", "dom"), None, None),
    )
    out_specs = (P(("groups", "dom"), None), P(("groups", "dom"), None, None))
    return jax.shard_map(
        on_device, mesh=mesh, in_specs=in_specs, out_specs=out_specs, check_vma=False
    )
```

```python
import functools
import math

import jax
import jax.numpy as jnp
from jax import lax
from jax.experimental import pallas as pl
from jax.experimental.pallas import tpu as pltpu
from jax.sharding import PartitionSpec as P

ROT = 16
SIDE = 3
BOX = 128
FY = 32
SHIFTS = 9
TEAM = 4
PRIOR = 2.0
CTF_SIZE = math.hypot(0.995, 0.1)
CTF_TURN = math.atan2(0.1, 0.995)
SINE = (
    9.99999976e-01,
    -1.66666476e-01,
    8.33289854e-03,
    -1.98008185e-04,
    2.59032780e-06,
)
TWO_PI = 2.0 * math.pi
PI_A = 3.140625
PI_B = 0.0009670257568359375
PI_C = math.pi - PI_A - PI_B
HIGHEST = lax.Precision.HIGHEST
GRID = tuple((t // SIDE - SIDE // 2, t % SIDE - SIDE // 2) for t in range(SHIFTS))


def half_turn_sine(x):
    s = x * x
    p = SINE[4]
    for c in SINE[3::-1]:
        p = p * s + c
    return x * p


def turn_cos(turns):
    t = jnp.abs(turns - jnp.round(turns))
    return half_turn_sine(TWO_PI * (0.25 - t))


def turn_sin(turns):
    return turn_cos(turns - 0.25)


def freq_rows(width, rows):
    f = lax.broadcasted_iota(jnp.int32, (rows, width), 1)
    kx = (f // FY).astype(jnp.float32)
    ky = (f % FY - FY // 2).astype(jnp.float32)
    return kx, ky


def dot_nt(a, b):
    return lax.dot_general(
        a, b, (((1,), (1,)), ((), ())), preferred_element_type=jnp.float32
    )


def dot_nn(a, b):
    return lax.dot_general(
        a, b, (((1,), (0,)), ((), ())), preferred_element_type=jnp.float32
    )


def exact_dot_nn(a, b):
    return lax.dot_general(
        a, b, (((1,), (0,)), ((), ())), precision=HIGHEST, preferred_element_type=jnp.float32
    )


def halves(x):
    high = x.astype(jnp.bfloat16)
    return high, (x - high.astype(jnp.float32)).astype(jnp.bfloat16)


def deep_at(half, part):
    return 384 * part + 128 * half, 384 * part + 256 + 64 * half


def deep_lanes(a, b):
    empty = jnp.zeros((a.shape[0], 64), jnp.float32)
    tail = jnp.concatenate([a[:, 128:], empty], axis=1) + pltpu.roll(
        jnp.concatenate([b[:, 128:], empty], axis=1), 64, 1
    )
    high, low = halves(jnp.concatenate([a[:, :128], b[:, :128], tail], axis=1))
    return jnp.concatenate([high, high, low], axis=1)


def grid_phases(width):
    kx, ky = freq_rows(width, 1)
    out = []
    for t, (gx, gy) in enumerate(GRID):
        if t < SHIFTS // 2:
            m = (kx * gx + ky * gy) * (1.0 / BOX)
            out.append((turn_cos(m), turn_sin(m)))
    return out


def phase_of(phases, t):
    mid = SHIFTS // 2
    if t < mid:
        return phases[t]
    c, s = phases[SHIFTS - 1 - t]
    return c, -s


def prepared_rows(src, facts, inverse_noise, out):
    slots, width = src.shape
    freq = width // 2
    columns = jnp.concatenate([facts, jnp.zeros((120, 128), jnp.float32)], axis=0).T[:slots]
    focus = columns[:, 0:1]
    off_x = columns[:, 1:2]
    off_y = columns[:, 2:3]
    group_col = columns[:, 4:5]

    kx, ky = freq_rows(freq, 1)
    chi = focus * ((kx * kx + ky * ky) * (1.0 / 1024.0))
    k = jnp.round(chi * (1.0 / math.pi))
    rest_angle = ((chi - k * PI_A) - k * PI_B) - k * PI_C
    shifted_angle = rest_angle + CTF_TURN
    over = shifted_angle > (0.5 * math.pi)
    folded = jnp.where(over, math.pi - shifted_angle, shifted_angle)
    parity = 0.5 * k
    sign = (parity - jnp.floor(parity)) * (4.0 * CTF_SIZE) - CTF_SIZE
    ctf = half_turn_sine(folded) * sign
    kx0, ky0 = freq_rows(128, 1)
    m = (kx0 * off_x + ky0 * off_y) * (1.0 / BOX)
    pc, ps = turn_cos(m), turn_sin(m)
    step = off_x * ((128 // FY) / BOX) + jnp.zeros((slots, 128), jnp.float32)
    sc, ss = turn_cos(step), turn_sin(step)

    total = inverse_noise.shape[0]
    onehot = (
        group_col == lax.broadcasted_iota(jnp.int32, (slots, total), 1).astype(jnp.float32)
    ).astype(jnp.float32)
    noise_rows = exact_dot_nn(onehot, inverse_noise)
    scaled = ctf * noise_rows
    out[:slots, width:] = ctf * scaled
    for n in range(freq // 128):
        part = slice(128 * n, 128 * (n + 1))
        twin = slice(freq + 128 * n, freq + 128 * (n + 1))
        co = pc * scaled[:, part]
        si = ps * scaled[:, part]
        pc, ps = pc * sc - ps * ss, ps * sc + pc * ss
        xr, xi = src[:, part], src[:, twin]
        out[:slots, part] = xr * co - xi * si
        out[:slots, twin] = xr * si + xi * co
    out[slots:, :128] = facts
    out[slots:, 128:] = jnp.zeros((8, width + freq - 128), jnp.float32)


def own_kernel(
    src_at, focus_at, offsets_at, prior_at, group_at, noise_at, live_count, out, facts_out,
    inverse_out, src, focus, offsets, prior, group, noise, sems
):
    moves = (
        (focus_at, focus), (offsets_at, offsets), (prior_at, prior), (group_at, group),
        (noise_at, noise), (src_at, src),
    )
    copies = [pltpu.make_async_copy(x, y, sems.at[n]) for n, (x, y) in enumerate(moves)]
    for copy in copies:
        copy.start()
    slots = src.shape[0]
    facts_out[...] = jnp.zeros_like(facts_out)
    slot = lax.broadcasted_iota(jnp.int32, (1, slots), 1)
    for copy in copies:
        copy.wait()
    facts_out[5:6, :slots] = (slot < live_count[0]).astype(jnp.float32)
    facts_out[0:1, :slots] = focus[...]
    facts_out[1:3, :slots] = offsets[...].astype(jnp.float32)
    facts_out[3:4, :slots] = prior[...].astype(jnp.float32)
    facts_out[4:5, :slots] = group[...].astype(jnp.float32)
    inverse = 1.0 / noise[...]
    inverse_out[...] = inverse
    prepared_rows(src, facts_out[...], inverse, out)


def neighbour_kernel(src, facts, inverse_noise, out):
    prepared_rows(src, facts[...], inverse_noise[...], out)


def first_at(part, row):
    return 192 * part + row


def both_at(half, part, row):
    main, left = deep_at(half, part)
    return main + row if row < 128 else left + row - 128


def place_half(own, ynb, y_out, power_out, parts, at):
    width = y_out.shape[1]
    slots = own.shape[0] - 8
    main = 128 - slots
    for cols, out in ((slice(0, width), y_out), (slice(width, None), power_out)):
        pieces = ((own, 0, slots, 0), (ynb, 0, main, slots), (ynb, main, slots, 128))
        for src, start, stop, to in pieces:
            pair = halves(src[start:stop, cols])
            for part in range(parts):
                row = at(part, to)
                out[row : row + stop - start] = pair[part % 2]


def placed(out, part, at):
    main, left = at(part, 0), at(part, 128)
    return jnp.concatenate([out[main : main + 128], out[left : left + 64]], axis=0)


def half_facts(own, ynb):
    slots = own.shape[0] - 8
    x, y = own[slots:, :128], pltpu.roll(ynb[slots:, :128], slots, 1)
    lane = lax.broadcasted_iota(jnp.int32, (8, 128), 1)
    return jnp.concatenate([jnp.where(lane < slots, x, y), y], axis=1)


def by_device(x, slots):
    lane = lax.broadcasted_iota(jnp.int32, (x.shape[0], 128), 1)
    main, left = pltpu.roll(x[:, :128], 128 - slots, 1), pltpu.roll(x[:, 128:], 128 - slots, 1)
    return x[:, :128], jnp.where(lane < 128 - slots, main, left)


def in_half(x, y, slots):
    lane = lax.broadcasted_iota(jnp.int32, (x.shape[0], 128), 1)
    y = pltpu.roll(y, slots, 1)
    return jnp.concatenate([jnp.where(lane < slots, x, y), y], axis=1)


def team_order(tiles):
    me = lax.axis_index("dom")
    even, first = me % 2 == 0, (me // 2) % 2 == 0
    a, b, c, d = tiles
    a, b, c, d = (jnp.where(even, x, y) for x, y in ((a, c), (b, d), (c, a), (d, b)))
    return [jnp.where(first, x, y) for x, y in ((a, b), (b, a), (c, d), (d, c))]


def prior_rows(facts, per, lanes):
    r = (lax.broadcasted_iota(jnp.int32, (per, lanes), 0) % ROT).astype(jnp.float32)
    return PRIOR * turn_cos((r - facts[3:4, :lanes]) * (1.0 / ROT))


def prepare_refs(ref, phases, r_high, r_low, q_high, q_low):
    per, width = ref.shape
    freq = width // 2
    rr, ri = ref[:, :freq], ref[:, freq:]
    mid = SHIFTS // 2

    def store(t, re, im):
        rows = slice(t * per, (t + 1) * per)
        r_high[rows, :freq], r_low[rows, :freq] = halves(re)
        r_high[rows, freq:], r_low[rows, freq:] = halves(im)

    store(mid, rr, ri)
    for t in range(mid):
        c, s = phases[t]
        a, b, d, e = rr * c, ri * s, ri * c, rr * s
        store(t, a + b, d - e)
        store(SHIFTS - 1 - t, a - b, d + e)
    q_high[...], q_low[...] = halves(rr * rr + ri * ri)


def block_scores(prepared, particles, prior):
    r_high, r_low, q_high, q_low = (x[...] for x in prepared)
    y_high, y_low, p_high, p_low = particles
    quad = dot_nt(q_high, p_high) + dot_nt(q_low, p_high) + dot_nt(q_high, p_low)
    score = dot_nt(r_high, y_high) + dot_nt(r_low, y_high) + dot_nt(r_high, y_low)
    per, lanes = prior.shape
    return score.reshape(SHIFTS, per, lanes) + (prior - 0.5 * quad)[None]


def weigh(score, e_out):
    top = jnp.max(jnp.max(score, axis=0), axis=0, keepdims=True)
    e = jnp.exp(score - top[None])
    e_out[...] = e
    side = SIDE // 2
    by_x = [sum(e[SIDE * x + y] for y in range(SIDE)) for x in range(SIDE)]
    by_y = [sum(e[SIDE * x + y] for x in range(SIDE)) for y in range(SIDE)]
    sums = [sum(by_x)]
    for by in (by_x, by_y):
        sums.append(sum(by[k] * float(k - side) for k in range(SIDE) if k != side))
    return top, [jnp.sum(x, axis=0, keepdims=True) for x in sums]


def joined_sums(tops, sums):
    top = tops[0]
    for other in tops[1:]:
        top = jnp.maximum(top, other)
    factors = [jnp.exp(other - top) for other in tops]
    return top, [sum(f * x for f, x in zip(factors, column)) for column in zip(*sums)]


def early_kernel(own_at, near, *rest):
    *prepared, own, sem = rest
    copy = pltpu.make_async_copy(own_at, own, sem)
    copy.start()
    phases = grid_phases(own.shape[1] // 2)
    prepare_refs(near, phases, *prepared[4:])
    copy.wait()
    prepare_refs(own, phases, *prepared[:4])


def middle_kernel(wait, *rest):
    count = len(rest) // 5
    refs, prepared = rest[:count], rest[count:]
    phases = grid_phases(refs[0].shape[1] // 2)
    for n in range(count):
        prepare_refs(refs[n], phases, *prepared[4 * n : 4 * n + 4])


def score_kernel(half, blocks, own, ynb, *rest):
    prepared, rest = rest[: 4 * blocks], rest[4 * blocks :]
    if half:
        stats_in, tops_in, y_in, power_in, *rest = rest
    e_outs, rest = rest[:blocks], rest[blocks:]
    y_out, power_out, stats_out, tops_out, stats, tops_row = rest
    per, lanes = e_outs[0].shape[1:]
    slots = lanes // 2
    facts = half_facts(own, ynb)
    at = functools.partial(both_at, half) if half else first_at
    place_half(own, ynb, y_out, power_out, 2 + half, at)
    if half:
        for x, out in ((y_in, y_out), (power_in, power_out)):
            for part in range(3):
                for row, size in ((0, 128), (128, 64)):
                    here, to = first_at(part % 2, row), both_at(0, part, row)
                    out[to : to + size] = x[here : here + size]
    stats[...] = jnp.zeros_like(stats)
    tops_row[...] = jnp.zeros_like(tops_row)
    particles = [placed(out, part, at) for out in (y_out, power_out) for part in (0, 1)]
    prior = prior_rows(facts, per, lanes)
    tops, sums = [], []
    for n in range(blocks):
        score = block_scores(prepared[4 * n : 4 * n + 4], particles, prior)
        top, sums_here = weigh(score, e_outs[n])
        tops_row[n : n + 1, :lanes] = top
        tops.append(top)
        sums.append(sums_here)
    top, sums = joined_sums(tops, sums)
    for k, row in enumerate((top, *sums, facts[5:6, :lanes])):
        stats[k : k + 1, :lanes] = row
    if half == 0:
        stats_out[...] = stats[...]
        tops_out[...] = tops_row[...]
        return
    pair = by_device(stats_in[...], slots), by_device(stats[...], slots)
    tiles = team_order((*pair[0], *pair[1]))
    stats_out[...] = jnp.concatenate(tiles, axis=1)
    tops_out[:, :256] = tops_in[...]
    tops_out[:, 256:] = tops_row[...]


def chip_kernel(mine, other, out):
    pair = (mine[...], other[...])
    top, sums = joined_sums([x[0:1] for x in pair], [[x[k : k + 1] for k in (1, 2, 3)] for x in pair])
    out[...] = pair[0]
    for k, row in enumerate((top, *sums)):
        out[k : k + 1] = row


def sum_kernel(blocks, cuts, last, waits, here, there, tops, *rest):
    rest = rest[waits:]
    e_refs, (y_ref, power_ref, *outs) = rest[: 2 * len(blocks)], rest[2 * len(blocks) :]
    per, lanes = e_refs[0].shape[1:]
    slots = lanes // 2
    width = y_ref.shape[1]
    freq = width // 2
    pair = (here[...], there[...])
    top, (mass, *move) = joined_sums(
        [x[0:1] for x in pair], [[x[k : k + 1] for k in (1, 2, 3)] for x in pair]
    )
    live = pair[0][4:5] / mass
    rows = [top, live, *(x * live for x in move)]
    rows = jnp.concatenate([*rows, jnp.zeros((4, 512), jnp.float32)], axis=0)
    mine = team_order([rows[:, 128 * k : 128 * (k + 1)] for k in range(4)])
    if last:
        shift_out = outs.pop()
        shift_out[...] = mine[0][2:4, :slots]
    halves_rows = (in_half(mine[0], mine[1], slots), in_half(mine[2], mine[3], slots))
    per_block = []
    weight_sums = []
    for k, n in enumerate(blocks):
        w = []
        for half, row in enumerate(halves_rows):
            top_here = tops[n : n + 1, 256 * half : 256 * half + lanes]
            gain = jnp.exp(top_here - row[0:1, :lanes]) * row[1:2, :lanes]
            w.append(e_refs[2 * k + half][...] * gain[None])
        per_block.append(deep_lanes(*(x.reshape(SHIFTS * per, lanes) for x in w)))
        weight_sums.append(deep_lanes(*(jnp.sum(x, axis=0) for x in w)))
    flat_all = dot_nn(jnp.concatenate(per_block, axis=0), y_ref[...])
    weight_all = dot_nn(jnp.concatenate(weight_sums, axis=0), power_ref[...])
    phases = grid_phases(freq)
    count = len(cuts) - 1
    for k in range(len(blocks)):
        flat = flat_all[SHIFTS * per * k : SHIFTS * per * (k + 1)]
        weight = weight_all[per * k : per * (k + 1)]
        write_block(flat, weight, phases, cuts, outs[count * k : count * (k + 1)])


def write_block(flat, weight, phases, cuts, outs):
    per, freq = weight.shape
    width = 2 * freq
    mid = SHIFTS // 2

    def block(t):
        return flat[t * per : (t + 1) * per, :freq], flat[t * per : (t + 1) * per, freq:]

    re, im = block(mid)
    for t in range(mid):
        c, s = phases[t]
        ar, ai = block(t)
        br, bi = block(SHIFTS - 1 - t)
        re = re + (ar + br) * c - (ai - bi) * s
        im = im + (ar - br) * s + (ai + bi) * c
    for start, stop, out in zip(cuts, cuts[1:], outs):
        part = slice(start, stop)
        out[:, :freq] = re[part]
        out[:, freq:width] = im[part]
        out[:, width:] = weight[part]


def add_kernel(a, *rest):
    *parts, out = rest
    at = 0
    for part in parts:
        rows = slice(at, at + part.shape[0])
        out[rows] = a[rows] + part[...]
        at += part.shape[0]


def final_kernel(row_cuts, *refs):
    own, *parts, signal, out = refs
    rows, width = out.shape
    freq = width // 2
    inverse = 1.0 / signal[...]
    every = sorted({cut for cuts in row_cuts for cut in cuts})
    for start, stop in zip(every, every[1:]):
        total = own[start:stop]
        at = 0
        for cuts in row_cuts:
            for low, high in zip(cuts, cuts[1:]):
                if low <= start and stop <= high:
                    total = total + parts[at][start - low : stop - low]
                at += 1
        denominator = total[:, width:] + inverse
        out[start:stop, :freq] = total[:, :freq] / denominator
        out[start:stop, freq:] = total[:, freq:width] / denominator


def params(mib):
    return pltpu.CompilerParams(vmem_limit_bytes=mib * 1024 * 1024)


def crossed(block, mask):
    size = lax.axis_size("dom")
    return lax.ppermute(block, "dom", [(i, i ^ mask) for i in range(size)])


def on_device(
    particle_fourier,
    defocus,
    particle_offset,
    prior_rotation,
    group_id,
    live_count,
    noise_power,
    signal_power,
    class_refs,
):
    slots, width = particle_fourier.shape
    freq = width // 2
    size = lax.axis_size("dom")
    blocks = size // TEAM
    refs_own = class_refs.reshape(-1, width)
    per = refs_own.shape[0]
    f32 = jnp.float32
    vmem = pl.BlockSpec(memory_space=pltpu.VMEM)
    no_cost = pl.CostEstimate(flops=0, bytes_accessed=0, transcendentals=0)
    much = pl.CostEstimate(flops=16 * 10**9, bytes_accessed=0, transcendentals=0)

    def gated(x, *waits):
        return pl.pallas_call(
            lambda *a: None,
            out_shape=jax.ShapeDtypeStruct(x.shape, x.dtype),
            in_specs=[anywhere] * (1 + len(waits)),
            out_specs=anywhere,
            input_output_aliases={0: 0},
            compiler_params=params(1),
            cost_estimate=no_cost,
            name="gate",
        )(x, *waits)

    ynb = crossed(particle_fourier, 2)
    anywhere = pl.BlockSpec(memory_space=pl.ANY)
    def gated(x, *waits):
        return pl.pallas_call(
            lambda *a: None,
            out_shape=jax.ShapeDtypeStruct(x.shape, x.dtype),
            in_specs=[anywhere] * (1 + len(waits)),
            out_specs=anywhere,
            input_output_aliases={0: 0},
            compiler_params=params(1),
            cost_estimate=no_cost,
            name="gate",
        )(x, *waits)

    ynb = crossed(particle_fourier, 2)
    anywhere = pl.BlockSpec(memory_space=pl.ANY)
    def gated(arrays, waits, cost):
        return pl.pallas_call(
            lambda *a: None,
            out_shape=tuple(jax.ShapeDtypeStruct(x.shape, x.dtype) for x in arrays),
            in_specs=[anywhere] * (len(arrays) + len(waits)),
            out_specs=(anywhere,) * len(arrays),
            input_output_aliases={n: n for n in range(len(arrays))},
            compiler_params=params(1),
            cost_estimate=cost,
            name="gate",
        )(*arrays, *waits)

    def gated(x, *waits):
        return pl.pallas_call(
            lambda *a: None,
            out_shape=jax.ShapeDtypeStruct(x.shape, x.dtype),
            in_specs=[anywhere] * (1 + len(waits)),
            out_specs=anywhere,
            input_output_aliases={0: 0},
            compiler_params=params(1),
            cost_estimate=no_cost,
            name="gate",
        )(x, *waits)

    ynb = crossed(particle_fourier, 2)
    anywhere = pl.BlockSpec(memory_space=pl.ANY)
    def gated(x, *waits):
        return pl.pallas_call(
            lambda *a: None,
            out_shape=jax.ShapeDtypeStruct(x.shape, x.dtype),
            in_specs=[anywhere] * (1 + len(waits)),
            out_specs=anywhere,
            input_output_aliases={0: 0},
            compiler_params=params(1),
            cost_estimate=no_cost,
            name="gate",
        )(x, *waits)

    ynb = crossed(particle_fourier, 2)
    refs = {0: refs_own, 1: crossed(refs_own, TEAM)}
    for n in range(2, blocks, 2):
        refs[n] = crossed(refs_own, TEAM * n)
    own_facts = (
        particle_fourier,
        defocus.reshape(1, slots),
        particle_offset.T,
        prior_rotation.reshape(1, slots),
        group_id.reshape(1, slots),
        noise_power,
    )
    own, facts, inverse_noise = pl.pallas_call(
        own_kernel,
        out_shape=(
            jax.ShapeDtypeStruct((slots + 8, width + freq), f32),
            jax.ShapeDtypeStruct((8, 128), f32),
            jax.ShapeDtypeStruct(noise_power.shape, f32),
        ),
        in_specs=[anywhere] * 6 + [pl.BlockSpec(memory_space=pltpu.SMEM)],
        out_specs=(vmem,) * 3,
        scratch_shapes=[pltpu.VMEM(x.shape, x.dtype) for x in own_facts]
        + [pltpu.SemaphoreType.DMA((6,))],
        compiler_params=params(6),
        cost_estimate=no_cost,
        name="own",
    )(*(pltpu.with_memory_space_constraint(x, pltpu.HBM) for x in own_facts), live_count)
    cnb = crossed(own, 1)
    for n in range(2, blocks, 2):
        refs[n] = gated(refs[n], facts)
        refs[n + 1] = crossed(refs[n], TEAM)
    refs = [refs[n] for n in range(blocks)]
    both = 2 * slots
    bf16 = jnp.bfloat16
    early = 2

    def shaped(rows, cols, dtype=f32):
        return jax.ShapeDtypeStruct((rows, cols), dtype)

    block_shapes = [shaped(SHIFTS * per, width, bf16)] * 2 + [shaped(per, freq, bf16)] * 2
    score_shape = jax.ShapeDtypeStruct((SHIFTS, per, both), f32)

    def call(kernel, operands, out_shape, name, mib, cost=None, scratch=()):
        return pl.pallas_call(
            kernel,
            cost_estimate=cost,
            out_shape=tuple(out_shape),
            in_specs=[vmem] * len(operands),
            out_specs=(vmem,) * len(out_shape),
            scratch_shapes=list(scratch),
            compiler_params=params(mib),
            name=name,
        )(*operands)

    prepared = pl.pallas_call(
        early_kernel,
        out_shape=tuple(block_shapes * early),
        in_specs=[anywhere, vmem],
        out_specs=(vmem,) * (4 * early),
        scratch_shapes=[pltpu.VMEM(refs_own.shape, f32), pltpu.SemaphoreType.DMA],
        compiler_params=params(8),
        name="early",
    )(pltpu.with_memory_space_constraint(refs_own, pltpu.HBM), refs[1])
    ynb_prepared = pl.pallas_call(
        neighbour_kernel,
        out_shape=jax.ShapeDtypeStruct((slots + 8, width + freq), f32),
        in_specs=[vmem] * 3,
        out_specs=vmem,
        compiler_params=params(6),
        cost_estimate=no_cost,
        name="neighbour",
    )(ynb, crossed(facts, 2), inverse_noise)
    cynb = crossed(ynb_prepared, 1)

    late = blocks - early
    outs = pl.pallas_call(
        middle_kernel,
        out_shape=tuple(block_shapes * late),
        in_specs=[anywhere] + [vmem] * late,
        out_specs=(vmem,) * (4 * late),
        compiler_params=params(4 + 2 * blocks),
        cost_estimate=much,
        name="middle",
    )(ynb_prepared, *refs[early:])
    prepared = (*prepared, *outs)
    top_rows = -(-blocks // 8) * 8

    def scores(half, particles, before, cost):
        lanes = 256 * (1 + half)
        rows = (6 if half else 2) * both
        return pl.pallas_call(
            lambda *a: score_kernel(half, blocks, *a),
            out_shape=(
                *[score_shape] * blocks,
                shaped(rows, width, bf16),
                shaped(rows, freq, bf16),
                shaped(8, lanes),
                shaped(top_rows, lanes),
            ),
            in_specs=[vmem] * (2 + 4 * blocks + len(before)),
            out_specs=(vmem,) * (blocks + 4),
            scratch_shapes=[pltpu.VMEM((8, 256), f32), pltpu.VMEM((top_rows, 256), f32)],
            compiler_params=params(8 + 2 * blocks),
            cost_estimate=cost,
            name="scores",
        )(*particles, *prepared, *before)

    *e_own, y, power, stats, tops = scores(0, (own, ynb_prepared), (), much)
    *e_other, y, power, stats, tops = scores(1, (cnb, cynb), (stats, tops, y, power), None)

    (here,) = call(chip_kernel, (stats, crossed(stats, 1)), [shaped(8, 512)], "chip", 1)
    there = crossed(here, 2)

    def sums(numbers, cuts, last=False, waits=()):
        out_shape = [shaped(b - a, width + freq) for a, b in zip(cuts, cuts[1:])] * len(numbers)
        if last:
            out_shape.append(shaped(2, slots))
        weights = [e[n] for n in numbers for e in (e_own, e_other)]
        return pl.pallas_call(
            lambda *a: sum_kernel(numbers, cuts, last, len(waits), *a),
            out_shape=tuple(out_shape),
            in_specs=[vmem] * 3 + [anywhere] * len(waits) + [vmem] * (2 + len(weights)),
            out_specs=(vmem,) * len(out_shape),
            compiler_params=params(12),
            name="sums",
        )(here, there, tops, *waits, *weights, y, power)

    def combined(mine, others, cost=None):
        return pl.pallas_call(
            add_kernel,
            out_shape=jax.ShapeDtypeStruct(mine.shape, f32),
            in_specs=[vmem] * (1 + len(others)),
            out_specs=vmem,
            compiler_params=params(4),
            cost_estimate=cost,
            name="combined",
        )(mine, *others)

    whole, cut = (0, per), (0, per // 2, per)
    far = []
    waits = []
    for n in range(2, blocks, 2):
        handed = sums((n + 1, 1) if n == 2 else (n + 1,), cut)
        if n == 2:
            near = handed[2:]
        mine = sums((n,), cut, waits=handed[:1])
        joined = [combined(x, [crossed(y, TEAM)]) for x, y in zip(mine, handed)]
        far.extend(crossed(x, TEAM * n) for x in joined)
        waits.extend(joined)
    own_part, shift = sums((0,), whole, last=True, waits=waits)
    own_part = combined(own_part, [crossed(x, TEAM) for x in near], much)
    row_cuts = [cut] * (len(far) // 2)

    refs_new = pl.pallas_call(
        lambda *a: final_kernel(row_cuts, *a),
        out_shape=jax.ShapeDtypeStruct((per, width), f32),
        in_specs=[vmem] * (len(far) + 2),
        out_specs=vmem,
        compiler_params=params(2 + blocks),
        name="update",
    )(own_part, *far, signal_power.reshape(1, freq))

    return (shift.T, refs_new.reshape(class_refs.shape))


def solution(mesh):
    in_specs = (
        P(("groups", "dom"), None),
        P(("groups", "dom")),
        P(("groups", "dom"), None),
        P(("groups", "dom")),
        P(("groups", "dom")),
        P(("groups", "dom")),
        P("groups", None),
        P("groups"),
        P(("groups", "dom"), None, None),
    )
    out_specs = (P(("groups", "dom"), None), P(("groups", "dom"), None, None))
    return jax.shard_map(
        on_device, mesh=mesh, in_specs=in_specs, out_specs=out_specs, check_vma=False
    )
```

```python
import functools
import math

import jax
import jax.numpy as jnp
from jax import lax
from jax.experimental import pallas as pl
from jax.experimental.pallas import tpu as pltpu
from jax.sharding import PartitionSpec as P

ROT = 16
SIDE = 3
BOX = 128
FY = 32
SHIFTS = 9
TEAM = 4
PRIOR = 2.0
CTF_SIZE = math.hypot(0.995, 0.1)
CTF_TURN = math.atan2(0.1, 0.995)
SINE = (
    9.99999976e-01,
    -1.66666476e-01,
    8.33289854e-03,
    -1.98008185e-04,
    2.59032780e-06,
)
TWO_PI = 2.0 * math.pi
PI_A = 3.140625
PI_B = 0.0009670257568359375
PI_C = math.pi - PI_A - PI_B
HIGHEST = lax.Precision.HIGHEST
GRID = tuple((t // SIDE - SIDE // 2, t % SIDE - SIDE // 2) for t in range(SHIFTS))


def half_turn_sine(x):
    s = x * x
    p = SINE[4]
    for c in SINE[3::-1]:
        p = p * s + c
    return x * p


def turn_cos(turns):
    t = jnp.abs(turns - jnp.round(turns))
    return half_turn_sine(TWO_PI * (0.25 - t))


def turn_sin(turns):
    return turn_cos(turns - 0.25)


def freq_rows(width, rows):
    f = lax.broadcasted_iota(jnp.int32, (rows, width), 1)
    kx = (f // FY).astype(jnp.float32)
    ky = (f % FY - FY // 2).astype(jnp.float32)
    return kx, ky


def dot_nt(a, b):
    return lax.dot_general(
        a, b, (((1,), (1,)), ((), ())), preferred_element_type=jnp.float32
    )


def dot_nn(a, b):
    return lax.dot_general(
        a, b, (((1,), (0,)), ((), ())), preferred_element_type=jnp.float32
    )


def exact_dot_nn(a, b):
    return lax.dot_general(
        a, b, (((1,), (0,)), ((), ())), precision=HIGHEST, preferred_element_type=jnp.float32
    )


def halves(x):
    high = x.astype(jnp.bfloat16)
    return high, (x - high.astype(jnp.float32)).astype(jnp.bfloat16)


def deep_at(half, part):
    return 384 * part + 128 * half, 384 * part + 256 + 64 * half


def deep_lanes(a, b):
    empty = jnp.zeros((a.shape[0], 64), jnp.float32)
    tail = jnp.concatenate([a[:, 128:], empty], axis=1) + pltpu.roll(
        jnp.concatenate([b[:, 128:], empty], axis=1), 64, 1
    )
    high, low = halves(jnp.concatenate([a[:, :128], b[:, :128], tail], axis=1))
    return jnp.concatenate([high, high, low], axis=1)


def grid_phases(width):
    kx, ky = freq_rows(width, 1)
    out = []
    for t, (gx, gy) in enumerate(GRID):
        if t < SHIFTS // 2:
            m = (kx * gx + ky * gy) * (1.0 / BOX)
            out.append((turn_cos(m), turn_sin(m)))
    return out


def phase_of(phases, t):
    mid = SHIFTS // 2
    if t < mid:
        return phases[t]
    c, s = phases[SHIFTS - 1 - t]
    return c, -s


def prepared_rows(src, facts, inverse_noise, out):
    slots, width = src.shape
    freq = width // 2
    columns = jnp.concatenate([facts, jnp.zeros((120, 128), jnp.float32)], axis=0).T[:slots]
    focus = columns[:, 0:1]
    off_x = columns[:, 1:2]
    off_y = columns[:, 2:3]
    group_col = columns[:, 4:5]

    kx, ky = freq_rows(freq, 1)
    chi = focus * ((kx * kx + ky * ky) * (1.0 / 1024.0))
    k = jnp.round(chi * (1.0 / math.pi))
    rest_angle = ((chi - k * PI_A) - k * PI_B) - k * PI_C
    shifted_angle = rest_angle + CTF_TURN
    over = shifted_angle > (0.5 * math.pi)
    folded = jnp.where(over, math.pi - shifted_angle, shifted_angle)
    parity = 0.5 * k
    sign = (parity - jnp.floor(parity)) * (4.0 * CTF_SIZE) - CTF_SIZE
    ctf = half_turn_sine(folded) * sign
    kx0, ky0 = freq_rows(128, 1)
    m = (kx0 * off_x + ky0 * off_y) * (1.0 / BOX)
    pc, ps = turn_cos(m), turn_sin(m)
    step = off_x * ((128 // FY) / BOX) + jnp.zeros((slots, 128), jnp.float32)
    sc, ss = turn_cos(step), turn_sin(step)

    total = inverse_noise.shape[0]
    onehot = (
        group_col == lax.broadcasted_iota(jnp.int32, (slots, total), 1).astype(jnp.float32)
    ).astype(jnp.float32)
    noise_rows = exact_dot_nn(onehot, inverse_noise)
    scaled = ctf * noise_rows
    out[:slots, width:] = ctf * scaled
    for n in range(freq // 128):
        part = slice(128 * n, 128 * (n + 1))
        twin = slice(freq + 128 * n, freq + 128 * (n + 1))
        co = pc * scaled[:, part]
        si = ps * scaled[:, part]
        pc, ps = pc * sc - ps * ss, ps * sc + pc * ss
        xr, xi = src[:, part], src[:, twin]
        out[:slots, part] = xr * co - xi * si
        out[:slots, twin] = xr * si + xi * co
    out[slots:, :128] = facts
    out[slots:, 128:] = jnp.zeros((8, width + freq - 128), jnp.float32)


def own_kernel(
    src_at, focus_at, offsets_at, prior_at, group_at, noise_at, live_count, out, facts_out,
    inverse_out, src, focus, offsets, prior, group, noise, sems
):
    moves = (
        (focus_at, focus), (offsets_at, offsets), (prior_at, prior), (group_at, group),
        (noise_at, noise), (src_at, src),
    )
    copies = [pltpu.make_async_copy(x, y, sems.at[n]) for n, (x, y) in enumerate(moves)]
    for copy in copies:
        copy.start()
    slots = src.shape[0]
    facts_out[...] = jnp.zeros_like(facts_out)
    slot = lax.broadcasted_iota(jnp.int32, (1, slots), 1)
    for copy in copies:
        copy.wait()
    facts_out[5:6, :slots] = (slot < live_count[0]).astype(jnp.float32)
    facts_out[0:1, :slots] = focus[...]
    facts_out[1:3, :slots] = offsets[...].astype(jnp.float32)
    facts_out[3:4, :slots] = prior[...].astype(jnp.float32)
    facts_out[4:5, :slots] = group[...].astype(jnp.float32)
    inverse = 1.0 / noise[...]
    inverse_out[...] = inverse
    prepared_rows(src, facts_out[...], inverse, out)


def neighbour_kernel(src, facts, inverse_noise, out):
    prepared_rows(src, facts[...], inverse_noise[...], out)


def first_at(part, row):
    return 192 * part + row


def both_at(half, part, row):
    main, left = deep_at(half, part)
    return main + row if row < 128 else left + row - 128


def place_half(own, ynb, y_out, power_out, parts, at):
    width = y_out.shape[1]
    slots = own.shape[0] - 8
    main = 128 - slots
    for cols, out in ((slice(0, width), y_out), (slice(width, None), power_out)):
        pieces = ((own, 0, slots, 0), (ynb, 0, main, slots), (ynb, main, slots, 128))
        for src, start, stop, to in pieces:
            pair = halves(src[start:stop, cols])
            for part in range(parts):
                row = at(part, to)
                out[row : row + stop - start] = pair[part % 2]


def placed(out, part, at):
    main, left = at(part, 0), at(part, 128)
    return jnp.concatenate([out[main : main + 128], out[left : left + 64]], axis=0)


def half_facts(own, ynb):
    slots = own.shape[0] - 8
    x, y = own[slots:, :128], pltpu.roll(ynb[slots:, :128], slots, 1)
    lane = lax.broadcasted_iota(jnp.int32, (8, 128), 1)
    return jnp.concatenate([jnp.where(lane < slots, x, y), y], axis=1)


def by_device(x, slots):
    lane = lax.broadcasted_iota(jnp.int32, (x.shape[0], 128), 1)
    main, left = pltpu.roll(x[:, :128], 128 - slots, 1), pltpu.roll(x[:, 128:], 128 - slots, 1)
    return x[:, :128], jnp.where(lane < 128 - slots, main, left)


def in_half(x, y, slots):
    lane = lax.broadcasted_iota(jnp.int32, (x.shape[0], 128), 1)
    y = pltpu.roll(y, slots, 1)
    return jnp.concatenate([jnp.where(lane < slots, x, y), y], axis=1)


def team_order(tiles):
    me = lax.axis_index("dom")
    even, first = me % 2 == 0, (me // 2) % 2 == 0
    a, b, c, d = tiles
    a, b, c, d = (jnp.where(even, x, y) for x, y in ((a, c), (b, d), (c, a), (d, b)))
    return [jnp.where(first, x, y) for x, y in ((a, b), (b, a), (c, d), (d, c))]


def prior_rows(facts, per, lanes):
    r = (lax.broadcasted_iota(jnp.int32, (per, lanes), 0) % ROT).astype(jnp.float32)
    return PRIOR * turn_cos((r - facts[3:4, :lanes]) * (1.0 / ROT))


def prepare_refs(ref, phases, r_high, r_low, q_high, q_low):
    per, width = ref.shape
    freq = width // 2
    rr, ri = ref[:, :freq], ref[:, freq:]
    mid = SHIFTS // 2

    def store(t, re, im):
        rows = slice(t * per, (t + 1) * per)
        r_high[rows, :freq], r_low[rows, :freq] = halves(re)
        r_high[rows, freq:], r_low[rows, freq:] = halves(im)

    store(mid, rr, ri)
    for t in range(mid):
        c, s = phases[t]
        a, b, d, e = rr * c, ri * s, ri * c, rr * s
        store(t, a + b, d - e)
        store(SHIFTS - 1 - t, a - b, d + e)
    q_high[...], q_low[...] = halves(rr * rr + ri * ri)


def block_scores(prepared, particles, prior):
    r_high, r_low, q_high, q_low = (x[...] for x in prepared)
    y_high, y_low, p_high, p_low = particles
    quad = dot_nt(q_high, p_high) + dot_nt(q_low, p_high) + dot_nt(q_high, p_low)
    score = dot_nt(r_high, y_high) + dot_nt(r_low, y_high) + dot_nt(r_high, y_low)
    per, lanes = prior.shape
    return score.reshape(SHIFTS, per, lanes) + (prior - 0.5 * quad)[None]


def weigh(score, e_out):
    top = jnp.max(jnp.max(score, axis=0), axis=0, keepdims=True)
    e = jnp.exp(score - top[None])
    e_out[...] = e
    side = SIDE // 2
    by_x = [sum(e[SIDE * x + y] for y in range(SIDE)) for x in range(SIDE)]
    by_y = [sum(e[SIDE * x + y] for x in range(SIDE)) for y in range(SIDE)]
    sums = [sum(by_x)]
    for by in (by_x, by_y):
        sums.append(sum(by[k] * float(k - side) for k in range(SIDE) if k != side))
    return top, [jnp.sum(x, axis=0, keepdims=True) for x in sums]


def joined_sums(tops, sums):
    top = tops[0]
    for other in tops[1:]:
        top = jnp.maximum(top, other)
    factors = [jnp.exp(other - top) for other in tops]
    return top, [sum(f * x for f, x in zip(factors, column)) for column in zip(*sums)]


def early_kernel(own_at, near, *rest):
    *prepared, own, sem = rest
    copy = pltpu.make_async_copy(own_at, own, sem)
    copy.start()
    phases = grid_phases(own.shape[1] // 2)
    prepare_refs(near, phases, *prepared[4:])
    copy.wait()
    prepare_refs(own, phases, *prepared[:4])


def middle_kernel(wait, *rest):
    count = len(rest) // 5
    refs, prepared = rest[:count], rest[count:]
    phases = grid_phases(refs[0].shape[1] // 2)
    for n in range(count):
        prepare_refs(refs[n], phases, *prepared[4 * n : 4 * n + 4])


def score_kernel(half, blocks, own, ynb, *rest):
    prepared, rest = rest[: 4 * blocks], rest[4 * blocks :]
    if half:
        stats_in, tops_in, y_in, power_in, *rest = rest
    e_outs, rest = rest[:blocks], rest[blocks:]
    y_out, power_out, stats_out, tops_out, stats, tops_row = rest
    per, lanes = e_outs[0].shape[1:]
    slots = lanes // 2
    facts = half_facts(own, ynb)
    at = functools.partial(both_at, half) if half else first_at
    place_half(own, ynb, y_out, power_out, 2 + half, at)
    if half:
        for x, out in ((y_in, y_out), (power_in, power_out)):
            for part in range(3):
                for row, size in ((0, 128), (128, 64)):
                    here, to = first_at(part % 2, row), both_at(0, part, row)
                    out[to : to + size] = x[here : here + size]
    stats[...] = jnp.zeros_like(stats)
    tops_row[...] = jnp.zeros_like(tops_row)
    particles = [placed(out, part, at) for out in (y_out, power_out) for part in (0, 1)]
    prior = prior_rows(facts, per, lanes)
    tops, sums = [], []
    for n in range(blocks):
        score = block_scores(prepared[4 * n : 4 * n + 4], particles, prior)
        top, sums_here = weigh(score, e_outs[n])
        tops_row[n : n + 1, :lanes] = top
        tops.append(top)
        sums.append(sums_here)
    top, sums = joined_sums(tops, sums)
    for k, row in enumerate((top, *sums, facts[5:6, :lanes])):
        stats[k : k + 1, :lanes] = row
    if half == 0:
        stats_out[...] = stats[...]
        tops_out[...] = tops_row[...]
        return
    pair = by_device(stats_in[...], slots), by_device(stats[...], slots)
    tiles = team_order((*pair[0], *pair[1]))
    stats_out[...] = jnp.concatenate(tiles, axis=1)
    tops_out[:, :256] = tops_in[...]
    tops_out[:, 256:] = tops_row[...]


def sum_kernel(blocks, cuts, last, waits, *rest):
    team, tops, rest = rest[:TEAM], rest[TEAM], rest[TEAM + 1 + waits :]
    e_refs, (y_ref, power_ref, *outs) = rest[: 2 * len(blocks)], rest[2 * len(blocks) :]
    per, lanes = e_refs[0].shape[1:]
    slots = lanes // 2
    width = y_ref.shape[1]
    freq = width // 2
    pair = [x[...] for x in team]
    top, (mass, *move) = joined_sums(
        [x[0:1] for x in pair], [[x[k : k + 1] for k in (1, 2, 3)] for x in pair]
    )
    live = pair[0][4:5] / mass
    rows = [top, live, *(x * live for x in move)]
    rows = jnp.concatenate([*rows, jnp.zeros((4, 512), jnp.float32)], axis=0)
    mine = team_order([rows[:, 128 * k : 128 * (k + 1)] for k in range(4)])
    if last:
        shift_out = outs.pop()
        shift_out[...] = mine[0][2:4, :slots]
    halves_rows = (in_half(mine[0], mine[1], slots), in_half(mine[2], mine[3], slots))
    per_block = []
    weight_sums = []
    for k, n in enumerate(blocks):
        w = []
        for half, row in enumerate(halves_rows):
            top_here = tops[n : n + 1, 256 * half : 256 * half + lanes]
            gain = jnp.exp(top_here - row[0:1, :lanes]) * row[1:2, :lanes]
            w.append(e_refs[2 * k + half][...] * gain[None])
        per_block.append(deep_lanes(*(x.reshape(SHIFTS * per, lanes) for x in w)))
        weight_sums.append(deep_lanes(*(jnp.sum(x, axis=0) for x in w)))
    flat_all = dot_nn(jnp.concatenate(per_block, axis=0), y_ref[...])
    weight_all = dot_nn(jnp.concatenate(weight_sums, axis=0), power_ref[...])
    phases = grid_phases(freq)
    count = len(cuts) - 1
    for k in range(len(blocks)):
        flat = flat_all[SHIFTS * per * k : SHIFTS * per * (k + 1)]
        weight = weight_all[per * k : per * (k + 1)]
        write_block(flat, weight, phases, cuts, outs[count * k : count * (k + 1)])


def write_block(flat, weight, phases, cuts, outs):
    per, freq = weight.shape
    width = 2 * freq
    mid = SHIFTS // 2

    def block(t):
        return flat[t * per : (t + 1) * per, :freq], flat[t * per : (t + 1) * per, freq:]

    re, im = block(mid)
    for t in range(mid):
        c, s = phases[t]
        ar, ai = block(t)
        br, bi = block(SHIFTS - 1 - t)
        re = re + (ar + br) * c - (ai - bi) * s
        im = im + (ar - br) * s + (ai + bi) * c
    for start, stop, out in zip(cuts, cuts[1:], outs):
        part = slice(start, stop)
        out[:, :freq] = re[part]
        out[:, freq:width] = im[part]
        out[:, width:] = weight[part]


def add_kernel(a, *rest):
    *parts, out = rest
    at = 0
    for part in parts:
        rows = slice(at, at + part.shape[0])
        out[rows] = a[rows] + part[...]
        at += part.shape[0]


def final_kernel(row_cuts, *refs):
    own, *parts, signal, out = refs
    rows, width = out.shape
    freq = width // 2
    inverse = 1.0 / signal[...]
    every = sorted({cut for cuts in row_cuts for cut in cuts})
    for start, stop in zip(every, every[1:]):
        total = own[start:stop]
        at = 0
        for cuts in row_cuts:
            for low, high in zip(cuts, cuts[1:]):
                if low <= start and stop <= high:
                    total = total + parts[at][start - low : stop - low]
                at += 1
        denominator = total[:, width:] + inverse
        out[start:stop, :freq] = total[:, :freq] / denominator
        out[start:stop, freq:] = total[:, freq:width] / denominator


def params(mib):
    return pltpu.CompilerParams(vmem_limit_bytes=mib * 1024 * 1024)


def crossed(block, mask):
    size = lax.axis_size("dom")
    return lax.ppermute(block, "dom", [(i, i ^ mask) for i in range(size)])


def on_device(
    particle_fourier,
    defocus,
    particle_offset,
    prior_rotation,
    group_id,
    live_count,
    noise_power,
    signal_power,
    class_refs,
):
    slots, width = particle_fourier.shape
    freq = width // 2
    size = lax.axis_size("dom")
    blocks = size // TEAM
    refs_own = class_refs.reshape(-1, width)
    per = refs_own.shape[0]
    f32 = jnp.float32
    vmem = pl.BlockSpec(memory_space=pltpu.VMEM)
    no_cost = pl.CostEstimate(flops=0, bytes_accessed=0, transcendentals=0)
    much = pl.CostEstimate(flops=16 * 10**9, bytes_accessed=0, transcendentals=0)

    def gated(x, *waits):
        return pl.pallas_call(
            lambda *a: None,
            out_shape=jax.ShapeDtypeStruct(x.shape, x.dtype),
            in_specs=[anywhere] * (1 + len(waits)),
            out_specs=anywhere,
            input_output_aliases={0: 0},
            compiler_params=params(1),
            cost_estimate=no_cost,
            name="gate",
        )(x, *waits)

    ynb = crossed(particle_fourier, 2)
    anywhere = pl.BlockSpec(memory_space=pl.ANY)
    def gated(x, *waits):
        return pl.pallas_call(
            lambda *a: None,
            out_shape=jax.ShapeDtypeStruct(x.shape, x.dtype),
            in_specs=[anywhere] * (1 + len(waits)),
            out_specs=anywhere,
            input_output_aliases={0: 0},
            compiler_params=params(1),
            cost_estimate=no_cost,
            name="gate",
        )(x, *waits)

    ynb = crossed(particle_fourier, 2)
    anywhere = pl.BlockSpec(memory_space=pl.ANY)
    def gated(arrays, waits, cost):
        return pl.pallas_call(
            lambda *a: None,
            out_shape=tuple(jax.ShapeDtypeStruct(x.shape, x.dtype) for x in arrays),
            in_specs=[anywhere] * (len(arrays) + len(waits)),
            out_specs=(anywhere,) * len(arrays),
            input_output_aliases={n: n for n in range(len(arrays))},
            compiler_params=params(1),
            cost_estimate=cost,
            name="gate",
        )(*arrays, *waits)

    def gated(x, *waits):
        return pl.pallas_call(
            lambda *a: None,
            out_shape=jax.ShapeDtypeStruct(x.shape, x.dtype),
            in_specs=[anywhere] * (1 + len(waits)),
            out_specs=anywhere,
            input_output_aliases={0: 0},
            compiler_params=params(1),
            cost_estimate=no_cost,
            name="gate",
        )(x, *waits)

    ynb = crossed(particle_fourier, 2)
    anywhere = pl.BlockSpec(memory_space=pl.ANY)
    def gated(x, *waits):
        return pl.pallas_call(
            lambda *a: None,
            out_shape=jax.ShapeDtypeStruct(x.shape, x.dtype),
            in_specs=[anywhere] * (1 + len(waits)),
            out_specs=anywhere,
            input_output_aliases={0: 0},
            compiler_params=params(1),
            cost_estimate=no_cost,
            name="gate",
        )(x, *waits)

    ynb = crossed(particle_fourier, 2)
    refs = {0: refs_own, 1: crossed(refs_own, TEAM)}
    for n in range(2, blocks, 2):
        refs[n] = crossed(refs_own, TEAM * n)
    own_facts = (
        particle_fourier,
        defocus.reshape(1, slots),
        particle_offset.T,
        prior_rotation.reshape(1, slots),
        group_id.reshape(1, slots),
        noise_power,
    )
    own, facts, inverse_noise = pl.pallas_call(
        own_kernel,
        out_shape=(
            jax.ShapeDtypeStruct((slots + 8, width + freq), f32),
            jax.ShapeDtypeStruct((8, 128), f32),
            jax.ShapeDtypeStruct(noise_power.shape, f32),
        ),
        in_specs=[anywhere] * 6 + [pl.BlockSpec(memory_space=pltpu.SMEM)],
        out_specs=(vmem,) * 3,
        scratch_shapes=[pltpu.VMEM(x.shape, x.dtype) for x in own_facts]
        + [pltpu.SemaphoreType.DMA((6,))],
        compiler_params=params(6),
        cost_estimate=no_cost,
        name="own",
    )(*(pltpu.with_memory_space_constraint(x, pltpu.HBM) for x in own_facts), live_count)
    cnb = crossed(own, 1)
    both = 2 * slots
    bf16 = jnp.bfloat16
    early = 2

    def shaped(rows, cols, dtype=f32):
        return jax.ShapeDtypeStruct((rows, cols), dtype)

    block_shapes = [shaped(SHIFTS * per, width, bf16)] * 2 + [shaped(per, freq, bf16)] * 2
    score_shape = jax.ShapeDtypeStruct((SHIFTS, per, both), f32)

    def call(kernel, operands, out_shape, name, mib, cost=None, scratch=()):
        return pl.pallas_call(
            kernel,
            cost_estimate=cost,
            out_shape=tuple(out_shape),
            in_specs=[vmem] * len(operands),
            out_specs=(vmem,) * len(out_shape),
            scratch_shapes=list(scratch),
            compiler_params=params(mib),
            name=name,
        )(*operands)

    prepared = pl.pallas_call(
        early_kernel,
        out_shape=tuple(block_shapes * early),
        in_specs=[anywhere, vmem],
        out_specs=(vmem,) * (4 * early),
        scratch_shapes=[pltpu.VMEM(refs_own.shape, f32), pltpu.SemaphoreType.DMA],
        compiler_params=params(8),
        name="early",
    )(pltpu.with_memory_space_constraint(refs_own, pltpu.HBM), refs[1])
    for n in range(2, blocks, 2):
        refs[n] = gated(refs[n], facts, prepared[2])
        refs[n + 1] = crossed(refs[n], TEAM)
    refs = [refs[n] for n in range(blocks)]
    ynb_prepared = pl.pallas_call(
        neighbour_kernel,
        out_shape=jax.ShapeDtypeStruct((slots + 8, width + freq), f32),
        in_specs=[vmem] * 3,
        out_specs=vmem,
        compiler_params=params(6),
        cost_estimate=no_cost,
        name="neighbour",
    )(ynb, crossed(facts, 2), inverse_noise)
    cynb = crossed(ynb_prepared, 1)

    late = blocks - early
    outs = pl.pallas_call(
        middle_kernel,
        out_shape=tuple(block_shapes * late),
        in_specs=[anywhere] + [vmem] * late,
        out_specs=(vmem,) * (4 * late),
        compiler_params=params(4 + 2 * blocks),
        cost_estimate=much,
        name="middle",
    )(ynb_prepared, *refs[early:])
    prepared = (*prepared, *outs)
    top_rows = -(-blocks // 8) * 8

    def scores(half, particles, before, cost):
        lanes = 256 * (1 + half)
        rows = (6 if half else 2) * both
        return pl.pallas_call(
            lambda *a: score_kernel(half, blocks, *a),
            out_shape=(
                *[score_shape] * blocks,
                shaped(rows, width, bf16),
                shaped(rows, freq, bf16),
                shaped(8, lanes),
                shaped(top_rows, lanes),
            ),
            in_specs=[vmem] * (2 + 4 * blocks + len(before)),
            out_specs=(vmem,) * (blocks + 4),
            scratch_shapes=[pltpu.VMEM((8, 256), f32), pltpu.VMEM((top_rows, 256), f32)],
            compiler_params=params(8 + 2 * blocks),
            cost_estimate=cost,
            name="scores",
        )(*particles, *prepared, *before)

    *e_own, y, power, stats, tops = scores(0, (own, ynb_prepared), (), much)
    *e_other, y, power, stats, tops = scores(1, (cnb, cynb), (stats, tops, y, power), None)

    team = [stats] + [crossed(stats, n) for n in range(1, TEAM)]

    def sums(numbers, cuts, last=False, waits=()):
        out_shape = [shaped(b - a, width + freq) for a, b in zip(cuts, cuts[1:])] * len(numbers)
        if last:
            out_shape.append(shaped(2, slots))
        weights = [e[n] for n in numbers for e in (e_own, e_other)]
        return pl.pallas_call(
            lambda *a: sum_kernel(numbers, cuts, last, len(waits), *a),
            out_shape=tuple(out_shape),
            in_specs=[vmem] * (TEAM + 1) + [anywhere] * len(waits) + [vmem] * (2 + len(weights)),
            out_specs=(vmem,) * len(out_shape),
            compiler_params=params(12),
            name="sums",
        )(*team, tops, *waits, *weights, y, power)

    def combined(mine, others, cost=None):
        return pl.pallas_call(
            add_kernel,
            out_shape=jax.ShapeDtypeStruct(mine.shape, f32),
            in_specs=[vmem] * (1 + len(others)),
            out_specs=vmem,
            compiler_params=params(4),
            cost_estimate=cost,
            name="combined",
        )(mine, *others)

    whole, cut = (0, per), (0, per // 2, per)
    far = []
    waits = []
    for n in range(2, blocks, 2):
        handed = sums((n + 1,), cut)
        mine = sums((n,), cut, waits=handed[:1])
        if n == 2:
            near = sums((1,), cut, waits=mine[:1])
        joined = [combined(x, [crossed(y, TEAM)]) for x, y in zip(mine, handed)]
        far.extend(crossed(x, TEAM * n) for x in joined)
        waits.extend(joined)
    own_part, shift = sums((0,), whole, last=True, waits=waits)
    own_part = combined(own_part, [crossed(x, TEAM) for x in near], much)
    row_cuts = [cut] * (len(far) // 2)

    refs_new = pl.pallas_call(
        lambda *a: final_kernel(row_cuts, *a),
        out_shape=jax.ShapeDtypeStruct((per, width), f32),
        in_specs=[vmem] * (len(far) + 2),
        out_specs=vmem,
        compiler_params=params(2 + blocks),
        name="update",
    )(own_part, *far, signal_power.reshape(1, freq))

    return (shift.T, refs_new.reshape(class_refs.shape))


def solution(mesh):
    in_specs = (
        P(("groups", "dom"), None),
        P(("groups", "dom")),
        P(("groups", "dom"), None),
        P(("groups", "dom")),
        P(("groups", "dom")),
        P(("groups", "dom")),
        P("groups", None),
        P("groups"),
        P(("groups", "dom"), None, None),
    )
    out_specs = (P(("groups", "dom"), None), P(("groups", "dom"), None, None))
    return jax.shard_map(
        on_device, mesh=mesh, in_specs=in_specs, out_specs=out_specs, check_vma=False
    )
```

```python
import math

import jax
import jax.numpy as jnp
from jax import lax
from jax.experimental import pallas as pl
from jax.experimental.pallas import tpu as pltpu
from jax.sharding import PartitionSpec as P

ROT = 16
SIDE = 3
BOX = 128
FY = 32
SHIFTS = 9
TEAM = 4
PRIOR = 2.0
CTF_SIZE = math.hypot(0.995, 0.1)
CTF_TURN = math.atan2(0.1, 0.995)
SINE = (
    9.99999976e-01,
    -1.66666476e-01,
    8.33289854e-03,
    -1.98008185e-04,
    2.59032780e-06,
)
TWO_PI = 2.0 * math.pi
PI_A = 3.140625
PI_B = 0.0009670257568359375
PI_C = math.pi - PI_A - PI_B
HIGHEST = lax.Precision.HIGHEST
GRID = tuple((t // SIDE - SIDE // 2, t % SIDE - SIDE // 2) for t in range(SHIFTS))


def half_turn_sine(x):
    s = x * x
    p = SINE[4]
    for c in SINE[3::-1]:
        p = p * s + c
    return x * p


def turn_cos(turns):
    t = jnp.abs(turns - jnp.round(turns))
    return half_turn_sine(TWO_PI * (0.25 - t))


def turn_sin(turns):
    return turn_cos(turns - 0.25)


def freq_rows(width, rows):
    f = lax.broadcasted_iota(jnp.int32, (rows, width), 1)
    kx = (f // FY).astype(jnp.float32)
    ky = (f % FY - FY // 2).astype(jnp.float32)
    return kx, ky


def dot_nt(a, b):
    return lax.dot_general(
        a, b, (((1,), (1,)), ((), ())), preferred_element_type=jnp.float32
    )


def dot_nn(a, b):
    return lax.dot_general(
        a, b, (((1,), (0,)), ((), ())), preferred_element_type=jnp.float32
    )


def exact_dot_nn(a, b):
    return lax.dot_general(
        a, b, (((1,), (0,)), ((), ())), precision=HIGHEST, preferred_element_type=jnp.float32
    )


def halves(x):
    high = x.astype(jnp.bfloat16)
    return high, (x - high.astype(jnp.float32)).astype(jnp.bfloat16)


MAIN = 256


def deep_at(part, row):
    return MAIN * part + row if row < MAIN else 3 * MAIN + 32 * part + row - MAIN


def deep_lanes(x):
    rows, lanes = x.shape
    left = lanes - MAIN
    high, low = halves(x[:, :MAIN])
    tail = jnp.concatenate([x[:, MAIN:], jnp.zeros((rows, 128 - left), jnp.float32)], axis=1)
    tail_high = tail.astype(jnp.bfloat16).astype(jnp.float32)
    tail_low = tail - tail_high
    mixed = tail_high + pltpu.roll(tail_high, left, 1) + pltpu.roll(tail_low, 2 * left, 1)
    return jnp.concatenate([high, high, low, mixed.astype(jnp.bfloat16)], axis=1)


def grid_phases(width):
    kx, ky = freq_rows(width, 1)
    out = []
    for t, (gx, gy) in enumerate(GRID):
        if t < SHIFTS // 2:
            m = (kx * gx + ky * gy) * (1.0 / BOX)
            out.append((turn_cos(m), turn_sin(m)))
    return out


def phase_of(phases, t):
    mid = SHIFTS // 2
    if t < mid:
        return phases[t]
    c, s = phases[SHIFTS - 1 - t]
    return c, -s


def prepared_rows(src, facts, inverse_noise, out):
    slots, width = src.shape
    freq = width // 2
    columns = jnp.concatenate([facts, jnp.zeros((120, 128), jnp.float32)], axis=0).T[:slots]
    focus = columns[:, 0:1]
    off_x = columns[:, 1:2]
    off_y = columns[:, 2:3]
    group_col = columns[:, 4:5]

    kx, ky = freq_rows(freq, 1)
    chi = focus * ((kx * kx + ky * ky) * (1.0 / 1024.0))
    k = jnp.round(chi * (1.0 / math.pi))
    rest_angle = ((chi - k * PI_A) - k * PI_B) - k * PI_C
    shifted_angle = rest_angle + CTF_TURN
    over = shifted_angle > (0.5 * math.pi)
    folded = jnp.where(over, math.pi - shifted_angle, shifted_angle)
    parity = 0.5 * k
    sign = (parity - jnp.floor(parity)) * (4.0 * CTF_SIZE) - CTF_SIZE
    ctf = half_turn_sine(folded) * sign
    kx0, ky0 = freq_rows(128, 1)
    m = (kx0 * off_x + ky0 * off_y) * (1.0 / BOX)
    pc, ps = turn_cos(m), turn_sin(m)
    step = off_x * ((128 // FY) / BOX) + jnp.zeros((slots, 128), jnp.float32)
    sc, ss = turn_cos(step), turn_sin(step)

    total = inverse_noise.shape[0]
    onehot = (
        group_col == lax.broadcasted_iota(jnp.int32, (slots, total), 1).astype(jnp.float32)
    ).astype(jnp.float32)
    noise_rows = exact_dot_nn(onehot, inverse_noise)
    scaled = ctf * noise_rows
    out[:slots, width:] = ctf * scaled
    for n in range(freq // 128):
        part = slice(128 * n, 128 * (n + 1))
        twin = slice(freq + 128 * n, freq + 128 * (n + 1))
        co = pc * scaled[:, part]
        si = ps * scaled[:, part]
        pc, ps = pc * sc - ps * ss, ps * sc + pc * ss
        xr, xi = src[:, part], src[:, twin]
        out[:slots, part] = xr * co - xi * si
        out[:slots, twin] = xr * si + xi * co
    out[slots:, :128] = facts
    out[slots:, 128:] = jnp.zeros((8, width + freq - 128), jnp.float32)


def own_kernel(
    src_at, focus_at, offsets_at, prior_at, group_at, noise_at, live_count, out, facts_out,
    inverse_out, src, focus, offsets, prior, group, noise, sems
):
    moves = (
        (focus_at, focus), (offsets_at, offsets), (prior_at, prior), (group_at, group),
        (noise_at, noise), (src_at, src),
    )
    copies = [pltpu.make_async_copy(x, y, sems.at[n]) for n, (x, y) in enumerate(moves)]
    for copy in copies:
        copy.start()
    slots = src.shape[0]
    facts_out[...] = jnp.zeros_like(facts_out)
    slot = lax.broadcasted_iota(jnp.int32, (1, slots), 1)
    for copy in copies:
        copy.wait()
    facts_out[5:6, :slots] = (slot < live_count[0]).astype(jnp.float32)
    facts_out[0:1, :slots] = focus[...]
    facts_out[1:3, :slots] = offsets[...].astype(jnp.float32)
    facts_out[3:4, :slots] = prior[...].astype(jnp.float32)
    facts_out[4:5, :slots] = group[...].astype(jnp.float32)
    inverse = 1.0 / noise[...]
    inverse_out[...] = inverse
    prepared_rows(src, facts_out[...], inverse, out)


def neighbour_kernel(src, facts, inverse_noise, wait, out):
    prepared_rows(src, facts[...], inverse_noise[...], out)


def team_order(own, cnb, ynb, cynb):
    for even in (True, False):
        for first in (True, False):
            heavy, light = ((own, ynb), (cnb, cynb)) if even else ((cnb, cynb), (own, ynb))
            if not first:
                heavy, light = heavy[::-1], light[::-1]
            yield even, first, heavy, light


def place_rows(even, first, parts, y_out, power_out):
    width = y_out.shape[1]
    slots = parts[0].shape[0] - 8
    half = slots // 2
    cut = MAIN - 2 * slots - half

    def place(src, start, stop, to):
        for cols, out in ((slice(0, width), y_out), (slice(width, None), power_out)):
            pair = halves(src[start:stop, cols])
            for part in range(3):
                row = deep_at(part, to)
                out[row : row + stop - start] = pair[part % 2]

    for is_even, is_first, heavy, light in team_order(*parts):

        @pl.when(jnp.logical_and(even == is_even, first == is_first))
        def _(heavy=heavy, light=light):
            place(heavy[0], 0, slots, 0)
            place(heavy[1], 0, slots, slots)
            place(light[0], 0, half, 2 * slots)
            place(light[1], 0, cut, 2 * slots + half)
            place(light[1], cut, half, MAIN)


def placed(out, part, rows):
    main, left = deep_at(part, 0), deep_at(part, MAIN)
    return jnp.concatenate([out[main : main + MAIN], out[left : left + rows - MAIN]], axis=0)


def lane_index():
    return lax.broadcasted_iota(jnp.int32, (8, 128), 1)


def row_facts(even, first, parts):
    lane = lane_index()
    own, cnb, ynb, cynb = (x[x.shape[0] - 8 :, :128] for x in parts)
    heavy = (jnp.where(even, own, cnb), jnp.where(even, ynb, cynb))
    light = (jnp.where(even, cnb, own), jnp.where(even, cynb, ynb))
    a0, b0 = (jnp.where(first, x[0], x[1]) for x in (heavy, light))
    a1, b1 = (jnp.where(first, x[1], x[0]) for x in (heavy, light))
    a1 = pltpu.roll(a1, 96, 1)
    b1 = pltpu.roll(b1, 112, 1)
    middle = jnp.where(lane < 64, a1, jnp.where(lane < 112, pltpu.roll(b0, 64, 1), b1))
    return jnp.concatenate([jnp.where(lane < 96, a0, a1), middle, b1], axis=1)


def own_lanes(even, first, x):
    lane = lane_index()
    a, b, c = x[:, :128], x[:, 128:256], x[:, 256:]
    heavy_far = jnp.where(lane < 32, pltpu.roll(a, 32, 1), pltpu.roll(b, 32, 1))
    light_far = jnp.where(lane < 16, pltpu.roll(b, 16, 1), pltpu.roll(c, 16, 1))
    light = jnp.where(first, pltpu.roll(b, 64, 1), light_far)
    heavy = jnp.where(first, a, heavy_far)
    return jnp.where(even, heavy, jnp.where(lane < 48, light, 0.0))


def place_of_device():
    me = lax.axis_index("dom")
    return me % 2 == 0, (me // 2) % 2 == 0


def prior_rows(facts, per, lanes):
    r = (lax.broadcasted_iota(jnp.int32, (per, lanes), 0) % ROT).astype(jnp.float32)
    return PRIOR * turn_cos((r - facts[3:4, :lanes]) * (1.0 / ROT))


def prepare_refs(ref, phases, r_high, r_low, q_high, q_low):
    per, width = ref.shape
    freq = width // 2
    rr, ri = ref[:, :freq], ref[:, freq:]
    mid = SHIFTS // 2

    def store(t, re, im):
        rows = slice(t * per, (t + 1) * per)
        r_high[rows, :freq], r_low[rows, :freq] = halves(re)
        r_high[rows, freq:], r_low[rows, freq:] = halves(im)

    store(mid, rr, ri)
    for t in range(mid):
        c, s = phases[t]
        a, b, d, e = rr * c, ri * s, ri * c, rr * s
        store(t, a + b, d - e)
        store(SHIFTS - 1 - t, a - b, d + e)
    q_high[...], q_low[...] = halves(rr * rr + ri * ri)


def block_scores(prepared, y_terms, power_terms, prior):
    r_high, r_low, q_high, q_low = (x[...] for x in prepared)
    quad = dot_nt(jnp.concatenate([q_high, q_low, q_high], axis=1), power_terms)
    score = dot_nt(jnp.concatenate([r_high, r_low, r_high], axis=1), y_terms)
    per, lanes = prior.shape
    return score.reshape(SHIFTS, per, lanes) + (prior - 0.5 * quad)[None]


def weigh(score, e_out):
    top = jnp.max(jnp.max(score, axis=0), axis=0, keepdims=True)
    e = jnp.exp(score - top[None])
    e_out[...] = e
    side = SIDE // 2
    by_x = [sum(e[SIDE * x + y] for y in range(SIDE)) for x in range(SIDE)]
    by_y = [sum(e[SIDE * x + y] for x in range(SIDE)) for y in range(SIDE)]
    sums = [sum(by_x)]
    for by in (by_x, by_y):
        sums.append(sum(by[k] * float(k - side) for k in range(SIDE) if k != side))
    return top, [jnp.sum(x, axis=0, keepdims=True) for x in sums]


def joined_sums(tops, sums):
    top = tops[0]
    for other in tops[1:]:
        top = jnp.maximum(top, other)
    factors = [jnp.exp(other - top) for other in tops]
    return top, [sum(f * x for f, x in zip(factors, column)) for column in zip(*sums)]


def early_kernel(own_at, near, *rest):
    *prepared, own, sem = rest
    copy = pltpu.make_async_copy(own_at, own, sem)
    copy.start()
    phases = grid_phases(own.shape[1] // 2)
    prepare_refs(near, phases, *prepared[4:])
    copy.wait()
    prepare_refs(own, phases, *prepared[:4])


def middle_kernel(*rest):
    count = len(rest) // 5
    refs, prepared = rest[:count], rest[count:]
    phases = grid_phases(refs[0].shape[1] // 2)
    for n in range(count):
        prepare_refs(refs[n], phases, *prepared[4 * n : 4 * n + 4])


def late_kernel(blocks, own, cnb, ynb, cynb, *rest):
    prepared, rest = rest[: 4 * blocks], rest[4 * blocks :]
    e_outs, (y_out, power_out, stats_out, tops_out) = rest[:blocks], rest[blocks:]
    per, lanes = e_outs[0].shape[1:]
    parts = (own, cnb, ynb, cynb)
    even, first = place_of_device()
    place_rows(even, first, parts, y_out, power_out)
    facts = row_facts(even, first, parts)
    empty = deep_at(2, lanes)
    for out in (y_out, power_out):
        out[empty:] = jnp.zeros_like(out[empty:])
    stats_out[...] = jnp.zeros_like(stats_out)
    tops_out[...] = jnp.zeros_like(tops_out)
    terms = []
    for out in (y_out, power_out):
        high, low = (placed(out, part, lanes) for part in (0, 1))
        terms.append(jnp.concatenate([high, high, low], axis=1))
    prior = prior_rows(facts, per, lanes)
    tops, sums = [], []
    for n in range(blocks):
        score = block_scores(prepared[4 * n : 4 * n + 4], *terms, prior)
        top, sums_here = weigh(score, e_outs[n])
        tops_out[n : n + 1, :lanes] = top
        tops.append(top)
        sums.append(sums_here)
    top, sums = joined_sums(tops, sums)
    for k, row in enumerate((top, *sums, facts[5:6, :lanes])):
        stats_out[k : k + 1, :lanes] = row


def sum_kernel(n, cuts, last, waits, *rest):
    team, tops, rest = rest[:TEAM], rest[TEAM], rest[TEAM + 1 + waits :]
    e_ref, y_ref, power_ref, *outs = rest
    per, lanes = e_ref.shape[1:]
    width = y_ref.shape[1]
    freq = width // 2
    team = [x[...] for x in team]
    top, (mass, *move) = joined_sums(
        [x[0:1] for x in team], [[x[k : k + 1] for k in (1, 2, 3)] for x in team]
    )
    live = team[0][4:5] / mass
    gain = (jnp.exp(tops[n : n + 1] - top) * live)[:, :lanes]
    if last:
        shift_out = outs.pop()
        move = [x * live for x in move] + [jnp.zeros((6, live.shape[1]), jnp.float32)]
        move = own_lanes(*place_of_device(), jnp.concatenate(move, axis=0))
        shift_out[...] = move[:2, : shift_out.shape[1]]
    w = e_ref[...] * gain[None]
    flat = dot_nn(deep_lanes(w.reshape(SHIFTS * per, lanes)), y_ref[...])
    weight = dot_nn(deep_lanes(jnp.sum(w, axis=0)), power_ref[...])
    phases = grid_phases(freq)
    mid = SHIFTS // 2

    def block(t):
        return flat[t * per : (t + 1) * per, :freq], flat[t * per : (t + 1) * per, freq:]

    re, im = block(mid)
    for t in range(mid):
        c, s = phases[t]
        ar, ai = block(t)
        br, bi = block(SHIFTS - 1 - t)
        re = re + (ar + br) * c - (ai - bi) * s
        im = im + (ar - br) * s + (ai + bi) * c
    for start, stop, out in zip(cuts, cuts[1:], outs):
        part = slice(start, stop)
        out[:, :freq] = re[part]
        out[:, freq:width] = im[part]
        out[:, width:] = weight[part]


def add_kernel(a, *rest):
    *parts, out = rest
    at = 0
    for part in parts:
        rows = slice(at, at + part.shape[0])
        out[rows] = a[rows] + part[...]
        at += part.shape[0]


def final_kernel(row_cuts, *refs):
    own, *parts, signal, out = refs
    rows, width = out.shape
    freq = width // 2
    inverse = 1.0 / signal[...]
    every = sorted({cut for cuts in row_cuts for cut in cuts})
    for start, stop in zip(every, every[1:]):
        total = own[start:stop]
        at = 0
        for cuts in row_cuts:
            for low, high in zip(cuts, cuts[1:]):
                if low <= start and stop <= high:
                    total = total + parts[at][start - low : stop - low]
                at += 1
        denominator = total[:, width:] + inverse
        out[start:stop, :freq] = total[:, :freq] / denominator
        out[start:stop, freq:] = total[:, freq:width] / denominator


def params(mib):
    return pltpu.CompilerParams(vmem_limit_bytes=mib * 1024 * 1024)


def crossed(block, mask):
    size = lax.axis_size("dom")
    return lax.ppermute(block, "dom", [(i, i ^ mask) for i in range(size)])


def on_device(
    particle_fourier,
    defocus,
    particle_offset,
    prior_rotation,
    group_id,
    live_count,
    noise_power,
    signal_power,
    class_refs,
):
    slots, width = particle_fourier.shape
    freq = width // 2
    size = lax.axis_size("dom")
    blocks = size // TEAM
    refs_own = class_refs.reshape(-1, width)
    per = refs_own.shape[0]
    f32 = jnp.float32
    vmem = pl.BlockSpec(memory_space=pltpu.VMEM)
    no_cost = pl.CostEstimate(flops=0, bytes_accessed=0, transcendentals=0)
    much = pl.CostEstimate(flops=16 * 10**9, bytes_accessed=0, transcendentals=0)

    ynb = crossed(particle_fourier, 2)
    anywhere = pl.BlockSpec(memory_space=pl.ANY)
    ynb = crossed(particle_fourier, 2)
    anywhere = pl.BlockSpec(memory_space=pl.ANY)
    def gated(arrays, waits, cost):
        return pl.pallas_call(
            lambda *a: None,
            out_shape=tuple(jax.ShapeDtypeStruct(x.shape, x.dtype) for x in arrays),
            in_specs=[anywhere] * (len(arrays) + len(waits)),
            out_specs=(anywhere,) * len(arrays),
            input_output_aliases={n: n for n in range(len(arrays))},
            compiler_params=params(1),
            cost_estimate=cost,
            name="gate",
        )(*arrays, *waits)

    ynb = crossed(particle_fourier, 2)
    anywhere = pl.BlockSpec(memory_space=pl.ANY)
    ynb = crossed(particle_fourier, 2)
    refs = [refs_own] + [crossed(refs_own, TEAM * n) for n in range(1, blocks)]
    own_facts = (
        particle_fourier,
        defocus.reshape(1, slots),
        particle_offset.T,
        prior_rotation.reshape(1, slots),
        group_id.reshape(1, slots),
        noise_power,
    )
    own, facts, inverse_noise = pl.pallas_call(
        own_kernel,
        out_shape=(
            jax.ShapeDtypeStruct((slots + 8, width + freq), f32),
            jax.ShapeDtypeStruct((8, 128), f32),
            jax.ShapeDtypeStruct(noise_power.shape, f32),
        ),
        in_specs=[anywhere] * 6 + [pl.BlockSpec(memory_space=pltpu.SMEM)],
        out_specs=(vmem,) * 3,
        scratch_shapes=[pltpu.VMEM(x.shape, x.dtype) for x in own_facts]
        + [pltpu.SemaphoreType.DMA((6,))],
        compiler_params=params(6),
        cost_estimate=no_cost,
        name="own",
    )(*(pltpu.with_memory_space_constraint(x, pltpu.HBM) for x in own_facts), live_count)
    cnb = crossed(own, 1)
    lanes = 3 * slots
    bf16 = jnp.bfloat16
    early = 2

    def shaped(rows, cols, dtype=f32):
        return jax.ShapeDtypeStruct((rows, cols), dtype)

    block_shapes = [shaped(SHIFTS * per, width, bf16)] * 2 + [shaped(per, freq, bf16)] * 2
    score_shape = jax.ShapeDtypeStruct((SHIFTS, per, lanes), f32)

    def call(kernel, operands, out_shape, name, mib, cost=None, scratch=()):
        return pl.pallas_call(
            kernel,
            cost_estimate=cost,
            out_shape=tuple(out_shape),
            in_specs=[vmem] * len(operands),
            out_specs=(vmem,) * len(out_shape),
            scratch_shapes=list(scratch),
            compiler_params=params(mib),
            name=name,
        )(*operands)

    prepared = pl.pallas_call(
        early_kernel,
        out_shape=tuple(block_shapes * early),
        in_specs=[anywhere, vmem],
        out_specs=(vmem,) * (4 * early),
        scratch_shapes=[pltpu.VMEM(refs_own.shape, f32), pltpu.SemaphoreType.DMA],
        compiler_params=params(8),
        name="early",
    )(pltpu.with_memory_space_constraint(refs_own, pltpu.HBM), refs[1])
    ynb_prepared = pl.pallas_call(
        neighbour_kernel,
        out_shape=jax.ShapeDtypeStruct((slots + 8, width + freq), f32),
        in_specs=[vmem] * 3 + [anywhere],
        out_specs=vmem,
        compiler_params=params(6),
        cost_estimate=no_cost,
        name="neighbour",
    )(ynb, crossed(facts, 2), inverse_noise, prepared[2])
    cynb = crossed(ynb_prepared, 1)

    late = blocks - early
    outs = call(
        middle_kernel,
        refs[early:],
        block_shapes * late,
        "middle",
        4 + 2 * blocks,
        much,
    )
    prepared = (*prepared, *outs)
    deep = 3 * MAIN + 128
    top_rows = -(-blocks // 8) * 8
    outs = call(
        lambda *a: late_kernel(blocks, *a),
        (own, cnb, ynb_prepared, cynb, *prepared),
        [score_shape] * blocks
        + [shaped(deep, width, bf16), shaped(deep, freq, bf16)]
        + [shaped(8, 384), shaped(top_rows, 384)],
        "late",
        8 + 2 * blocks,
    )
    weights, (y, power, stats, tops) = outs[:blocks], outs[blocks:]

    team = [stats] + [crossed(stats, n) for n in range(1, TEAM)]

    def sums(n, cuts, last=False, waits=()):
        out_shape = [shaped(b - a, width + freq) for a, b in zip(cuts, cuts[1:])]
        if last:
            out_shape.append(shaped(2, slots))
        return pl.pallas_call(
            lambda *a: sum_kernel(n, cuts, last, len(waits), *a),
            out_shape=tuple(out_shape),
            in_specs=[vmem] * (TEAM + 1) + [anywhere] * len(waits) + [vmem] * 3,
            out_specs=(vmem,) * len(out_shape),
            compiler_params=params(8),
            name="sums",
        )(*team, tops, *waits, weights[n], y, power)

    def combined(mine, others, cost=None):
        return pl.pallas_call(
            add_kernel,
            out_shape=jax.ShapeDtypeStruct(mine.shape, f32),
            in_specs=[vmem] * (1 + len(others)),
            out_specs=vmem,
            compiler_params=params(4),
            cost_estimate=cost,
            name="combined",
        )(mine, *others)

    whole, cut = (0, per), (0, per // 2, per)
    far = []
    waits = []
    for n in range(2, blocks, 2):
        handed = sums(n + 1, cut)
        mine = sums(n, cut, waits=handed[:1])
        if n == 2:
            near = sums(1, cut, waits=mine[:1])
        joined = [combined(x, [crossed(y, TEAM)]) for x, y in zip(mine, handed)]
        far.extend(crossed(x, TEAM * n) for x in joined)
        waits.extend(joined)
    own_part, shift = sums(0, whole, last=True, waits=waits)
    own_part = combined(own_part, [crossed(x, TEAM) for x in near], much)
    row_cuts = [cut] * (len(far) // 2)

    refs_new = pl.pallas_call(
        lambda *a: final_kernel(row_cuts, *a),
        out_shape=jax.ShapeDtypeStruct((per, width), f32),
        in_specs=[vmem] * (len(far) + 2),
        out_specs=vmem,
        compiler_params=params(2 + blocks),
        name="update",
    )(own_part, *far, signal_power.reshape(1, freq))

    return (shift.T, refs_new.reshape(class_refs.shape))


def solution(mesh):
    in_specs = (
        P(("groups", "dom"), None),
        P(("groups", "dom")),
        P(("groups", "dom"), None),
        P(("groups", "dom")),
        P(("groups", "dom")),
        P(("groups", "dom")),
        P("groups", None),
        P("groups"),
        P(("groups", "dom"), None, None),
    )
    out_specs = (P(("groups", "dom"), None), P(("groups", "dom"), None, None))
    return jax.shard_map(
        on_device, mesh=mesh, in_specs=in_specs, out_specs=out_specs, check_vma=False
    )
```

```python
import math

import jax
import jax.numpy as jnp
from jax import lax
from jax.experimental import pallas as pl
from jax.experimental.pallas import tpu as pltpu
from jax.sharding import PartitionSpec as P

ROT = 16
SIDE = 3
BOX = 128
FY = 32
SHIFTS = 9
TEAM = 4
PRIOR = 2.0
CTF_SIZE = math.hypot(0.995, 0.1)
CTF_TURN = math.atan2(0.1, 0.995)
SINE = (
    9.99999976e-01,
    -1.66666476e-01,
    8.33289854e-03,
    -1.98008185e-04,
    2.59032780e-06,
)
TWO_PI = 2.0 * math.pi
PI_A = 3.140625
PI_B = 0.0009670257568359375
PI_C = math.pi - PI_A - PI_B
HIGHEST = lax.Precision.HIGHEST
GRID = tuple((t // SIDE - SIDE // 2, t % SIDE - SIDE // 2) for t in range(SHIFTS))


def half_turn_sine(x):
    s = x * x
    p = SINE[4]
    for c in SINE[3::-1]:
        p = p * s + c
    return x * p


def turn_cos(turns):
    t = jnp.abs(turns - jnp.round(turns))
    return half_turn_sine(TWO_PI * (0.25 - t))


def turn_sin(turns):
    return turn_cos(turns - 0.25)


def freq_rows(width, rows):
    f = lax.broadcasted_iota(jnp.int32, (rows, width), 1)
    kx = (f // FY).astype(jnp.float32)
    ky = (f % FY - FY // 2).astype(jnp.float32)
    return kx, ky


def dot_nt(a, b):
    return lax.dot_general(
        a, b, (((1,), (1,)), ((), ())), preferred_element_type=jnp.float32
    )


def dot_nn(a, b):
    return lax.dot_general(
        a, b, (((1,), (0,)), ((), ())), preferred_element_type=jnp.float32
    )


def exact_dot_nn(a, b):
    return lax.dot_general(
        a, b, (((1,), (0,)), ((), ())), precision=HIGHEST, preferred_element_type=jnp.float32
    )


def halves(x):
    high = x.astype(jnp.bfloat16)
    return high, (x - high.astype(jnp.float32)).astype(jnp.bfloat16)


MAIN = 256


def deep_at(part, row):
    return MAIN * part + row if row < MAIN else 3 * MAIN + 32 * part + row - MAIN


def deep_lanes(x):
    rows, lanes = x.shape
    left = lanes - MAIN
    high, low = halves(x[:, :MAIN])
    tail = jnp.concatenate([x[:, MAIN:], jnp.zeros((rows, 128 - left), jnp.float32)], axis=1)
    tail_high = tail.astype(jnp.bfloat16).astype(jnp.float32)
    tail_low = tail - tail_high
    mixed = tail_high + pltpu.roll(tail_high, left, 1) + pltpu.roll(tail_low, 2 * left, 1)
    return jnp.concatenate([high, high, low, mixed.astype(jnp.bfloat16)], axis=1)


def grid_phases(width):
    kx, ky = freq_rows(width, 1)
    out = []
    for t, (gx, gy) in enumerate(GRID):
        if t < SHIFTS // 2:
            m = (kx * gx + ky * gy) * (1.0 / BOX)
            out.append((turn_cos(m), turn_sin(m)))
    return out


def phase_of(phases, t):
    mid = SHIFTS // 2
    if t < mid:
        return phases[t]
    c, s = phases[SHIFTS - 1 - t]
    return c, -s


def prepared_rows(src, facts, inverse_noise, out):
    slots, width = src.shape
    freq = width // 2
    columns = jnp.concatenate([facts, jnp.zeros((120, 128), jnp.float32)], axis=0).T[:slots]
    focus = columns[:, 0:1]
    off_x = columns[:, 1:2]
    off_y = columns[:, 2:3]
    group_col = columns[:, 4:5]

    kx, ky = freq_rows(freq, 1)
    chi = focus * ((kx * kx + ky * ky) * (1.0 / 1024.0))
    k = jnp.round(chi * (1.0 / math.pi))
    rest_angle = ((chi - k * PI_A) - k * PI_B) - k * PI_C
    shifted_angle = rest_angle + CTF_TURN
    over = shifted_angle > (0.5 * math.pi)
    folded = jnp.where(over, math.pi - shifted_angle, shifted_angle)
    parity = 0.5 * k
    sign = (parity - jnp.floor(parity)) * (4.0 * CTF_SIZE) - CTF_SIZE
    ctf = half_turn_sine(folded) * sign
    kx0, ky0 = freq_rows(128, 1)
    m = (kx0 * off_x + ky0 * off_y) * (1.0 / BOX)
    pc, ps = turn_cos(m), turn_sin(m)
    step = off_x * ((128 // FY) / BOX) + jnp.zeros((slots, 128), jnp.float32)
    sc, ss = turn_cos(step), turn_sin(step)

    total = inverse_noise.shape[0]
    onehot = (
        group_col == lax.broadcasted_iota(jnp.int32, (slots, total), 1).astype(jnp.float32)
    ).astype(jnp.float32)
    noise_rows = exact_dot_nn(onehot, inverse_noise)
    scaled = ctf * noise_rows
    out[:slots, width:] = ctf * scaled
    for n in range(freq // 128):
        part = slice(128 * n, 128 * (n + 1))
        twin = slice(freq + 128 * n, freq + 128 * (n + 1))
        co = pc * scaled[:, part]
        si = ps * scaled[:, part]
        pc, ps = pc * sc - ps * ss, ps * sc + pc * ss
        xr, xi = src[:, part], src[:, twin]
        out[:slots, part] = xr * co - xi * si
        out[:slots, twin] = xr * si + xi * co
    out[slots:, :128] = facts
    out[slots:, 128:] = jnp.zeros((8, width + freq - 128), jnp.float32)


def own_kernel(
    src_at, focus_at, offsets_at, prior_at, group_at, noise_at, live_count, out, facts_out,
    inverse_out, src, focus, offsets, prior, group, noise, sems
):
    moves = (
        (focus_at, focus), (offsets_at, offsets), (prior_at, prior), (group_at, group),
        (noise_at, noise), (src_at, src),
    )
    copies = [pltpu.make_async_copy(x, y, sems.at[n]) for n, (x, y) in enumerate(moves)]
    for copy in copies:
        copy.start()
    slots = src.shape[0]
    facts_out[...] = jnp.zeros_like(facts_out)
    slot = lax.broadcasted_iota(jnp.int32, (1, slots), 1)
    for copy in copies:
        copy.wait()
    facts_out[5:6, :slots] = (slot < live_count[0]).astype(jnp.float32)
    facts_out[0:1, :slots] = focus[...]
    facts_out[1:3, :slots] = offsets[...].astype(jnp.float32)
    facts_out[3:4, :slots] = prior[...].astype(jnp.float32)
    facts_out[4:5, :slots] = group[...].astype(jnp.float32)
    inverse = 1.0 / noise[...]
    inverse_out[...] = inverse
    prepared_rows(src, facts_out[...], inverse, out)


def neighbour_kernel(src, facts, inverse_noise, wait, out):
    prepared_rows(src, facts[...], inverse_noise[...], out)


def team_order(own, cnb, ynb, cynb):
    for even in (True, False):
        for first in (True, False):
            heavy, light = ((own, ynb), (cnb, cynb)) if even else ((cnb, cynb), (own, ynb))
            if not first:
                heavy, light = heavy[::-1], light[::-1]
            yield even, first, heavy, light


def place_rows(even, first, parts, y_out, power_out, left_out):
    width = y_out.shape[1]
    slots = parts[0].shape[0] - 8
    half = slots // 2
    cut = MAIN - 2 * slots - half

    def place(src, start, stop, to):
        for cols, out in ((slice(0, width), y_out), (slice(width, None), power_out)):
            pair = halves(src[start:stop, cols])
            for part in range(3):
                row = deep_at(part, to)
                out[row : row + stop - start] = pair[part % 2]

    for is_even, is_first, heavy, light in team_order(*parts):

        @pl.when(jnp.logical_and(even == is_even, first == is_first))
        def _(heavy=heavy, light=light):
            place(heavy[0], 0, slots, 0)
            place(heavy[1], 0, slots, slots)
            place(light[0], 0, half, 2 * slots)
            place(light[1], 0, cut, 2 * slots + half)
            place(light[1], cut, half, MAIN)
            left_out[...] = light[1][cut:half, :width]


def lane_index():
    return lax.broadcasted_iota(jnp.int32, (8, 128), 1)


def row_facts(even, first, parts):
    lane = lane_index()
    own, cnb, ynb, cynb = (x[x.shape[0] - 8 :, :128] for x in parts)
    heavy = (jnp.where(even, own, cnb), jnp.where(even, ynb, cynb))
    light = (jnp.where(even, cnb, own), jnp.where(even, cynb, ynb))
    a0, b0 = (jnp.where(first, x[0], x[1]) for x in (heavy, light))
    a1, b1 = (jnp.where(first, x[1], x[0]) for x in (heavy, light))
    a1 = pltpu.roll(a1, 96, 1)
    b1 = pltpu.roll(b1, 112, 1)
    middle = jnp.where(lane < 64, a1, jnp.where(lane < 112, pltpu.roll(b0, 64, 1), b1))
    return jnp.concatenate([jnp.where(lane < 96, a0, a1), middle, b1], axis=1)


def own_lanes(even, first, x):
    lane = lane_index()
    a, b, c = x[:, :128], x[:, 128:256], x[:, 256:]
    heavy_far = jnp.where(lane < 32, pltpu.roll(a, 32, 1), pltpu.roll(b, 32, 1))
    light_far = jnp.where(lane < 16, pltpu.roll(b, 16, 1), pltpu.roll(c, 16, 1))
    light = jnp.where(first, pltpu.roll(b, 64, 1), light_far)
    heavy = jnp.where(first, a, heavy_far)
    return jnp.where(even, heavy, jnp.where(lane < 48, light, 0.0))


def place_of_device():
    me = lax.axis_index("dom")
    return me % 2 == 0, (me // 2) % 2 == 0


def prior_rows(facts, per, lanes):
    r = (lax.broadcasted_iota(jnp.int32, (per, lanes), 0) % ROT).astype(jnp.float32)
    return PRIOR * turn_cos((r - facts[3:4, :lanes]) * (1.0 / ROT))


def prepare_refs(ref, phases, r_high, r_low, q_high, q_low):
    per, width = ref.shape
    freq = width // 2
    rr, ri = ref[:, :freq], ref[:, freq:]
    mid = SHIFTS // 2

    def store(t, re, im):
        rows = slice(t * per, (t + 1) * per)
        r_high[rows, :freq], r_low[rows, :freq] = halves(re)
        r_high[rows, freq:], r_low[rows, freq:] = halves(im)

    store(mid, rr, ri)
    for t in range(mid):
        c, s = phases[t]
        a, b, d, e = rr * c, ri * s, ri * c, rr * s
        store(t, a + b, d - e)
        store(SHIFTS - 1 - t, a - b, d + e)
    q_high[...], q_low[...] = halves(rr * rr + ri * ri)


def terms(high, low):
    return jnp.concatenate([high, high, low], axis=1)


def terms_left(high, low):
    return jnp.concatenate([high, low, high], axis=1)


def shifted_rows(rows, phases):
    freq = rows.shape[1] // 2
    re, im = rows[:, :freq], rows[:, freq:]
    mid = SHIFTS // 2
    out = [None] * SHIFTS
    out[mid] = rows
    for t in range(mid):
        c, s = phases[t]
        a, b, d, e = re * c, im * s, im * c, re * s
        out[t] = jnp.concatenate([a - b, e + d], axis=1)
        out[SHIFTS - 1 - t] = jnp.concatenate([a + b, d - e], axis=1)
    return jnp.concatenate(out, axis=0)


def weigh(score, e_out):
    top = jnp.max(jnp.max(score, axis=0), axis=0, keepdims=True)
    e = jnp.exp(score - top[None])
    e_out[...] = e
    side = SIDE // 2
    by_x = [sum(e[SIDE * x + y] for y in range(SIDE)) for x in range(SIDE)]
    by_y = [sum(e[SIDE * x + y] for x in range(SIDE)) for y in range(SIDE)]
    sums = [sum(by_x)]
    for by in (by_x, by_y):
        sums.append(sum(by[k] * float(k - side) for k in range(SIDE) if k != side))
    return top, [jnp.sum(x, axis=0, keepdims=True) for x in sums]


def joined_sums(tops, sums):
    top = tops[0]
    for other in tops[1:]:
        top = jnp.maximum(top, other)
    factors = [jnp.exp(other - top) for other in tops]
    return top, [sum(f * x for f, x in zip(factors, column)) for column in zip(*sums)]


def early_kernel(own_at, near, *rest):
    *prepared, own, sem = rest
    copy = pltpu.make_async_copy(own_at, own, sem)
    copy.start()
    phases = grid_phases(own.shape[1] // 2)
    prepare_refs(near, phases, *prepared[4:])
    copy.wait()
    prepare_refs(own, phases, *prepared[:4])


def middle_kernel(*rest):
    count = len(rest) // 5
    refs, prepared = rest[:count], rest[count:]
    phases = grid_phases(refs[0].shape[1] // 2)
    for n in range(count):
        prepare_refs(refs[n], phases, *prepared[4 * n : 4 * n + 4])


def late_kernel(blocks, own, cnb, ynb, cynb, *rest):
    prepared, rest = rest[: 4 * blocks], rest[4 * blocks :]
    e_outs, rest = rest[:blocks], rest[blocks:]
    y_out, power_out, stats_out, tops_out, left_rows = rest
    per, lanes = e_outs[0].shape[1:]
    freq = power_out.shape[1]
    left = lanes - MAIN
    parts = (own, cnb, ynb, cynb)
    even, first = place_of_device()
    place_rows(even, first, parts, y_out, power_out, left_rows)
    facts = row_facts(even, first, parts)
    empty = deep_at(2, lanes)
    for out in (y_out, power_out):
        out[empty:] = jnp.zeros_like(out[empty:])
    stats_out[...] = jnp.zeros_like(stats_out)
    tops_out[...] = jnp.zeros_like(tops_out)

    def rows(out, part, size):
        at = deep_at(part, 0)
        main = out[at : at + MAIN]
        at = deep_at(part, MAIN)
        return jnp.concatenate([main, out[at : at + left]], axis=0)[:size]

    q_terms = [terms_left(prepared[4 * n + 2][...], prepared[4 * n + 3][...]) for n in range(blocks)]
    quad = dot_nt(
        jnp.concatenate(q_terms, axis=0), terms(*(rows(power_out, k, lanes) for k in (0, 1)))
    )
    prior = prior_rows(facts, per, lanes)
    mid = slice(SHIFTS // 2 * per, (SHIFTS // 2 + 1) * per)
    r_terms = [terms_left(prepared[4 * n][mid], prepared[4 * n + 1][mid]) for n in range(blocks)]
    moved = terms(*halves(shifted_rows(left_rows[...], grid_phases(freq))))
    far = dot_nt(jnp.concatenate(r_terms, axis=0), moved)
    far = jnp.concatenate([far, jnp.zeros((blocks * per, 384 - SHIFTS * left), jnp.float32)], axis=1)
    step = 128 // left
    far = [
        pltpu.roll(far[:, 128 * (t // step) : 128 * (t // step + 1)], -left * (t % step) % 128, 1)
        for t in range(SHIFTS)
    ]
    main_terms = terms(*(rows(y_out, k, MAIN) for k in (0, 1)))
    tops, sums = [], []
    for n in range(blocks):
        part = slice(n * per, (n + 1) * per)
        base = prior - 0.5 * quad[part]
        score = dot_nt(terms_left(prepared[4 * n][...], prepared[4 * n + 1][...]), main_terms)
        score = score.reshape(SHIFTS, per, MAIN)
        tail = jnp.stack([x[part, :left] for x in far])
        score = jnp.concatenate([score, tail], axis=2) + base[None]
        top, sums_here = weigh(score, e_outs[n])
        tops_out[n : n + 1, :lanes] = top
        tops.append(top)
        sums.append(sums_here)
    top, sums = joined_sums(tops, sums)
    for k, row in enumerate((top, *sums, facts[5:6, :lanes])):
        stats_out[k : k + 1, :lanes] = row


def sum_kernel(n, cuts, last, waits, *rest):
    team, tops, rest = rest[:TEAM], rest[TEAM], rest[TEAM + 1 + waits :]
    e_ref, y_ref, power_ref, *outs = rest
    per, lanes = e_ref.shape[1:]
    width = y_ref.shape[1]
    freq = width // 2
    team = [x[...] for x in team]
    top, (mass, *move) = joined_sums(
        [x[0:1] for x in team], [[x[k : k + 1] for k in (1, 2, 3)] for x in team]
    )
    live = team[0][4:5] / mass
    gain = (jnp.exp(tops[n : n + 1] - top) * live)[:, :lanes]
    if last:
        shift_out = outs.pop()
        move = [x * live for x in move] + [jnp.zeros((6, live.shape[1]), jnp.float32)]
        move = own_lanes(*place_of_device(), jnp.concatenate(move, axis=0))
        shift_out[...] = move[:2, : shift_out.shape[1]]
    w = e_ref[...] * gain[None]
    flat = dot_nn(deep_lanes(w.reshape(SHIFTS * per, lanes)), y_ref[...])
    weight = dot_nn(deep_lanes(jnp.sum(w, axis=0)), power_ref[...])
    phases = grid_phases(freq)
    mid = SHIFTS // 2

    def block(t):
        return flat[t * per : (t + 1) * per, :freq], flat[t * per : (t + 1) * per, freq:]

    re, im = block(mid)
    for t in range(mid):
        c, s = phases[t]
        ar, ai = block(t)
        br, bi = block(SHIFTS - 1 - t)
        re = re + (ar + br) * c - (ai - bi) * s
        im = im + (ar - br) * s + (ai + bi) * c
    for start, stop, out in zip(cuts, cuts[1:], outs):
        part = slice(start, stop)
        out[:, :freq] = re[part]
        out[:, freq:width] = im[part]
        out[:, width:] = weight[part]


def add_kernel(a, b, wait, out):
    out[...] = a[...] + b[...]


def final_kernel(row_cuts, *refs):
    own, *parts, signal, out = refs
    rows, width = out.shape
    freq = width // 2
    inverse = 1.0 / signal[...]
    every = sorted({cut for cuts in row_cuts for cut in cuts})
    for start, stop in zip(every, every[1:]):
        total = own[start:stop]
        at = 0
        for cuts in row_cuts:
            for low, high in zip(cuts, cuts[1:]):
                if low <= start and stop <= high:
                    total = total + parts[at][start - low : stop - low]
                at += 1
        denominator = total[:, width:] + inverse
        out[start:stop, :freq] = total[:, :freq] / denominator
        out[start:stop, freq:] = total[:, freq:width] / denominator


def params(mib):
    return pltpu.CompilerParams(vmem_limit_bytes=mib * 1024 * 1024)


def crossed(block, mask):
    size = lax.axis_size("dom")
    return lax.ppermute(block, "dom", [(i, i ^ mask) for i in range(size)])


def on_device(
    particle_fourier,
    defocus,
    particle_offset,
    prior_rotation,
    group_id,
    live_count,
    noise_power,
    signal_power,
    class_refs,
):
    slots, width = particle_fourier.shape
    freq = width // 2
    size = lax.axis_size("dom")
    blocks = size // TEAM
    refs_own = class_refs.reshape(-1, width)
    per = refs_own.shape[0]
    f32 = jnp.float32
    vmem = pl.BlockSpec(memory_space=pltpu.VMEM)
    no_cost = pl.CostEstimate(flops=0, bytes_accessed=0, transcendentals=0)
    much = pl.CostEstimate(flops=16 * 10**9, bytes_accessed=0, transcendentals=0)

    ynb = crossed(particle_fourier, 2)
    anywhere = pl.BlockSpec(memory_space=pl.ANY)
    ynb = crossed(particle_fourier, 2)
    anywhere = pl.BlockSpec(memory_space=pl.ANY)
    def gated(arrays, waits, cost):
        return pl.pallas_call(
            lambda *a: None,
            out_shape=tuple(jax.ShapeDtypeStruct(x.shape, x.dtype) for x in arrays),
            in_specs=[anywhere] * (len(arrays) + len(waits)),
            out_specs=(anywhere,) * len(arrays),
            input_output_aliases={n: n for n in range(len(arrays))},
            compiler_params=params(1),
            cost_estimate=cost,
            name="gate",
        )(*arrays, *waits)

    ynb = crossed(particle_fourier, 2)
    anywhere = pl.BlockSpec(memory_space=pl.ANY)
    ynb = crossed(particle_fourier, 2)
    refs = [refs_own] + [crossed(refs_own, TEAM * n) for n in range(1, blocks)]
    own_facts = (
        particle_fourier,
        defocus.reshape(1, slots),
        particle_offset.T,
        prior_rotation.reshape(1, slots),
        group_id.reshape(1, slots),
        noise_power,
    )
    own, facts, inverse_noise = pl.pallas_call(
        own_kernel,
        out_shape=(
            jax.ShapeDtypeStruct((slots + 8, width + freq), f32),
            jax.ShapeDtypeStruct((8, 128), f32),
            jax.ShapeDtypeStruct(noise_power.shape, f32),
        ),
        in_specs=[anywhere] * 6 + [pl.BlockSpec(memory_space=pltpu.SMEM)],
        out_specs=(vmem,) * 3,
        scratch_shapes=[pltpu.VMEM(x.shape, x.dtype) for x in own_facts]
        + [pltpu.SemaphoreType.DMA((6,))],
        compiler_params=params(6),
        cost_estimate=no_cost,
        name="own",
    )(*(pltpu.with_memory_space_constraint(x, pltpu.HBM) for x in own_facts), live_count)
    cnb = crossed(own, 1)
    lanes = 3 * slots
    bf16 = jnp.bfloat16
    early = 2

    def shaped(rows, cols, dtype=f32):
        return jax.ShapeDtypeStruct((rows, cols), dtype)

    block_shapes = [shaped(SHIFTS * per, width, bf16)] * 2 + [shaped(per, freq, bf16)] * 2
    score_shape = jax.ShapeDtypeStruct((SHIFTS, per, lanes), f32)

    def call(kernel, operands, out_shape, name, mib, cost=None, scratch=()):
        return pl.pallas_call(
            kernel,
            cost_estimate=cost,
            out_shape=tuple(out_shape),
            in_specs=[vmem] * len(operands),
            out_specs=(vmem,) * len(out_shape),
            scratch_shapes=list(scratch),
            compiler_params=params(mib),
            name=name,
        )(*operands)

    prepared = pl.pallas_call(
        early_kernel,
        out_shape=tuple(block_shapes * early),
        in_specs=[anywhere, vmem],
        out_specs=(vmem,) * (4 * early),
        scratch_shapes=[pltpu.VMEM(refs_own.shape, f32), pltpu.SemaphoreType.DMA],
        compiler_params=params(8),
        name="early",
    )(pltpu.with_memory_space_constraint(refs_own, pltpu.HBM), refs[1])
    ynb_prepared = pl.pallas_call(
        neighbour_kernel,
        out_shape=jax.ShapeDtypeStruct((slots + 8, width + freq), f32),
        in_specs=[vmem] * 3 + [anywhere],
        out_specs=vmem,
        compiler_params=params(6),
        cost_estimate=no_cost,
        name="neighbour",
    )(ynb, crossed(facts, 2), inverse_noise, prepared[2])
    cynb = crossed(ynb_prepared, 1)

    late = blocks - early
    outs = call(
        middle_kernel,
        refs[early:],
        block_shapes * late,
        "middle",
        4 + 2 * blocks,
        much,
    )
    prepared = (*prepared, *outs)
    deep = 3 * MAIN + 128
    top_rows = -(-blocks // 8) * 8
    outs = call(
        lambda *a: late_kernel(blocks, *a),
        (own, cnb, ynb_prepared, cynb, *prepared),
        [score_shape] * blocks
        + [shaped(deep, width, bf16), shaped(deep, freq, bf16)]
        + [shaped(8, 384), shaped(top_rows, 384)],
        "late",
        8 + 2 * blocks,
        scratch=[pltpu.VMEM((lanes - MAIN, width), f32)],
    )
    weights, (y, power, stats, tops) = outs[:blocks], outs[blocks:]

    team = [stats] + [crossed(stats, n) for n in range(1, TEAM)]

    def sums(n, cuts, last=False, waits=()):
        out_shape = [shaped(b - a, width + freq) for a, b in zip(cuts, cuts[1:])]
        if last:
            out_shape.append(shaped(2, slots))
        return pl.pallas_call(
            lambda *a: sum_kernel(n, cuts, last, len(waits), *a),
            out_shape=tuple(out_shape),
            in_specs=[vmem] * (TEAM + 1) + [anywhere] * len(waits) + [vmem] * 3,
            out_specs=(vmem,) * len(out_shape),
            compiler_params=params(8),
            name="sums",
        )(*team, tops, *waits, weights[n], y, power)

    def combined(mine, other, wait):
        return pl.pallas_call(
            add_kernel,
            out_shape=jax.ShapeDtypeStruct(mine.shape, f32),
            in_specs=[vmem] * 2 + [anywhere],
            out_specs=vmem,
            compiler_params=params(4),
            name="combined",
        )(mine, other, wait)

    def gated(arrays, cost):
        return pl.pallas_call(
            lambda *a: None,
            out_shape=tuple(jax.ShapeDtypeStruct(x.shape, x.dtype) for x in arrays),
            in_specs=[anywhere] * len(arrays),
            out_specs=(anywhere,) * len(arrays),
            input_output_aliases={n: n for n in range(len(arrays))},
            compiler_params=params(1),
            cost_estimate=cost,
            name="gate",
        )(*arrays)

    whole, cut = (0, per), (0, per // 2, per)
    far = []
    waits = []
    for n in range(2, blocks, 2):
        handed = sums(n + 1, cut)
        mine = sums(n, cut, waits=handed[:1])
        if n == 2:
            (near,) = sums(1, whole, waits=mine[:1])
        joined = [combined(x, crossed(y, TEAM), near) for x, y in zip(mine, handed)]
        far.extend(crossed(x, TEAM * n) for x in joined)
        waits.extend(joined)
    own_part, shift = sums(0, whole, last=True, waits=waits)
    far = [crossed(near, TEAM), *gated(far, much)]
    row_cuts = [whole] + [cut] * (len(far) // 2)

    refs_new = pl.pallas_call(
        lambda *a: final_kernel(row_cuts, *a),
        out_shape=jax.ShapeDtypeStruct((per, width), f32),
        in_specs=[vmem] * (len(far) + 2),
        out_specs=vmem,
        compiler_params=params(2 + blocks),
        name="update",
    )(own_part, *far, signal_power.reshape(1, freq))

    return (shift.T, refs_new.reshape(class_refs.shape))


def solution(mesh):
    in_specs = (
        P(("groups", "dom"), None),
        P(("groups", "dom")),
        P(("groups", "dom"), None),
        P(("groups", "dom")),
        P(("groups", "dom")),
        P(("groups", "dom")),
        P("groups", None),
        P("groups"),
        P(("groups", "dom"), None, None),
    )
    out_specs = (P(("groups", "dom"), None), P(("groups", "dom"), None, None))
    return jax.shard_map(
        on_device, mesh=mesh, in_specs=in_specs, out_specs=out_specs, check_vma=False
    )
```

```python
import math

import jax
import jax.numpy as jnp
from jax import lax
from jax.experimental import pallas as pl
from jax.experimental.pallas import tpu as pltpu
from jax.sharding import PartitionSpec as P

ROT = 16
SIDE = 3
BOX = 128
FY = 32
SHIFTS = 9
TEAM = 4
PRIOR = 2.0
CTF_SIZE = math.hypot(0.995, 0.1)
CTF_TURN = math.atan2(0.1, 0.995)
SINE = (
    9.99999976e-01,
    -1.66666476e-01,
    8.33289854e-03,
    -1.98008185e-04,
    2.59032780e-06,
)
TWO_PI = 2.0 * math.pi
PI_A = 3.140625
PI_B = 0.0009670257568359375
PI_C = math.pi - PI_A - PI_B
HIGHEST = lax.Precision.HIGHEST
GRID = tuple((t // SIDE - SIDE // 2, t % SIDE - SIDE // 2) for t in range(SHIFTS))


def half_turn_sine(x):
    s = x * x
    p = SINE[4]
    for c in SINE[3::-1]:
        p = p * s + c
    return x * p


def turn_cos(turns):
    t = jnp.abs(turns - jnp.round(turns))
    return half_turn_sine(TWO_PI * (0.25 - t))


def turn_sin(turns):
    return turn_cos(turns - 0.25)


def freq_rows(width, rows):
    f = lax.broadcasted_iota(jnp.int32, (rows, width), 1)
    kx = (f // FY).astype(jnp.float32)
    ky = (f % FY - FY // 2).astype(jnp.float32)
    return kx, ky


def dot_nt(a, b):
    return lax.dot_general(
        a, b, (((1,), (1,)), ((), ())), preferred_element_type=jnp.float32
    )


def dot_nn(a, b):
    return lax.dot_general(
        a, b, (((1,), (0,)), ((), ())), preferred_element_type=jnp.float32
    )


def exact_dot_nn(a, b):
    return lax.dot_general(
        a, b, (((1,), (0,)), ((), ())), precision=HIGHEST, preferred_element_type=jnp.float32
    )


def halves(x):
    high = x.astype(jnp.bfloat16)
    return high, (x - high.astype(jnp.float32)).astype(jnp.bfloat16)


MAIN = 256


def deep_at(part, row):
    return MAIN * part + row if row < MAIN else 3 * MAIN + 32 * part + row - MAIN


def deep_lanes(x):
    rows, lanes = x.shape
    left = lanes - MAIN
    high, low = halves(x[:, :MAIN])
    tail = jnp.concatenate([x[:, MAIN:], jnp.zeros((rows, 128 - left), jnp.float32)], axis=1)
    tail_high = tail.astype(jnp.bfloat16).astype(jnp.float32)
    tail_low = tail - tail_high
    mixed = tail_high + pltpu.roll(tail_high, left, 1) + pltpu.roll(tail_low, 2 * left, 1)
    return jnp.concatenate([high, high, low, mixed.astype(jnp.bfloat16)], axis=1)


def grid_phases(width):
    kx, ky = freq_rows(width, 1)
    out = []
    for t, (gx, gy) in enumerate(GRID):
        if t < SHIFTS // 2:
            m = (kx * gx + ky * gy) * (1.0 / BOX)
            out.append((turn_cos(m), turn_sin(m)))
    return out


def phase_of(phases, t):
    mid = SHIFTS // 2
    if t < mid:
        return phases[t]
    c, s = phases[SHIFTS - 1 - t]
    return c, -s


def prepared_rows(src, facts, inverse_noise, out):
    slots, width = src.shape
    freq = width // 2
    columns = jnp.concatenate([facts, jnp.zeros((120, 128), jnp.float32)], axis=0).T[:slots]
    focus = columns[:, 0:1]
    off_x = columns[:, 1:2]
    off_y = columns[:, 2:3]
    group_col = columns[:, 4:5]

    kx, ky = freq_rows(freq, 1)
    chi = focus * ((kx * kx + ky * ky) * (1.0 / 1024.0))
    k = jnp.round(chi * (1.0 / math.pi))
    rest_angle = ((chi - k * PI_A) - k * PI_B) - k * PI_C
    shifted_angle = rest_angle + CTF_TURN
    over = shifted_angle > (0.5 * math.pi)
    folded = jnp.where(over, math.pi - shifted_angle, shifted_angle)
    parity = 0.5 * k
    sign = (parity - jnp.floor(parity)) * (4.0 * CTF_SIZE) - CTF_SIZE
    ctf = half_turn_sine(folded) * sign
    kx0, ky0 = freq_rows(128, 1)
    m = (kx0 * off_x + ky0 * off_y) * (1.0 / BOX)
    pc, ps = turn_cos(m), turn_sin(m)
    step = off_x * ((128 // FY) / BOX) + jnp.zeros((slots, 128), jnp.float32)
    sc, ss = turn_cos(step), turn_sin(step)

    total = inverse_noise.shape[0]
    onehot = (
        group_col == lax.broadcasted_iota(jnp.int32, (slots, total), 1).astype(jnp.float32)
    ).astype(jnp.float32)
    noise_rows = exact_dot_nn(onehot, inverse_noise)
    scaled = ctf * noise_rows
    out[:slots, width:] = ctf * scaled
    for n in range(freq // 128):
        part = slice(128 * n, 128 * (n + 1))
        twin = slice(freq + 128 * n, freq + 128 * (n + 1))
        co = pc * scaled[:, part]
        si = ps * scaled[:, part]
        pc, ps = pc * sc - ps * ss, ps * sc + pc * ss
        xr, xi = src[:, part], src[:, twin]
        out[:slots, part] = xr * co - xi * si
        out[:slots, twin] = xr * si + xi * co
    out[slots:, :128] = facts
    out[slots:, 128:] = jnp.zeros((8, width + freq - 128), jnp.float32)


def own_kernel(
    src_at, focus_at, offsets_at, prior_at, group_at, noise_at, live_count, out, facts_out,
    inverse_out, src, focus, offsets, prior, group, noise, sems
):
    moves = (
        (focus_at, focus), (offsets_at, offsets), (prior_at, prior), (group_at, group),
        (noise_at, noise), (src_at, src),
    )
    copies = [pltpu.make_async_copy(x, y, sems.at[n]) for n, (x, y) in enumerate(moves)]
    for copy in copies:
        copy.start()
    slots = src.shape[0]
    facts_out[...] = jnp.zeros_like(facts_out)
    slot = lax.broadcasted_iota(jnp.int32, (1, slots), 1)
    for copy in copies:
        copy.wait()
    facts_out[5:6, :slots] = (slot < live_count[0]).astype(jnp.float32)
    facts_out[0:1, :slots] = focus[...]
    facts_out[1:3, :slots] = offsets[...].astype(jnp.float32)
    facts_out[3:4, :slots] = prior[...].astype(jnp.float32)
    facts_out[4:5, :slots] = group[...].astype(jnp.float32)
    inverse = 1.0 / noise[...]
    inverse_out[...] = inverse
    prepared_rows(src, facts_out[...], inverse, out)


def neighbour_kernel(src, facts, inverse_noise, wait, out):
    prepared_rows(src, facts[...], inverse_noise[...], out)


def team_order(own, cnb, ynb, cynb):
    for even in (True, False):
        for first in (True, False):
            heavy, light = ((own, ynb), (cnb, cynb)) if even else ((cnb, cynb), (own, ynb))
            if not first:
                heavy, light = heavy[::-1], light[::-1]
            yield even, first, heavy, light


def place_rows(even, first, parts, y_out, power_out, left_out):
    width = y_out.shape[1]
    slots = parts[0].shape[0] - 8
    half = slots // 2
    cut = MAIN - 2 * slots - half

    def place(src, start, stop, to):
        for cols, out in ((slice(0, width), y_out), (slice(width, None), power_out)):
            pair = halves(src[start:stop, cols])
            for part in range(3):
                row = deep_at(part, to)
                out[row : row + stop - start] = pair[part % 2]

    for is_even, is_first, heavy, light in team_order(*parts):

        @pl.when(jnp.logical_and(even == is_even, first == is_first))
        def _(heavy=heavy, light=light):
            place(heavy[0], 0, slots, 0)
            place(heavy[1], 0, slots, slots)
            place(light[0], 0, half, 2 * slots)
            place(light[1], 0, cut, 2 * slots + half)
            place(light[1], cut, half, MAIN)
            left_out[...] = light[1][cut:half, :width]


def lane_index():
    return lax.broadcasted_iota(jnp.int32, (8, 128), 1)


def row_facts(even, first, parts):
    lane = lane_index()
    own, cnb, ynb, cynb = (x[x.shape[0] - 8 :, :128] for x in parts)
    heavy = (jnp.where(even, own, cnb), jnp.where(even, ynb, cynb))
    light = (jnp.where(even, cnb, own), jnp.where(even, cynb, ynb))
    a0, b0 = (jnp.where(first, x[0], x[1]) for x in (heavy, light))
    a1, b1 = (jnp.where(first, x[1], x[0]) for x in (heavy, light))
    a1 = pltpu.roll(a1, 96, 1)
    b1 = pltpu.roll(b1, 112, 1)
    middle = jnp.where(lane < 64, a1, jnp.where(lane < 112, pltpu.roll(b0, 64, 1), b1))
    return jnp.concatenate([jnp.where(lane < 96, a0, a1), middle, b1], axis=1)


def own_lanes(even, first, x):
    lane = lane_index()
    a, b, c = x[:, :128], x[:, 128:256], x[:, 256:]
    heavy_far = jnp.where(lane < 32, pltpu.roll(a, 32, 1), pltpu.roll(b, 32, 1))
    light_far = jnp.where(lane < 16, pltpu.roll(b, 16, 1), pltpu.roll(c, 16, 1))
    light = jnp.where(first, pltpu.roll(b, 64, 1), light_far)
    heavy = jnp.where(first, a, heavy_far)
    return jnp.where(even, heavy, jnp.where(lane < 48, light, 0.0))


def place_of_device():
    me = lax.axis_index("dom")
    return me % 2 == 0, (me // 2) % 2 == 0


def prior_rows(facts, per, lanes):
    r = (lax.broadcasted_iota(jnp.int32, (per, lanes), 0) % ROT).astype(jnp.float32)
    return PRIOR * turn_cos((r - facts[3:4, :lanes]) * (1.0 / ROT))


def prepare_refs(ref, phases, r_high, r_low, q_high, q_low):
    per, width = ref.shape
    freq = width // 2
    rr, ri = ref[:, :freq], ref[:, freq:]
    mid = SHIFTS // 2

    def store(t, re, im):
        rows = slice(t * per, (t + 1) * per)
        r_high[rows, :freq], r_low[rows, :freq] = halves(re)
        r_high[rows, freq:], r_low[rows, freq:] = halves(im)

    store(mid, rr, ri)
    for t in range(mid):
        c, s = phases[t]
        a, b, d, e = rr * c, ri * s, ri * c, rr * s
        store(t, a + b, d - e)
        store(SHIFTS - 1 - t, a - b, d + e)
    q_high[...], q_low[...] = halves(rr * rr + ri * ri)


def terms(high, low):
    return jnp.concatenate([high, high, low], axis=1)


def terms_left(high, low):
    return jnp.concatenate([high, low, high], axis=1)


def shifted_rows(rows, phases):
    freq = rows.shape[1] // 2
    re, im = rows[:, :freq], rows[:, freq:]
    mid = SHIFTS // 2
    out = [None] * SHIFTS
    out[mid] = rows
    for t in range(mid):
        c, s = phases[t]
        a, b, d, e = re * c, im * s, im * c, re * s
        out[t] = jnp.concatenate([a - b, e + d], axis=1)
        out[SHIFTS - 1 - t] = jnp.concatenate([a + b, d - e], axis=1)
    return jnp.concatenate(out, axis=0)


def weigh(score, e_out):
    top = jnp.max(jnp.max(score, axis=0), axis=0, keepdims=True)
    e = jnp.exp(score - top[None])
    e_out[...] = e
    side = SIDE // 2
    by_x = [sum(e[SIDE * x + y] for y in range(SIDE)) for x in range(SIDE)]
    by_y = [sum(e[SIDE * x + y] for x in range(SIDE)) for y in range(SIDE)]
    sums = [sum(by_x)]
    for by in (by_x, by_y):
        sums.append(sum(by[k] * float(k - side) for k in range(SIDE) if k != side))
    return top, [jnp.sum(x, axis=0, keepdims=True) for x in sums]


def joined_sums(tops, sums):
    top = tops[0]
    for other in tops[1:]:
        top = jnp.maximum(top, other)
    factors = [jnp.exp(other - top) for other in tops]
    return top, [sum(f * x for f, x in zip(factors, column)) for column in zip(*sums)]


def early_kernel(own_at, near, *rest):
    *prepared, own, sem = rest
    copy = pltpu.make_async_copy(own_at, own, sem)
    copy.start()
    phases = grid_phases(own.shape[1] // 2)
    prepare_refs(near, phases, *prepared[4:])
    copy.wait()
    prepare_refs(own, phases, *prepared[:4])


def middle_kernel(*rest):
    count = len(rest) // 5
    refs, prepared = rest[:count], rest[count:]
    phases = grid_phases(refs[0].shape[1] // 2)
    for n in range(count):
        prepare_refs(refs[n], phases, *prepared[4 * n : 4 * n + 4])


def late_kernel(blocks, own, cnb, ynb, cynb, *rest):
    prepared, rest = rest[: 4 * blocks], rest[4 * blocks :]
    e_outs, rest = rest[:blocks], rest[blocks:]
    y_out, power_out, stats_out, tops_out, left_rows = rest
    per, lanes = e_outs[0].shape[1:]
    freq = power_out.shape[1]
    left = lanes - MAIN
    parts = (own, cnb, ynb, cynb)
    even, first = place_of_device()
    place_rows(even, first, parts, y_out, power_out, left_rows)
    facts = row_facts(even, first, parts)
    empty = deep_at(2, lanes)
    for out in (y_out, power_out):
        out[empty:] = jnp.zeros_like(out[empty:])
    stats_out[...] = jnp.zeros_like(stats_out)
    tops_out[...] = jnp.zeros_like(tops_out)

    def rows(out, part, size):
        at = deep_at(part, 0)
        main = out[at : at + MAIN]
        at = deep_at(part, MAIN)
        return jnp.concatenate([main, out[at : at + left]], axis=0)[:size]

    q_terms = [terms_left(prepared[4 * n + 2][...], prepared[4 * n + 3][...]) for n in range(blocks)]
    quad = dot_nt(
        jnp.concatenate(q_terms, axis=0), terms(*(rows(power_out, k, lanes) for k in (0, 1)))
    )
    prior = prior_rows(facts, per, lanes)
    mid = slice(SHIFTS // 2 * per, (SHIFTS // 2 + 1) * per)
    r_terms = [terms_left(prepared[4 * n][mid], prepared[4 * n + 1][mid]) for n in range(blocks)]
    moved = terms(*halves(shifted_rows(left_rows[...], grid_phases(freq))))
    far = dot_nt(jnp.concatenate(r_terms, axis=0), moved)
    far = jnp.concatenate([far, jnp.zeros((blocks * per, 384 - SHIFTS * left), jnp.float32)], axis=1)
    step = 128 // left
    far = [
        pltpu.roll(far[:, 128 * (t // step) : 128 * (t // step + 1)], -left * (t % step) % 128, 1)
        for t in range(SHIFTS)
    ]
    main_terms = terms(*(rows(y_out, k, MAIN) for k in (0, 1)))
    tops, sums = [], []
    for n in range(blocks):
        part = slice(n * per, (n + 1) * per)
        base = prior - 0.5 * quad[part]
        score = dot_nt(terms_left(prepared[4 * n][...], prepared[4 * n + 1][...]), main_terms)
        score = score.reshape(SHIFTS, per, MAIN)
        tail = jnp.stack([x[part, :left] for x in far])
        score = jnp.concatenate([score, tail], axis=2) + base[None]
        top, sums_here = weigh(score, e_outs[n])
        tops_out[n : n + 1, :lanes] = top
        tops.append(top)
        sums.append(sums_here)
    top, sums = joined_sums(tops, sums)
    for k, row in enumerate((top, *sums, facts[5:6, :lanes])):
        stats_out[k : k + 1, :lanes] = row


def sum_kernel(n, cuts, last, waits, *rest):
    team, tops, rest = rest[:TEAM], rest[TEAM], rest[TEAM + 1 + waits :]
    e_ref, y_ref, power_ref, *outs = rest
    per, lanes = e_ref.shape[1:]
    width = y_ref.shape[1]
    freq = width // 2
    team = [x[...] for x in team]
    top, (mass, *move) = joined_sums(
        [x[0:1] for x in team], [[x[k : k + 1] for k in (1, 2, 3)] for x in team]
    )
    live = team[0][4:5] / mass
    gain = (jnp.exp(tops[n : n + 1] - top) * live)[:, :lanes]
    if last:
        shift_out = outs.pop()
        move = [x * live for x in move] + [jnp.zeros((6, live.shape[1]), jnp.float32)]
        move = own_lanes(*place_of_device(), jnp.concatenate(move, axis=0))
        shift_out[...] = move[:2, : shift_out.shape[1]]
    w = e_ref[...] * gain[None]
    flat = dot_nn(deep_lanes(w.reshape(SHIFTS * per, lanes)), y_ref[...])
    weight = dot_nn(deep_lanes(jnp.sum(w, axis=0)), power_ref[...])
    phases = grid_phases(freq)
    mid = SHIFTS // 2

    def block(t):
        return flat[t * per : (t + 1) * per, :freq], flat[t * per : (t + 1) * per, freq:]

    re, im = block(mid)
    for t in range(mid):
        c, s = phases[t]
        ar, ai = block(t)
        br, bi = block(SHIFTS - 1 - t)
        re = re + (ar + br) * c - (ai - bi) * s
        im = im + (ar - br) * s + (ai + bi) * c
    for start, stop, out in zip(cuts, cuts[1:], outs):
        part = slice(start, stop)
        out[:, :freq] = re[part]
        out[:, freq:width] = im[part]
        out[:, width:] = weight[part]


def add_kernel(a, b, wait, out):
    out[...] = a[...] + b[...]


def final_kernel(row_cuts, *refs):
    own, *parts, signal, out = refs
    rows, width = out.shape
    freq = width // 2
    inverse = 1.0 / signal[...]
    every = sorted({cut for cuts in row_cuts for cut in cuts})
    for start, stop in zip(every, every[1:]):
        total = own[start:stop]
        at = 0
        for cuts in row_cuts:
            for low, high in zip(cuts, cuts[1:]):
                if low <= start and stop <= high:
                    total = total + parts[at][start - low : stop - low]
                at += 1
        denominator = total[:, width:] + inverse
        out[start:stop, :freq] = total[:, :freq] / denominator
        out[start:stop, freq:] = total[:, freq:width] / denominator


def params(mib):
    return pltpu.CompilerParams(vmem_limit_bytes=mib * 1024 * 1024)


def crossed(block, mask):
    size = lax.axis_size("dom")
    return lax.ppermute(block, "dom", [(i, i ^ mask) for i in range(size)])


def on_device(
    particle_fourier,
    defocus,
    particle_offset,
    prior_rotation,
    group_id,
    live_count,
    noise_power,
    signal_power,
    class_refs,
):
    slots, width = particle_fourier.shape
    freq = width // 2
    size = lax.axis_size("dom")
    blocks = size // TEAM
    refs_own = class_refs.reshape(-1, width)
    per = refs_own.shape[0]
    f32 = jnp.float32
    vmem = pl.BlockSpec(memory_space=pltpu.VMEM)
    no_cost = pl.CostEstimate(flops=0, bytes_accessed=0, transcendentals=0)
    much = pl.CostEstimate(flops=16 * 10**9, bytes_accessed=0, transcendentals=0)

    def gated(arrays, cost, waits=()):
        return pl.pallas_call(
            lambda *a: None,
            out_shape=tuple(jax.ShapeDtypeStruct(x.shape, x.dtype) for x in arrays),
            in_specs=[anywhere] * (len(arrays) + len(waits)),
            out_specs=(anywhere,) * len(arrays),
            input_output_aliases={n: n for n in range(len(arrays))},
            compiler_params=params(1),
            cost_estimate=cost,
            name="gate",
        )(*arrays, *waits)

    ynb = crossed(particle_fourier, 2)
    anywhere = pl.BlockSpec(memory_space=pl.ANY)
    ynb = crossed(particle_fourier, 2)
    anywhere = pl.BlockSpec(memory_space=pl.ANY)
    ynb = crossed(particle_fourier, 2)
    anywhere = pl.BlockSpec(memory_space=pl.ANY)
    ynb = crossed(particle_fourier, 2)
    refs = {0: refs_own, 1: crossed(refs_own, TEAM)}
    for n in range(2, blocks, 2):
        refs[n] = crossed(refs_own, TEAM * n)
    own_facts = (
        particle_fourier,
        defocus.reshape(1, slots),
        particle_offset.T,
        prior_rotation.reshape(1, slots),
        group_id.reshape(1, slots),
        noise_power,
    )
    own, facts, inverse_noise = pl.pallas_call(
        own_kernel,
        out_shape=(
            jax.ShapeDtypeStruct((slots + 8, width + freq), f32),
            jax.ShapeDtypeStruct((8, 128), f32),
            jax.ShapeDtypeStruct(noise_power.shape, f32),
        ),
        in_specs=[anywhere] * 6 + [pl.BlockSpec(memory_space=pltpu.SMEM)],
        out_specs=(vmem,) * 3,
        scratch_shapes=[pltpu.VMEM(x.shape, x.dtype) for x in own_facts]
        + [pltpu.SemaphoreType.DMA((6,))],
        compiler_params=params(6),
        cost_estimate=no_cost,
        name="own",
    )(*(pltpu.with_memory_space_constraint(x, pltpu.HBM) for x in own_facts), live_count)
    cnb = crossed(own, 1)
    ynb_facts = crossed(facts, 2)
    lanes = 3 * slots
    bf16 = jnp.bfloat16
    early = 2

    def shaped(rows, cols, dtype=f32):
        return jax.ShapeDtypeStruct((rows, cols), dtype)

    block_shapes = [shaped(SHIFTS * per, width, bf16)] * 2 + [shaped(per, freq, bf16)] * 2
    score_shape = jax.ShapeDtypeStruct((SHIFTS, per, lanes), f32)

    def call(kernel, operands, out_shape, name, mib, cost=None, scratch=()):
        return pl.pallas_call(
            kernel,
            cost_estimate=cost,
            out_shape=tuple(out_shape),
            in_specs=[vmem] * len(operands),
            out_specs=(vmem,) * len(out_shape),
            scratch_shapes=list(scratch),
            compiler_params=params(mib),
            name=name,
        )(*operands)

    prepared = pl.pallas_call(
        early_kernel,
        out_shape=tuple(block_shapes * early),
        in_specs=[anywhere, vmem],
        out_specs=(vmem,) * (4 * early),
        scratch_shapes=[pltpu.VMEM(refs_own.shape, f32), pltpu.SemaphoreType.DMA],
        compiler_params=params(8),
        name="early",
    )(pltpu.with_memory_space_constraint(refs_own, pltpu.HBM), refs[1])
    for n in range(2, blocks, 2):
        (refs[n],) = gated([refs[n]], no_cost, [ynb_facts, prepared[2]])
        refs[n + 1] = crossed(refs[n], TEAM)
    refs = [refs[n] for n in range(blocks)]
    ynb_prepared = pl.pallas_call(
        neighbour_kernel,
        out_shape=jax.ShapeDtypeStruct((slots + 8, width + freq), f32),
        in_specs=[vmem] * 3 + [anywhere],
        out_specs=vmem,
        compiler_params=params(6),
        cost_estimate=no_cost,
        name="neighbour",
    )(ynb, ynb_facts, inverse_noise, prepared[2])
    cynb = crossed(ynb_prepared, 1)

    outs = []
    for n in range(early, blocks):
        outs += call(
            middle_kernel, [refs[n]], block_shapes, "middle", 6, much if n == blocks - 1 else None
        )
    prepared = (*prepared, *outs)
    deep = 3 * MAIN + 128
    top_rows = -(-blocks // 8) * 8
    outs = call(
        lambda *a: late_kernel(blocks, *a),
        (own, cnb, ynb_prepared, cynb, *prepared),
        [score_shape] * blocks
        + [shaped(deep, width, bf16), shaped(deep, freq, bf16)]
        + [shaped(8, 384), shaped(top_rows, 384)],
        "late",
        8 + 2 * blocks,
        scratch=[pltpu.VMEM((lanes - MAIN, width), f32)],
    )
    weights, (y, power, stats, tops) = outs[:blocks], outs[blocks:]

    team = [stats] + [crossed(stats, n) for n in range(1, TEAM)]

    def sums(n, cuts, last=False, waits=()):
        out_shape = [shaped(b - a, width + freq) for a, b in zip(cuts, cuts[1:])]
        if last:
            out_shape.append(shaped(2, slots))
        return pl.pallas_call(
            lambda *a: sum_kernel(n, cuts, last, len(waits), *a),
            out_shape=tuple(out_shape),
            in_specs=[vmem] * (TEAM + 1) + [anywhere] * len(waits) + [vmem] * 3,
            out_specs=(vmem,) * len(out_shape),
            compiler_params=params(8),
            name="sums",
        )(*team, tops, *waits, weights[n], y, power)

    def combined(mine, other, wait):
        return pl.pallas_call(
            add_kernel,
            out_shape=jax.ShapeDtypeStruct(mine.shape, f32),
            in_specs=[vmem] * 2 + [anywhere],
            out_specs=vmem,
            compiler_params=params(4),
            name="combined",
        )(mine, other, wait)

    whole, cut = (0, per), (0, per // 2, per)
    far = []
    waits = []
    for n in range(2, blocks, 2):
        handed = sums(n + 1, cut)
        mine = sums(n, cut, waits=handed[:1])
        if n == 2:
            (near,) = sums(1, whole, waits=mine[:1])
        joined = [combined(x, crossed(y, TEAM), near) for x, y in zip(mine, handed)]
        far.extend(crossed(x, TEAM * n) for x in joined)
        waits.extend(joined)
    own_part, shift = sums(0, whole, last=True, waits=waits)
    far = [crossed(near, TEAM), *gated(far, much)]
    row_cuts = [whole] + [cut] * (len(far) // 2)

    refs_new = pl.pallas_call(
        lambda *a: final_kernel(row_cuts, *a),
        out_shape=jax.ShapeDtypeStruct((per, width), f32),
        in_specs=[vmem] * (len(far) + 2),
        out_specs=vmem,
        compiler_params=params(2 + blocks),
        name="update",
    )(own_part, *far, signal_power.reshape(1, freq))

    return (shift.T, refs_new.reshape(class_refs.shape))


def solution(mesh):
    in_specs = (
        P(("groups", "dom"), None),
        P(("groups", "dom")),
        P(("groups", "dom"), None),
        P(("groups", "dom")),
        P(("groups", "dom")),
        P(("groups", "dom")),
        P("groups", None),
        P("groups"),
        P(("groups", "dom"), None, None),
    )
    out_specs = (P(("groups", "dom"), None), P(("groups", "dom"), None, None))
    return jax.shard_map(
        on_device, mesh=mesh, in_specs=in_specs, out_specs=out_specs, check_vma=False
    )
```

```python
import math

import jax
import jax.numpy as jnp
from jax import lax
from jax.experimental import pallas as pl
from jax.experimental.pallas import tpu as pltpu
from jax.sharding import PartitionSpec as P

ROT = 16
SIDE = 3
BOX = 128
FY = 32
SHIFTS = 9
TEAM = 4
PRIOR = 2.0
CTF_SIZE = math.hypot(0.995, 0.1)
CTF_TURN = math.atan2(0.1, 0.995)
SINE = (
    9.99999976e-01,
    -1.66666476e-01,
    8.33289854e-03,
    -1.98008185e-04,
    2.59032780e-06,
)
TWO_PI = 2.0 * math.pi
PI_A = 3.140625
PI_B = 0.0009670257568359375
PI_C = math.pi - PI_A - PI_B
HIGHEST = lax.Precision.HIGHEST
GRID = tuple((t // SIDE - SIDE // 2, t % SIDE - SIDE // 2) for t in range(SHIFTS))


def half_turn_sine(x):
    s = x * x
    p = SINE[4]
    for c in SINE[3::-1]:
        p = p * s + c
    return x * p


def turn_cos(turns):
    t = jnp.abs(turns - jnp.round(turns))
    return half_turn_sine(TWO_PI * (0.25 - t))


def turn_sin(turns):
    return turn_cos(turns - 0.25)


def freq_rows(width, rows):
    f = lax.broadcasted_iota(jnp.int32, (rows, width), 1)
    kx = (f // FY).astype(jnp.float32)
    ky = (f % FY - FY // 2).astype(jnp.float32)
    return kx, ky


def dot_nt(a, b):
    return lax.dot_general(
        a, b, (((1,), (1,)), ((), ())), preferred_element_type=jnp.float32
    )


def dot_nn(a, b):
    return lax.dot_general(
        a, b, (((1,), (0,)), ((), ())), preferred_element_type=jnp.float32
    )


def exact_dot_nn(a, b):
    return lax.dot_general(
        a, b, (((1,), (0,)), ((), ())), precision=HIGHEST, preferred_element_type=jnp.float32
    )


def halves(x):
    high = x.astype(jnp.bfloat16)
    return high, (x - high.astype(jnp.float32)).astype(jnp.bfloat16)


MAIN = 256


def deep_at(part, row):
    return MAIN * part + row if row < MAIN else 3 * MAIN + 32 * part + row - MAIN


def deep_lanes(x):
    rows, lanes = x.shape
    left = lanes - MAIN
    high, low = halves(x[:, :MAIN])
    tail = jnp.concatenate([x[:, MAIN:], jnp.zeros((rows, 128 - left), jnp.float32)], axis=1)
    tail_high = tail.astype(jnp.bfloat16).astype(jnp.float32)
    tail_low = tail - tail_high
    mixed = tail_high + pltpu.roll(tail_high, left, 1) + pltpu.roll(tail_low, 2 * left, 1)
    return jnp.concatenate([high, high, low, mixed.astype(jnp.bfloat16)], axis=1)


def grid_phases(width):
    kx, ky = freq_rows(width, 1)
    out = []
    for t, (gx, gy) in enumerate(GRID):
        if t < SHIFTS // 2:
            m = (kx * gx + ky * gy) * (1.0 / BOX)
            out.append((turn_cos(m), turn_sin(m)))
    return out


def phase_of(phases, t):
    mid = SHIFTS // 2
    if t < mid:
        return phases[t]
    c, s = phases[SHIFTS - 1 - t]
    return c, -s


def prepared_rows(src, facts, inverse_noise, out):
    slots, width = src.shape
    freq = width // 2
    columns = jnp.concatenate([facts, jnp.zeros((120, 128), jnp.float32)], axis=0).T[:slots]
    focus = columns[:, 0:1]
    off_x = columns[:, 1:2]
    off_y = columns[:, 2:3]
    group_col = columns[:, 4:5]

    kx, ky = freq_rows(freq, 1)
    chi = focus * ((kx * kx + ky * ky) * (1.0 / 1024.0))
    k = jnp.round(chi * (1.0 / math.pi))
    rest_angle = ((chi - k * PI_A) - k * PI_B) - k * PI_C
    shifted_angle = rest_angle + CTF_TURN
    over = shifted_angle > (0.5 * math.pi)
    folded = jnp.where(over, math.pi - shifted_angle, shifted_angle)
    parity = 0.5 * k
    sign = (parity - jnp.floor(parity)) * (4.0 * CTF_SIZE) - CTF_SIZE
    ctf = half_turn_sine(folded) * sign
    kx0, ky0 = freq_rows(128, 1)
    m = (kx0 * off_x + ky0 * off_y) * (1.0 / BOX)
    pc, ps = turn_cos(m), turn_sin(m)
    step = off_x * ((128 // FY) / BOX) + jnp.zeros((slots, 128), jnp.float32)
    sc, ss = turn_cos(step), turn_sin(step)

    total = inverse_noise.shape[0]
    onehot = (
        group_col == lax.broadcasted_iota(jnp.int32, (slots, total), 1).astype(jnp.float32)
    ).astype(jnp.float32)
    noise_rows = exact_dot_nn(onehot, inverse_noise)
    scaled = ctf * noise_rows
    out[:slots, width:] = ctf * scaled
    for n in range(freq // 128):
        part = slice(128 * n, 128 * (n + 1))
        twin = slice(freq + 128 * n, freq + 128 * (n + 1))
        co = pc * scaled[:, part]
        si = ps * scaled[:, part]
        pc, ps = pc * sc - ps * ss, ps * sc + pc * ss
        xr, xi = src[:, part], src[:, twin]
        out[:slots, part] = xr * co - xi * si
        out[:slots, twin] = xr * si + xi * co
    out[slots:, :128] = facts
    out[slots:, 128:] = jnp.zeros((8, width + freq - 128), jnp.float32)


def own_kernel(
    src_at, focus_at, offsets_at, prior_at, group_at, noise_at, live_count, out, facts_out,
    inverse_out, src, focus, offsets, prior, group, noise, sems
):
    moves = (
        (focus_at, focus), (offsets_at, offsets), (prior_at, prior), (group_at, group),
        (noise_at, noise), (src_at, src),
    )
    copies = [pltpu.make_async_copy(x, y, sems.at[n]) for n, (x, y) in enumerate(moves)]
    for copy in copies:
        copy.start()
    slots = src.shape[0]
    facts_out[...] = jnp.zeros_like(facts_out)
    slot = lax.broadcasted_iota(jnp.int32, (1, slots), 1)
    for copy in copies:
        copy.wait()
    facts_out[5:6, :slots] = (slot < live_count[0]).astype(jnp.float32)
    facts_out[0:1, :slots] = focus[...]
    facts_out[1:3, :slots] = offsets[...].astype(jnp.float32)
    facts_out[3:4, :slots] = prior[...].astype(jnp.float32)
    facts_out[4:5, :slots] = group[...].astype(jnp.float32)
    inverse = 1.0 / noise[...]
    inverse_out[...] = inverse
    prepared_rows(src, facts_out[...], inverse, out)


def neighbour_kernel(src, facts, inverse_noise, wait, out):
    prepared_rows(src, facts[...], inverse_noise[...], out)


def team_order(own, cnb, ynb, cynb):
    for even in (True, False):
        for first in (True, False):
            heavy, light = ((own, ynb), (cnb, cynb)) if even else ((cnb, cynb), (own, ynb))
            if not first:
                heavy, light = heavy[::-1], light[::-1]
            yield even, first, heavy, light


def place_rows(even, first, parts, y_out, power_out, left_out):
    width = y_out.shape[1]
    slots = parts[0].shape[0] - 8
    half = slots // 2
    cut = MAIN - 2 * slots - half

    def place(src, start, stop, to):
        for cols, out in ((slice(0, width), y_out), (slice(width, None), power_out)):
            pair = halves(src[start:stop, cols])
            for part in range(3):
                row = deep_at(part, to)
                out[row : row + stop - start] = pair[part % 2]

    for is_even, is_first, heavy, light in team_order(*parts):

        @pl.when(jnp.logical_and(even == is_even, first == is_first))
        def _(heavy=heavy, light=light):
            place(heavy[0], 0, slots, 0)
            place(heavy[1], 0, slots, slots)
            place(light[0], 0, half, 2 * slots)
            place(light[1], 0, cut, 2 * slots + half)
            place(light[1], cut, half, MAIN)
            left_out[...] = light[1][cut:half, :width]


def lane_index():
    return lax.broadcasted_iota(jnp.int32, (8, 128), 1)


def row_facts(even, first, parts):
    lane = lane_index()
    own, cnb, ynb, cynb = (x[x.shape[0] - 8 :, :128] for x in parts)
    heavy = (jnp.where(even, own, cnb), jnp.where(even, ynb, cynb))
    light = (jnp.where(even, cnb, own), jnp.where(even, cynb, ynb))
    a0, b0 = (jnp.where(first, x[0], x[1]) for x in (heavy, light))
    a1, b1 = (jnp.where(first, x[1], x[0]) for x in (heavy, light))
    a1 = pltpu.roll(a1, 96, 1)
    b1 = pltpu.roll(b1, 112, 1)
    middle = jnp.where(lane < 64, a1, jnp.where(lane < 112, pltpu.roll(b0, 64, 1), b1))
    return jnp.concatenate([jnp.where(lane < 96, a0, a1), middle, b1], axis=1)


def own_lanes(even, first, x):
    lane = lane_index()
    a, b, c = x[:, :128], x[:, 128:256], x[:, 256:]
    heavy_far = jnp.where(lane < 32, pltpu.roll(a, 32, 1), pltpu.roll(b, 32, 1))
    light_far = jnp.where(lane < 16, pltpu.roll(b, 16, 1), pltpu.roll(c, 16, 1))
    light = jnp.where(first, pltpu.roll(b, 64, 1), light_far)
    heavy = jnp.where(first, a, heavy_far)
    return jnp.where(even, heavy, jnp.where(lane < 48, light, 0.0))


def place_of_device():
    me = lax.axis_index("dom")
    return me % 2 == 0, (me // 2) % 2 == 0


def prior_rows(facts, per, lanes):
    r = (lax.broadcasted_iota(jnp.int32, (per, lanes), 0) % ROT).astype(jnp.float32)
    return PRIOR * turn_cos((r - facts[3:4, :lanes]) * (1.0 / ROT))


def prepare_refs(ref, phases, r_high, r_low, q_high, q_low):
    per, width = ref.shape
    freq = width // 2
    rr, ri = ref[:, :freq], ref[:, freq:]
    mid = SHIFTS // 2

    def store(t, re, im):
        rows = slice(t * per, (t + 1) * per)
        r_high[rows, :freq], r_low[rows, :freq] = halves(re)
        r_high[rows, freq:], r_low[rows, freq:] = halves(im)

    store(mid, rr, ri)
    for t in range(mid):
        c, s = phases[t]
        a, b, d, e = rr * c, ri * s, ri * c, rr * s
        store(t, a + b, d - e)
        store(SHIFTS - 1 - t, a - b, d + e)
    q_high[...], q_low[...] = halves(rr * rr + ri * ri)


def terms(high, low):
    return jnp.concatenate([high, high, low], axis=1)


def terms_left(high, low):
    return jnp.concatenate([high, low, high], axis=1)


def shifted_rows(rows, phases):
    freq = rows.shape[1] // 2
    re, im = rows[:, :freq], rows[:, freq:]
    mid = SHIFTS // 2
    out = [None] * SHIFTS
    out[mid] = rows
    for t in range(mid):
        c, s = phases[t]
        a, b, d, e = re * c, im * s, im * c, re * s
        out[t] = jnp.concatenate([a - b, e + d], axis=1)
        out[SHIFTS - 1 - t] = jnp.concatenate([a + b, d - e], axis=1)
    return jnp.concatenate(out, axis=0)


def weigh(score, e_out):
    top = jnp.max(jnp.max(score, axis=0), axis=0, keepdims=True)
    e = jnp.exp(score - top[None])
    e_out[...] = e
    side = SIDE // 2
    by_x = [sum(e[SIDE * x + y] for y in range(SIDE)) for x in range(SIDE)]
    by_y = [sum(e[SIDE * x + y] for x in range(SIDE)) for y in range(SIDE)]
    sums = [sum(by_x)]
    for by in (by_x, by_y):
        sums.append(sum(by[k] * float(k - side) for k in range(SIDE) if k != side))
    return top, [jnp.sum(x, axis=0, keepdims=True) for x in sums]


def joined_sums(tops, sums):
    top = tops[0]
    for other in tops[1:]:
        top = jnp.maximum(top, other)
    factors = [jnp.exp(other - top) for other in tops]
    return top, [sum(f * x for f, x in zip(factors, column)) for column in zip(*sums)]


def early_kernel(own_at, near, *rest):
    *prepared, own, sem = rest
    copy = pltpu.make_async_copy(own_at, own, sem)
    copy.start()
    phases = grid_phases(own.shape[1] // 2)
    prepare_refs(near, phases, *prepared[4:])
    copy.wait()
    prepare_refs(own, phases, *prepared[:4])


def middle_kernel(*rest):
    count = len(rest) // 5
    refs, prepared = rest[:count], rest[count:]
    phases = grid_phases(refs[0].shape[1] // 2)
    for n in range(count):
        prepare_refs(refs[n], phases, *prepared[4 * n : 4 * n + 4])


def late_kernel(blocks, own, cnb, ynb, cynb, *rest):
    prepared, rest = rest[: 4 * blocks], rest[4 * blocks :]
    e_outs, rest = rest[:blocks], rest[blocks:]
    y_out, power_out, stats_out, tops_out, left_rows = rest
    per, lanes = e_outs[0].shape[1:]
    freq = power_out.shape[1]
    left = lanes - MAIN
    parts = (own, cnb, ynb, cynb)
    even, first = place_of_device()
    place_rows(even, first, parts, y_out, power_out, left_rows)
    facts = row_facts(even, first, parts)
    empty = deep_at(2, lanes)
    for out in (y_out, power_out):
        out[empty:] = jnp.zeros_like(out[empty:])
    stats_out[...] = jnp.zeros_like(stats_out)
    tops_out[...] = jnp.zeros_like(tops_out)

    def rows(out, part, size):
        at = deep_at(part, 0)
        main = out[at : at + MAIN]
        at = deep_at(part, MAIN)
        return jnp.concatenate([main, out[at : at + left]], axis=0)[:size]

    q_terms = [terms_left(prepared[4 * n + 2][...], prepared[4 * n + 3][...]) for n in range(blocks)]
    quad = dot_nt(
        jnp.concatenate(q_terms, axis=0), terms(*(rows(power_out, k, lanes) for k in (0, 1)))
    )
    prior = prior_rows(facts, per, lanes)
    mid = slice(SHIFTS // 2 * per, (SHIFTS // 2 + 1) * per)
    r_terms = [terms_left(prepared[4 * n][mid], prepared[4 * n + 1][mid]) for n in range(blocks)]
    moved = terms(*halves(shifted_rows(left_rows[...], grid_phases(freq))))
    far = dot_nt(jnp.concatenate(r_terms, axis=0), moved)
    far = jnp.concatenate([far, jnp.zeros((blocks * per, 384 - SHIFTS * left), jnp.float32)], axis=1)
    step = 128 // left
    far = [
        pltpu.roll(far[:, 128 * (t // step) : 128 * (t // step + 1)], -left * (t % step) % 128, 1)
        for t in range(SHIFTS)
    ]
    main_terms = terms(*(rows(y_out, k, MAIN) for k in (0, 1)))
    tops, sums = [], []
    for n in range(blocks):
        part = slice(n * per, (n + 1) * per)
        base = prior - 0.5 * quad[part]
        score = dot_nt(terms_left(prepared[4 * n][...], prepared[4 * n + 1][...]), main_terms)
        score = score.reshape(SHIFTS, per, MAIN)
        tail = jnp.stack([x[part, :left] for x in far])
        score = jnp.concatenate([score, tail], axis=2) + base[None]
        top, sums_here = weigh(score, e_outs[n])
        tops_out[n : n + 1, :lanes] = top
        tops.append(top)
        sums.append(sums_here)
    top, sums = joined_sums(tops, sums)
    for k, row in enumerate((top, *sums, facts[5:6, :lanes])):
        stats_out[k : k + 1, :lanes] = row


def sum_kernel(n, cuts, last, waits, *rest):
    team, tops, rest = rest[:TEAM], rest[TEAM], rest[TEAM + 1 + waits :]
    e_ref, y_ref, power_ref, *outs = rest
    per, lanes = e_ref.shape[1:]
    width = y_ref.shape[1]
    freq = width // 2
    team = [x[...] for x in team]
    top, (mass, *move) = joined_sums(
        [x[0:1] for x in team], [[x[k : k + 1] for k in (1, 2, 3)] for x in team]
    )
    live = team[0][4:5] / mass
    gain = (jnp.exp(tops[n : n + 1] - top) * live)[:, :lanes]
    if last:
        shift_out = outs.pop()
        move = [x * live for x in move] + [jnp.zeros((6, live.shape[1]), jnp.float32)]
        move = own_lanes(*place_of_device(), jnp.concatenate(move, axis=0))
        shift_out[...] = move[:2, : shift_out.shape[1]]
    w = e_ref[...] * gain[None]
    flat = dot_nn(deep_lanes(w.reshape(SHIFTS * per, lanes)), y_ref[...])
    weight = dot_nn(deep_lanes(jnp.sum(w, axis=0)), power_ref[...])
    phases = grid_phases(freq)
    mid = SHIFTS // 2

    def block(t):
        return flat[t * per : (t + 1) * per, :freq], flat[t * per : (t + 1) * per, freq:]

    re, im = block(mid)
    for t in range(mid):
        c, s = phases[t]
        ar, ai = block(t)
        br, bi = block(SHIFTS - 1 - t)
        re = re + (ar + br) * c - (ai - bi) * s
        im = im + (ar - br) * s + (ai + bi) * c
    for start, stop, out in zip(cuts, cuts[1:], outs):
        part = slice(start, stop)
        out[:, :freq] = re[part]
        out[:, freq:width] = im[part]
        out[:, width:] = weight[part]


def add_kernel(a, b, wait, out):
    out[...] = a[...] + b[...]


def final_kernel(row_cuts, *refs):
    own, *parts, signal, out = refs
    rows, width = out.shape
    freq = width // 2
    inverse = 1.0 / signal[...]
    every = sorted({cut for cuts in row_cuts for cut in cuts})
    for start, stop in zip(every, every[1:]):
        total = own[start:stop]
        at = 0
        for cuts in row_cuts:
            for low, high in zip(cuts, cuts[1:]):
                if low <= start and stop <= high:
                    total = total + parts[at][start - low : stop - low]
                at += 1
        denominator = total[:, width:] + inverse
        out[start:stop, :freq] = total[:, :freq] / denominator
        out[start:stop, freq:] = total[:, freq:width] / denominator


def params(mib):
    return pltpu.CompilerParams(vmem_limit_bytes=mib * 1024 * 1024)


def crossed(block, mask):
    size = lax.axis_size("dom")
    return lax.ppermute(block, "dom", [(i, i ^ mask) for i in range(size)])


def on_device(
    particle_fourier,
    defocus,
    particle_offset,
    prior_rotation,
    group_id,
    live_count,
    noise_power,
    signal_power,
    class_refs,
):
    slots, width = particle_fourier.shape
    freq = width // 2
    size = lax.axis_size("dom")
    blocks = size // TEAM
    refs_own = class_refs.reshape(-1, width)
    per = refs_own.shape[0]
    f32 = jnp.float32
    vmem = pl.BlockSpec(memory_space=pltpu.VMEM)
    no_cost = pl.CostEstimate(flops=0, bytes_accessed=0, transcendentals=0)
    much = pl.CostEstimate(flops=16 * 10**9, bytes_accessed=0, transcendentals=0)

    def gated(arrays, cost, waits=()):
        return pl.pallas_call(
            lambda *a: None,
            out_shape=tuple(jax.ShapeDtypeStruct(x.shape, x.dtype) for x in arrays),
            in_specs=[anywhere] * (len(arrays) + len(waits)),
            out_specs=(anywhere,) * len(arrays),
            input_output_aliases={n: n for n in range(len(arrays))},
            compiler_params=params(1),
            cost_estimate=cost,
            name="gate",
        )(*arrays, *waits)

    ynb = crossed(particle_fourier, 2)
    anywhere = pl.BlockSpec(memory_space=pl.ANY)
    ynb = crossed(particle_fourier, 2)
    anywhere = pl.BlockSpec(memory_space=pl.ANY)
    ynb = crossed(particle_fourier, 2)
    anywhere = pl.BlockSpec(memory_space=pl.ANY)
    ynb = crossed(particle_fourier, 2)
    refs = {0: refs_own, 1: crossed(refs_own, TEAM)}
    for n in range(2, blocks, 2):
        refs[n] = crossed(refs_own, TEAM * n)
    own_facts = (
        particle_fourier,
        defocus.reshape(1, slots),
        particle_offset.T,
        prior_rotation.reshape(1, slots),
        group_id.reshape(1, slots),
        noise_power,
    )
    own, facts, inverse_noise = pl.pallas_call(
        own_kernel,
        out_shape=(
            jax.ShapeDtypeStruct((slots + 8, width + freq), f32),
            jax.ShapeDtypeStruct((8, 128), f32),
            jax.ShapeDtypeStruct(noise_power.shape, f32),
        ),
        in_specs=[anywhere] * 6 + [pl.BlockSpec(memory_space=pltpu.SMEM)],
        out_specs=(vmem,) * 3,
        scratch_shapes=[pltpu.VMEM(x.shape, x.dtype) for x in own_facts]
        + [pltpu.SemaphoreType.DMA((6,))],
        compiler_params=params(6),
        cost_estimate=no_cost,
        name="own",
    )(*(pltpu.with_memory_space_constraint(x, pltpu.HBM) for x in own_facts), live_count)
    cnb = crossed(own, 1)
    ynb_facts = crossed(facts, 2)
    lanes = 3 * slots
    bf16 = jnp.bfloat16
    early = 2

    def shaped(rows, cols, dtype=f32):
        return jax.ShapeDtypeStruct((rows, cols), dtype)

    block_shapes = [shaped(SHIFTS * per, width, bf16)] * 2 + [shaped(per, freq, bf16)] * 2
    score_shape = jax.ShapeDtypeStruct((SHIFTS, per, lanes), f32)

    def call(kernel, operands, out_shape, name, mib, cost=None, scratch=()):
        return pl.pallas_call(
            kernel,
            cost_estimate=cost,
            out_shape=tuple(out_shape),
            in_specs=[vmem] * len(operands),
            out_specs=(vmem,) * len(out_shape),
            scratch_shapes=list(scratch),
            compiler_params=params(mib),
            name=name,
        )(*operands)

    prepared = pl.pallas_call(
        early_kernel,
        out_shape=tuple(block_shapes * early),
        in_specs=[anywhere, vmem],
        out_specs=(vmem,) * (4 * early),
        scratch_shapes=[pltpu.VMEM(refs_own.shape, f32), pltpu.SemaphoreType.DMA],
        compiler_params=params(8),
        name="early",
    )(pltpu.with_memory_space_constraint(refs_own, pltpu.HBM), refs[1])
    for n in range(2, blocks, 2):
        (refs[n],) = gated([refs[n]], no_cost, [ynb_facts, prepared[2]])
        refs[n + 1] = crossed(refs[n], TEAM)
    refs = [refs[n] for n in range(blocks)]
    ynb_prepared = pl.pallas_call(
        neighbour_kernel,
        out_shape=jax.ShapeDtypeStruct((slots + 8, width + freq), f32),
        in_specs=[vmem] * 3 + [anywhere],
        out_specs=vmem,
        compiler_params=params(6),
        cost_estimate=no_cost,
        name="neighbour",
    )(ynb, ynb_facts, inverse_noise, prepared[2])
    cynb = crossed(ynb_prepared, 1)

    outs = []
    for n in range(early, blocks):
        outs += call(
            middle_kernel, [refs[n]], block_shapes, "middle", 6, much if n == blocks - 1 else None
        )
    prepared = (*prepared, *outs)
    deep = 3 * MAIN + 128
    top_rows = -(-blocks // 8) * 8
    outs = call(
        lambda *a: late_kernel(blocks, *a),
        (own, cnb, ynb_prepared, cynb, *prepared),
        [score_shape] * blocks
        + [shaped(deep, width, bf16), shaped(deep, freq, bf16)]
        + [shaped(8, 384), shaped(top_rows, 384)],
        "late",
        8 + 2 * blocks,
        scratch=[pltpu.VMEM((lanes - MAIN, width), f32)],
    )
    weights, (y, power, stats, tops) = outs[:blocks], outs[blocks:]

    team = [stats] + [crossed(stats, n) for n in range(1, TEAM)]

    def sums(n, cuts, last=False, waits=()):
        out_shape = [shaped(b - a, width + freq) for a, b in zip(cuts, cuts[1:])]
        if last:
            out_shape.append(shaped(2, slots))
        return pl.pallas_call(
            lambda *a: sum_kernel(n, cuts, last, len(waits), *a),
            out_shape=tuple(out_shape),
            in_specs=[vmem] * (TEAM + 1) + [anywhere] * len(waits) + [vmem] * 3,
            out_specs=(vmem,) * len(out_shape),
            compiler_params=params(8),
            name="sums",
        )(*team, tops, *waits, weights[n], y, power)

    def combined(mine, other, wait):
        return pl.pallas_call(
            add_kernel,
            out_shape=jax.ShapeDtypeStruct(mine.shape, f32),
            in_specs=[vmem] * 2 + [anywhere],
            out_specs=vmem,
            compiler_params=params(4),
            name="combined",
        )(mine, other, wait)

    whole, cut = (0, per), (0, per // 2, per)
    far = []
    waits = []
    for n in range(2, blocks, 2):
        handed = sums(n + 1, cut)
        mine = sums(n, cut, waits=handed[:1])
        if n == 2:
            near = sums(1, cut, waits=mine[:1])
        joined = [combined(x, crossed(y, TEAM), near[0]) for x, y in zip(mine, handed)]
        far.extend(crossed(x, TEAM * n) for x in joined)
        waits.extend(joined)
    own_part, shift = sums(0, whole, last=True, waits=waits)
    near = gated([crossed(x, TEAM) for x in near], much, [shift])
    far = [*near, *far]
    row_cuts = [cut] * (len(far) // 2)

    refs_new = pl.pallas_call(
        lambda *a: final_kernel(row_cuts, *a),
        out_shape=jax.ShapeDtypeStruct((per, width), f32),
        in_specs=[vmem] * (len(far) + 2),
        out_specs=vmem,
        compiler_params=params(2 + blocks),
        name="update",
    )(own_part, *far, signal_power.reshape(1, freq))

    return (shift.T, refs_new.reshape(class_refs.shape))


def solution(mesh):
    in_specs = (
        P(("groups", "dom"), None),
        P(("groups", "dom")),
        P(("groups", "dom"), None),
        P(("groups", "dom")),
        P(("groups", "dom")),
        P(("groups", "dom")),
        P("groups", None),
        P("groups"),
        P(("groups", "dom"), None, None),
    )
    out_specs = (P(("groups", "dom"), None), P(("groups", "dom"), None, None))
    return jax.shard_map(
        on_device, mesh=mesh, in_specs=in_specs, out_specs=out_specs, check_vma=False
    )
```

```python
import math

import jax
import jax.numpy as jnp
from jax import lax
from jax.experimental import pallas as pl
from jax.experimental.pallas import tpu as pltpu
from jax.sharding import PartitionSpec as P

ROT = 16
SIDE = 3
BOX = 128
FY = 32
SHIFTS = 9
TEAM = 4
PRIOR = 2.0
CTF_SIZE = math.hypot(0.995, 0.1)
CTF_TURN = math.atan2(0.1, 0.995)
SINE = (
    9.99999976e-01,
    -1.66666476e-01,
    8.33289854e-03,
    -1.98008185e-04,
    2.59032780e-06,
)
TWO_PI = 2.0 * math.pi
PI_A = 3.140625
PI_B = 0.0009670257568359375
PI_C = math.pi - PI_A - PI_B
HIGHEST = lax.Precision.HIGHEST
GRID = tuple((t // SIDE - SIDE // 2, t % SIDE - SIDE // 2) for t in range(SHIFTS))


def half_turn_sine(x):
    s = x * x
    p = SINE[4]
    for c in SINE[3::-1]:
        p = p * s + c
    return x * p


def turn_cos(turns):
    t = jnp.abs(turns - jnp.round(turns))
    return half_turn_sine(TWO_PI * (0.25 - t))


def turn_sin(turns):
    return turn_cos(turns - 0.25)


def freq_rows(width, rows):
    f = lax.broadcasted_iota(jnp.int32, (rows, width), 1)
    kx = (f // FY).astype(jnp.float32)
    ky = (f % FY - FY // 2).astype(jnp.float32)
    return kx, ky


def dot_nt(a, b):
    return lax.dot_general(
        a, b, (((1,), (1,)), ((), ())), preferred_element_type=jnp.float32
    )


def dot_nn(a, b):
    return lax.dot_general(
        a, b, (((1,), (0,)), ((), ())), preferred_element_type=jnp.float32
    )


def exact_dot_nn(a, b):
    return lax.dot_general(
        a, b, (((1,), (0,)), ((), ())), precision=HIGHEST, preferred_element_type=jnp.float32
    )


def halves(x):
    high = x.astype(jnp.bfloat16)
    return high, (x - high.astype(jnp.float32)).astype(jnp.bfloat16)


MAIN = 256


def deep_at(part, row):
    return MAIN * part + row if row < MAIN else 3 * MAIN + 32 * part + row - MAIN


def deep_lanes(x):
    rows, lanes = x.shape
    left = lanes - MAIN
    high, low = halves(x[:, :MAIN])
    tail = jnp.concatenate([x[:, MAIN:], jnp.zeros((rows, 128 - left), jnp.float32)], axis=1)
    tail_high = tail.astype(jnp.bfloat16).astype(jnp.float32)
    tail_low = tail - tail_high
    mixed = tail_high + pltpu.roll(tail_high, left, 1) + pltpu.roll(tail_low, 2 * left, 1)
    return jnp.concatenate([high, high, low, mixed.astype(jnp.bfloat16)], axis=1)


def grid_phases(width):
    kx, ky = freq_rows(width, 1)
    out = []
    for t, (gx, gy) in enumerate(GRID):
        if t < SHIFTS // 2:
            m = (kx * gx + ky * gy) * (1.0 / BOX)
            out.append((turn_cos(m), turn_sin(m)))
    return out


def phase_of(phases, t):
    mid = SHIFTS // 2
    if t < mid:
        return phases[t]
    c, s = phases[SHIFTS - 1 - t]
    return c, -s


def prepared_rows(src, facts, inverse_noise, out):
    slots, width = src.shape
    freq = width // 2
    columns = jnp.concatenate([facts, jnp.zeros((120, 128), jnp.float32)], axis=0).T[:slots]
    focus = columns[:, 0:1]
    off_x = columns[:, 1:2]
    off_y = columns[:, 2:3]
    group_col = columns[:, 4:5]

    kx, ky = freq_rows(freq, 1)
    chi = focus * ((kx * kx + ky * ky) * (1.0 / 1024.0))
    k = jnp.round(chi * (1.0 / math.pi))
    rest_angle = ((chi - k * PI_A) - k * PI_B) - k * PI_C
    shifted_angle = rest_angle + CTF_TURN
    over = shifted_angle > (0.5 * math.pi)
    folded = jnp.where(over, math.pi - shifted_angle, shifted_angle)
    parity = 0.5 * k
    sign = (parity - jnp.floor(parity)) * (4.0 * CTF_SIZE) - CTF_SIZE
    ctf = half_turn_sine(folded) * sign
    kx0, ky0 = freq_rows(128, 1)
    m = (kx0 * off_x + ky0 * off_y) * (1.0 / BOX)
    pc, ps = turn_cos(m), turn_sin(m)
    step = off_x * ((128 // FY) / BOX) + jnp.zeros((slots, 128), jnp.float32)
    sc, ss = turn_cos(step), turn_sin(step)

    total = inverse_noise.shape[0]
    onehot = (
        group_col == lax.broadcasted_iota(jnp.int32, (slots, total), 1).astype(jnp.float32)
    ).astype(jnp.float32)
    noise_rows = exact_dot_nn(onehot, inverse_noise)
    scaled = ctf * noise_rows
    out[:slots, width:] = ctf * scaled
    for n in range(freq // 128):
        part = slice(128 * n, 128 * (n + 1))
        twin = slice(freq + 128 * n, freq + 128 * (n + 1))
        co = pc * scaled[:, part]
        si = ps * scaled[:, part]
        pc, ps = pc * sc - ps * ss, ps * sc + pc * ss
        xr, xi = src[:, part], src[:, twin]
        out[:slots, part] = xr * co - xi * si
        out[:slots, twin] = xr * si + xi * co
    out[slots:, :128] = facts
    out[slots:, 128:] = jnp.zeros((8, width + freq - 128), jnp.float32)


def own_kernel(
    src_at, focus_at, offsets_at, prior_at, group_at, noise_at, live_count, out, facts_out,
    inverse_out, src, focus, offsets, prior, group, noise, sems
):
    moves = (
        (focus_at, focus), (offsets_at, offsets), (prior_at, prior), (group_at, group),
        (noise_at, noise), (src_at, src),
    )
    copies = [pltpu.make_async_copy(x, y, sems.at[n]) for n, (x, y) in enumerate(moves)]
    for copy in copies:
        copy.start()
    slots = src.shape[0]
    facts_out[...] = jnp.zeros_like(facts_out)
    slot = lax.broadcasted_iota(jnp.int32, (1, slots), 1)
    for copy in copies:
        copy.wait()
    facts_out[5:6, :slots] = (slot < live_count[0]).astype(jnp.float32)
    facts_out[0:1, :slots] = focus[...]
    facts_out[1:3, :slots] = offsets[...].astype(jnp.float32)
    facts_out[3:4, :slots] = prior[...].astype(jnp.float32)
    facts_out[4:5, :slots] = group[...].astype(jnp.float32)
    inverse = 1.0 / noise[...]
    inverse_out[...] = inverse
    prepared_rows(src, facts_out[...], inverse, out)


def neighbour_kernel(src_even, src_odd, facts, inverse_noise, wait, out, src):
    half = src_odd.shape[0]
    even, _ = place_of_device()

    @pl.when(even)
    def _():
        src[...] = src_even[...]

    @pl.when(jnp.logical_not(even))
    def _():
        src[:half] = src_odd[...]
        src[half:] = jnp.zeros_like(src[half:])

    prepared_rows(src, facts[...], inverse_noise[...], out)


def team_order(own, cnb, ynb, cynb):
    for even in (True, False):
        for first in (True, False):
            heavy, light = ((own, ynb), (cnb, cynb)) if even else ((cnb, cynb), (own, ynb))
            if not first:
                heavy, light = heavy[::-1], light[::-1]
            yield even, first, heavy, light


def place_rows(even, first, parts, y_out, power_out, left_out):
    width = y_out.shape[1]
    slots = parts[0].shape[0] - 8
    half = slots // 2
    cut = MAIN - 2 * slots - half

    def place(src, start, stop, to):
        for cols, out in ((slice(0, width), y_out), (slice(width, None), power_out)):
            pair = halves(src[start:stop, cols])
            for part in range(3):
                row = deep_at(part, to)
                out[row : row + stop - start] = pair[part % 2]

    for is_even, is_first, heavy, light in team_order(*parts):

        @pl.when(jnp.logical_and(even == is_even, first == is_first))
        def _(heavy=heavy, light=light):
            place(heavy[0], 0, slots, 0)
            place(heavy[1], 0, slots, slots)
            place(light[0], 0, half, 2 * slots)
            place(light[1], 0, cut, 2 * slots + half)
            place(light[1], cut, half, MAIN)
            left_out[...] = light[1][cut:half, :width]


def lane_index():
    return lax.broadcasted_iota(jnp.int32, (8, 128), 1)


def row_facts(even, first, parts):
    lane = lane_index()
    own, cnb, ynb, cynb = (x[x.shape[0] - 8 :, :128] for x in parts)
    heavy = (jnp.where(even, own, cnb), jnp.where(even, ynb, cynb))
    light = (jnp.where(even, cnb, own), jnp.where(even, cynb, ynb))
    a0, b0 = (jnp.where(first, x[0], x[1]) for x in (heavy, light))
    a1, b1 = (jnp.where(first, x[1], x[0]) for x in (heavy, light))
    a1 = pltpu.roll(a1, 96, 1)
    b1 = pltpu.roll(b1, 112, 1)
    middle = jnp.where(lane < 64, a1, jnp.where(lane < 112, pltpu.roll(b0, 64, 1), b1))
    return jnp.concatenate([jnp.where(lane < 96, a0, a1), middle, b1], axis=1)


def own_lanes(even, first, x):
    lane = lane_index()
    a, b, c = x[:, :128], x[:, 128:256], x[:, 256:]
    heavy_far = jnp.where(lane < 32, pltpu.roll(a, 32, 1), pltpu.roll(b, 32, 1))
    light_far = jnp.where(lane < 16, pltpu.roll(b, 16, 1), pltpu.roll(c, 16, 1))
    light = jnp.where(first, pltpu.roll(b, 64, 1), light_far)
    heavy = jnp.where(first, a, heavy_far)
    return jnp.where(even, heavy, jnp.where(lane < 48, light, 0.0))


def place_of_device():
    me = lax.axis_index("dom")
    return me % 2 == 0, (me // 2) % 2 == 0


def prior_rows(facts, per, lanes):
    r = (lax.broadcasted_iota(jnp.int32, (per, lanes), 0) % ROT).astype(jnp.float32)
    return PRIOR * turn_cos((r - facts[3:4, :lanes]) * (1.0 / ROT))


def prepare_refs(ref, phases, r_high, r_low, q_high, q_low):
    per, width = ref.shape
    freq = width // 2
    rr, ri = ref[:, :freq], ref[:, freq:]
    mid = SHIFTS // 2

    def store(t, re, im):
        rows = slice(t * per, (t + 1) * per)
        r_high[rows, :freq], r_low[rows, :freq] = halves(re)
        r_high[rows, freq:], r_low[rows, freq:] = halves(im)

    store(mid, rr, ri)
    for t in range(mid):
        c, s = phases[t]
        a, b, d, e = rr * c, ri * s, ri * c, rr * s
        store(t, a + b, d - e)
        store(SHIFTS - 1 - t, a - b, d + e)
    q_high[...], q_low[...] = halves(rr * rr + ri * ri)


def terms(high, low):
    return jnp.concatenate([high, high, low], axis=1)


def terms_left(high, low):
    return jnp.concatenate([high, low, high], axis=1)


def shifted_rows(rows, phases):
    freq = rows.shape[1] // 2
    re, im = rows[:, :freq], rows[:, freq:]
    mid = SHIFTS // 2
    out = [None] * SHIFTS
    out[mid] = rows
    for t in range(mid):
        c, s = phases[t]
        a, b, d, e = re * c, im * s, im * c, re * s
        out[t] = jnp.concatenate([a - b, e + d], axis=1)
        out[SHIFTS - 1 - t] = jnp.concatenate([a + b, d - e], axis=1)
    return jnp.concatenate(out, axis=0)


def weigh(score, e_out):
    top = jnp.max(jnp.max(score, axis=0), axis=0, keepdims=True)
    e = jnp.exp(score - top[None])
    e_out[...] = e
    side = SIDE // 2
    by_x = [sum(e[SIDE * x + y] for y in range(SIDE)) for x in range(SIDE)]
    by_y = [sum(e[SIDE * x + y] for x in range(SIDE)) for y in range(SIDE)]
    sums = [sum(by_x)]
    for by in (by_x, by_y):
        sums.append(sum(by[k] * float(k - side) for k in range(SIDE) if k != side))
    return top, [jnp.sum(x, axis=0, keepdims=True) for x in sums]


def joined_sums(tops, sums):
    top = tops[0]
    for other in tops[1:]:
        top = jnp.maximum(top, other)
    factors = [jnp.exp(other - top) for other in tops]
    return top, [sum(f * x for f, x in zip(factors, column)) for column in zip(*sums)]


def early_kernel(own_at, near, *rest):
    *prepared, own, sem = rest
    copy = pltpu.make_async_copy(own_at, own, sem)
    copy.start()
    phases = grid_phases(own.shape[1] // 2)
    prepare_refs(near, phases, *prepared[4:])
    copy.wait()
    prepare_refs(own, phases, *prepared[:4])


def middle_kernel(*rest):
    count = len(rest) // 5
    refs, prepared = rest[:count], rest[count:]
    phases = grid_phases(refs[0].shape[1] // 2)
    for n in range(count):
        prepare_refs(refs[n], phases, *prepared[4 * n : 4 * n + 4])


def late_kernel(blocks, own, cnb, ynb, cynb, *rest):
    prepared, rest = rest[: 4 * blocks], rest[4 * blocks :]
    e_outs, rest = rest[:blocks], rest[blocks:]
    y_out, power_out, stats_out, tops_out, left_rows = rest
    per, lanes = e_outs[0].shape[1:]
    freq = power_out.shape[1]
    left = lanes - MAIN
    parts = (own, cnb, ynb, cynb)
    even, first = place_of_device()
    place_rows(even, first, parts, y_out, power_out, left_rows)
    facts = row_facts(even, first, parts)
    empty = deep_at(2, lanes)
    for out in (y_out, power_out):
        out[empty:] = jnp.zeros_like(out[empty:])
    stats_out[...] = jnp.zeros_like(stats_out)
    tops_out[...] = jnp.zeros_like(tops_out)

    def rows(out, part, size):
        at = deep_at(part, 0)
        main = out[at : at + MAIN]
        at = deep_at(part, MAIN)
        return jnp.concatenate([main, out[at : at + left]], axis=0)[:size]

    q_terms = [terms_left(prepared[4 * n + 2][...], prepared[4 * n + 3][...]) for n in range(blocks)]
    quad = dot_nt(
        jnp.concatenate(q_terms, axis=0), terms(*(rows(power_out, k, lanes) for k in (0, 1)))
    )
    prior = prior_rows(facts, per, lanes)
    mid = slice(SHIFTS // 2 * per, (SHIFTS // 2 + 1) * per)
    r_terms = [terms_left(prepared[4 * n][mid], prepared[4 * n + 1][mid]) for n in range(blocks)]
    moved = terms(*halves(shifted_rows(left_rows[...], grid_phases(freq))))
    far = dot_nt(jnp.concatenate(r_terms, axis=0), moved)
    far = jnp.concatenate([far, jnp.zeros((blocks * per, 384 - SHIFTS * left), jnp.float32)], axis=1)
    step = 128 // left
    far = [
        pltpu.roll(far[:, 128 * (t // step) : 128 * (t // step + 1)], -left * (t % step) % 128, 1)
        for t in range(SHIFTS)
    ]
    main_terms = terms(*(rows(y_out, k, MAIN) for k in (0, 1)))
    tops, sums = [], []
    for n in range(blocks):
        part = slice(n * per, (n + 1) * per)
        base = prior - 0.5 * quad[part]
        score = dot_nt(terms_left(prepared[4 * n][...], prepared[4 * n + 1][...]), main_terms)
        score = score.reshape(SHIFTS, per, MAIN)
        tail = jnp.stack([x[part, :left] for x in far])
        score = jnp.concatenate([score, tail], axis=2) + base[None]
        top, sums_here = weigh(score, e_outs[n])
        tops_out[n : n + 1, :lanes] = top
        tops.append(top)
        sums.append(sums_here)
    top, sums = joined_sums(tops, sums)
    for k, row in enumerate((top, *sums, facts[5:6, :lanes])):
        stats_out[k : k + 1, :lanes] = row


def sum_kernel(n, cuts, last, waits, *rest):
    team, tops, rest = rest[:TEAM], rest[TEAM], rest[TEAM + 1 + waits :]
    e_ref, y_ref, power_ref, *outs = rest
    per, lanes = e_ref.shape[1:]
    width = y_ref.shape[1]
    freq = width // 2
    team = [x[...] for x in team]
    top, (mass, *move) = joined_sums(
        [x[0:1] for x in team], [[x[k : k + 1] for k in (1, 2, 3)] for x in team]
    )
    live = team[0][4:5] / mass
    gain = (jnp.exp(tops[n : n + 1] - top) * live)[:, :lanes]
    if last:
        shift_out = outs.pop()
        move = [x * live for x in move] + [jnp.zeros((6, live.shape[1]), jnp.float32)]
        move = own_lanes(*place_of_device(), jnp.concatenate(move, axis=0))
        shift_out[...] = move[:2, : shift_out.shape[1]]
    w = e_ref[...] * gain[None]
    flat = dot_nn(deep_lanes(w.reshape(SHIFTS * per, lanes)), y_ref[...])
    weight = dot_nn(deep_lanes(jnp.sum(w, axis=0)), power_ref[...])
    phases = grid_phases(freq)
    mid = SHIFTS // 2

    def block(t):
        return flat[t * per : (t + 1) * per, :freq], flat[t * per : (t + 1) * per, freq:]

    re, im = block(mid)
    for t in range(mid):
        c, s = phases[t]
        ar, ai = block(t)
        br, bi = block(SHIFTS - 1 - t)
        re = re + (ar + br) * c - (ai - bi) * s
        im = im + (ar - br) * s + (ai + bi) * c
    for start, stop, out in zip(cuts, cuts[1:], outs):
        part = slice(start, stop)
        out[:, :freq] = re[part]
        out[:, freq:width] = im[part]
        out[:, width:] = weight[part]


def add_kernel(a, b, wait, out):
    out[...] = a[...] + b[...]


def final_kernel(row_cuts, *refs):
    own, *parts, signal, out = refs
    rows, width = out.shape
    freq = width // 2
    inverse = 1.0 / signal[...]
    every = sorted({cut for cuts in row_cuts for cut in cuts})
    for start, stop in zip(every, every[1:]):
        total = own[start:stop]
        at = 0
        for cuts in row_cuts:
            for low, high in zip(cuts, cuts[1:]):
                if low <= start and stop <= high:
                    total = total + parts[at][start - low : stop - low]
                at += 1
        denominator = total[:, width:] + inverse
        out[start:stop, :freq] = total[:, :freq] / denominator
        out[start:stop, freq:] = total[:, freq:width] / denominator


def params(mib):
    return pltpu.CompilerParams(vmem_limit_bytes=mib * 1024 * 1024)


def crossed(block, mask, core=None):
    devices = [i for i in range(lax.axis_size("dom")) if core is None or i % 2 == core]
    return lax.ppermute(block, "dom", [(i, i ^ mask) for i in devices])


def on_device(
    particle_fourier,
    defocus,
    particle_offset,
    prior_rotation,
    group_id,
    live_count,
    noise_power,
    signal_power,
    class_refs,
):
    slots, width = particle_fourier.shape
    freq = width // 2
    size = lax.axis_size("dom")
    blocks = size // TEAM
    refs_own = class_refs.reshape(-1, width)
    per = refs_own.shape[0]
    f32 = jnp.float32
    vmem = pl.BlockSpec(memory_space=pltpu.VMEM)
    no_cost = pl.CostEstimate(flops=0, bytes_accessed=0, transcendentals=0)
    much = pl.CostEstimate(flops=16 * 10**9, bytes_accessed=0, transcendentals=0)

    def gated(arrays, cost, waits=()):
        return pl.pallas_call(
            lambda *a: None,
            out_shape=tuple(jax.ShapeDtypeStruct(x.shape, x.dtype) for x in arrays),
            in_specs=[anywhere] * (len(arrays) + len(waits)),
            out_specs=(anywhere,) * len(arrays),
            input_output_aliases={n: n for n in range(len(arrays))},
            compiler_params=params(1),
            cost_estimate=cost,
            name="gate",
        )(*arrays, *waits)

    ynb_even = crossed(particle_fourier, 2, 0)
    ynb_odd = crossed(particle_fourier[: slots // 2], 2, 1)
    anywhere = pl.BlockSpec(memory_space=pl.ANY)
    ynb_even = crossed(particle_fourier, 2, 0)
    ynb_odd = crossed(particle_fourier[: slots // 2], 2, 1)
    anywhere = pl.BlockSpec(memory_space=pl.ANY)
    ynb_even = crossed(particle_fourier, 2, 0)
    ynb_odd = crossed(particle_fourier[: slots // 2], 2, 1)
    anywhere = pl.BlockSpec(memory_space=pl.ANY)
    ynb_even = crossed(particle_fourier, 2, 0)
    ynb_odd = crossed(particle_fourier[: slots // 2], 2, 1)
    refs = {0: refs_own, 1: crossed(refs_own, TEAM)}
    for n in range(2, blocks, 2):
        refs[n] = crossed(refs_own, TEAM * n)
    own_facts = (
        particle_fourier,
        defocus.reshape(1, slots),
        particle_offset.T,
        prior_rotation.reshape(1, slots),
        group_id.reshape(1, slots),
        noise_power,
    )
    own, facts, inverse_noise = pl.pallas_call(
        own_kernel,
        out_shape=(
            jax.ShapeDtypeStruct((slots + 8, width + freq), f32),
            jax.ShapeDtypeStruct((8, 128), f32),
            jax.ShapeDtypeStruct(noise_power.shape, f32),
        ),
        in_specs=[anywhere] * 6 + [pl.BlockSpec(memory_space=pltpu.SMEM)],
        out_specs=(vmem,) * 3,
        scratch_shapes=[pltpu.VMEM(x.shape, x.dtype) for x in own_facts]
        + [pltpu.SemaphoreType.DMA((6,))],
        compiler_params=params(6),
        cost_estimate=no_cost,
        name="own",
    )(*(pltpu.with_memory_space_constraint(x, pltpu.HBM) for x in own_facts), live_count)
    cnb = crossed(own, 1)
    ynb_facts = crossed(facts, 2)
    lanes = 3 * slots
    bf16 = jnp.bfloat16
    early = 2

    def shaped(rows, cols, dtype=f32):
        return jax.ShapeDtypeStruct((rows, cols), dtype)

    block_shapes = [shaped(SHIFTS * per, width, bf16)] * 2 + [shaped(per, freq, bf16)] * 2
    score_shape = jax.ShapeDtypeStruct((SHIFTS, per, lanes), f32)

    def call(kernel, operands, out_shape, name, mib, cost=None, scratch=()):
        return pl.pallas_call(
            kernel,
            cost_estimate=cost,
            out_shape=tuple(out_shape),
            in_specs=[vmem] * len(operands),
            out_specs=(vmem,) * len(out_shape),
            scratch_shapes=list(scratch),
            compiler_params=params(mib),
            name=name,
        )(*operands)

    prepared = pl.pallas_call(
        early_kernel,
        out_shape=tuple(block_shapes * early),
        in_specs=[anywhere, vmem],
        out_specs=(vmem,) * (4 * early),
        scratch_shapes=[pltpu.VMEM(refs_own.shape, f32), pltpu.SemaphoreType.DMA],
        compiler_params=params(8),
        name="early",
    )(pltpu.with_memory_space_constraint(refs_own, pltpu.HBM), refs[1])
    for n in range(2, blocks, 2):
        (refs[n],) = gated([refs[n]], no_cost, [ynb_facts, prepared[2]])
        refs[n + 1] = crossed(refs[n], TEAM)
    refs = [refs[n] for n in range(blocks)]
    ynb_prepared = pl.pallas_call(
        neighbour_kernel,
        out_shape=jax.ShapeDtypeStruct((slots + 8, width + freq), f32),
        in_specs=[vmem] * 4 + [anywhere],
        out_specs=vmem,
        scratch_shapes=[pltpu.VMEM((slots, width), f32)],
        compiler_params=params(6),
        cost_estimate=no_cost,
        name="neighbour",
    )(ynb_even, ynb_odd, ynb_facts, inverse_noise, prepared[2])
    cynb = crossed(ynb_prepared, 1)

    outs = []
    for n in range(early, blocks):
        outs += call(
            middle_kernel, [refs[n]], block_shapes, "middle", 6, much if n == blocks - 1 else None
        )
    prepared = (*prepared, *outs)
    deep = 3 * MAIN + 128
    top_rows = -(-blocks // 8) * 8
    outs = call(
        lambda *a: late_kernel(blocks, *a),
        (own, cnb, ynb_prepared, cynb, *prepared),
        [score_shape] * blocks
        + [shaped(deep, width, bf16), shaped(deep, freq, bf16)]
        + [shaped(8, 384), shaped(top_rows, 384)],
        "late",
        8 + 2 * blocks,
        scratch=[pltpu.VMEM((lanes - MAIN, width), f32)],
    )
    weights, (y, power, stats, tops) = outs[:blocks], outs[blocks:]

    team = [stats] + [crossed(stats, n) for n in range(1, TEAM)]

    def sums(n, cuts, last=False, waits=()):
        out_shape = [shaped(b - a, width + freq) for a, b in zip(cuts, cuts[1:])]
        if last:
            out_shape.append(shaped(2, slots))
        return pl.pallas_call(
            lambda *a: sum_kernel(n, cuts, last, len(waits), *a),
            out_shape=tuple(out_shape),
            in_specs=[vmem] * (TEAM + 1) + [anywhere] * len(waits) + [vmem] * 3,
            out_specs=(vmem,) * len(out_shape),
            compiler_params=params(8),
            name="sums",
        )(*team, tops, *waits, weights[n], y, power)

    def combined(mine, other, wait):
        return pl.pallas_call(
            add_kernel,
            out_shape=jax.ShapeDtypeStruct(mine.shape, f32),
            in_specs=[vmem] * 2 + [anywhere],
            out_specs=vmem,
            compiler_params=params(4),
            name="combined",
        )(mine, other, wait)

    whole, cut = (0, per), (0, per // 2, per)
    far = []
    waits = []
    for n in range(2, blocks, 2):
        handed = sums(n + 1, cut)
        mine = sums(n, cut, waits=handed[:1])
        if n == 2:
            (near,) = sums(1, whole, waits=mine[:1])
        joined = [combined(x, crossed(y, TEAM), near) for x, y in zip(mine, handed)]
        far.extend(crossed(x, TEAM * n) for x in joined)
        waits.extend(joined)
    own_part, shift = sums(0, whole, last=True, waits=waits)
    far = [crossed(near, TEAM), *gated(far, much)]
    row_cuts = [whole] + [cut] * (len(far) // 2)

    refs_new = pl.pallas_call(
        lambda *a: final_kernel(row_cuts, *a),
        out_shape=jax.ShapeDtypeStruct((per, width), f32),
        in_specs=[vmem] * (len(far) + 2),
        out_specs=vmem,
        compiler_params=params(2 + blocks),
        name="update",
    )(own_part, *far, signal_power.reshape(1, freq))

    return (shift.T, refs_new.reshape(class_refs.shape))


def solution(mesh):
    in_specs = (
        P(("groups", "dom"), None),
        P(("groups", "dom")),
        P(("groups", "dom"), None),
        P(("groups", "dom")),
        P(("groups", "dom")),
        P(("groups", "dom")),
        P("groups", None),
        P("groups"),
        P(("groups", "dom"), None, None),
    )
    out_specs = (P(("groups", "dom"), None), P(("groups", "dom"), None, None))
    return jax.shard_map(
        on_device, mesh=mesh, in_specs=in_specs, out_specs=out_specs, check_vma=False
    )
```

```python
import math

import jax
import jax.numpy as jnp
from jax import lax
from jax.experimental import pallas as pl
from jax.experimental.pallas import tpu as pltpu
from jax.sharding import PartitionSpec as P

ROT = 16
SIDE = 3
BOX = 128
FY = 32
SHIFTS = 9
TEAM = 4
PRIOR = 2.0
CTF_SIZE = math.hypot(0.995, 0.1)
CTF_TURN = math.atan2(0.1, 0.995)
SINE = (
    9.99999976e-01,
    -1.66666476e-01,
    8.33289854e-03,
    -1.98008185e-04,
    2.59032780e-06,
)
TWO_PI = 2.0 * math.pi
PI_A = 3.140625
PI_B = 0.0009670257568359375
PI_C = math.pi - PI_A - PI_B
HIGHEST = lax.Precision.HIGHEST
GRID = tuple((t // SIDE - SIDE // 2, t % SIDE - SIDE // 2) for t in range(SHIFTS))


def half_turn_sine(x):
    s = x * x
    p = SINE[4]
    for c in SINE[3::-1]:
        p = p * s + c
    return x * p


def turn_cos(turns):
    t = jnp.abs(turns - jnp.round(turns))
    return half_turn_sine(TWO_PI * (0.25 - t))


def turn_sin(turns):
    return turn_cos(turns - 0.25)


def freq_rows(width, rows):
    f = lax.broadcasted_iota(jnp.int32, (rows, width), 1)
    kx = (f // FY).astype(jnp.float32)
    ky = (f % FY - FY // 2).astype(jnp.float32)
    return kx, ky


def dot_nt(a, b):
    return lax.dot_general(
        a, b, (((1,), (1,)), ((), ())), preferred_element_type=jnp.float32
    )


def dot_nn(a, b):
    return lax.dot_general(
        a, b, (((1,), (0,)), ((), ())), preferred_element_type=jnp.float32
    )


def exact_dot_nn(a, b):
    return lax.dot_general(
        a, b, (((1,), (0,)), ((), ())), precision=HIGHEST, preferred_element_type=jnp.float32
    )


def halves(x):
    high = x.astype(jnp.bfloat16)
    return high, (x - high.astype(jnp.float32)).astype(jnp.bfloat16)


MAIN = 256


def deep_at(part, row):
    return MAIN * part + row if row < MAIN else 3 * MAIN + 32 * part + row - MAIN


def deep_lanes(x):
    rows, lanes = x.shape
    left = lanes - MAIN
    high, low = halves(x[:, :MAIN])
    tail = jnp.concatenate([x[:, MAIN:], jnp.zeros((rows, 128 - left), jnp.float32)], axis=1)
    tail_high = tail.astype(jnp.bfloat16).astype(jnp.float32)
    tail_low = tail - tail_high
    mixed = tail_high + pltpu.roll(tail_high, left, 1) + pltpu.roll(tail_low, 2 * left, 1)
    return jnp.concatenate([high, high, low, mixed.astype(jnp.bfloat16)], axis=1)


def grid_phases(width):
    kx, ky = freq_rows(width, 1)
    out = []
    for t, (gx, gy) in enumerate(GRID):
        if t < SHIFTS // 2:
            m = (kx * gx + ky * gy) * (1.0 / BOX)
            out.append((turn_cos(m), turn_sin(m)))
    return out


def phase_of(phases, t):
    mid = SHIFTS // 2
    if t < mid:
        return phases[t]
    c, s = phases[SHIFTS - 1 - t]
    return c, -s


def prepared_rows(src, facts, inverse_noise, out):
    slots, width = src.shape
    freq = width // 2
    columns = jnp.concatenate([facts, jnp.zeros((120, 128), jnp.float32)], axis=0).T[:slots]
    focus = columns[:, 0:1]
    off_x = columns[:, 1:2]
    off_y = columns[:, 2:3]
    group_col = columns[:, 4:5]

    kx, ky = freq_rows(freq, 1)
    chi = focus * ((kx * kx + ky * ky) * (1.0 / 1024.0))
    k = jnp.round(chi * (1.0 / math.pi))
    rest_angle = ((chi - k * PI_A) - k * PI_B) - k * PI_C
    shifted_angle = rest_angle + CTF_TURN
    over = shifted_angle > (0.5 * math.pi)
    folded = jnp.where(over, math.pi - shifted_angle, shifted_angle)
    parity = 0.5 * k
    sign = (parity - jnp.floor(parity)) * (4.0 * CTF_SIZE) - CTF_SIZE
    ctf = half_turn_sine(folded) * sign
    kx0, ky0 = freq_rows(128, 1)
    m = (kx0 * off_x + ky0 * off_y) * (1.0 / BOX)
    pc, ps = turn_cos(m), turn_sin(m)
    step = off_x * ((128 // FY) / BOX) + jnp.zeros((slots, 128), jnp.float32)
    sc, ss = turn_cos(step), turn_sin(step)

    total = inverse_noise.shape[0]
    onehot = (
        group_col == lax.broadcasted_iota(jnp.int32, (slots, total), 1).astype(jnp.float32)
    ).astype(jnp.float32)
    noise_rows = exact_dot_nn(onehot, inverse_noise)
    scaled = ctf * noise_rows
    out[:slots, width:] = ctf * scaled
    for n in range(freq // 128):
        part = slice(128 * n, 128 * (n + 1))
        twin = slice(freq + 128 * n, freq + 128 * (n + 1))
        co = pc * scaled[:, part]
        si = ps * scaled[:, part]
        pc, ps = pc * sc - ps * ss, ps * sc + pc * ss
        xr, xi = src[:, part], src[:, twin]
        out[:slots, part] = xr * co - xi * si
        out[:slots, twin] = xr * si + xi * co
    out[slots:, :128] = facts
    out[slots:, 128:] = jnp.zeros((8, width + freq - 128), jnp.float32)


def own_kernel(
    src_at, focus_at, offsets_at, prior_at, group_at, noise_at, live_count, out, facts_out,
    inverse_out, src, focus, offsets, prior, group, noise, sems
):
    moves = (
        (focus_at, focus), (offsets_at, offsets), (prior_at, prior), (group_at, group),
        (noise_at, noise), (src_at, src),
    )
    copies = [pltpu.make_async_copy(x, y, sems.at[n]) for n, (x, y) in enumerate(moves)]
    for copy in copies:
        copy.start()
    slots = src.shape[0]
    facts_out[...] = jnp.zeros_like(facts_out)
    slot = lax.broadcasted_iota(jnp.int32, (1, slots), 1)
    for copy in copies:
        copy.wait()
    facts_out[5:6, :slots] = (slot < live_count[0]).astype(jnp.float32)
    facts_out[0:1, :slots] = focus[...]
    facts_out[1:3, :slots] = offsets[...].astype(jnp.float32)
    facts_out[3:4, :slots] = prior[...].astype(jnp.float32)
    facts_out[4:5, :slots] = group[...].astype(jnp.float32)
    inverse = 1.0 / noise[...]
    inverse_out[...] = inverse
    prepared_rows(src, facts_out[...], inverse, out)


def neighbour_kernel(src, facts, inverse_noise, wait, out):
    prepared_rows(src, facts[...], inverse_noise[...], out)


def team_order(own, cnb, ynb, cynb):
    for even in (True, False):
        for first in (True, False):
            heavy, light = ((own, ynb), (cnb, cynb)) if even else ((cnb, cynb), (own, ynb))
            if not first:
                heavy, light = heavy[::-1], light[::-1]
            yield even, first, heavy, light


def place_rows(even, first, parts, y_out, power_out, left_out):
    width = y_out.shape[1]
    slots = parts[0].shape[0] - 8
    half = slots // 2
    cut = MAIN - 2 * slots - half

    def place(src, start, stop, to):
        for cols, out in ((slice(0, width), y_out), (slice(width, None), power_out)):
            pair = halves(src[start:stop, cols])
            for part in range(3):
                row = deep_at(part, to)
                out[row : row + stop - start] = pair[part % 2]

    for is_even, is_first, heavy, light in team_order(*parts):

        @pl.when(jnp.logical_and(even == is_even, first == is_first))
        def _(heavy=heavy, light=light):
            place(heavy[0], 0, slots, 0)
            place(heavy[1], 0, slots, slots)
            place(light[0], 0, half, 2 * slots)
            place(light[1], 0, cut, 2 * slots + half)
            place(light[1], cut, half, MAIN)
            left_out[...] = light[1][cut:half, :width]


def lane_index():
    return lax.broadcasted_iota(jnp.int32, (8, 128), 1)


def row_facts(even, first, parts):
    lane = lane_index()
    own, cnb, ynb, cynb = (x[x.shape[0] - 8 :, :128] for x in parts)
    heavy = (jnp.where(even, own, cnb), jnp.where(even, ynb, cynb))
    light = (jnp.where(even, cnb, own), jnp.where(even, cynb, ynb))
    a0, b0 = (jnp.where(first, x[0], x[1]) for x in (heavy, light))
    a1, b1 = (jnp.where(first, x[1], x[0]) for x in (heavy, light))
    a1 = pltpu.roll(a1, 96, 1)
    b1 = pltpu.roll(b1, 112, 1)
    middle = jnp.where(lane < 64, a1, jnp.where(lane < 112, pltpu.roll(b0, 64, 1), b1))
    return jnp.concatenate([jnp.where(lane < 96, a0, a1), middle, b1], axis=1)


def own_lanes(even, first, x):
    lane = lane_index()
    a, b, c = x[:, :128], x[:, 128:256], x[:, 256:]
    heavy_far = jnp.where(lane < 32, pltpu.roll(a, 32, 1), pltpu.roll(b, 32, 1))
    light_far = jnp.where(lane < 16, pltpu.roll(b, 16, 1), pltpu.roll(c, 16, 1))
    light = jnp.where(first, pltpu.roll(b, 64, 1), light_far)
    heavy = jnp.where(first, a, heavy_far)
    return jnp.where(even, heavy, jnp.where(lane < 48, light, 0.0))


def place_of_device():
    me = lax.axis_index("dom")
    return me % 2 == 0, (me // 2) % 2 == 0


def prior_rows(facts, per, lanes):
    r = (lax.broadcasted_iota(jnp.int32, (per, lanes), 0) % ROT).astype(jnp.float32)
    return PRIOR * turn_cos((r - facts[3:4, :lanes]) * (1.0 / ROT))


def prepare_refs(ref, phases, r_high, r_low, q_high, q_low):
    per, width = ref.shape
    freq = width // 2
    rr, ri = ref[:, :freq], ref[:, freq:]
    mid = SHIFTS // 2

    def store(t, re, im):
        rows = slice(t * per, (t + 1) * per)
        r_high[rows, :freq], r_low[rows, :freq] = halves(re)
        r_high[rows, freq:], r_low[rows, freq:] = halves(im)

    store(mid, rr, ri)
    for t in range(mid):
        c, s = phases[t]
        a, b, d, e = rr * c, ri * s, ri * c, rr * s
        store(t, a + b, d - e)
        store(SHIFTS - 1 - t, a - b, d + e)
    q_high[...], q_low[...] = halves(rr * rr + ri * ri)


def terms(high, low):
    return jnp.concatenate([high, high, low], axis=1)


def terms_left(high, low):
    return jnp.concatenate([high, low, high], axis=1)


def shifted_rows(rows, phases):
    freq = rows.shape[1] // 2
    re, im = rows[:, :freq], rows[:, freq:]
    mid = SHIFTS // 2
    out = [None] * SHIFTS
    out[mid] = rows
    for t in range(mid):
        c, s = phases[t]
        a, b, d, e = re * c, im * s, im * c, re * s
        out[t] = jnp.concatenate([a - b, e + d], axis=1)
        out[SHIFTS - 1 - t] = jnp.concatenate([a + b, d - e], axis=1)
    return jnp.concatenate(out, axis=0)


def weigh(score, e_out):
    top = jnp.max(jnp.max(score, axis=0), axis=0, keepdims=True)
    e = jnp.exp(score - top[None])
    e_out[...] = e
    side = SIDE // 2
    by_x = [sum(e[SIDE * x + y] for y in range(SIDE)) for x in range(SIDE)]
    by_y = [sum(e[SIDE * x + y] for x in range(SIDE)) for y in range(SIDE)]
    sums = [sum(by_x)]
    for by in (by_x, by_y):
        sums.append(sum(by[k] * float(k - side) for k in range(SIDE) if k != side))
    return top, [jnp.sum(x, axis=0, keepdims=True) for x in sums]


def joined_sums(tops, sums):
    top = tops[0]
    for other in tops[1:]:
        top = jnp.maximum(top, other)
    factors = [jnp.exp(other - top) for other in tops]
    return top, [sum(f * x for f, x in zip(factors, column)) for column in zip(*sums)]


def own_refs_kernel(own_at, wait, *rest):
    *prepared, own, sem = rest
    copy = pltpu.make_async_copy(own_at, own, sem)
    copy.start()
    phases = grid_phases(own.shape[1] // 2)
    copy.wait()
    prepare_refs(own, phases, *prepared)


def refs_kernel(ref, wait, *prepared):
    prepare_refs(ref, grid_phases(ref.shape[1] // 2), *prepared)


def late_kernel(blocks, own, cnb, ynb, cynb, *rest):
    prepared, rest = rest[: 4 * blocks], rest[4 * blocks :]
    e_outs, rest = rest[:blocks], rest[blocks:]
    y_out, power_out, stats_out, tops_out, left_rows = rest
    per, lanes = e_outs[0].shape[1:]
    freq = power_out.shape[1]
    left = lanes - MAIN
    parts = (own, cnb, ynb, cynb)
    even, first = place_of_device()
    place_rows(even, first, parts, y_out, power_out, left_rows)
    facts = row_facts(even, first, parts)
    empty = deep_at(2, lanes)
    for out in (y_out, power_out):
        out[empty:] = jnp.zeros_like(out[empty:])
    stats_out[...] = jnp.zeros_like(stats_out)
    tops_out[...] = jnp.zeros_like(tops_out)

    def rows(out, part, size):
        at = deep_at(part, 0)
        main = out[at : at + MAIN]
        at = deep_at(part, MAIN)
        return jnp.concatenate([main, out[at : at + left]], axis=0)[:size]

    q_terms = [terms_left(prepared[4 * n + 2][...], prepared[4 * n + 3][...]) for n in range(blocks)]
    quad = dot_nt(
        jnp.concatenate(q_terms, axis=0), terms(*(rows(power_out, k, lanes) for k in (0, 1)))
    )
    prior = prior_rows(facts, per, lanes)
    mid = slice(SHIFTS // 2 * per, (SHIFTS // 2 + 1) * per)
    r_terms = [terms_left(prepared[4 * n][mid], prepared[4 * n + 1][mid]) for n in range(blocks)]
    moved = terms(*halves(shifted_rows(left_rows[...], grid_phases(freq))))
    far = dot_nt(jnp.concatenate(r_terms, axis=0), moved)
    far = jnp.concatenate([far, jnp.zeros((blocks * per, 384 - SHIFTS * left), jnp.float32)], axis=1)
    step = 128 // left
    far = [
        pltpu.roll(far[:, 128 * (t // step) : 128 * (t // step + 1)], -left * (t % step) % 128, 1)
        for t in range(SHIFTS)
    ]
    main_terms = terms(*(rows(y_out, k, MAIN) for k in (0, 1)))
    tops, sums = [], []
    for n in range(blocks):
        part = slice(n * per, (n + 1) * per)
        base = prior - 0.5 * quad[part]
        score = dot_nt(terms_left(prepared[4 * n][...], prepared[4 * n + 1][...]), main_terms)
        score = score.reshape(SHIFTS, per, MAIN)
        tail = jnp.stack([x[part, :left] for x in far])
        score = jnp.concatenate([score, tail], axis=2) + base[None]
        top, sums_here = weigh(score, e_outs[n])
        tops_out[n : n + 1, :lanes] = top
        tops.append(top)
        sums.append(sums_here)
    top, sums = joined_sums(tops, sums)
    for k, row in enumerate((top, *sums, facts[5:6, :lanes])):
        stats_out[k : k + 1, :lanes] = row


def sum_kernel(n, cuts, last, waits, *rest):
    team, tops, rest = rest[:TEAM], rest[TEAM], rest[TEAM + 1 + waits :]
    e_ref, y_ref, power_ref, *outs = rest
    per, lanes = e_ref.shape[1:]
    width = y_ref.shape[1]
    freq = width // 2
    team = [x[...] for x in team]
    top, (mass, *move) = joined_sums(
        [x[0:1] for x in team], [[x[k : k + 1] for k in (1, 2, 3)] for x in team]
    )
    live = team[0][4:5] / mass
    gain = (jnp.exp(tops[n : n + 1] - top) * live)[:, :lanes]
    if last:
        shift_out = outs.pop()
        move = [x * live for x in move] + [jnp.zeros((6, live.shape[1]), jnp.float32)]
        move = own_lanes(*place_of_device(), jnp.concatenate(move, axis=0))
        shift_out[...] = move[:2, : shift_out.shape[1]]
    w = e_ref[...] * gain[None]
    flat = dot_nn(deep_lanes(w.reshape(SHIFTS * per, lanes)), y_ref[...])
    weight = dot_nn(deep_lanes(jnp.sum(w, axis=0)), power_ref[...])
    phases = grid_phases(freq)
    mid = SHIFTS // 2

    def block(t):
        return flat[t * per : (t + 1) * per, :freq], flat[t * per : (t + 1) * per, freq:]

    re, im = block(mid)
    for t in range(mid):
        c, s = phases[t]
        ar, ai = block(t)
        br, bi = block(SHIFTS - 1 - t)
        re = re + (ar + br) * c - (ai - bi) * s
        im = im + (ar - br) * s + (ai + bi) * c
    for start, stop, out in zip(cuts, cuts[1:], outs):
        part = slice(start, stop)
        out[:, :freq] = re[part]
        out[:, freq:width] = im[part]
        out[:, width:] = weight[part]


def add_kernel(a, b, wait, out):
    out[...] = a[...] + b[...]


def final_kernel(row_cuts, *refs):
    own, *parts, signal, out = refs
    rows, width = out.shape
    freq = width // 2
    inverse = 1.0 / signal[...]
    every = sorted({cut for cuts in row_cuts for cut in cuts})
    for start, stop in zip(every, every[1:]):
        total = own[start:stop]
        at = 0
        for cuts in row_cuts:
            for low, high in zip(cuts, cuts[1:]):
                if low <= start and stop <= high:
                    total = total + parts[at][start - low : stop - low]
                at += 1
        denominator = total[:, width:] + inverse
        out[start:stop, :freq] = total[:, :freq] / denominator
        out[start:stop, freq:] = total[:, freq:width] / denominator


def params(mib):
    return pltpu.CompilerParams(vmem_limit_bytes=mib * 1024 * 1024)


def crossed(block, mask):
    size = lax.axis_size("dom")
    return lax.ppermute(block, "dom", [(i, i ^ mask) for i in range(size)])


def on_device(
    particle_fourier,
    defocus,
    particle_offset,
    prior_rotation,
    group_id,
    live_count,
    noise_power,
    signal_power,
    class_refs,
):
    slots, width = particle_fourier.shape
    freq = width // 2
    size = lax.axis_size("dom")
    blocks = size // TEAM
    refs_own = class_refs.reshape(-1, width)
    per = refs_own.shape[0]
    f32 = jnp.float32
    vmem = pl.BlockSpec(memory_space=pltpu.VMEM)
    no_cost = pl.CostEstimate(flops=0, bytes_accessed=0, transcendentals=0)
    much = pl.CostEstimate(flops=16 * 10**9, bytes_accessed=0, transcendentals=0)

    ynb = crossed(particle_fourier, 2)
    anywhere = pl.BlockSpec(memory_space=pl.ANY)
    ynb = crossed(particle_fourier, 2)
    anywhere = pl.BlockSpec(memory_space=pl.ANY)
    ynb = crossed(particle_fourier, 2)
    anywhere = pl.BlockSpec(memory_space=pl.ANY)
    ynb = crossed(particle_fourier, 2)
    refs = [refs_own] + [crossed(refs_own, TEAM * n) for n in range(1, blocks)]
    own_facts = (
        particle_fourier,
        defocus.reshape(1, slots),
        particle_offset.T,
        prior_rotation.reshape(1, slots),
        group_id.reshape(1, slots),
        noise_power,
    )
    own, facts, inverse_noise = pl.pallas_call(
        own_kernel,
        out_shape=(
            jax.ShapeDtypeStruct((slots + 8, width + freq), f32),
            jax.ShapeDtypeStruct((8, 128), f32),
            jax.ShapeDtypeStruct(noise_power.shape, f32),
        ),
        in_specs=[anywhere] * 6 + [pl.BlockSpec(memory_space=pltpu.SMEM)],
        out_specs=(vmem,) * 3,
        scratch_shapes=[pltpu.VMEM(x.shape, x.dtype) for x in own_facts]
        + [pltpu.SemaphoreType.DMA((6,))],
        compiler_params=params(6),
        cost_estimate=no_cost,
        name="own",
    )(*(pltpu.with_memory_space_constraint(x, pltpu.HBM) for x in own_facts), live_count)
    cnb = crossed(own, 1)
    lanes = 3 * slots
    bf16 = jnp.bfloat16

    def shaped(rows, cols, dtype=f32):
        return jax.ShapeDtypeStruct((rows, cols), dtype)

    block_shapes = [shaped(SHIFTS * per, width, bf16)] * 2 + [shaped(per, freq, bf16)] * 2
    score_shape = jax.ShapeDtypeStruct((SHIFTS, per, lanes), f32)

    def call(kernel, operands, out_shape, name, mib, cost=None, scratch=()):
        return pl.pallas_call(
            kernel,
            cost_estimate=cost,
            out_shape=tuple(out_shape),
            in_specs=[vmem] * len(operands),
            out_specs=(vmem,) * len(out_shape),
            scratch_shapes=list(scratch),
            compiler_params=params(mib),
            name=name,
        )(*operands)

    prepared = pl.pallas_call(
        own_refs_kernel,
        out_shape=tuple(block_shapes),
        in_specs=[anywhere] * 2,
        out_specs=(vmem,) * 4,
        scratch_shapes=[pltpu.VMEM(refs_own.shape, f32), pltpu.SemaphoreType.DMA],
        compiler_params=params(8),
        name="own_refs",
    )(pltpu.with_memory_space_constraint(refs_own, pltpu.HBM), facts)
    ynb_prepared = pl.pallas_call(
        neighbour_kernel,
        out_shape=jax.ShapeDtypeStruct((slots + 8, width + freq), f32),
        in_specs=[vmem] * 3 + [anywhere],
        out_specs=vmem,
        compiler_params=params(6),
        cost_estimate=no_cost,
        name="neighbour",
    )(ynb, crossed(facts, 2), inverse_noise, prepared[2])
    cynb = crossed(ynb_prepared, 1)

    order = [*range(blocks - 1, 2, -1), 1, 2]
    wait = ynb_prepared
    by_block = {0: prepared}
    for n in order:
        by_block[n] = pl.pallas_call(
            refs_kernel,
            out_shape=tuple(block_shapes),
            in_specs=[vmem, anywhere],
            out_specs=(vmem,) * 4,
            compiler_params=params(6),
            cost_estimate=much if n == order[-1] else None,
            name="refs",
        )(refs[n], wait)
        wait = by_block[n][2]
    prepared = [x for n in range(blocks) for x in by_block[n]]
    deep = 3 * MAIN + 128
    top_rows = -(-blocks // 8) * 8
    outs = call(
        lambda *a: late_kernel(blocks, *a),
        (own, cnb, ynb_prepared, cynb, *prepared),
        [score_shape] * blocks
        + [shaped(deep, width, bf16), shaped(deep, freq, bf16)]
        + [shaped(8, 384), shaped(top_rows, 384)],
        "late",
        8 + 2 * blocks,
        scratch=[pltpu.VMEM((lanes - MAIN, width), f32)],
    )
    weights, (y, power, stats, tops) = outs[:blocks], outs[blocks:]

    team = [stats] + [crossed(stats, n) for n in range(1, TEAM)]

    def sums(n, cuts, last=False, waits=()):
        out_shape = [shaped(b - a, width + freq) for a, b in zip(cuts, cuts[1:])]
        if last:
            out_shape.append(shaped(2, slots))
        return pl.pallas_call(
            lambda *a: sum_kernel(n, cuts, last, len(waits), *a),
            out_shape=tuple(out_shape),
            in_specs=[vmem] * (TEAM + 1) + [anywhere] * len(waits) + [vmem] * 3,
            out_specs=(vmem,) * len(out_shape),
            compiler_params=params(8),
            name="sums",
        )(*team, tops, *waits, weights[n], y, power)

    def combined(mine, other, wait):
        return pl.pallas_call(
            add_kernel,
            out_shape=jax.ShapeDtypeStruct(mine.shape, f32),
            in_specs=[vmem] * 2 + [anywhere],
            out_specs=vmem,
            compiler_params=params(4),
            name="combined",
        )(mine, other, wait)

    def gated(arrays, cost):
        return pl.pallas_call(
            lambda *a: None,
            out_shape=tuple(jax.ShapeDtypeStruct(x.shape, x.dtype) for x in arrays),
            in_specs=[anywhere] * len(arrays),
            out_specs=(anywhere,) * len(arrays),
            input_output_aliases={n: n for n in range(len(arrays))},
            compiler_params=params(1),
            cost_estimate=cost,
            name="gate",
        )(*arrays)

    whole, cut = (0, per), (0, per // 2, per)
    far = []
    waits = []
    for n in range(2, blocks, 2):
        handed = sums(n + 1, cut)
        mine = sums(n, cut, waits=handed[:1])
        if n == 2:
            (near,) = sums(1, whole, waits=mine[:1])
        joined = [combined(x, crossed(y, TEAM), near) for x, y in zip(mine, handed)]
        far.extend(crossed(x, TEAM * n) for x in joined)
        waits.extend(joined)
    own_part, shift = sums(0, whole, last=True, waits=waits)
    far = [crossed(near, TEAM), *gated(far, much)]
    row_cuts = [whole] + [cut] * (len(far) // 2)

    refs_new = pl.pallas_call(
        lambda *a: final_kernel(row_cuts, *a),
        out_shape=jax.ShapeDtypeStruct((per, width), f32),
        in_specs=[vmem] * (len(far) + 2),
        out_specs=vmem,
        compiler_params=params(2 + blocks),
        name="update",
    )(own_part, *far, signal_power.reshape(1, freq))

    return (shift.T, refs_new.reshape(class_refs.shape))


def solution(mesh):
    in_specs = (
        P(("groups", "dom"), None),
        P(("groups", "dom")),
        P(("groups", "dom"), None),
        P(("groups", "dom")),
        P(("groups", "dom")),
        P(("groups", "dom")),
        P("groups", None),
        P("groups"),
        P(("groups", "dom"), None, None),
    )
    out_specs = (P(("groups", "dom"), None), P(("groups", "dom"), None, None))
    return jax.shard_map(
        on_device, mesh=mesh, in_specs=in_specs, out_specs=out_specs, check_vma=False
    )
```

```python
import math

import jax
import jax.numpy as jnp
from jax import lax
from jax.experimental import pallas as pl
from jax.experimental.pallas import tpu as pltpu
from jax.sharding import PartitionSpec as P

ROT = 16
SIDE = 3
BOX = 128
FY = 32
SHIFTS = 9
TEAM = 4
PRIOR = 2.0
CTF_SIZE = math.hypot(0.995, 0.1)
CTF_TURN = math.atan2(0.1, 0.995)
SINE = (
    9.99999976e-01,
    -1.66666476e-01,
    8.33289854e-03,
    -1.98008185e-04,
    2.59032780e-06,
)
TWO_PI = 2.0 * math.pi
PI_A = 3.140625
PI_B = 0.0009670257568359375
PI_C = math.pi - PI_A - PI_B
HIGHEST = lax.Precision.HIGHEST
GRID = tuple((t // SIDE - SIDE // 2, t % SIDE - SIDE // 2) for t in range(SHIFTS))


def half_turn_sine(x):
    s = x * x
    p = SINE[4]
    for c in SINE[3::-1]:
        p = p * s + c
    return x * p


def turn_cos(turns):
    t = jnp.abs(turns - jnp.round(turns))
    return half_turn_sine(TWO_PI * (0.25 - t))


def turn_sin(turns):
    return turn_cos(turns - 0.25)


def freq_rows(width, rows):
    f = lax.broadcasted_iota(jnp.int32, (rows, width), 1)
    kx = (f // FY).astype(jnp.float32)
    ky = (f % FY - FY // 2).astype(jnp.float32)
    return kx, ky


def dot_nt(a, b):
    return lax.dot_general(
        a, b, (((1,), (1,)), ((), ())), preferred_element_type=jnp.float32
    )


def dot_nn(a, b):
    return lax.dot_general(
        a, b, (((1,), (0,)), ((), ())), preferred_element_type=jnp.float32
    )


def exact_dot_nn(a, b):
    return lax.dot_general(
        a, b, (((1,), (0,)), ((), ())), precision=HIGHEST, preferred_element_type=jnp.float32
    )


def halves(x):
    high = x.astype(jnp.bfloat16)
    return high, (x - high.astype(jnp.float32)).astype(jnp.bfloat16)


MAIN = 256


def deep_at(part, row):
    return MAIN * part + row if row < MAIN else 3 * MAIN + 32 * part + row - MAIN


def deep_lanes(x):
    rows, lanes = x.shape
    left = lanes - MAIN
    high, low = halves(x[:, :MAIN])
    tail = jnp.concatenate([x[:, MAIN:], jnp.zeros((rows, 128 - left), jnp.float32)], axis=1)
    tail_high = tail.astype(jnp.bfloat16).astype(jnp.float32)
    tail_low = tail - tail_high
    mixed = tail_high + pltpu.roll(tail_high, left, 1) + pltpu.roll(tail_low, 2 * left, 1)
    return jnp.concatenate([high, high, low, mixed.astype(jnp.bfloat16)], axis=1)


def grid_phases(width):
    kx, ky = freq_rows(width, 1)
    out = []
    for t, (gx, gy) in enumerate(GRID):
        if t < SHIFTS // 2:
            m = (kx * gx + ky * gy) * (1.0 / BOX)
            out.append((turn_cos(m), turn_sin(m)))
    return out


def phase_of(phases, t):
    mid = SHIFTS // 2
    if t < mid:
        return phases[t]
    c, s = phases[SHIFTS - 1 - t]
    return c, -s


def prepared_rows(src, facts, inverse_noise, out):
    slots, width = src.shape
    freq = width // 2
    columns = jnp.concatenate([facts, jnp.zeros((120, 128), jnp.float32)], axis=0).T[:slots]
    focus = columns[:, 0:1]
    off_x = columns[:, 1:2]
    off_y = columns[:, 2:3]
    group_col = columns[:, 4:5]

    kx, ky = freq_rows(freq, 1)
    chi = focus * ((kx * kx + ky * ky) * (1.0 / 1024.0))
    k = jnp.round(chi * (1.0 / math.pi))
    rest_angle = ((chi - k * PI_A) - k * PI_B) - k * PI_C
    shifted_angle = rest_angle + CTF_TURN
    over = shifted_angle > (0.5 * math.pi)
    folded = jnp.where(over, math.pi - shifted_angle, shifted_angle)
    parity = 0.5 * k
    sign = (parity - jnp.floor(parity)) * (4.0 * CTF_SIZE) - CTF_SIZE
    ctf = half_turn_sine(folded) * sign
    kx0, ky0 = freq_rows(128, 1)
    m = (kx0 * off_x + ky0 * off_y) * (1.0 / BOX)
    pc, ps = turn_cos(m), turn_sin(m)
    step = off_x * ((128 // FY) / BOX) + jnp.zeros((slots, 128), jnp.float32)
    sc, ss = turn_cos(step), turn_sin(step)

    total = inverse_noise.shape[0]
    onehot = (
        group_col == lax.broadcasted_iota(jnp.int32, (slots, total), 1).astype(jnp.float32)
    ).astype(jnp.float32)
    noise_rows = exact_dot_nn(onehot, inverse_noise)
    scaled = ctf * noise_rows
    out[:slots, width:] = ctf * scaled
    for n in range(freq // 128):
        part = slice(128 * n, 128 * (n + 1))
        twin = slice(freq + 128 * n, freq + 128 * (n + 1))
        co = pc * scaled[:, part]
        si = ps * scaled[:, part]
        pc, ps = pc * sc - ps * ss, ps * sc + pc * ss
        xr, xi = src[:, part], src[:, twin]
        out[:slots, part] = xr * co - xi * si
        out[:slots, twin] = xr * si + xi * co
    out[slots:, :128] = facts
    out[slots:, 128:] = jnp.zeros((8, width + freq - 128), jnp.float32)


def own_kernel(
    src_at, focus_at, offsets_at, prior_at, group_at, noise_at, live_count, out, facts_out,
    inverse_out, src, focus, offsets, prior, group, noise, sems
):
    moves = (
        (focus_at, focus), (offsets_at, offsets), (prior_at, prior), (group_at, group),
        (noise_at, noise), (src_at, src),
    )
    copies = [pltpu.make_async_copy(x, y, sems.at[n]) for n, (x, y) in enumerate(moves)]
    for copy in copies:
        copy.start()
    slots = src.shape[0]
    facts_out[...] = jnp.zeros_like(facts_out)
    slot = lax.broadcasted_iota(jnp.int32, (1, slots), 1)
    for copy in copies:
        copy.wait()
    facts_out[5:6, :slots] = (slot < live_count[0]).astype(jnp.float32)
    facts_out[0:1, :slots] = focus[...]
    facts_out[1:3, :slots] = offsets[...].astype(jnp.float32)
    facts_out[3:4, :slots] = prior[...].astype(jnp.float32)
    facts_out[4:5, :slots] = group[...].astype(jnp.float32)
    inverse = 1.0 / noise[...]
    inverse_out[...] = inverse
    prepared_rows(src, facts_out[...], inverse, out)


def neighbour_kernel(src, facts, inverse_noise, wait, out):
    prepared_rows(src, facts[...], inverse_noise[...], out)


def team_order(own, cnb, ynb, cynb):
    for even in (True, False):
        for first in (True, False):
            heavy, light = ((own, ynb), (cnb, cynb)) if even else ((cnb, cynb), (own, ynb))
            if not first:
                heavy, light = heavy[::-1], light[::-1]
            yield even, first, heavy, light


def place_rows(even, first, parts, y_out, power_out, left_out):
    width = y_out.shape[1]
    slots = parts[0].shape[0] - 8
    half = slots // 2
    cut = MAIN - 2 * slots - half

    def place(src, start, stop, to):
        for cols, out in ((slice(0, width), y_out), (slice(width, None), power_out)):
            pair = halves(src[start:stop, cols])
            for part in range(3):
                row = deep_at(part, to)
                out[row : row + stop - start] = pair[part % 2]

    for is_even, is_first, heavy, light in team_order(*parts):

        @pl.when(jnp.logical_and(even == is_even, first == is_first))
        def _(heavy=heavy, light=light):
            place(heavy[0], 0, slots, 0)
            place(heavy[1], 0, slots, slots)
            place(light[0], 0, half, 2 * slots)
            place(light[1], 0, cut, 2 * slots + half)
            place(light[1], cut, half, MAIN)
            left_out[...] = light[1][cut:half, :width]


def lane_index():
    return lax.broadcasted_iota(jnp.int32, (8, 128), 1)


def row_facts(even, first, parts):
    lane = lane_index()
    own, cnb, ynb, cynb = (x[x.shape[0] - 8 :, :128] for x in parts)
    heavy = (jnp.where(even, own, cnb), jnp.where(even, ynb, cynb))
    light = (jnp.where(even, cnb, own), jnp.where(even, cynb, ynb))
    a0, b0 = (jnp.where(first, x[0], x[1]) for x in (heavy, light))
    a1, b1 = (jnp.where(first, x[1], x[0]) for x in (heavy, light))
    a1 = pltpu.roll(a1, 96, 1)
    b1 = pltpu.roll(b1, 112, 1)
    middle = jnp.where(lane < 64, a1, jnp.where(lane < 112, pltpu.roll(b0, 64, 1), b1))
    return jnp.concatenate([jnp.where(lane < 96, a0, a1), middle, b1], axis=1)


def own_lanes(even, first, x):
    lane = lane_index()
    a, b, c = x[:, :128], x[:, 128:256], x[:, 256:]
    heavy_far = jnp.where(lane < 32, pltpu.roll(a, 32, 1), pltpu.roll(b, 32, 1))
    light_far = jnp.where(lane < 16, pltpu.roll(b, 16, 1), pltpu.roll(c, 16, 1))
    light = jnp.where(first, pltpu.roll(b, 64, 1), light_far)
    heavy = jnp.where(first, a, heavy_far)
    return jnp.where(even, heavy, jnp.where(lane < 48, light, 0.0))


def place_of_device():
    me = lax.axis_index("dom")
    return me % 2 == 0, (me // 2) % 2 == 0


def prior_rows(facts, per, lanes):
    r = (lax.broadcasted_iota(jnp.int32, (per, lanes), 0) % ROT).astype(jnp.float32)
    return PRIOR * turn_cos((r - facts[3:4, :lanes]) * (1.0 / ROT))


def prepare_refs(ref, phases, r_high, r_low, q_high, q_low):
    per, width = ref.shape
    freq = width // 2
    rr, ri = ref[:, :freq], ref[:, freq:]
    mid = SHIFTS // 2

    def store(t, re, im):
        rows = slice(t * per, (t + 1) * per)
        r_high[rows, :freq], r_low[rows, :freq] = halves(re)
        r_high[rows, freq:], r_low[rows, freq:] = halves(im)

    store(mid, rr, ri)
    for t in range(mid):
        c, s = phases[t]
        a, b, d, e = rr * c, ri * s, ri * c, rr * s
        store(t, a + b, d - e)
        store(SHIFTS - 1 - t, a - b, d + e)
    q_high[...], q_low[...] = halves(rr * rr + ri * ri)


def terms(high, low):
    return jnp.concatenate([high, high, low], axis=1)


def terms_left(high, low):
    return jnp.concatenate([high, low, high], axis=1)


def shifted_rows(rows, phases):
    freq = rows.shape[1] // 2
    re, im = rows[:, :freq], rows[:, freq:]
    mid = SHIFTS // 2
    out = [None] * SHIFTS
    out[mid] = rows
    for t in range(mid):
        c, s = phases[t]
        a, b, d, e = re * c, im * s, im * c, re * s
        out[t] = jnp.concatenate([a - b, e + d], axis=1)
        out[SHIFTS - 1 - t] = jnp.concatenate([a + b, d - e], axis=1)
    return jnp.concatenate(out, axis=0)


def weigh(score, e_out):
    top = jnp.max(jnp.max(score, axis=0), axis=0, keepdims=True)
    e = jnp.exp(score - top[None])
    e_out[...] = e
    side = SIDE // 2
    by_x = [sum(e[SIDE * x + y] for y in range(SIDE)) for x in range(SIDE)]
    by_y = [sum(e[SIDE * x + y] for x in range(SIDE)) for y in range(SIDE)]
    sums = [sum(by_x)]
    for by in (by_x, by_y):
        sums.append(sum(by[k] * float(k - side) for k in range(SIDE) if k != side))
    return top, [jnp.sum(x, axis=0, keepdims=True) for x in sums]


def joined_sums(tops, sums):
    top = tops[0]
    for other in tops[1:]:
        top = jnp.maximum(top, other)
    factors = [jnp.exp(other - top) for other in tops]
    return top, [sum(f * x for f, x in zip(factors, column)) for column in zip(*sums)]


def own_refs_kernel(own_at, wait, *rest):
    *prepared, own, sem = rest
    copy = pltpu.make_async_copy(own_at, own, sem)
    copy.start()
    phases = grid_phases(own.shape[1] // 2)
    copy.wait()
    prepare_refs(own, phases, *prepared)


def refs_kernel(ref, wait, *prepared):
    prepare_refs(ref, grid_phases(ref.shape[1] // 2), *prepared)


def late_kernel(blocks, own, cnb, ynb, cynb, *rest):
    prepared, rest = rest[: 4 * blocks], rest[4 * blocks :]
    e_outs, rest = rest[:blocks], rest[blocks:]
    y_out, power_out, stats_out, tops_out, left_rows = rest
    per, lanes = e_outs[0].shape[1:]
    freq = power_out.shape[1]
    left = lanes - MAIN
    parts = (own, cnb, ynb, cynb)
    even, first = place_of_device()
    place_rows(even, first, parts, y_out, power_out, left_rows)
    facts = row_facts(even, first, parts)
    empty = deep_at(2, lanes)
    for out in (y_out, power_out):
        out[empty:] = jnp.zeros_like(out[empty:])
    stats_out[...] = jnp.zeros_like(stats_out)
    tops_out[...] = jnp.zeros_like(tops_out)

    def rows(out, part, size):
        at = deep_at(part, 0)
        main = out[at : at + MAIN]
        at = deep_at(part, MAIN)
        return jnp.concatenate([main, out[at : at + left]], axis=0)[:size]

    q_terms = [terms_left(prepared[4 * n + 2][...], prepared[4 * n + 3][...]) for n in range(blocks)]
    quad = dot_nt(
        jnp.concatenate(q_terms, axis=0), terms(*(rows(power_out, k, lanes) for k in (0, 1)))
    )
    prior = prior_rows(facts, per, lanes)
    mid = slice(SHIFTS // 2 * per, (SHIFTS // 2 + 1) * per)
    r_terms = [terms_left(prepared[4 * n][mid], prepared[4 * n + 1][mid]) for n in range(blocks)]
    moved = terms(*halves(shifted_rows(left_rows[...], grid_phases(freq))))
    far = dot_nt(jnp.concatenate(r_terms, axis=0), moved)
    far = jnp.concatenate([far, jnp.zeros((blocks * per, 384 - SHIFTS * left), jnp.float32)], axis=1)
    step = 128 // left
    far = [
        pltpu.roll(far[:, 128 * (t // step) : 128 * (t // step + 1)], -left * (t % step) % 128, 1)
        for t in range(SHIFTS)
    ]
    main_terms = terms(*(rows(y_out, k, MAIN) for k in (0, 1)))
    tops, sums = [], []
    for n in range(blocks):
        part = slice(n * per, (n + 1) * per)
        base = prior - 0.5 * quad[part]
        score = dot_nt(terms_left(prepared[4 * n][...], prepared[4 * n + 1][...]), main_terms)
        score = score.reshape(SHIFTS, per, MAIN)
        tail = jnp.stack([x[part, :left] for x in far])
        score = jnp.concatenate([score, tail], axis=2) + base[None]
        top, sums_here = weigh(score, e_outs[n])
        tops_out[n : n + 1, :lanes] = top
        tops.append(top)
        sums.append(sums_here)
    top, sums = joined_sums(tops, sums)
    for k, row in enumerate((top, *sums, facts[5:6, :lanes])):
        stats_out[k : k + 1, :lanes] = row


def sum_kernel(n, cuts, last, waits, *rest):
    team, tops, rest = rest[:TEAM], rest[TEAM], rest[TEAM + 1 + waits :]
    e_ref, y_ref, power_ref, *outs = rest
    per, lanes = e_ref.shape[1:]
    width = y_ref.shape[1]
    freq = width // 2
    team = [x[...] for x in team]
    top, (mass, *move) = joined_sums(
        [x[0:1] for x in team], [[x[k : k + 1] for k in (1, 2, 3)] for x in team]
    )
    live = team[0][4:5] / mass
    gain = (jnp.exp(tops[n : n + 1] - top) * live)[:, :lanes]
    if last:
        shift_out = outs.pop()
        move = [x * live for x in move] + [jnp.zeros((6, live.shape[1]), jnp.float32)]
        move = own_lanes(*place_of_device(), jnp.concatenate(move, axis=0))
        shift_out[...] = move[:2, : shift_out.shape[1]]
    w = e_ref[...] * gain[None]
    flat = dot_nn(deep_lanes(w.reshape(SHIFTS * per, lanes)), y_ref[...])
    weight = dot_nn(deep_lanes(jnp.sum(w, axis=0)), power_ref[...])
    phases = grid_phases(freq)
    mid = SHIFTS // 2

    def block(t):
        return flat[t * per : (t + 1) * per, :freq], flat[t * per : (t + 1) * per, freq:]

    re, im = block(mid)
    for t in range(mid):
        c, s = phases[t]
        ar, ai = block(t)
        br, bi = block(SHIFTS - 1 - t)
        re = re + (ar + br) * c - (ai - bi) * s
        im = im + (ar - br) * s + (ai + bi) * c
    for start, stop, out in zip(cuts, cuts[1:], outs):
        part = slice(start, stop)
        out[:, :freq] = re[part]
        out[:, freq:width] = im[part]
        out[:, width:] = weight[part]


def add_kernel(a, b, wait, out):
    out[...] = a[...] + b[...]


def final_kernel(row_cuts, *refs):
    own, *parts, signal, out = refs
    rows, width = out.shape
    freq = width // 2
    inverse = 1.0 / signal[...]
    every = sorted({cut for cuts in row_cuts for cut in cuts})
    for start, stop in zip(every, every[1:]):
        total = own[start:stop]
        at = 0
        for cuts in row_cuts:
            for low, high in zip(cuts, cuts[1:]):
                if low <= start and stop <= high:
                    total = total + parts[at][start - low : stop - low]
                at += 1
        denominator = total[:, width:] + inverse
        out[start:stop, :freq] = total[:, :freq] / denominator
        out[start:stop, freq:] = total[:, freq:width] / denominator


def params(mib):
    return pltpu.CompilerParams(vmem_limit_bytes=mib * 1024 * 1024)


def crossed(block, mask):
    size = lax.axis_size("dom")
    return lax.ppermute(block, "dom", [(i, i ^ mask) for i in range(size)])


def on_device(
    particle_fourier,
    defocus,
    particle_offset,
    prior_rotation,
    group_id,
    live_count,
    noise_power,
    signal_power,
    class_refs,
):
    slots, width = particle_fourier.shape
    freq = width // 2
    size = lax.axis_size("dom")
    blocks = size // TEAM
    refs_own = class_refs.reshape(-1, width)
    per = refs_own.shape[0]
    f32 = jnp.float32
    vmem = pl.BlockSpec(memory_space=pltpu.VMEM)
    no_cost = pl.CostEstimate(flops=0, bytes_accessed=0, transcendentals=0)
    much = pl.CostEstimate(flops=16 * 10**9, bytes_accessed=0, transcendentals=0)

    ynb = crossed(particle_fourier, 2)
    anywhere = pl.BlockSpec(memory_space=pl.ANY)
    ynb = crossed(particle_fourier, 2)
    anywhere = pl.BlockSpec(memory_space=pl.ANY)
    ynb = crossed(particle_fourier, 2)
    anywhere = pl.BlockSpec(memory_space=pl.ANY)
    ynb = crossed(particle_fourier, 2)
    refs = [refs_own] + [crossed(refs_own, TEAM * n) for n in range(1, blocks)]
    own_facts = (
        particle_fourier,
        defocus.reshape(1, slots),
        particle_offset.T,
        prior_rotation.reshape(1, slots),
        group_id.reshape(1, slots),
        noise_power,
    )
    own, facts, inverse_noise = pl.pallas_call(
        own_kernel,
        out_shape=(
            jax.ShapeDtypeStruct((slots + 8, width + freq), f32),
            jax.ShapeDtypeStruct((8, 128), f32),
            jax.ShapeDtypeStruct(noise_power.shape, f32),
        ),
        in_specs=[anywhere] * 6 + [pl.BlockSpec(memory_space=pltpu.SMEM)],
        out_specs=(vmem,) * 3,
        scratch_shapes=[pltpu.VMEM(x.shape, x.dtype) for x in own_facts]
        + [pltpu.SemaphoreType.DMA((6,))],
        compiler_params=params(6),
        cost_estimate=no_cost,
        name="own",
    )(*(pltpu.with_memory_space_constraint(x, pltpu.HBM) for x in own_facts), live_count)
    cnb = crossed(own, 1)
    lanes = 3 * slots
    bf16 = jnp.bfloat16

    def shaped(rows, cols, dtype=f32):
        return jax.ShapeDtypeStruct((rows, cols), dtype)

    block_shapes = [shaped(SHIFTS * per, width, bf16)] * 2 + [shaped(per, freq, bf16)] * 2
    score_shape = jax.ShapeDtypeStruct((SHIFTS, per, lanes), f32)

    def call(kernel, operands, out_shape, name, mib, cost=None, scratch=()):
        return pl.pallas_call(
            kernel,
            cost_estimate=cost,
            out_shape=tuple(out_shape),
            in_specs=[vmem] * len(operands),
            out_specs=(vmem,) * len(out_shape),
            scratch_shapes=list(scratch),
            compiler_params=params(mib),
            name=name,
        )(*operands)

    prepared = pl.pallas_call(
        own_refs_kernel,
        out_shape=tuple(block_shapes),
        in_specs=[anywhere] * 2,
        out_specs=(vmem,) * 4,
        scratch_shapes=[pltpu.VMEM(refs_own.shape, f32), pltpu.SemaphoreType.DMA],
        compiler_params=params(8),
        name="own_refs",
    )(pltpu.with_memory_space_constraint(refs_own, pltpu.HBM), facts)
    ynb_prepared = pl.pallas_call(
        neighbour_kernel,
        out_shape=jax.ShapeDtypeStruct((slots + 8, width + freq), f32),
        in_specs=[vmem] * 3 + [anywhere],
        out_specs=vmem,
        compiler_params=params(6),
        cost_estimate=no_cost,
        name="neighbour",
    )(ynb, crossed(facts, 2), inverse_noise, prepared[2])
    cynb = crossed(ynb_prepared, 1)

    order = [*range(2, blocks - 1), 1, blocks - 1]
    wait = ynb_prepared
    by_block = {0: prepared}
    for n in order:
        by_block[n] = pl.pallas_call(
            refs_kernel,
            out_shape=tuple(block_shapes),
            in_specs=[vmem, anywhere],
            out_specs=(vmem,) * 4,
            compiler_params=params(6),
            cost_estimate=much if n == order[-1] else None,
            name="refs",
        )(refs[n], wait)
        wait = by_block[n][2]
    prepared = [x for n in range(blocks) for x in by_block[n]]
    deep = 3 * MAIN + 128
    top_rows = -(-blocks // 8) * 8
    outs = call(
        lambda *a: late_kernel(blocks, *a),
        (own, cnb, ynb_prepared, cynb, *prepared),
        [score_shape] * blocks
        + [shaped(deep, width, bf16), shaped(deep, freq, bf16)]
        + [shaped(8, 384), shaped(top_rows, 384)],
        "late",
        8 + 2 * blocks,
        scratch=[pltpu.VMEM((lanes - MAIN, width), f32)],
    )
    weights, (y, power, stats, tops) = outs[:blocks], outs[blocks:]

    team = [stats] + [crossed(stats, n) for n in range(1, TEAM)]

    def sums(n, cuts, last=False, waits=()):
        out_shape = [shaped(b - a, width + freq) for a, b in zip(cuts, cuts[1:])]
        if last:
            out_shape.append(shaped(2, slots))
        return pl.pallas_call(
            lambda *a: sum_kernel(n, cuts, last, len(waits), *a),
            out_shape=tuple(out_shape),
            in_specs=[vmem] * (TEAM + 1) + [anywhere] * len(waits) + [vmem] * 3,
            out_specs=(vmem,) * len(out_shape),
            compiler_params=params(8),
            name="sums",
        )(*team, tops, *waits, weights[n], y, power)

    def combined(mine, other, wait):
        return pl.pallas_call(
            add_kernel,
            out_shape=jax.ShapeDtypeStruct(mine.shape, f32),
            in_specs=[vmem] * 2 + [anywhere],
            out_specs=vmem,
            compiler_params=params(4),
            name="combined",
        )(mine, other, wait)

    def gated(arrays, cost):
        return pl.pallas_call(
            lambda *a: None,
            out_shape=tuple(jax.ShapeDtypeStruct(x.shape, x.dtype) for x in arrays),
            in_specs=[anywhere] * len(arrays),
            out_specs=(anywhere,) * len(arrays),
            input_output_aliases={n: n for n in range(len(arrays))},
            compiler_params=params(1),
            cost_estimate=cost,
            name="gate",
        )(*arrays)

    whole, cut = (0, per), (0, per // 2, per)
    far = []
    waits = []
    for n in range(2, blocks, 2):
        handed = sums(n + 1, cut)
        mine = sums(n, cut, waits=handed[:1])
        if n == 2:
            (near,) = sums(1, whole, waits=mine[:1])
        joined = [combined(x, crossed(y, TEAM), near) for x, y in zip(mine, handed)]
        far.extend(crossed(x, TEAM * n) for x in joined)
        waits.extend(joined)
    own_part, shift = sums(0, whole, last=True, waits=waits)
    far = [crossed(near, TEAM), *gated(far, much)]
    row_cuts = [whole] + [cut] * (len(far) // 2)

    refs_new = pl.pallas_call(
        lambda *a: final_kernel(row_cuts, *a),
        out_shape=jax.ShapeDtypeStruct((per, width), f32),
        in_specs=[vmem] * (len(far) + 2),
        out_specs=vmem,
        compiler_params=params(2 + blocks),
        name="update",
    )(own_part, *far, signal_power.reshape(1, freq))

    return (shift.T, refs_new.reshape(class_refs.shape))


def solution(mesh):
    in_specs = (
        P(("groups", "dom"), None),
        P(("groups", "dom")),
        P(("groups", "dom"), None),
        P(("groups", "dom")),
        P(("groups", "dom")),
        P(("groups", "dom")),
        P("groups", None),
        P("groups"),
        P(("groups", "dom"), None, None),
    )
    out_specs = (P(("groups", "dom"), None), P(("groups", "dom"), None, None))
    return jax.shard_map(
        on_device, mesh=mesh, in_specs=in_specs, out_specs=out_specs, check_vma=False
    )
```

```python
import math

import jax
import jax.numpy as jnp
from jax import lax
from jax.experimental import pallas as pl
from jax.experimental.pallas import tpu as pltpu
from jax.sharding import PartitionSpec as P

ROT = 16
SIDE = 3
BOX = 128
FY = 32
SHIFTS = 9
TEAM = 4
PRIOR = 2.0
CTF_SIZE = math.hypot(0.995, 0.1)
CTF_TURN = math.atan2(0.1, 0.995)
SINE = (
    9.99999976e-01,
    -1.66666476e-01,
    8.33289854e-03,
    -1.98008185e-04,
    2.59032780e-06,
)
TWO_PI = 2.0 * math.pi
PI_A = 3.140625
PI_B = 0.0009670257568359375
PI_C = math.pi - PI_A - PI_B
HIGHEST = lax.Precision.HIGHEST
GRID = tuple((t // SIDE - SIDE // 2, t % SIDE - SIDE // 2) for t in range(SHIFTS))


def half_turn_sine(x):
    s = x * x
    p = SINE[4]
    for c in SINE[3::-1]:
        p = p * s + c
    return x * p


def turn_cos(turns):
    t = jnp.abs(turns - jnp.round(turns))
    return half_turn_sine(TWO_PI * (0.25 - t))


def turn_sin(turns):
    return turn_cos(turns - 0.25)


def freq_rows(width, rows):
    f = lax.broadcasted_iota(jnp.int32, (rows, width), 1)
    kx = (f // FY).astype(jnp.float32)
    ky = (f % FY - FY // 2).astype(jnp.float32)
    return kx, ky


def dot_nt(a, b):
    return lax.dot_general(
        a, b, (((1,), (1,)), ((), ())), preferred_element_type=jnp.float32
    )


def dot_nn(a, b):
    return lax.dot_general(
        a, b, (((1,), (0,)), ((), ())), preferred_element_type=jnp.float32
    )


def exact_dot_nn(a, b):
    return lax.dot_general(
        a, b, (((1,), (0,)), ((), ())), precision=HIGHEST, preferred_element_type=jnp.float32
    )


def halves(x):
    high = x.astype(jnp.bfloat16)
    return high, (x - high.astype(jnp.float32)).astype(jnp.bfloat16)


MAIN = 256


def deep_at(part, row):
    return MAIN * part + row if row < MAIN else 3 * MAIN + 32 * part + row - MAIN


def deep_lanes(x):
    rows, lanes = x.shape
    left = lanes - MAIN
    high, low = halves(x[:, :MAIN])
    tail = jnp.concatenate([x[:, MAIN:], jnp.zeros((rows, 128 - left), jnp.float32)], axis=1)
    tail_high = tail.astype(jnp.bfloat16).astype(jnp.float32)
    tail_low = tail - tail_high
    mixed = tail_high + pltpu.roll(tail_high, left, 1) + pltpu.roll(tail_low, 2 * left, 1)
    return jnp.concatenate([high, high, low, mixed.astype(jnp.bfloat16)], axis=1)


def grid_phases(width):
    kx, ky = freq_rows(width, 1)
    out = []
    for t, (gx, gy) in enumerate(GRID):
        if t < SHIFTS // 2:
            m = (kx * gx + ky * gy) * (1.0 / BOX)
            out.append((turn_cos(m), turn_sin(m)))
    return out


def phase_of(phases, t):
    mid = SHIFTS // 2
    if t < mid:
        return phases[t]
    c, s = phases[SHIFTS - 1 - t]
    return c, -s


def prepared_rows(src, facts, inverse_noise, out):
    slots, width = src.shape
    freq = width // 2
    columns = jnp.concatenate([facts, jnp.zeros((120, 128), jnp.float32)], axis=0).T[:slots]
    focus = columns[:, 0:1]
    off_x = columns[:, 1:2]
    off_y = columns[:, 2:3]
    group_col = columns[:, 4:5]

    kx, ky = freq_rows(freq, 1)
    chi = focus * ((kx * kx + ky * ky) * (1.0 / 1024.0))
    k = jnp.round(chi * (1.0 / math.pi))
    rest_angle = ((chi - k * PI_A) - k * PI_B) - k * PI_C
    shifted_angle = rest_angle + CTF_TURN
    over = shifted_angle > (0.5 * math.pi)
    folded = jnp.where(over, math.pi - shifted_angle, shifted_angle)
    parity = 0.5 * k
    sign = (parity - jnp.floor(parity)) * (4.0 * CTF_SIZE) - CTF_SIZE
    ctf = half_turn_sine(folded) * sign
    kx0, ky0 = freq_rows(128, 1)
    m = (kx0 * off_x + ky0 * off_y) * (1.0 / BOX)
    pc, ps = turn_cos(m), turn_sin(m)
    step = off_x * ((128 // FY) / BOX) + jnp.zeros((slots, 128), jnp.float32)
    sc, ss = turn_cos(step), turn_sin(step)

    total = inverse_noise.shape[0]
    onehot = (
        group_col == lax.broadcasted_iota(jnp.int32, (slots, total), 1).astype(jnp.float32)
    ).astype(jnp.float32)
    noise_rows = exact_dot_nn(onehot, inverse_noise)
    scaled = ctf * noise_rows
    out[:slots, width:] = ctf * scaled
    for n in range(freq // 128):
        part = slice(128 * n, 128 * (n + 1))
        twin = slice(freq + 128 * n, freq + 128 * (n + 1))
        co = pc * scaled[:, part]
        si = ps * scaled[:, part]
        pc, ps = pc * sc - ps * ss, ps * sc + pc * ss
        xr, xi = src[:, part], src[:, twin]
        out[:slots, part] = xr * co - xi * si
        out[:slots, twin] = xr * si + xi * co
    out[slots:, :128] = facts
    out[slots:, 128:] = jnp.zeros((8, width + freq - 128), jnp.float32)


def own_kernel(
    src_at, focus_at, offsets_at, prior_at, group_at, noise_at, live_count, out, facts_out,
    inverse_out, src, focus, offsets, prior, group, noise, sems
):
    moves = (
        (focus_at, focus), (offsets_at, offsets), (prior_at, prior), (group_at, group),
        (noise_at, noise), (src_at, src),
    )
    copies = [pltpu.make_async_copy(x, y, sems.at[n]) for n, (x, y) in enumerate(moves)]
    for copy in copies:
        copy.start()
    slots = src.shape[0]
    facts_out[...] = jnp.zeros_like(facts_out)
    slot = lax.broadcasted_iota(jnp.int32, (1, slots), 1)
    for copy in copies:
        copy.wait()
    facts_out[5:6, :slots] = (slot < live_count[0]).astype(jnp.float32)
    facts_out[0:1, :slots] = focus[...]
    facts_out[1:3, :slots] = offsets[...].astype(jnp.float32)
    facts_out[3:4, :slots] = prior[...].astype(jnp.float32)
    facts_out[4:5, :slots] = group[...].astype(jnp.float32)
    inverse = 1.0 / noise[...]
    inverse_out[...] = inverse
    prepared_rows(src, facts_out[...], inverse, out)


def neighbour_kernel(src, facts, inverse_noise, wait, out):
    prepared_rows(src, facts[...], inverse_noise[...], out)


def team_order(own, cnb, ynb, cynb):
    for even in (True, False):
        for first in (True, False):
            heavy, light = ((own, ynb), (cnb, cynb)) if even else ((cnb, cynb), (own, ynb))
            if not first:
                heavy, light = heavy[::-1], light[::-1]
            yield even, first, heavy, light


def place_rows(even, first, parts, y_out, power_out, left_out):
    width = y_out.shape[1]
    slots = parts[0].shape[0] - 8
    half = slots // 2
    cut = MAIN - 2 * slots - half

    def place(src, start, stop, to):
        for cols, out in ((slice(0, width), y_out), (slice(width, None), power_out)):
            pair = halves(src[start:stop, cols])
            for part in range(3):
                row = deep_at(part, to)
                out[row : row + stop - start] = pair[part % 2]

    for is_even, is_first, heavy, light in team_order(*parts):

        @pl.when(jnp.logical_and(even == is_even, first == is_first))
        def _(heavy=heavy, light=light):
            place(heavy[0], 0, slots, 0)
            place(heavy[1], 0, slots, slots)
            place(light[0], 0, half, 2 * slots)
            place(light[1], 0, cut, 2 * slots + half)
            place(light[1], cut, half, MAIN)
            left_out[...] = light[1][cut:half, :width]


def lane_index():
    return lax.broadcasted_iota(jnp.int32, (8, 128), 1)


def row_facts(even, first, parts):
    lane = lane_index()
    own, cnb, ynb, cynb = (x[x.shape[0] - 8 :, :128] for x in parts)
    heavy = (jnp.where(even, own, cnb), jnp.where(even, ynb, cynb))
    light = (jnp.where(even, cnb, own), jnp.where(even, cynb, ynb))
    a0, b0 = (jnp.where(first, x[0], x[1]) for x in (heavy, light))
    a1, b1 = (jnp.where(first, x[1], x[0]) for x in (heavy, light))
    a1 = pltpu.roll(a1, 96, 1)
    b1 = pltpu.roll(b1, 112, 1)
    middle = jnp.where(lane < 64, a1, jnp.where(lane < 112, pltpu.roll(b0, 64, 1), b1))
    return jnp.concatenate([jnp.where(lane < 96, a0, a1), middle, b1], axis=1)


def own_lanes(even, first, x):
    lane = lane_index()
    a, b, c = x[:, :128], x[:, 128:256], x[:, 256:]
    heavy_far = jnp.where(lane < 32, pltpu.roll(a, 32, 1), pltpu.roll(b, 32, 1))
    light_far = jnp.where(lane < 16, pltpu.roll(b, 16, 1), pltpu.roll(c, 16, 1))
    light = jnp.where(first, pltpu.roll(b, 64, 1), light_far)
    heavy = jnp.where(first, a, heavy_far)
    return jnp.where(even, heavy, jnp.where(lane < 48, light, 0.0))


def place_of_device():
    me = lax.axis_index("dom")
    return me % 2 == 0, (me // 2) % 2 == 0


def prior_rows(facts, per, lanes):
    r = (lax.broadcasted_iota(jnp.int32, (per, lanes), 0) % ROT).astype(jnp.float32)
    return PRIOR * turn_cos((r - facts[3:4, :lanes]) * (1.0 / ROT))


def prepare_refs(ref, phases, r_high, r_low, q_high, q_low):
    per, width = ref.shape
    freq = width // 2
    rr, ri = ref[:, :freq], ref[:, freq:]
    mid = SHIFTS // 2

    def store(t, re, im):
        rows = slice(t * per, (t + 1) * per)
        r_high[rows, :freq], r_low[rows, :freq] = halves(re)
        r_high[rows, freq:], r_low[rows, freq:] = halves(im)

    store(mid, rr, ri)
    for t in range(mid):
        c, s = phases[t]
        a, b, d, e = rr * c, ri * s, ri * c, rr * s
        store(t, a + b, d - e)
        store(SHIFTS - 1 - t, a - b, d + e)
    q_high[...], q_low[...] = halves(rr * rr + ri * ri)


def terms(high, low):
    return jnp.concatenate([high, high, low], axis=1)


def terms_left(high, low):
    return jnp.concatenate([high, low, high], axis=1)


def shifted_rows(rows, phases):
    freq = rows.shape[1] // 2
    re, im = rows[:, :freq], rows[:, freq:]
    mid = SHIFTS // 2
    out = [None] * SHIFTS
    out[mid] = rows
    for t in range(mid):
        c, s = phases[t]
        a, b, d, e = re * c, im * s, im * c, re * s
        out[t] = jnp.concatenate([a - b, e + d], axis=1)
        out[SHIFTS - 1 - t] = jnp.concatenate([a + b, d - e], axis=1)
    return jnp.concatenate(out, axis=0)


def weigh(score, e_out):
    top = jnp.max(jnp.max(score, axis=0), axis=0, keepdims=True)
    e = jnp.exp(score - top[None])
    e_out[...] = e
    side = SIDE // 2
    by_x = [sum(e[SIDE * x + y] for y in range(SIDE)) for x in range(SIDE)]
    by_y = [sum(e[SIDE * x + y] for x in range(SIDE)) for y in range(SIDE)]
    sums = [sum(by_x)]
    for by in (by_x, by_y):
        sums.append(sum(by[k] * float(k - side) for k in range(SIDE) if k != side))
    return top, [jnp.sum(x, axis=0, keepdims=True) for x in sums]


def joined_sums(tops, sums):
    top = tops[0]
    for other in tops[1:]:
        top = jnp.maximum(top, other)
    factors = [jnp.exp(other - top) for other in tops]
    return top, [sum(f * x for f, x in zip(factors, column)) for column in zip(*sums)]


def own_refs_kernel(own_at, wait, *rest):
    *prepared, own, sem = rest
    copy = pltpu.make_async_copy(own_at, own, sem)
    copy.start()
    phases = grid_phases(own.shape[1] // 2)
    copy.wait()
    prepare_refs(own, phases, *prepared)


def refs_kernel(ref, wait, *prepared):
    prepare_refs(ref, grid_phases(ref.shape[1] // 2), *prepared)


def late_kernel(blocks, own, cnb, ynb, cynb, *rest):
    prepared, rest = rest[: 4 * blocks], rest[4 * blocks :]
    e_outs, rest = rest[:blocks], rest[blocks:]
    y_out, power_out, stats_out, tops_out, left_rows = rest
    per, lanes = e_outs[0].shape[1:]
    freq = power_out.shape[1]
    left = lanes - MAIN
    parts = (own, cnb, ynb, cynb)
    even, first = place_of_device()
    place_rows(even, first, parts, y_out, power_out, left_rows)
    facts = row_facts(even, first, parts)
    empty = deep_at(2, lanes)
    for out in (y_out, power_out):
        out[empty:] = jnp.zeros_like(out[empty:])
    stats_out[...] = jnp.zeros_like(stats_out)
    tops_out[...] = jnp.zeros_like(tops_out)

    def rows(out, part, size):
        at = deep_at(part, 0)
        main = out[at : at + MAIN]
        at = deep_at(part, MAIN)
        return jnp.concatenate([main, out[at : at + left]], axis=0)[:size]

    q_terms = [terms_left(prepared[4 * n + 2][...], prepared[4 * n + 3][...]) for n in range(blocks)]
    quad = dot_nt(
        jnp.concatenate(q_terms, axis=0), terms(*(rows(power_out, k, lanes) for k in (0, 1)))
    )
    prior = prior_rows(facts, per, lanes)
    mid = slice(SHIFTS // 2 * per, (SHIFTS // 2 + 1) * per)
    r_terms = [terms_left(prepared[4 * n][mid], prepared[4 * n + 1][mid]) for n in range(blocks)]
    moved = terms(*halves(shifted_rows(left_rows[...], grid_phases(freq))))
    far = dot_nt(jnp.concatenate(r_terms, axis=0), moved)
    far = jnp.concatenate([far, jnp.zeros((blocks * per, 384 - SHIFTS * left), jnp.float32)], axis=1)
    step = 128 // left
    far = [
        pltpu.roll(far[:, 128 * (t // step) : 128 * (t // step + 1)], -left * (t % step) % 128, 1)
        for t in range(SHIFTS)
    ]
    main_terms = terms(*(rows(y_out, k, MAIN) for k in (0, 1)))
    tops, sums = [], []
    for n in range(blocks):
        part = slice(n * per, (n + 1) * per)
        base = prior - 0.5 * quad[part]
        score = dot_nt(terms_left(prepared[4 * n][...], prepared[4 * n + 1][...]), main_terms)
        score = score.reshape(SHIFTS, per, MAIN)
        tail = jnp.stack([x[part, :left] for x in far])
        score = jnp.concatenate([score, tail], axis=2) + base[None]
        top, sums_here = weigh(score, e_outs[n])
        tops_out[n : n + 1, :lanes] = top
        tops.append(top)
        sums.append(sums_here)
    top, sums = joined_sums(tops, sums)
    for k, row in enumerate((top, *sums, facts[5:6, :lanes])):
        stats_out[k : k + 1, :lanes] = row


def sum_kernel(n, cuts, last, waits, *rest):
    team, tops, rest = rest[:TEAM], rest[TEAM], rest[TEAM + 1 + waits :]
    e_ref, y_ref, power_ref, *outs = rest
    per, lanes = e_ref.shape[1:]
    width = y_ref.shape[1]
    freq = width // 2
    team = [x[...] for x in team]
    top, (mass, *move) = joined_sums(
        [x[0:1] for x in team], [[x[k : k + 1] for k in (1, 2, 3)] for x in team]
    )
    live = team[0][4:5] / mass
    gain = (jnp.exp(tops[n : n + 1] - top) * live)[:, :lanes]
    if last:
        shift_out = outs.pop()
        move = [x * live for x in move] + [jnp.zeros((6, live.shape[1]), jnp.float32)]
        move = own_lanes(*place_of_device(), jnp.concatenate(move, axis=0))
        shift_out[...] = move[:2, : shift_out.shape[1]]
    w = e_ref[...] * gain[None]
    flat = dot_nn(deep_lanes(w.reshape(SHIFTS * per, lanes)), y_ref[...])
    weight = dot_nn(deep_lanes(jnp.sum(w, axis=0)), power_ref[...])
    phases = grid_phases(freq)
    mid = SHIFTS // 2

    def block(t):
        return flat[t * per : (t + 1) * per, :freq], flat[t * per : (t + 1) * per, freq:]

    re, im = block(mid)
    for t in range(mid):
        c, s = phases[t]
        ar, ai = block(t)
        br, bi = block(SHIFTS - 1 - t)
        re = re + (ar + br) * c - (ai - bi) * s
        im = im + (ar - br) * s + (ai + bi) * c
    for start, stop, out in zip(cuts, cuts[1:], outs):
        part = slice(start, stop)
        out[:, :freq] = re[part]
        out[:, freq:width] = im[part]
        out[:, width:] = weight[part]


def add_kernel(a, b, wait, out):
    out[...] = a[...] + b[...]


def final_kernel(row_cuts, *refs):
    own, *parts, signal, out = refs
    rows, width = out.shape
    freq = width // 2
    inverse = 1.0 / signal[...]
    every = sorted({cut for cuts in row_cuts for cut in cuts})
    for start, stop in zip(every, every[1:]):
        total = own[start:stop]
        at = 0
        for cuts in row_cuts:
            for low, high in zip(cuts, cuts[1:]):
                if low <= start and stop <= high:
                    total = total + parts[at][start - low : stop - low]
                at += 1
        denominator = total[:, width:] + inverse
        out[start:stop, :freq] = total[:, :freq] / denominator
        out[start:stop, freq:] = total[:, freq:width] / denominator


def params(mib):
    return pltpu.CompilerParams(vmem_limit_bytes=mib * 1024 * 1024)


def crossed(block, mask):
    size = lax.axis_size("dom")
    return lax.ppermute(block, "dom", [(i, i ^ mask) for i in range(size)])


def on_device(
    particle_fourier,
    defocus,
    particle_offset,
    prior_rotation,
    group_id,
    live_count,
    noise_power,
    signal_power,
    class_refs,
):
    slots, width = particle_fourier.shape
    freq = width // 2
    size = lax.axis_size("dom")
    blocks = size // TEAM
    refs_own = class_refs.reshape(-1, width)
    per = refs_own.shape[0]
    f32 = jnp.float32
    vmem = pl.BlockSpec(memory_space=pltpu.VMEM)
    no_cost = pl.CostEstimate(flops=0, bytes_accessed=0, transcendentals=0)
    much = pl.CostEstimate(flops=16 * 10**9, bytes_accessed=0, transcendentals=0)

    ynb = crossed(particle_fourier, 2)
    anywhere = pl.BlockSpec(memory_space=pl.ANY)
    ynb = crossed(particle_fourier, 2)
    anywhere = pl.BlockSpec(memory_space=pl.ANY)
    ynb = crossed(particle_fourier, 2)
    anywhere = pl.BlockSpec(memory_space=pl.ANY)
    ynb = crossed(particle_fourier, 2)
    refs = [refs_own] + [crossed(refs_own, TEAM * n) for n in range(1, blocks)]
    own_facts = (
        particle_fourier,
        defocus.reshape(1, slots),
        particle_offset.T,
        prior_rotation.reshape(1, slots),
        group_id.reshape(1, slots),
        noise_power,
    )
    own, facts, inverse_noise = pl.pallas_call(
        own_kernel,
        out_shape=(
            jax.ShapeDtypeStruct((slots + 8, width + freq), f32),
            jax.ShapeDtypeStruct((8, 128), f32),
            jax.ShapeDtypeStruct(noise_power.shape, f32),
        ),
        in_specs=[anywhere] * 6 + [pl.BlockSpec(memory_space=pltpu.SMEM)],
        out_specs=(vmem,) * 3,
        scratch_shapes=[pltpu.VMEM(x.shape, x.dtype) for x in own_facts]
        + [pltpu.SemaphoreType.DMA((6,))],
        compiler_params=params(6),
        cost_estimate=no_cost,
        name="own",
    )(*(pltpu.with_memory_space_constraint(x, pltpu.HBM) for x in own_facts), live_count)
    cnb = crossed(own, 1)
    lanes = 3 * slots
    bf16 = jnp.bfloat16

    def shaped(rows, cols, dtype=f32):
        return jax.ShapeDtypeStruct((rows, cols), dtype)

    block_shapes = [shaped(SHIFTS * per, width, bf16)] * 2 + [shaped(per, freq, bf16)] * 2
    score_shape = jax.ShapeDtypeStruct((SHIFTS, per, lanes), f32)

    def call(kernel, operands, out_shape, name, mib, cost=None, scratch=()):
        return pl.pallas_call(
            kernel,
            cost_estimate=cost,
            out_shape=tuple(out_shape),
            in_specs=[vmem] * len(operands),
            out_specs=(vmem,) * len(out_shape),
            scratch_shapes=list(scratch),
            compiler_params=params(mib),
            name=name,
        )(*operands)

    prepared = pl.pallas_call(
        own_refs_kernel,
        out_shape=tuple(block_shapes),
        in_specs=[anywhere] * 2,
        out_specs=(vmem,) * 4,
        scratch_shapes=[pltpu.VMEM(refs_own.shape, f32), pltpu.SemaphoreType.DMA],
        compiler_params=params(8),
        name="own_refs",
    )(pltpu.with_memory_space_constraint(refs_own, pltpu.HBM), facts)
    ynb_prepared = pl.pallas_call(
        neighbour_kernel,
        out_shape=jax.ShapeDtypeStruct((slots + 8, width + freq), f32),
        in_specs=[vmem] * 3 + [anywhere],
        out_specs=vmem,
        compiler_params=params(6),
        cost_estimate=no_cost,
        name="neighbour",
    )(ynb, crossed(facts, 2), inverse_noise, prepared[2])
    cynb = crossed(ynb_prepared, 1)

    order = [*range(blocks - 1, 2, -1), 1, 2]
    wait = ynb_prepared
    by_block = {0: prepared}
    for n in order:
        by_block[n] = pl.pallas_call(
            refs_kernel,
            out_shape=tuple(block_shapes),
            in_specs=[vmem, anywhere],
            out_specs=(vmem,) * 4,
            compiler_params=params(6),
            cost_estimate=much if n == order[-1] else None,
            name="refs",
        )(refs[n], wait)
        wait = by_block[n][2]
    prepared = [x for n in range(blocks) for x in by_block[n]]
    deep = 3 * MAIN + 128
    top_rows = -(-blocks // 8) * 8
    outs = call(
        lambda *a: late_kernel(blocks, *a),
        (own, cnb, ynb_prepared, cynb, *prepared),
        [score_shape] * blocks
        + [shaped(deep, width, bf16), shaped(deep, freq, bf16)]
        + [shaped(8, 384), shaped(top_rows, 384)],
        "late",
        8 + 2 * blocks,
        scratch=[pltpu.VMEM((lanes - MAIN, width), f32)],
    )
    weights, (y, power, stats, tops) = outs[:blocks], outs[blocks:]

    team = [stats] + [crossed(stats, n) for n in range(1, TEAM)]

    def sums(n, cuts, last=False, waits=()):
        out_shape = [shaped(b - a, width + freq) for a, b in zip(cuts, cuts[1:])]
        if last:
            out_shape.append(shaped(2, slots))
        return pl.pallas_call(
            lambda *a: sum_kernel(n, cuts, last, len(waits), *a),
            out_shape=tuple(out_shape),
            in_specs=[vmem] * (TEAM + 1) + [anywhere] * len(waits) + [vmem] * 3,
            out_specs=(vmem,) * len(out_shape),
            compiler_params=params(8),
            name="sums",
        )(*team, tops, *waits, weights[n], y, power)

    def combined(mine, other, wait):
        return pl.pallas_call(
            add_kernel,
            out_shape=jax.ShapeDtypeStruct(mine.shape, f32),
            in_specs=[vmem] * 2 + [anywhere],
            out_specs=vmem,
            compiler_params=params(4),
            name="combined",
        )(mine, other, wait)

    def gated(arrays, cost):
        return pl.pallas_call(
            lambda *a: None,
            out_shape=tuple(jax.ShapeDtypeStruct(x.shape, x.dtype) for x in arrays),
            in_specs=[anywhere] * len(arrays),
            out_specs=(anywhere,) * len(arrays),
            input_output_aliases={n: n for n in range(len(arrays))},
            compiler_params=params(1),
            cost_estimate=cost,
            name="gate",
        )(*arrays)

    whole = (0, per)
    far = []
    waits = []
    for n in range(2, blocks, 2):
        handed = sums(n + 1, whole)
        mine = sums(n, whole, waits=handed)
        if n == 2:
            (near,) = sums(1, whole, waits=mine[:1])
        joined = [combined(x, crossed(y, TEAM), near) for x, y in zip(mine, handed)]
        far.extend(crossed(x, TEAM * n) for x in joined)
        waits.extend(joined)
    own_part, shift = sums(0, whole, last=True, waits=waits)
    far = [crossed(near, TEAM), *gated(far, much)]
    row_cuts = [whole] * len(far)

    refs_new = pl.pallas_call(
        lambda *a: final_kernel(row_cuts, *a),
        out_shape=jax.ShapeDtypeStruct((per, width), f32),
        in_specs=[vmem] * (len(far) + 2),
        out_specs=vmem,
        compiler_params=params(2 + blocks),
        name="update",
    )(own_part, *far, signal_power.reshape(1, freq))

    return (shift.T, refs_new.reshape(class_refs.shape))


def solution(mesh):
    in_specs = (
        P(("groups", "dom"), None),
        P(("groups", "dom")),
        P(("groups", "dom"), None),
        P(("groups", "dom")),
        P(("groups", "dom")),
        P(("groups", "dom")),
        P("groups", None),
        P("groups"),
        P(("groups", "dom"), None, None),
    )
    out_specs = (P(("groups", "dom"), None), P(("groups", "dom"), None, None))
    return jax.shard_map(
        on_device, mesh=mesh, in_specs=in_specs, out_specs=out_specs, check_vma=False
    )
```

```python
import math

import jax
import jax.numpy as jnp
from jax import lax
from jax.experimental import pallas as pl
from jax.experimental.pallas import tpu as pltpu
from jax.sharding import PartitionSpec as P

ROT = 16
SIDE = 3
BOX = 128
FY = 32
SHIFTS = 9
TEAM = 4
PRIOR = 2.0
CTF_SIZE = math.hypot(0.995, 0.1)
CTF_TURN = math.atan2(0.1, 0.995)
SINE = (
    9.99999976e-01,
    -1.66666476e-01,
    8.33289854e-03,
    -1.98008185e-04,
    2.59032780e-06,
)
TWO_PI = 2.0 * math.pi
PI_A = 3.140625
PI_B = 0.0009670257568359375
PI_C = math.pi - PI_A - PI_B
HIGHEST = lax.Precision.HIGHEST
GRID = tuple((t // SIDE - SIDE // 2, t % SIDE - SIDE // 2) for t in range(SHIFTS))


def half_turn_sine(x):
    s = x * x
    p = SINE[4]
    for c in SINE[3::-1]:
        p = p * s + c
    return x * p


def turn_cos(turns):
    t = jnp.abs(turns - jnp.round(turns))
    return half_turn_sine(TWO_PI * (0.25 - t))


def turn_sin(turns):
    return turn_cos(turns - 0.25)


def freq_rows(width, rows):
    f = lax.broadcasted_iota(jnp.int32, (rows, width), 1)
    kx = (f // FY).astype(jnp.float32)
    ky = (f % FY - FY // 2).astype(jnp.float32)
    return kx, ky


def dot_nt(a, b):
    return lax.dot_general(
        a, b, (((1,), (1,)), ((), ())), preferred_element_type=jnp.float32
    )


def dot_nn(a, b):
    return lax.dot_general(
        a, b, (((1,), (0,)), ((), ())), preferred_element_type=jnp.float32
    )


def exact_dot_nn(a, b):
    return lax.dot_general(
        a, b, (((1,), (0,)), ((), ())), precision=HIGHEST, preferred_element_type=jnp.float32
    )


def halves(x):
    high = x.astype(jnp.bfloat16)
    return high, (x - high.astype(jnp.float32)).astype(jnp.bfloat16)


MAIN = 256


def deep_at(part, row):
    return MAIN * part + row if row < MAIN else 3 * MAIN + 32 * part + row - MAIN


def deep_lanes(x):
    rows, lanes = x.shape
    left = lanes - MAIN
    high, low = halves(x[:, :MAIN])
    tail = jnp.concatenate([x[:, MAIN:], jnp.zeros((rows, 128 - left), jnp.float32)], axis=1)
    tail_high = tail.astype(jnp.bfloat16).astype(jnp.float32)
    tail_low = tail - tail_high
    mixed = tail_high + pltpu.roll(tail_high, left, 1) + pltpu.roll(tail_low, 2 * left, 1)
    return jnp.concatenate([high, high, low, mixed.astype(jnp.bfloat16)], axis=1)


def grid_phases(width):
    kx, ky = freq_rows(width, 1)
    out = []
    for t, (gx, gy) in enumerate(GRID):
        if t < SHIFTS // 2:
            m = (kx * gx + ky * gy) * (1.0 / BOX)
            out.append((turn_cos(m), turn_sin(m)))
    return out


def phase_of(phases, t):
    mid = SHIFTS // 2
    if t < mid:
        return phases[t]
    c, s = phases[SHIFTS - 1 - t]
    return c, -s


def prepared_rows(src, facts, inverse_noise, out):
    slots, width = src.shape
    freq = width // 2
    columns = jnp.concatenate([facts, jnp.zeros((120, 128), jnp.float32)], axis=0).T[:slots]
    focus = columns[:, 0:1]
    off_x = columns[:, 1:2]
    off_y = columns[:, 2:3]
    group_col = columns[:, 4:5]

    kx, ky = freq_rows(freq, 1)
    chi = focus * ((kx * kx + ky * ky) * (1.0 / 1024.0))
    k = jnp.round(chi * (1.0 / math.pi))
    rest_angle = ((chi - k * PI_A) - k * PI_B) - k * PI_C
    shifted_angle = rest_angle + CTF_TURN
    over = shifted_angle > (0.5 * math.pi)
    folded = jnp.where(over, math.pi - shifted_angle, shifted_angle)
    parity = 0.5 * k
    sign = (parity - jnp.floor(parity)) * (4.0 * CTF_SIZE) - CTF_SIZE
    ctf = half_turn_sine(folded) * sign
    kx0, ky0 = freq_rows(128, 1)
    m = (kx0 * off_x + ky0 * off_y) * (1.0 / BOX)
    pc, ps = turn_cos(m), turn_sin(m)
    step = off_x * ((128 // FY) / BOX) + jnp.zeros((slots, 128), jnp.float32)
    sc, ss = turn_cos(step), turn_sin(step)

    total = inverse_noise.shape[0]
    onehot = (
        group_col == lax.broadcasted_iota(jnp.int32, (slots, total), 1).astype(jnp.float32)
    ).astype(jnp.float32)
    noise_rows = exact_dot_nn(onehot, inverse_noise)
    scaled = ctf * noise_rows
    out[:slots, width:] = ctf * scaled
    for n in range(freq // 128):
        part = slice(128 * n, 128 * (n + 1))
        twin = slice(freq + 128 * n, freq + 128 * (n + 1))
        co = pc * scaled[:, part]
        si = ps * scaled[:, part]
        pc, ps = pc * sc - ps * ss, ps * sc + pc * ss
        xr, xi = src[:, part], src[:, twin]
        out[:slots, part] = xr * co - xi * si
        out[:slots, twin] = xr * si + xi * co
    out[slots:, :128] = facts
    out[slots:, 128:] = jnp.zeros((8, width + freq - 128), jnp.float32)


def own_kernel(
    src_at, focus_at, offsets_at, prior_at, group_at, noise_at, live_count, out, facts_out,
    inverse_out, src, focus, offsets, prior, group, noise, sems
):
    moves = (
        (focus_at, focus), (offsets_at, offsets), (prior_at, prior), (group_at, group),
        (noise_at, noise), (src_at, src),
    )
    copies = [pltpu.make_async_copy(x, y, sems.at[n]) for n, (x, y) in enumerate(moves)]
    for copy in copies:
        copy.start()
    slots = src.shape[0]
    facts_out[...] = jnp.zeros_like(facts_out)
    slot = lax.broadcasted_iota(jnp.int32, (1, slots), 1)
    for copy in copies:
        copy.wait()
    facts_out[5:6, :slots] = (slot < live_count[0]).astype(jnp.float32)
    facts_out[0:1, :slots] = focus[...]
    facts_out[1:3, :slots] = offsets[...].astype(jnp.float32)
    facts_out[3:4, :slots] = prior[...].astype(jnp.float32)
    facts_out[4:5, :slots] = group[...].astype(jnp.float32)
    inverse = 1.0 / noise[...]
    inverse_out[...] = inverse
    prepared_rows(src, facts_out[...], inverse, out)


def neighbour_kernel(src, facts, inverse_noise, wait, out):
    prepared_rows(src, facts[...], inverse_noise[...], out)


def team_order(own, cnb, ynb, cynb):
    for even in (True, False):
        for first in (True, False):
            heavy, light = ((own, ynb), (cnb, cynb)) if even else ((cnb, cynb), (own, ynb))
            if not first:
                heavy, light = heavy[::-1], light[::-1]
            yield even, first, heavy, light


def place_rows(even, first, parts, y_out, power_out, left_out):
    width = y_out.shape[1]
    slots = parts[0].shape[0] - 8
    half = slots // 2
    cut = MAIN - 2 * slots - half

    def place(src, start, stop, to):
        for cols, out in ((slice(0, width), y_out), (slice(width, None), power_out)):
            pair = halves(src[start:stop, cols])
            for part in range(3):
                row = deep_at(part, to)
                out[row : row + stop - start] = pair[part % 2]

    for is_even, is_first, heavy, light in team_order(*parts):

        @pl.when(jnp.logical_and(even == is_even, first == is_first))
        def _(heavy=heavy, light=light):
            place(heavy[0], 0, slots, 0)
            place(heavy[1], 0, slots, slots)
            place(light[0], 0, half, 2 * slots)
            place(light[1], 0, cut, 2 * slots + half)
            place(light[1], cut, half, MAIN)
            left_out[...] = light[1][cut:half, :width]


def lane_index():
    return lax.broadcasted_iota(jnp.int32, (8, 128), 1)


def row_facts(even, first, parts):
    lane = lane_index()
    own, cnb, ynb, cynb = (x[x.shape[0] - 8 :, :128] for x in parts)
    heavy = (jnp.where(even, own, cnb), jnp.where(even, ynb, cynb))
    light = (jnp.where(even, cnb, own), jnp.where(even, cynb, ynb))
    a0, b0 = (jnp.where(first, x[0], x[1]) for x in (heavy, light))
    a1, b1 = (jnp.where(first, x[1], x[0]) for x in (heavy, light))
    a1 = pltpu.roll(a1, 96, 1)
    b1 = pltpu.roll(b1, 112, 1)
    middle = jnp.where(lane < 64, a1, jnp.where(lane < 112, pltpu.roll(b0, 64, 1), b1))
    return jnp.concatenate([jnp.where(lane < 96, a0, a1), middle, b1], axis=1)


def own_lanes(even, first, x):
    lane = lane_index()
    a, b, c = x[:, :128], x[:, 128:256], x[:, 256:]
    heavy_far = jnp.where(lane < 32, pltpu.roll(a, 32, 1), pltpu.roll(b, 32, 1))
    light_far = jnp.where(lane < 16, pltpu.roll(b, 16, 1), pltpu.roll(c, 16, 1))
    light = jnp.where(first, pltpu.roll(b, 64, 1), light_far)
    heavy = jnp.where(first, a, heavy_far)
    return jnp.where(even, heavy, jnp.where(lane < 48, light, 0.0))


def place_of_device():
    me = lax.axis_index("dom")
    return me % 2 == 0, (me // 2) % 2 == 0


def prior_rows(facts, per, lanes):
    r = (lax.broadcasted_iota(jnp.int32, (per, lanes), 0) % ROT).astype(jnp.float32)
    return PRIOR * turn_cos((r - facts[3:4, :lanes]) * (1.0 / ROT))


def prepare_refs(ref, phases, r_high, r_low, q_high, q_low):
    per, width = ref.shape
    freq = width // 2
    rr, ri = ref[:, :freq], ref[:, freq:]
    mid = SHIFTS // 2

    def store(t, re, im):
        rows = slice(t * per, (t + 1) * per)
        r_high[rows, :freq], r_low[rows, :freq] = halves(re)
        r_high[rows, freq:], r_low[rows, freq:] = halves(im)

    store(mid, rr, ri)
    for t in range(mid):
        c, s = phases[t]
        a, b, d, e = rr * c, ri * s, ri * c, rr * s
        store(t, a + b, d - e)
        store(SHIFTS - 1 - t, a - b, d + e)
    q_high[...], q_low[...] = halves(rr * rr + ri * ri)


def terms(high, low):
    return jnp.concatenate([high, high, low], axis=1)


def terms_left(high, low):
    return jnp.concatenate([high, low, high], axis=1)


def shifted_rows(rows, phases):
    freq = rows.shape[1] // 2
    re, im = rows[:, :freq], rows[:, freq:]
    mid = SHIFTS // 2
    out = [None] * SHIFTS
    out[mid] = rows
    for t in range(mid):
        c, s = phases[t]
        a, b, d, e = re * c, im * s, im * c, re * s
        out[t] = jnp.concatenate([a - b, e + d], axis=1)
        out[SHIFTS - 1 - t] = jnp.concatenate([a + b, d - e], axis=1)
    return jnp.concatenate(out, axis=0)


def weigh(score, e_out):
    top = jnp.max(jnp.max(score, axis=0), axis=0, keepdims=True)
    e = jnp.exp(score - top[None])
    e_out[...] = e
    side = SIDE // 2
    by_x = [sum(e[SIDE * x + y] for y in range(SIDE)) for x in range(SIDE)]
    by_y = [sum(e[SIDE * x + y] for x in range(SIDE)) for y in range(SIDE)]
    sums = [sum(by_x)]
    for by in (by_x, by_y):
        sums.append(sum(by[k] * float(k - side) for k in range(SIDE) if k != side))
    return top, [jnp.sum(x, axis=0, keepdims=True) for x in sums]


def joined_sums(tops, sums):
    top = tops[0]
    for other in tops[1:]:
        top = jnp.maximum(top, other)
    factors = [jnp.exp(other - top) for other in tops]
    return top, [sum(f * x for f, x in zip(factors, column)) for column in zip(*sums)]


def own_refs_kernel(own_at, wait, *rest):
    *prepared, own, sem = rest
    copy = pltpu.make_async_copy(own_at, own, sem)
    copy.start()
    phases = grid_phases(own.shape[1] // 2)
    copy.wait()
    prepare_refs(own, phases, *prepared)


def refs_kernel(ref, wait, *prepared):
    prepare_refs(ref, grid_phases(ref.shape[1] // 2), *prepared)


def late_kernel(blocks, own, cnb, ynb, cynb, *rest):
    prepared, rest = rest[: 4 * blocks], rest[4 * blocks :]
    e_outs, rest = rest[:blocks], rest[blocks:]
    y_out, power_out, stats_out, tops_out, left_rows = rest
    per, lanes = e_outs[0].shape[1:]
    freq = power_out.shape[1]
    left = lanes - MAIN
    parts = (own, cnb, ynb, cynb)
    even, first = place_of_device()
    place_rows(even, first, parts, y_out, power_out, left_rows)
    facts = row_facts(even, first, parts)
    empty = deep_at(2, lanes)
    for out in (y_out, power_out):
        out[empty:] = jnp.zeros_like(out[empty:])
    stats_out[...] = jnp.zeros_like(stats_out)
    tops_out[...] = jnp.zeros_like(tops_out)

    def rows(out, part, size):
        at = deep_at(part, 0)
        main = out[at : at + MAIN]
        at = deep_at(part, MAIN)
        return jnp.concatenate([main, out[at : at + left]], axis=0)[:size]

    q_terms = [terms_left(prepared[4 * n + 2][...], prepared[4 * n + 3][...]) for n in range(blocks)]
    quad = dot_nt(
        jnp.concatenate(q_terms, axis=0), terms(*(rows(power_out, k, lanes) for k in (0, 1)))
    )
    prior = prior_rows(facts, per, lanes)
    mid = slice(SHIFTS // 2 * per, (SHIFTS // 2 + 1) * per)
    r_terms = [terms_left(prepared[4 * n][mid], prepared[4 * n + 1][mid]) for n in range(blocks)]
    moved = terms(*halves(shifted_rows(left_rows[...], grid_phases(freq))))
    far = dot_nt(jnp.concatenate(r_terms, axis=0), moved)
    far = jnp.concatenate([far, jnp.zeros((blocks * per, 384 - SHIFTS * left), jnp.float32)], axis=1)
    step = 128 // left
    far = [
        pltpu.roll(far[:, 128 * (t // step) : 128 * (t // step + 1)], -left * (t % step) % 128, 1)
        for t in range(SHIFTS)
    ]
    main_terms = terms(*(rows(y_out, k, MAIN) for k in (0, 1)))
    tops, sums = [], []
    for n in range(blocks):
        part = slice(n * per, (n + 1) * per)
        base = prior - 0.5 * quad[part]
        score = dot_nt(terms_left(prepared[4 * n][...], prepared[4 * n + 1][...]), main_terms)
        score = score.reshape(SHIFTS, per, MAIN)
        tail = jnp.stack([x[part, :left] for x in far])
        score = jnp.concatenate([score, tail], axis=2) + base[None]
        top, sums_here = weigh(score, e_outs[n])
        tops_out[n : n + 1, :lanes] = top
        tops.append(top)
        sums.append(sums_here)
    top, sums = joined_sums(tops, sums)
    for k, row in enumerate((top, *sums, facts[5:6, :lanes])):
        stats_out[k : k + 1, :lanes] = row


def sum_kernel(n, cuts, last, waits, *rest):
    team, tops, rest = rest[:TEAM], rest[TEAM], rest[TEAM + 1 + waits :]
    e_ref, y_ref, power_ref, *outs = rest
    per, lanes = e_ref.shape[1:]
    width = y_ref.shape[1]
    freq = width // 2
    team = [x[...] for x in team]
    top, (mass, *move) = joined_sums(
        [x[0:1] for x in team], [[x[k : k + 1] for k in (1, 2, 3)] for x in team]
    )
    live = team[0][4:5] / mass
    gain = (jnp.exp(tops[n : n + 1] - top) * live)[:, :lanes]
    if last:
        shift_out = outs.pop()
        move = [x * live for x in move] + [jnp.zeros((6, live.shape[1]), jnp.float32)]
        move = own_lanes(*place_of_device(), jnp.concatenate(move, axis=0))
        shift_out[...] = move[:2, : shift_out.shape[1]]
    w = e_ref[...] * gain[None]
    flat = dot_nn(deep_lanes(w.reshape(SHIFTS * per, lanes)), y_ref[...])
    weight = dot_nn(deep_lanes(jnp.sum(w, axis=0)), power_ref[...])
    phases = grid_phases(freq)
    mid = SHIFTS // 2

    def block(t):
        return flat[t * per : (t + 1) * per, :freq], flat[t * per : (t + 1) * per, freq:]

    re, im = block(mid)
    for t in range(mid):
        c, s = phases[t]
        ar, ai = block(t)
        br, bi = block(SHIFTS - 1 - t)
        re = re + (ar + br) * c - (ai - bi) * s
        im = im + (ar - br) * s + (ai + bi) * c
    for start, stop, out in zip(cuts, cuts[1:], outs):
        part = slice(start, stop)
        out[:, :freq] = re[part]
        out[:, freq:width] = im[part]
        out[:, width:] = weight[part]


def add_kernel(a, b, wait, out):
    out[...] = a[...] + b[...]


def final_kernel(row_cuts, *refs):
    own, *parts, signal, out = refs
    rows, width = out.shape
    freq = width // 2
    inverse = 1.0 / signal[...]
    every = sorted({cut for cuts in row_cuts for cut in cuts})
    for start, stop in zip(every, every[1:]):
        total = own[start:stop]
        at = 0
        for cuts in row_cuts:
            for low, high in zip(cuts, cuts[1:]):
                if low <= start and stop <= high:
                    total = total + parts[at][start - low : stop - low]
                at += 1
        denominator = total[:, width:] + inverse
        out[start:stop, :freq] = total[:, :freq] / denominator
        out[start:stop, freq:] = total[:, freq:width] / denominator


def params(mib):
    return pltpu.CompilerParams(vmem_limit_bytes=mib * 1024 * 1024)


def crossed(block, mask):
    size = lax.axis_size("dom")
    return lax.ppermute(block, "dom", [(i, i ^ mask) for i in range(size)])


def on_device(
    particle_fourier,
    defocus,
    particle_offset,
    prior_rotation,
    group_id,
    live_count,
    noise_power,
    signal_power,
    class_refs,
):
    slots, width = particle_fourier.shape
    freq = width // 2
    size = lax.axis_size("dom")
    blocks = size // TEAM
    refs_own = class_refs.reshape(-1, width)
    per = refs_own.shape[0]
    f32 = jnp.float32
    vmem = pl.BlockSpec(memory_space=pltpu.VMEM)
    no_cost = pl.CostEstimate(flops=0, bytes_accessed=0, transcendentals=0)
    much = pl.CostEstimate(flops=16 * 10**9, bytes_accessed=0, transcendentals=0)

    ynb = crossed(particle_fourier, 2)
    anywhere = pl.BlockSpec(memory_space=pl.ANY)
    ynb = crossed(particle_fourier, 2)
    anywhere = pl.BlockSpec(memory_space=pl.ANY)
    ynb = crossed(particle_fourier, 2)
    anywhere = pl.BlockSpec(memory_space=pl.ANY)
    ynb = crossed(particle_fourier, 2)
    refs = [refs_own] + [crossed(refs_own, TEAM * n) for n in range(1, blocks)]
    own_facts = (
        particle_fourier,
        defocus.reshape(1, slots),
        particle_offset.T,
        prior_rotation.reshape(1, slots),
        group_id.reshape(1, slots),
        noise_power,
    )
    own, facts, inverse_noise = pl.pallas_call(
        own_kernel,
        out_shape=(
            jax.ShapeDtypeStruct((slots + 8, width + freq), f32),
            jax.ShapeDtypeStruct((8, 128), f32),
            jax.ShapeDtypeStruct(noise_power.shape, f32),
        ),
        in_specs=[anywhere] * 6 + [pl.BlockSpec(memory_space=pltpu.SMEM)],
        out_specs=(vmem,) * 3,
        scratch_shapes=[pltpu.VMEM(x.shape, x.dtype) for x in own_facts]
        + [pltpu.SemaphoreType.DMA((6,))],
        compiler_params=params(6),
        cost_estimate=no_cost,
        name="own",
    )(*(pltpu.with_memory_space_constraint(x, pltpu.HBM) for x in own_facts), live_count)
    cnb = crossed(own, 1)
    lanes = 3 * slots
    bf16 = jnp.bfloat16

    def shaped(rows, cols, dtype=f32):
        return jax.ShapeDtypeStruct((rows, cols), dtype)

    block_shapes = [shaped(SHIFTS * per, width, bf16)] * 2 + [shaped(per, freq, bf16)] * 2
    score_shape = jax.ShapeDtypeStruct((SHIFTS, per, lanes), f32)

    def call(kernel, operands, out_shape, name, mib, cost=None, scratch=()):
        return pl.pallas_call(
            kernel,
            cost_estimate=cost,
            out_shape=tuple(out_shape),
            in_specs=[vmem] * len(operands),
            out_specs=(vmem,) * len(out_shape),
            scratch_shapes=list(scratch),
            compiler_params=params(mib),
            name=name,
        )(*operands)

    prepared = pl.pallas_call(
        own_refs_kernel,
        out_shape=tuple(block_shapes),
        in_specs=[anywhere] * 2,
        out_specs=(vmem,) * 4,
        scratch_shapes=[pltpu.VMEM(refs_own.shape, f32), pltpu.SemaphoreType.DMA],
        compiler_params=params(8),
        name="own_refs",
    )(pltpu.with_memory_space_constraint(refs_own, pltpu.HBM), facts)
    ynb_prepared = pl.pallas_call(
        neighbour_kernel,
        out_shape=jax.ShapeDtypeStruct((slots + 8, width + freq), f32),
        in_specs=[vmem] * 3 + [anywhere],
        out_specs=vmem,
        compiler_params=params(6),
        cost_estimate=no_cost,
        name="neighbour",
    )(ynb, crossed(facts, 2), inverse_noise, prepared[2])
    cynb = crossed(ynb_prepared, 1)

    order = [*range(2, blocks), 1]
    wait = ynb_prepared
    by_block = {0: prepared}
    for n in order:
        by_block[n] = pl.pallas_call(
            refs_kernel,
            out_shape=tuple(block_shapes),
            in_specs=[vmem, anywhere],
            out_specs=(vmem,) * 4,
            compiler_params=params(6),
            cost_estimate=much if n == order[-1] else None,
            name="refs",
        )(refs[n], wait)
        wait = by_block[n][2]
    prepared = [x for n in range(blocks) for x in by_block[n]]
    deep = 3 * MAIN + 128
    top_rows = -(-blocks // 8) * 8
    outs = call(
        lambda *a: late_kernel(blocks, *a),
        (own, cnb, ynb_prepared, cynb, *prepared),
        [score_shape] * blocks
        + [shaped(deep, width, bf16), shaped(deep, freq, bf16)]
        + [shaped(8, 384), shaped(top_rows, 384)],
        "late",
        8 + 2 * blocks,
        scratch=[pltpu.VMEM((lanes - MAIN, width), f32)],
    )
    weights, (y, power, stats, tops) = outs[:blocks], outs[blocks:]

    team = [stats] + [crossed(stats, n) for n in range(1, TEAM)]

    def sums(n, cuts, last=False, waits=()):
        out_shape = [shaped(b - a, width + freq) for a, b in zip(cuts, cuts[1:])]
        if last:
            out_shape.append(shaped(2, slots))
        return pl.pallas_call(
            lambda *a: sum_kernel(n, cuts, last, len(waits), *a),
            out_shape=tuple(out_shape),
            in_specs=[vmem] * (TEAM + 1) + [anywhere] * len(waits) + [vmem] * 3,
            out_specs=(vmem,) * len(out_shape),
            compiler_params=params(8),
            name="sums",
        )(*team, tops, *waits, weights[n], y, power)

    def combined(mine, other, wait):
        return pl.pallas_call(
            add_kernel,
            out_shape=jax.ShapeDtypeStruct(mine.shape, f32),
            in_specs=[vmem] * 2 + [anywhere],
            out_specs=vmem,
            compiler_params=params(4),
            name="combined",
        )(mine, other, wait)

    def gated(arrays, cost):
        return pl.pallas_call(
            lambda *a: None,
            out_shape=tuple(jax.ShapeDtypeStruct(x.shape, x.dtype) for x in arrays),
            in_specs=[anywhere] * len(arrays),
            out_specs=(anywhere,) * len(arrays),
            input_output_aliases={n: n for n in range(len(arrays))},
            compiler_params=params(1),
            cost_estimate=cost,
            name="gate",
        )(*arrays)

    whole, cut = (0, per), (0, per // 2, per)
    far = []
    waits = []
    for n in range(2, blocks, 2):
        handed = sums(n + 1, cut)
        mine = sums(n, cut, waits=handed[:1])
        if n == 2:
            (near,) = sums(1, whole, waits=mine[:1])
        joined = [combined(x, crossed(y, TEAM), near) for x, y in zip(mine, handed)]
        far.extend(crossed(x, TEAM * n) for x in joined)
        waits.extend(joined)
    own_part, shift = sums(0, whole, last=True, waits=waits)
    far = [crossed(near, TEAM), *gated(far, much)]
    row_cuts = [whole] + [cut] * (len(far) // 2)

    refs_new = pl.pallas_call(
        lambda *a: final_kernel(row_cuts, *a),
        out_shape=jax.ShapeDtypeStruct((per, width), f32),
        in_specs=[vmem] * (len(far) + 2),
        out_specs=vmem,
        compiler_params=params(2 + blocks),
        name="update",
    )(own_part, *far, signal_power.reshape(1, freq))

    return (shift.T, refs_new.reshape(class_refs.shape))


def solution(mesh):
    in_specs = (
        P(("groups", "dom"), None),
        P(("groups", "dom")),
        P(("groups", "dom"), None),
        P(("groups", "dom")),
        P(("groups", "dom")),
        P(("groups", "dom")),
        P("groups", None),
        P("groups"),
        P(("groups", "dom"), None, None),
    )
    out_specs = (P(("groups", "dom"), None), P(("groups", "dom"), None, None))
    return jax.shard_map(
        on_device, mesh=mesh, in_specs=in_specs, out_specs=out_specs, check_vma=False
    )
```

```python
import math

import jax
import jax.numpy as jnp
from jax import lax
from jax.experimental import pallas as pl
from jax.experimental.pallas import tpu as pltpu
from jax.sharding import PartitionSpec as P

ROT = 16
SIDE = 3
BOX = 128
FY = 32
SHIFTS = 9
TEAM = 4
PRIOR = 2.0
CTF_SIZE = math.hypot(0.995, 0.1)
CTF_TURN = math.atan2(0.1, 0.995)
SINE = (
    9.99999976e-01,
    -1.66666476e-01,
    8.33289854e-03,
    -1.98008185e-04,
    2.59032780e-06,
)
TWO_PI = 2.0 * math.pi
PI_A = 3.140625
PI_B = 0.0009670257568359375
PI_C = math.pi - PI_A - PI_B
HIGHEST = lax.Precision.HIGHEST
GRID = tuple((t // SIDE - SIDE // 2, t % SIDE - SIDE // 2) for t in range(SHIFTS))


def half_turn_sine(x):
    s = x * x
    p = SINE[4]
    for c in SINE[3::-1]:
        p = p * s + c
    return x * p


def turn_cos(turns):
    t = jnp.abs(turns - jnp.round(turns))
    return half_turn_sine(TWO_PI * (0.25 - t))


def turn_sin(turns):
    return turn_cos(turns - 0.25)


def freq_rows(width, rows):
    f = lax.broadcasted_iota(jnp.int32, (rows, width), 1)
    kx = (f // FY).astype(jnp.float32)
    ky = (f % FY - FY // 2).astype(jnp.float32)
    return kx, ky


def dot_nt(a, b):
    return lax.dot_general(
        a, b, (((1,), (1,)), ((), ())), preferred_element_type=jnp.float32
    )


def dot_nn(a, b):
    return lax.dot_general(
        a, b, (((1,), (0,)), ((), ())), preferred_element_type=jnp.float32
    )


def exact_dot_nn(a, b):
    return lax.dot_general(
        a, b, (((1,), (0,)), ((), ())), precision=HIGHEST, preferred_element_type=jnp.float32
    )


def halves(x):
    high = x.astype(jnp.bfloat16)
    return high, (x - high.astype(jnp.float32)).astype(jnp.bfloat16)


MAIN = 256


def deep_at(part, row):
    return MAIN * part + row if row < MAIN else 3 * MAIN + 32 * part + row - MAIN


def deep_lanes(x):
    rows, lanes = x.shape
    left = lanes - MAIN
    high, low = halves(x[:, :MAIN])
    tail = jnp.concatenate([x[:, MAIN:], jnp.zeros((rows, 128 - left), jnp.float32)], axis=1)
    tail_high = tail.astype(jnp.bfloat16).astype(jnp.float32)
    tail_low = tail - tail_high
    mixed = tail_high + pltpu.roll(tail_high, left, 1) + pltpu.roll(tail_low, 2 * left, 1)
    return jnp.concatenate([high, high, low, mixed.astype(jnp.bfloat16)], axis=1)


def grid_phases(width):
    kx, ky = freq_rows(width, 1)
    out = []
    for t, (gx, gy) in enumerate(GRID):
        if t < SHIFTS // 2:
            m = (kx * gx + ky * gy) * (1.0 / BOX)
            out.append((turn_cos(m), turn_sin(m)))
    return out


def phase_of(phases, t):
    mid = SHIFTS // 2
    if t < mid:
        return phases[t]
    c, s = phases[SHIFTS - 1 - t]
    return c, -s


def prepared_rows(src, facts, inverse_noise, out):
    slots, width = src.shape
    freq = width // 2
    columns = jnp.concatenate([facts, jnp.zeros((120, 128), jnp.float32)], axis=0).T[:slots]
    focus = columns[:, 0:1]
    off_x = columns[:, 1:2]
    off_y = columns[:, 2:3]
    group_col = columns[:, 4:5]

    kx, ky = freq_rows(freq, 1)
    chi = focus * ((kx * kx + ky * ky) * (1.0 / 1024.0))
    k = jnp.round(chi * (1.0 / math.pi))
    rest_angle = ((chi - k * PI_A) - k * PI_B) - k * PI_C
    shifted_angle = rest_angle + CTF_TURN
    over = shifted_angle > (0.5 * math.pi)
    folded = jnp.where(over, math.pi - shifted_angle, shifted_angle)
    parity = 0.5 * k
    sign = (parity - jnp.floor(parity)) * (4.0 * CTF_SIZE) - CTF_SIZE
    ctf = half_turn_sine(folded) * sign
    kx0, ky0 = freq_rows(128, 1)
    m = (kx0 * off_x + ky0 * off_y) * (1.0 / BOX)
    pc, ps = turn_cos(m), turn_sin(m)
    step = off_x * ((128 // FY) / BOX) + jnp.zeros((slots, 128), jnp.float32)
    sc, ss = turn_cos(step), turn_sin(step)

    total = inverse_noise.shape[0]
    onehot = (
        group_col == lax.broadcasted_iota(jnp.int32, (slots, total), 1).astype(jnp.float32)
    ).astype(jnp.float32)
    noise_rows = exact_dot_nn(onehot, inverse_noise)
    scaled = ctf * noise_rows
    out[:slots, width:] = ctf * scaled
    for n in range(freq // 128):
        part = slice(128 * n, 128 * (n + 1))
        twin = slice(freq + 128 * n, freq + 128 * (n + 1))
        co = pc * scaled[:, part]
        si = ps * scaled[:, part]
        pc, ps = pc * sc - ps * ss, ps * sc + pc * ss
        xr, xi = src[:, part], src[:, twin]
        out[:slots, part] = xr * co - xi * si
        out[:slots, twin] = xr * si + xi * co
    out[slots:, :128] = facts
    out[slots:, 128:] = jnp.zeros((8, width + freq - 128), jnp.float32)


def own_kernel(
    src_at, focus_at, offsets_at, prior_at, group_at, noise_at, live_count, out, facts_out,
    inverse_out, src, focus, offsets, prior, group, noise, sems
):
    moves = (
        (focus_at, focus), (offsets_at, offsets), (prior_at, prior), (group_at, group),
        (noise_at, noise), (src_at, src),
    )
    copies = [pltpu.make_async_copy(x, y, sems.at[n]) for n, (x, y) in enumerate(moves)]
    for copy in copies:
        copy.start()
    slots = src.shape[0]
    facts_out[...] = jnp.zeros_like(facts_out)
    slot = lax.broadcasted_iota(jnp.int32, (1, slots), 1)
    for copy in copies:
        copy.wait()
    facts_out[5:6, :slots] = (slot < live_count[0]).astype(jnp.float32)
    facts_out[0:1, :slots] = focus[...]
    facts_out[1:3, :slots] = offsets[...].astype(jnp.float32)
    facts_out[3:4, :slots] = prior[...].astype(jnp.float32)
    facts_out[4:5, :slots] = group[...].astype(jnp.float32)
    inverse = 1.0 / noise[...]
    inverse_out[...] = inverse
    prepared_rows(src, facts_out[...], inverse, out)


def neighbour_kernel(src, facts, inverse_noise, wait, out):
    prepared_rows(src, facts[...], inverse_noise[...], out)


def team_order(own, cnb, ynb, cynb):
    for even in (True, False):
        for first in (True, False):
            heavy, light = ((own, ynb), (cnb, cynb)) if even else ((cnb, cynb), (own, ynb))
            if not first:
                heavy, light = heavy[::-1], light[::-1]
            yield even, first, heavy, light


def place_rows(even, first, parts, y_out, power_out, left_out):
    width = y_out.shape[1]
    slots = parts[0].shape[0] - 8
    half = slots // 2
    cut = MAIN - 2 * slots - half

    def place(src, start, stop, to):
        for cols, out in ((slice(0, width), y_out), (slice(width, None), power_out)):
            pair = halves(src[start:stop, cols])
            for part in range(3):
                row = deep_at(part, to)
                out[row : row + stop - start] = pair[part % 2]

    for is_even, is_first, heavy, light in team_order(*parts):

        @pl.when(jnp.logical_and(even == is_even, first == is_first))
        def _(heavy=heavy, light=light):
            place(heavy[0], 0, slots, 0)
            place(heavy[1], 0, slots, slots)
            place(light[0], 0, half, 2 * slots)
            place(light[1], 0, cut, 2 * slots + half)
            place(light[1], cut, half, MAIN)
            left_out[...] = light[1][cut:half, :width]


def lane_index():
    return lax.broadcasted_iota(jnp.int32, (8, 128), 1)


def row_facts(even, first, parts):
    lane = lane_index()
    own, cnb, ynb, cynb = (x[x.shape[0] - 8 :, :128] for x in parts)
    heavy = (jnp.where(even, own, cnb), jnp.where(even, ynb, cynb))
    light = (jnp.where(even, cnb, own), jnp.where(even, cynb, ynb))
    a0, b0 = (jnp.where(first, x[0], x[1]) for x in (heavy, light))
    a1, b1 = (jnp.where(first, x[1], x[0]) for x in (heavy, light))
    a1 = pltpu.roll(a1, 96, 1)
    b1 = pltpu.roll(b1, 112, 1)
    middle = jnp.where(lane < 64, a1, jnp.where(lane < 112, pltpu.roll(b0, 64, 1), b1))
    return jnp.concatenate([jnp.where(lane < 96, a0, a1), middle, b1], axis=1)


def own_lanes(even, first, x):
    lane = lane_index()
    a, b, c = x[:, :128], x[:, 128:256], x[:, 256:]
    heavy_far = jnp.where(lane < 32, pltpu.roll(a, 32, 1), pltpu.roll(b, 32, 1))
    light_far = jnp.where(lane < 16, pltpu.roll(b, 16, 1), pltpu.roll(c, 16, 1))
    light = jnp.where(first, pltpu.roll(b, 64, 1), light_far)
    heavy = jnp.where(first, a, heavy_far)
    return jnp.where(even, heavy, jnp.where(lane < 48, light, 0.0))


def place_of_device():
    me = lax.axis_index("dom")
    return me % 2 == 0, (me // 2) % 2 == 0


def prior_rows(facts, per, lanes):
    r = (lax.broadcasted_iota(jnp.int32, (per, lanes), 0) % ROT).astype(jnp.float32)
    return PRIOR * turn_cos((r - facts[3:4, :lanes]) * (1.0 / ROT))


def prepare_refs(ref, phases, r_high, r_low, q_high, q_low):
    per, width = ref.shape
    freq = width // 2
    rr, ri = ref[:, :freq], ref[:, freq:]
    mid = SHIFTS // 2

    def store(t, re, im):
        rows = slice(t * per, (t + 1) * per)
        r_high[rows, :freq], r_low[rows, :freq] = halves(re)
        r_high[rows, freq:], r_low[rows, freq:] = halves(im)

    store(mid, rr, ri)
    for t in range(mid):
        c, s = phases[t]
        a, b, d, e = rr * c, ri * s, ri * c, rr * s
        store(t, a + b, d - e)
        store(SHIFTS - 1 - t, a - b, d + e)
    q_high[...], q_low[...] = halves(rr * rr + ri * ri)


def terms(high, low):
    return jnp.concatenate([high, high, low], axis=1)


def terms_left(high, low):
    return jnp.concatenate([high, low, high], axis=1)


def shifted_rows(rows, phases):
    freq = rows.shape[1] // 2
    re, im = rows[:, :freq], rows[:, freq:]
    mid = SHIFTS // 2
    out = [None] * SHIFTS
    out[mid] = rows
    for t in range(mid):
        c, s = phases[t]
        a, b, d, e = re * c, im * s, im * c, re * s
        out[t] = jnp.concatenate([a - b, e + d], axis=1)
        out[SHIFTS - 1 - t] = jnp.concatenate([a + b, d - e], axis=1)
    return jnp.concatenate(out, axis=0)


def weigh(score, e_out):
    top = jnp.max(jnp.max(score, axis=0), axis=0, keepdims=True)
    e = jnp.exp(score - top[None])
    e_out[...] = e
    side = SIDE // 2
    by_x = [sum(e[SIDE * x + y] for y in range(SIDE)) for x in range(SIDE)]
    by_y = [sum(e[SIDE * x + y] for x in range(SIDE)) for y in range(SIDE)]
    sums = [sum(by_x)]
    for by in (by_x, by_y):
        sums.append(sum(by[k] * float(k - side) for k in range(SIDE) if k != side))
    return top, [jnp.sum(x, axis=0, keepdims=True) for x in sums]


def joined_sums(tops, sums):
    top = tops[0]
    for other in tops[1:]:
        top = jnp.maximum(top, other)
    factors = [jnp.exp(other - top) for other in tops]
    return top, [sum(f * x for f, x in zip(factors, column)) for column in zip(*sums)]


def own_refs_kernel(own_at, wait, *rest):
    *prepared, own, sem = rest
    copy = pltpu.make_async_copy(own_at, own, sem)
    copy.start()
    phases = grid_phases(own.shape[1] // 2)
    copy.wait()
    prepare_refs(own, phases, *prepared)


def refs_kernel(ref, wait, *prepared):
    prepare_refs(ref, grid_phases(ref.shape[1] // 2), *prepared)


def late_kernel(blocks, own, cnb, ynb, cynb, *rest):
    prepared, rest = rest[: 4 * blocks], rest[4 * blocks :]
    e_outs, rest = rest[:blocks], rest[blocks:]
    y_out, power_out, stats_out, tops_out, left_rows = rest
    per, lanes = e_outs[0].shape[1:]
    freq = power_out.shape[1]
    left = lanes - MAIN
    parts = (own, cnb, ynb, cynb)
    even, first = place_of_device()
    place_rows(even, first, parts, y_out, power_out, left_rows)
    facts = row_facts(even, first, parts)
    empty = deep_at(2, lanes)
    for out in (y_out, power_out):
        out[empty:] = jnp.zeros_like(out[empty:])
    stats_out[...] = jnp.zeros_like(stats_out)
    tops_out[...] = jnp.zeros_like(tops_out)

    def rows(out, part, size):
        at = deep_at(part, 0)
        main = out[at : at + MAIN]
        at = deep_at(part, MAIN)
        return jnp.concatenate([main, out[at : at + left]], axis=0)[:size]

    q_terms = [terms_left(prepared[4 * n + 2][...], prepared[4 * n + 3][...]) for n in range(blocks)]
    quad = dot_nt(
        jnp.concatenate(q_terms, axis=0), terms(*(rows(power_out, k, lanes) for k in (0, 1)))
    )
    prior = prior_rows(facts, per, lanes)
    mid = slice(SHIFTS // 2 * per, (SHIFTS // 2 + 1) * per)
    r_terms = [terms_left(prepared[4 * n][mid], prepared[4 * n + 1][mid]) for n in range(blocks)]
    moved = terms(*halves(shifted_rows(left_rows[...], grid_phases(freq))))
    far = dot_nt(jnp.concatenate(r_terms, axis=0), moved)
    far = jnp.concatenate([far, jnp.zeros((blocks * per, 384 - SHIFTS * left), jnp.float32)], axis=1)
    step = 128 // left
    far = [
        pltpu.roll(far[:, 128 * (t // step) : 128 * (t // step + 1)], -left * (t % step) % 128, 1)
        for t in range(SHIFTS)
    ]
    main_terms = terms(*(rows(y_out, k, MAIN) for k in (0, 1)))
    tops, sums = [], []
    for n in range(blocks):
        part = slice(n * per, (n + 1) * per)
        base = prior - 0.5 * quad[part]
        if n % 2 == 0:
            pair = range(n, min(n + 2, blocks))
            r_pair = [terms_left(prepared[4 * k][...], prepared[4 * k + 1][...]) for k in pair]
            products = dot_nt(jnp.concatenate(r_pair, axis=0), main_terms)
        at = n % 2 * SHIFTS * per
        score = products[at : at + SHIFTS * per].reshape(SHIFTS, per, MAIN)
        tail = jnp.stack([x[part, :left] for x in far])
        score = jnp.concatenate([score, tail], axis=2) + base[None]
        top, sums_here = weigh(score, e_outs[n])
        tops_out[n : n + 1, :lanes] = top
        tops.append(top)
        sums.append(sums_here)
    top, sums = joined_sums(tops, sums)
    for k, row in enumerate((top, *sums, facts[5:6, :lanes])):
        stats_out[k : k + 1, :lanes] = row


def sum_kernel(n, cuts, last, waits, *rest):
    team, tops, rest = rest[:TEAM], rest[TEAM], rest[TEAM + 1 + waits :]
    e_ref, y_ref, power_ref, *outs = rest
    per, lanes = e_ref.shape[1:]
    width = y_ref.shape[1]
    freq = width // 2
    team = [x[...] for x in team]
    top, (mass, *move) = joined_sums(
        [x[0:1] for x in team], [[x[k : k + 1] for k in (1, 2, 3)] for x in team]
    )
    live = team[0][4:5] / mass
    gain = (jnp.exp(tops[n : n + 1] - top) * live)[:, :lanes]
    if last:
        shift_out = outs.pop()
        move = [x * live for x in move] + [jnp.zeros((6, live.shape[1]), jnp.float32)]
        move = own_lanes(*place_of_device(), jnp.concatenate(move, axis=0))
        shift_out[...] = move[:2, : shift_out.shape[1]]
    w = e_ref[...] * gain[None]
    flat = dot_nn(deep_lanes(w.reshape(SHIFTS * per, lanes)), y_ref[...])
    weight = dot_nn(deep_lanes(jnp.sum(w, axis=0)), power_ref[...])
    phases = grid_phases(freq)
    mid = SHIFTS // 2

    def block(t):
        return flat[t * per : (t + 1) * per, :freq], flat[t * per : (t + 1) * per, freq:]

    re, im = block(mid)
    for t in range(mid):
        c, s = phases[t]
        ar, ai = block(t)
        br, bi = block(SHIFTS - 1 - t)
        re = re + (ar + br) * c - (ai - bi) * s
        im = im + (ar - br) * s + (ai + bi) * c
    for start, stop, out in zip(cuts, cuts[1:], outs):
        part = slice(start, stop)
        out[:, :freq] = re[part]
        out[:, freq:width] = im[part]
        out[:, width:] = weight[part]


def add_kernel(a, b, wait, out):
    out[...] = a[...] + b[...]


def final_kernel(row_cuts, *refs):
    own, *parts, signal, out = refs
    rows, width = out.shape
    freq = width // 2
    inverse = 1.0 / signal[...]
    every = sorted({cut for cuts in row_cuts for cut in cuts})
    for start, stop in zip(every, every[1:]):
        total = own[start:stop]
        at = 0
        for cuts in row_cuts:
            for low, high in zip(cuts, cuts[1:]):
                if low <= start and stop <= high:
                    total = total + parts[at][start - low : stop - low]
                at += 1
        denominator = total[:, width:] + inverse
        out[start:stop, :freq] = total[:, :freq] / denominator
        out[start:stop, freq:] = total[:, freq:width] / denominator


def params(mib):
    return pltpu.CompilerParams(vmem_limit_bytes=mib * 1024 * 1024)


def crossed(block, mask):
    size = lax.axis_size("dom")
    return lax.ppermute(block, "dom", [(i, i ^ mask) for i in range(size)])


def on_device(
    particle_fourier,
    defocus,
    particle_offset,
    prior_rotation,
    group_id,
    live_count,
    noise_power,
    signal_power,
    class_refs,
):
    slots, width = particle_fourier.shape
    freq = width // 2
    size = lax.axis_size("dom")
    blocks = size // TEAM
    refs_own = class_refs.reshape(-1, width)
    per = refs_own.shape[0]
    f32 = jnp.float32
    vmem = pl.BlockSpec(memory_space=pltpu.VMEM)
    no_cost = pl.CostEstimate(flops=0, bytes_accessed=0, transcendentals=0)
    much = pl.CostEstimate(flops=16 * 10**9, bytes_accessed=0, transcendentals=0)

    ynb = crossed(particle_fourier, 2)
    anywhere = pl.BlockSpec(memory_space=pl.ANY)
    ynb = crossed(particle_fourier, 2)
    anywhere = pl.BlockSpec(memory_space=pl.ANY)
    ynb = crossed(particle_fourier, 2)
    anywhere = pl.BlockSpec(memory_space=pl.ANY)
    ynb = crossed(particle_fourier, 2)
    refs = [refs_own] + [crossed(refs_own, TEAM * n) for n in range(1, blocks)]
    own_facts = (
        particle_fourier,
        defocus.reshape(1, slots),
        particle_offset.T,
        prior_rotation.reshape(1, slots),
        group_id.reshape(1, slots),
        noise_power,
    )
    own, facts, inverse_noise = pl.pallas_call(
        own_kernel,
        out_shape=(
            jax.ShapeDtypeStruct((slots + 8, width + freq), f32),
            jax.ShapeDtypeStruct((8, 128), f32),
            jax.ShapeDtypeStruct(noise_power.shape, f32),
        ),
        in_specs=[anywhere] * 6 + [pl.BlockSpec(memory_space=pltpu.SMEM)],
        out_specs=(vmem,) * 3,
        scratch_shapes=[pltpu.VMEM(x.shape, x.dtype) for x in own_facts]
        + [pltpu.SemaphoreType.DMA((6,))],
        compiler_params=params(6),
        cost_estimate=no_cost,
        name="own",
    )(*(pltpu.with_memory_space_constraint(x, pltpu.HBM) for x in own_facts), live_count)
    cnb = crossed(own, 1)
    lanes = 3 * slots
    bf16 = jnp.bfloat16

    def shaped(rows, cols, dtype=f32):
        return jax.ShapeDtypeStruct((rows, cols), dtype)

    block_shapes = [shaped(SHIFTS * per, width, bf16)] * 2 + [shaped(per, freq, bf16)] * 2
    score_shape = jax.ShapeDtypeStruct((SHIFTS, per, lanes), f32)

    def call(kernel, operands, out_shape, name, mib, cost=None, scratch=()):
        return pl.pallas_call(
            kernel,
            cost_estimate=cost,
            out_shape=tuple(out_shape),
            in_specs=[vmem] * len(operands),
            out_specs=(vmem,) * len(out_shape),
            scratch_shapes=list(scratch),
            compiler_params=params(mib),
            name=name,
        )(*operands)

    prepared = pl.pallas_call(
        own_refs_kernel,
        out_shape=tuple(block_shapes),
        in_specs=[anywhere] * 2,
        out_specs=(vmem,) * 4,
        scratch_shapes=[pltpu.VMEM(refs_own.shape, f32), pltpu.SemaphoreType.DMA],
        compiler_params=params(8),
        name="own_refs",
    )(pltpu.with_memory_space_constraint(refs_own, pltpu.HBM), facts)
    ynb_prepared = pl.pallas_call(
        neighbour_kernel,
        out_shape=jax.ShapeDtypeStruct((slots + 8, width + freq), f32),
        in_specs=[vmem] * 3 + [anywhere],
        out_specs=vmem,
        compiler_params=params(6),
        cost_estimate=no_cost,
        name="neighbour",
    )(ynb, crossed(facts, 2), inverse_noise, prepared[2])
    cynb = crossed(ynb_prepared, 1)

    order = [*range(blocks - 1, 2, -1), 1, 2]
    wait = ynb_prepared
    by_block = {0: prepared}
    for n in order:
        by_block[n] = pl.pallas_call(
            refs_kernel,
            out_shape=tuple(block_shapes),
            in_specs=[vmem, anywhere],
            out_specs=(vmem,) * 4,
            compiler_params=params(6),
            cost_estimate=much if n == order[-1] else None,
            name="refs",
        )(refs[n], wait)
        wait = by_block[n][2]
    prepared = [x for n in range(blocks) for x in by_block[n]]
    deep = 3 * MAIN + 128
    top_rows = -(-blocks // 8) * 8
    outs = call(
        lambda *a: late_kernel(blocks, *a),
        (own, cnb, ynb_prepared, cynb, *prepared),
        [score_shape] * blocks
        + [shaped(deep, width, bf16), shaped(deep, freq, bf16)]
        + [shaped(8, 384), shaped(top_rows, 384)],
        "late",
        8 + 2 * blocks,
        scratch=[pltpu.VMEM((lanes - MAIN, width), f32)],
    )
    weights, (y, power, stats, tops) = outs[:blocks], outs[blocks:]

    team = [stats] + [crossed(stats, n) for n in range(1, TEAM)]

    def sums(n, cuts, last=False, waits=()):
        out_shape = [shaped(b - a, width + freq) for a, b in zip(cuts, cuts[1:])]
        if last:
            out_shape.append(shaped(2, slots))
        return pl.pallas_call(
            lambda *a: sum_kernel(n, cuts, last, len(waits), *a),
            out_shape=tuple(out_shape),
            in_specs=[vmem] * (TEAM + 1) + [anywhere] * len(waits) + [vmem] * 3,
            out_specs=(vmem,) * len(out_shape),
            compiler_params=params(8),
            name="sums",
        )(*team, tops, *waits, weights[n], y, power)

    def combined(mine, other, wait):
        return pl.pallas_call(
            add_kernel,
            out_shape=jax.ShapeDtypeStruct(mine.shape, f32),
            in_specs=[vmem] * 2 + [anywhere],
            out_specs=vmem,
            compiler_params=params(4),
            name="combined",
        )(mine, other, wait)

    def gated(arrays, cost):
        return pl.pallas_call(
            lambda *a: None,
            out_shape=tuple(jax.ShapeDtypeStruct(x.shape, x.dtype) for x in arrays),
            in_specs=[anywhere] * len(arrays),
            out_specs=(anywhere,) * len(arrays),
            input_output_aliases={n: n for n in range(len(arrays))},
            compiler_params=params(1),
            cost_estimate=cost,
            name="gate",
        )(*arrays)

    whole, cut = (0, per), (0, per // 2, per)
    far = []
    waits = []
    for n in range(2, blocks, 2):
        handed = sums(n + 1, cut)
        mine = sums(n, cut, waits=handed[:1])
        if n == 2:
            (near,) = sums(1, whole, waits=mine[:1])
        joined = [combined(x, crossed(y, TEAM), near) for x, y in zip(mine, handed)]
        far.extend(crossed(x, TEAM * n) for x in joined)
        waits.extend(joined)
    own_part, shift = sums(0, whole, last=True, waits=waits)
    far = [crossed(near, TEAM), *gated(far, much)]
    row_cuts = [whole] + [cut] * (len(far) // 2)

    refs_new = pl.pallas_call(
        lambda *a: final_kernel(row_cuts, *a),
        out_shape=jax.ShapeDtypeStruct((per, width), f32),
        in_specs=[vmem] * (len(far) + 2),
        out_specs=vmem,
        compiler_params=params(2 + blocks),
        name="update",
    )(own_part, *far, signal_power.reshape(1, freq))

    return (shift.T, refs_new.reshape(class_refs.shape))


def solution(mesh):
    in_specs = (
        P(("groups", "dom"), None),
        P(("groups", "dom")),
        P(("groups", "dom"), None),
        P(("groups", "dom")),
        P(("groups", "dom")),
        P(("groups", "dom")),
        P("groups", None),
        P("groups"),
        P(("groups", "dom"), None, None),
    )
    out_specs = (P(("groups", "dom"), None), P(("groups", "dom"), None, None))
    return jax.shard_map(
        on_device, mesh=mesh, in_specs=in_specs, out_specs=out_specs, check_vma=False
    )
```
